32 devices in a mesh: dp: 8 (over y, x, core), fsdp: 4 (over z).
Axes of the slice: x: 2, y: 2, z: 4, core: 2. Of those that a mesh axis runs over, the one named last changes fastest.
Arguments:
- characters: bfloat16 [32, 512, 16, 256], P(('dp', 'fsdp')), may hold values from -6 to 6
- counts: int32 [32, 512], P(('dp', 'fsdp')), may hold values from 1 to 16
- separators: int32 [32, 512], P(('dp', 'fsdp')), may hold values 0 or 1
- cotangent: bfloat16 [32, 512, 512], P(('dp', 'fsdp')), may hold values from -6 to 6
- char_qkv: bfloat16 [256, 768], P('fsdp', 'dp'), may hold values from -0.375 to 0.375
- char_proj: bfloat16 [256, 256], P('fsdp', 'dp'), may hold values from -0.75 to 0.75
- char_up: bfloat16 [256, 1024], P('fsdp', 'dp'), may hold values from -0.375 to 0.375
- char_down: bfloat16 [1024, 256], P('fsdp', 'dp'), may hold values from -0.1875 to 0.1875
- char_gain_a: bfloat16 [256], P('dp'), may hold values from 0.5 to 1.5
- char_gain_b: bfloat16 [256], P('dp'), may hold values from 0.5 to 1.5
- pool_proj: bfloat16 [256, 512], P('fsdp', 'dp'), may hold values from -1 to 1
- word_qkv: bfloat16 [512, 1536], P('fsdp', 'dp'), may hold values from -0.25 to 0.25
- word_proj: bfloat16 [512, 512], P('fsdp', 'dp'), may hold values from -1 to 1
- word_up: bfloat16 [512, 2048], P('fsdp', 'dp'), may hold values from -0.25 to 0.25
- word_down: bfloat16 [2048, 512], P('fsdp', 'dp'), may hold values from -0.125 to 0.125
- word_gain_a: bfloat16 [512], P('dp'), may hold values from 0.5 to 1.5
- word_gain_b: bfloat16 [512], P('dp'), may hold values from 0.5 to 1.5
Outputs:
- word_out: bfloat16 [32, 512, 512], P(('dp', 'fsdp'))
- char_grad: bfloat16 [32, 512, 16, 256], P(('dp', 'fsdp'))
- grad_char_qkv: float32 [256, 768], P('fsdp', 'dp')
- grad_char_proj: float32 [256, 256], P('fsdp', 'dp')
- grad_char_up: float32 [256, 1024], P('fsdp', 'dp')
- grad_char_down: float32 [1024, 256], P('fsdp', 'dp')
- grad_char_gain_a: float32 [256], P('dp')
- grad_char_gain_b: float32 [256], P('dp')
- grad_pool_proj: float32 [256, 512], P('fsdp', 'dp')
- grad_word_qkv: float32 [512, 1536], P('fsdp', 'dp')
- grad_word_proj: float32 [512, 512], P('fsdp', 'dp')
- grad_word_up: float32 [512, 2048], P('fsdp', 'dp')
- grad_word_down: float32 [2048, 512], P('fsdp', 'dp')
- grad_word_gain_a: float32 [512], P('dp')
- grad_word_gain_b: float32 [512], P('dp')
The draws below stay inside these ranges and needn't reach their ends.
Inputs may be any that keep to these rules, and one draw needn't show every extreme that they name: Character slots at or past a word's counts are padding. `separators`: 1 marks a word that starts a new document in its row.
All inputs are finite; a program needn't handle non-finite values. No bound on the sum of `separators` on one device may be relied on, other than what follows from the above.
Results may differ from the reference program's by a relative error of at most 0.02.
Values may be sent and summed in bfloat16 or wider, within the bound.
A program may use at most 256 MiB of HBM per device.

```python
import jax
import jax.numpy as jnp
from jax import lax

ROW = 512
CHARS = 16
D_C = 256
CHAR_HEADS = 4
FF_C = 1024
D_W = 512
WORD_HEADS = 8
FF_W = 2048
ROWS = 32


def with_ends(values, key, low, largest):
    longest = values.shape.index(max(values.shape))
    spots = []
    for shift in (0, 1):
        where = [jax.random.randint(jax.random.fold_in(key, axis), (), 0, length) for axis, length in enumerate(values.shape)]
        where[longest] = (where[longest] + shift) % values.shape[longest]
        spots.append(tuple(where))
    return values.at[spots[0]].set(low).at[spots[1]].set(largest)


def block_scale(own_key, extent, shards, low, top_value):
    factor_of = 1.0
    for axis_at, blocks in shards:
        steps = jax.random.uniform(jax.random.fold_in(jax.random.fold_in(own_key, 6), axis_at), (blocks,), jnp.float32, low / len(shards), top_value / len(shards))
        factor_of = factor_of * jnp.repeat(jnp.exp(steps), extent[axis_at] // blocks).reshape((-1,) + (1,) * (len(extent) - 1 - axis_at))
    return factor_of


def bell_draw(own_key, shape, deviation, bound, pieces=(), kind=jnp.bfloat16):
    values = deviation * jax.random.normal(own_key, shape, jnp.float32)
    if pieces:
        values = values * block_scale(own_key, shape, pieces, -0.22, 0.18)
    return jnp.clip(values, -bound, bound).astype(kind)


def setup_inputs(seed: int = 0) -> dict:
    key_of = jax.random.split(jax.random.key(seed), 18)
    return {
        "characters": bell_draw(key_of[0], (ROWS, ROW, CHARS, D_C), 1.0, 6.0, ((0, 32),)),
        "counts": with_ends(jax.random.randint(key_of[1], (ROWS, ROW), 1, CHARS + 1), jax.random.fold_in(key_of[1], 1), 1, CHARS).astype(jnp.int32),
        "separators": with_ends((jax.random.randint(key_of[2], (ROWS, ROW), 0, 128) < 1).astype(jnp.int32), jax.random.fold_in(key_of[2], 1), 0, 1),
        "cotangent": bell_draw(key_of[3], (ROWS, ROW, D_W), 1.0, 6.0, ((0, 32),)),
        "char_qkv": bell_draw(key_of[4], (D_C, 3 * D_C), D_C ** -0.5, 0.375, ((0, 4), (1, 8))),
        "char_proj": bell_draw(key_of[5], (D_C, D_C), (D_C // 4) ** -0.5, 0.75, ((0, 4), (1, 8))),
        "char_up": bell_draw(key_of[6], (D_C, FF_C), D_C ** -0.5, 0.375, ((0, 4), (1, 8))),
        "char_down": bell_draw(key_of[7], (FF_C, D_C), FF_C ** -0.5, 0.1875, ((0, 4), (1, 8))),
        "char_gain_a": jnp.clip(1.0 + 0.1 * jax.random.normal(key_of[8], (D_C,), jnp.float32), 0.5, 1.5).astype(jnp.bfloat16),
        "char_gain_b": jnp.clip(1.0 + 0.1 * jax.random.normal(key_of[9], (D_C,), jnp.float32), 0.5, 1.5).astype(jnp.bfloat16),
        "pool_proj": bell_draw(key_of[10], (D_C, D_W), (D_C // 8) ** -0.5, 1.0, ((0, 4), (1, 8))),
        "word_qkv": bell_draw(key_of[11], (D_W, 3 * D_W), D_W ** -0.5, 0.25, ((0, 4), (1, 8))),
        "word_proj": bell_draw(key_of[12], (D_W, D_W), (D_W // 16) ** -0.5, 1.0, ((0, 4), (1, 8))),
        "word_up": bell_draw(key_of[13], (D_W, FF_W), D_W ** -0.5, 0.25, ((0, 4), (1, 8))),
        "word_down": bell_draw(key_of[14], (FF_W, D_W), FF_W ** -0.5, 0.125, ((0, 4), (1, 8))),
        "word_gain_a": jnp.clip(1.0 + 0.1 * jax.random.normal(key_of[15], (D_W,), jnp.float32), 0.5, 1.5).astype(jnp.bfloat16),
        "word_gain_b": jnp.clip(1.0 + 0.1 * jax.random.normal(key_of[16], (D_W,), jnp.float32), 0.5, 1.5).astype(jnp.bfloat16),
    }


EPS = 1e-05
NEGATIVE = -1e+30

@jax.custom_vjp
def low(v):
    return lax.optimization_barrier(v.astype(jnp.bfloat16)).astype(jnp.float32)

@jax.custom_vjp
def low_back(v):
    return v

def low_keep(v):
    return (low(v), None)

def low_pass(kept, grad):
    return (grad,)

def back_keep(v):
    return (v, None)

def back_low(kept, grad):
    return (low(grad),)
low.defvjp(low_keep, low_pass)
low_back.defvjp(back_keep, back_low)

def matmul(left_op, right_op):
    return jnp.dot(left_op, right_op, precision=lax.Precision.HIGHEST, preferred_element_type=jnp.float32)

def layer_norm(values, gain_vec):
    average = lax.optimization_barrier(jnp.mean(values, -1, keepdims=True))
    centred = values - average
    spread = lax.optimization_barrier(jnp.mean(centred * centred, -1, keepdims=True))
    return centred * lax.rsqrt(spread + EPS) * gain_vec

def attend(queries, key_rows, value_rows, allowed, factor):
    scores = low_back(jnp.einsum('bhqe,bhke->bhqk', queries, key_rows, precision=lax.Precision.HIGHEST) * factor)
    scores = jnp.where(allowed[:, None], scores, NEGATIVE)
    highest = lax.optimization_barrier(jnp.max(scores, -1, keepdims=True))
    shifted = jnp.exp(scores - highest)
    weights = low(shifted / lax.optimization_barrier(jnp.sum(shifted, -1, keepdims=True)))
    return jnp.einsum('bhqk,bhke->bhqe', weights, value_rows, precision=lax.Precision.HIGHEST)

def forward(chars_row, params, counts_row, separators_row):
    char_qkv, char_proj, char_up, char_down, char_gain_a, char_gain_b, pool_proj, word_qkv, word_proj, word_up, word_down, word_gain_a, word_gain_b = params
    length, letters, char_width = chars_row.shape
    word_width = pool_proj.shape[1]
    chars_flat = chars_row.reshape(length * letters, char_width)
    normed_a = low(layer_norm(chars_flat, char_gain_a))
    triple = low(low_back(matmul(normed_a, char_qkv)))
    head_size = char_width // CHAR_HEADS
    parts_c = triple.reshape(length, letters, 3, CHAR_HEADS, head_size).transpose(2, 0, 3, 1, 4)
    valid_chars = jnp.arange(letters, dtype=jnp.int32)[None, :] < counts_row[:, None]
    allowed_c = jnp.broadcast_to(valid_chars[:, None, :], (length, letters, letters))
    mixed_c = attend(parts_c[0], parts_c[1], parts_c[2], allowed_c, head_size ** (-0.5))
    mixed_c = low(low_back(mixed_c.transpose(0, 2, 1, 3).reshape(length * letters, char_width)))
    hidden_one = chars_flat + low_back(matmul(mixed_c, char_proj))
    normed_b = low(layer_norm(hidden_one, char_gain_b))
    char_act = low(jax.nn.gelu(low_back(matmul(normed_b, char_up))))
    hidden_two = hidden_one + low_back(matmul(char_act, char_down))
    summed_chars = lax.optimization_barrier(jnp.sum(jnp.where(valid_chars[:, :, None], hidden_two.reshape(length, letters, char_width), 0.0), 1))
    pooled = summed_chars / counts_row[:, None].astype(jnp.float32)
    word_in = low_back(matmul(low(pooled), pool_proj))
    normed_c = low(layer_norm(word_in, word_gain_a))
    triple_w = low(low_back(matmul(normed_c, word_qkv)))
    word_head = word_width // WORD_HEADS
    parts_w = triple_w.reshape(length, 3, WORD_HEADS, word_head).transpose(1, 2, 0, 3)[:, None]
    documents = jnp.cumsum(separators_row, dtype=jnp.int32)
    places = jnp.arange(length, dtype=jnp.int32)
    allowed_w = ((places[None, :] <= places[:, None]) & (documents[None, :] == documents[:, None]))[None]
    mixed_w = attend(parts_w[0], parts_w[1], parts_w[2], allowed_w, word_head ** (-0.5))
    mixed_w = low(low_back(mixed_w[0].transpose(1, 0, 2).reshape(length, word_width)))
    hidden_three = word_in + low_back(matmul(mixed_w, word_proj))
    normed_d = low(layer_norm(hidden_three, word_gain_b))
    word_act = low(jax.nn.gelu(low_back(matmul(normed_d, word_up))))
    return hidden_three + low_back(matmul(word_act, word_down))

def reference(characters, counts, separators, cotangent, char_qkv, char_proj, char_up, char_down, char_gain_a, char_gain_b, pool_proj, word_qkv, word_proj, word_up, word_down, word_gain_a, word_gain_b):
    params = tuple((weight.astype(jnp.float32) for weight in (char_qkv, char_proj, char_up, char_down, char_gain_a, char_gain_b, pool_proj, word_qkv, word_proj, word_up, word_down, word_gain_a, word_gain_b)))

    def one_row(summed, row_data):
        chars_row, counts_row, separators_row, cotangent_row = row_data

        def apply_row(chars_in, params_in):
            return forward(chars_in, params_in, counts_row, separators_row)
        output, pullback = jax.vjp(apply_row, chars_row.astype(jnp.float32), params)
        grad_chars, grad_params = pullback(cotangent_row.astype(jnp.float32))
        summed = tuple((earlier + added for earlier, added in zip(summed, grad_params)))
        return (summed, (output.astype(jnp.bfloat16), grad_chars.astype(jnp.bfloat16)))
    zero_sums = tuple((jnp.zeros(weight.shape, jnp.float32) for weight in params))
    grad_sums, outputs = lax.scan(one_row, zero_sums, (characters, counts, separators, cotangent))
    return (outputs[0], outputs[1], grad_sums[0], grad_sums[1], grad_sums[2], grad_sums[3], grad_sums[4], grad_sums[5], grad_sums[6], grad_sums[7], grad_sums[8], grad_sums[9], grad_sums[10], grad_sums[11], grad_sums[12])
```

```python
import functools

import jax
import jax.numpy as jnp
from jax import lax
from jax.experimental import pallas as pl
from jax.experimental.pallas import tpu as pltpu
from jax.sharding import PartitionSpec as P

CHAR_HEADS = 4
WORD_HEADS = 8
EPS = 1e-05
NEGATIVE = -1e30
LANES = 128
SPAN = 256
STEP = 512
GELU_A = 0.7978845608028654
GELU_B = 0.044715

bf16 = jnp.bfloat16
f32 = jnp.float32


def dot(a, b):
    return jnp.dot(a, b, preferred_element_type=f32)


def dot_nt(a, b):
    return lax.dot_general(a, b, (((1,), (1,)), ((), ())), preferred_element_type=f32)


def normed(v):
    c = v - jnp.mean(v, 0, keepdims=True)
    rs = lax.rsqrt(jnp.mean(c * c, 0, keepdims=True) + EPS)
    return c * rs, rs


def wide(g, n):
    return g if n == g.shape[1] else jnp.concatenate([g] * (n // g.shape[1]), 1)


def gelu_both(u):
    s = u * u
    t = jnp.tanh(u * (GELU_A + (GELU_A * GELU_B) * s))
    h = 0.5 * u
    r = 0.5 + 0.5 * t
    slope = r + h * (1.0 - t * t) * (GELU_A + (3.0 * GELU_A * GELU_B) * s)
    return u * r, slope


def lane_word(letters):
    return lax.broadcasted_iota(jnp.int32, (letters, LANES), 1) // letters


def pick_own(full, owner, letters):
    words = LANES // letters
    out = full[:letters]
    for w in range(1, words):
        out = jnp.where(owner == w, full[w * letters : (w + 1) * letters], out)
    return out


def own_blocks(letters):
    a = lax.broadcasted_iota(jnp.int32, (LANES, LANES), 0) // letters
    b = lax.broadcasted_iota(jnp.int32, (LANES, LANES), 1) // letters
    return jnp.where(a == b, 1.0, 0.0).astype(bf16)


def spread_own(compact, blocks, letters):
    return jnp.concatenate([compact] * (LANES // letters), 0) * blocks


def char_forward_kernel(
    letters, x_ref, tok_ref, cnt_ref, ga_ref, gb_ref, wqkv_ref, wproj_ref, wup_ref, wdown_ref,
    t_ref, o_ref, p_ref, z1_ref, rs1_ref, z2_ref, rs2_ref, m_ref, gp_ref, pool_ref,
):
    step = pl.program_id(0)
    width = x_ref.shape[1]
    head = width // CHAR_HEADS
    scale = head ** (-0.5)
    steps_per_block = LANES * letters // STEP
    owner = lane_word(letters)
    blocks = own_blocks(letters)
    key_slot = lax.broadcasted_iota(jnp.int32, (letters, LANES), 0)

    @pl.when(step % steps_per_block == 0)
    def _():
        pool_ref[...] = jnp.zeros_like(pool_ref)

    for part in range(STEP // SPAN):
        at = pl.ds(part * SPAN, SPAN)
        x = x_ref[at, :].astype(f32).T
        z1, rs1 = normed(x)
        z1_ref[0, :, at] = z1.astype(bf16)
        rs1_ref[0, :, at] = rs1
        a1 = (z1 * wide(ga_ref[...], SPAN)).astype(bf16)
        for n in range(3):
            rows = pl.ds(n * width, width)
            t_ref[0, rows, at] = dot(wqkv_ref[rows, :], a1).astype(bf16)
        for g in range(SPAN // LANES):
            lanes = pl.ds(part * SPAN + g * LANES, LANES)
            allowed = key_slot < tok_ref[0, :, lanes]
            for h in range(CHAR_HEADS):
                q = t_ref[0, pl.ds(h * head, head), lanes]
                k = t_ref[0, pl.ds(width + h * head, head), lanes]
                v = t_ref[0, pl.ds(2 * width + h * head, head), lanes]
                full = dot(k.T, q)
                s = jnp.where(allowed, pick_own(full, owner, letters) * scale, NEGATIVE)
                e = jnp.exp(s - jnp.max(s, 0, keepdims=True))
                p = e / jnp.sum(e, 0, keepdims=True)
                p_ref[0, pl.ds(h * letters, letters), lanes] = p
                o = dot(v, spread_own(p.astype(bf16), blocks, letters))
                o_ref[0, pl.ds(h * head, head), lanes] = o.astype(bf16)
        h1 = x + dot(wproj_ref[...], o_ref[0, :, at])
        z2, rs2 = normed(h1)
        z2_ref[0, :, at] = z2.astype(bf16)
        rs2_ref[0, :, at] = rs2
        a2 = (z2 * wide(gb_ref[...], SPAN)).astype(bf16)
        for n in range(wup_ref.shape[0] // 256):
            rows = pl.ds(n * 256, 256)
            m, gp = gelu_both(dot(wup_ref[rows, :], a2))
            m_ref[0, rows, at] = m.astype(bf16)
            gp_ref[0, rows, at] = gp.astype(bf16)
        h2 = h1 + dot(wdown_ref[...], m_ref[0, :, at])
        high = h2.astype(bf16)
        low = (h2 - high.astype(f32)).astype(bf16)
        row = lax.broadcasted_iota(jnp.int32, (SPAN, LANES), 0)
        word = lax.broadcasted_iota(jnp.int32, (SPAN, LANES), 1)
        first = (step % steps_per_block) * (STEP // letters) + part * (SPAN // letters)
        mine = (row // letters + first == word) & (row % letters < cnt_ref[...])
        gather = jnp.where(mine, 1.0, 0.0).astype(bf16)
        pool_ref[...] += dot(high, gather) + dot(low, gather)


def full_spec(a):
    nd = len(a.shape)
    return pl.BlockSpec(a.shape, lambda i: (0,) * nd)


def char_forward(x, tok, cnt, ga, gb, wqkv_t, wproj_t, wup_t, wdown_t, letters):
    tokens, width = x.shape
    steps = tokens // STEP
    hidden = wup_t.shape[0]
    per = LANES * letters // STEP

    def strip(rows, dtype=bf16):
        return (
            jax.ShapeDtypeStruct((steps, rows, STEP), dtype),
            pl.BlockSpec((1, rows, STEP), lambda i: (i, 0, 0)),
        )

    outs = [
        strip(3 * width), strip(width), strip(CHAR_HEADS * letters, f32), strip(width), strip(1, f32),
        strip(width), strip(1, f32), strip(hidden), strip(hidden),
        (jax.ShapeDtypeStruct((width, tokens // letters), f32), pl.BlockSpec((width, LANES), lambda i: (0, i // per))),
    ]
    return pl.pallas_call(
        functools.partial(char_forward_kernel, letters),
        grid=(steps,),
        in_specs=[
            pl.BlockSpec((STEP, width), lambda i: (i, 0)),
            pl.BlockSpec((1, 1, STEP), lambda i: (i, 0, 0)),
            pl.BlockSpec((1, LANES), lambda i: (0, i // per)),
        ] + [full_spec(a) for a in (ga, gb, wqkv_t, wproj_t, wup_t, wdown_t)],
        out_specs=[o[1] for o in outs],
        out_shape=[o[0] for o in outs],
        compiler_params=pltpu.CompilerParams(
            dimension_semantics=("arbitrary",), vmem_limit_bytes=56 * 2**20
        ),
        name="char_forward",
    )(x, tok, cnt, ga, gb, wqkv_t, wproj_t, wup_t, wdown_t)


def norm_back(dy, z, rs, gain):
    dz = dy * gain
    a = jnp.mean(dz, 0, keepdims=True)
    b = jnp.mean(dz * z, 0, keepdims=True)
    return rs * (dz - a - z * b)


def fold_lanes(v):
    out = v[:, :LANES]
    for n in range(1, v.shape[1] // LANES):
        out = out + v[:, n * LANES : (n + 1) * LANES]
    return out


def char_backward_kernel(
    letters, dp_ref, tok_ref, ga_ref, gb_ref, wqkv_ref, wproj_ref, wup_ref, wdown_ref,
    t_ref, o_ref, p_ref, z1_ref, rs1_ref, z2_ref, rs2_ref, m_ref, gp_ref,
    cg_ref, gqkv_ref, gproj_ref, gup_ref, gdown_ref, gga_ref, ggb_ref,
    dh2_ref, du_ref, dh1b_ref, do_ref, dt_ref,
):
    step = pl.program_id(0)
    width = cg_ref.shape[1]
    head = width // CHAR_HEADS
    scale = head ** (-0.5)
    steps_per_block = LANES * letters // STEP
    owner = lane_word(letters)
    blocks = own_blocks(letters)

    @pl.when(step == 0)
    def _():
        for ref in (gqkv_ref, gproj_ref, gup_ref, gdown_ref, gga_ref, ggb_ref):
            ref[...] = jnp.zeros_like(ref)

    for part in range(STEP // SPAN):
        at = pl.ds(part * SPAN, SPAN)
        word = lax.broadcasted_iota(jnp.int32, (LANES, SPAN), 0)
        col = lax.broadcasted_iota(jnp.int32, (LANES, SPAN), 1)
        first = (step % steps_per_block) * (STEP // letters) + part * (SPAN // letters)
        mine = (col // letters + first == word) & (col % letters < tok_ref[0, :, at])
        scatter = jnp.where(mine, 1.0, 0.0).astype(bf16)
        dh2 = dot(dp_ref[...], scatter)
        dh2b = dh2.astype(bf16)
        dh2_ref[:, at] = dh2b
        for n in range(wdown_ref.shape[0] // 256):
            rows = pl.ds(n * 256, 256)
            du_ref[rows, at] = (dot(wdown_ref[rows, :], dh2b) * gp_ref[0, rows, at].astype(f32)).astype(bf16)
        dy = dot(wup_ref[...], du_ref[:, at])
        z = z2_ref[0, :, at].astype(f32)
        ggb_ref[...] += fold_lanes(dy * z)
        dh1 = dh2 + norm_back(dy, z, rs2_ref[0, :, at], wide(gb_ref[...], SPAN))
        dh1b = dh1.astype(bf16)
        dh1b_ref[:, at] = dh1b
        do_ref[:, at] = dot(wproj_ref[...], dh1b).astype(bf16)
        for g in range(SPAN // LANES):
            lanes = pl.ds(part * SPAN + g * LANES, LANES)
            for h in range(CHAR_HEADS):
                q_rows = pl.ds(h * head, head)
                k_rows = pl.ds(width + h * head, head)
                v_rows = pl.ds(2 * width + h * head, head)
                q = t_ref[0, q_rows, lanes]
                k = t_ref[0, k_rows, lanes]
                v = t_ref[0, v_rows, lanes]
                do = do_ref[pl.ds(h * head, head), lanes]
                p = p_ref[0, pl.ds(h * letters, letters), lanes]
                dp = pick_own(dot(v.T, do), owner, letters)
                ds = p * (dp - jnp.sum(p * dp, 0, keepdims=True))
                pb = spread_own(p.astype(bf16), blocks, letters)
                dsb = spread_own(ds.astype(bf16), blocks, letters)
                dt_ref[q_rows, lanes] = (dot(k, dsb) * scale).astype(bf16)
                dt_ref[k_rows, lanes] = (dot_nt(q, dsb) * scale).astype(bf16)
                dt_ref[v_rows, lanes] = dot_nt(do, pb).astype(bf16)
        dy = dot(wqkv_ref[...], dt_ref[:, at])
        z = z1_ref[0, :, at].astype(f32)
        gga_ref[...] += fold_lanes(dy * z)
        dx = dh1 + norm_back(dy, z, rs1_ref[0, :, at], wide(ga_ref[...], SPAN))
        cg_ref[at, :] = dx.T.astype(bf16)
    gdown_ref[...] += dot_nt(m_ref[0], dh2_ref[...])
    gup_ref[...] += dot_nt(z2_ref[0], du_ref[...])
    gproj_ref[...] += dot_nt(o_ref[0], dh1b_ref[...])
    gqkv_ref[...] += dot_nt(z1_ref[0], dt_ref[...])

    @pl.when(step == pl.num_programs(0) - 1)
    def _():
        gup_ref[...] = gup_ref[...] * wide(gb_ref[...], gup_ref.shape[1])
        gqkv_ref[...] = gqkv_ref[...] * wide(ga_ref[...], gqkv_ref.shape[1])


def char_backward(dp, tok, ga, gb, wqkv, wproj, wup, wdown, saved, letters):
    t, o, p, z1, rs1, z2, rs2, m, gp = saved
    steps = t.shape[0]
    width = wqkv.shape[0]
    hidden = wup.shape[1]
    per = LANES * letters // STEP

    def whole(shape):
        return (jax.ShapeDtypeStruct(shape, f32), pl.BlockSpec(shape, lambda i: (0, 0)))

    outs = [
        (jax.ShapeDtypeStruct((steps * STEP, width), bf16), pl.BlockSpec((STEP, width), lambda i: (i, 0))),
        whole((width, 3 * width)), whole((width, width)), whole((width, hidden)), whole((hidden, width)),
        whole((width, LANES)), whole((width, LANES)),
    ]
    return pl.pallas_call(
        functools.partial(char_backward_kernel, letters),
        grid=(steps,),
        in_specs=[
            pl.BlockSpec((width, LANES), lambda i: (0, i // per)),
            pl.BlockSpec((1, 1, STEP), lambda i: (i, 0, 0)),
        ] + [full_spec(a) for a in (ga, gb, wqkv, wproj, wup, wdown)]
        + [pl.BlockSpec((1,) + s.shape[1:], lambda i: (i, 0, 0)) for s in saved],
        out_specs=[o[1] for o in outs],
        out_shape=[o[0] for o in outs],
        scratch_shapes=[
            pltpu.VMEM((width, STEP), bf16),
            pltpu.VMEM((hidden, STEP), bf16),
            pltpu.VMEM((width, STEP), bf16),
            pltpu.VMEM((width, STEP), bf16),
            pltpu.VMEM((3 * width, STEP), bf16),
        ],
        compiler_params=pltpu.CompilerParams(
            dimension_semantics=("arbitrary",), vmem_limit_bytes=56 * 2**20
        ),
        name="char_backward",
    )(dp, tok, ga, gb, wqkv, wproj, wup, wdown, *saved)


def word_kernel(
    pool_sum_ref, cnt_ref, sep_ref, cot_ref, ga_ref, gb_ref, wpool_ref, wqkv_ref, wproj_ref, wup_ref, wdown_ref,
    out_ref, dpool_ref, gpool_ref, gqkv_ref, gproj_ref, gup_ref, gdown_ref, gga_ref, ggb_ref,
    pooled, x, z3, rs3, a3, t, p, o, h3, z4, rs4, a4, m, gp, bias, cot, du, dh3, dh3b, do, dt, dtk,
):
    width, length = x.shape
    head = width // WORD_HEADS
    scale = head ** (-0.5)
    halves = [pl.ds(n * SPAN, SPAN) for n in range(length // SPAN)]
    pooled[...] = (pool_sum_ref[...] / cnt_ref[...]).astype(bf16)
    row = lax.broadcasted_iota(jnp.int32, (length, length), 0)
    col = lax.broadcasted_iota(jnp.int32, (length, length), 1)
    tri = jnp.where(row <= col, 1.0, 0.0).astype(bf16)
    sep = jnp.broadcast_to(sep_ref[...].astype(f32).astype(bf16), (16, length))
    doc_q = dot(sep, tri)[:1]
    doc_k = lax.dot_general(tri, sep, (((0,), (1,)), ((), ())), preferred_element_type=f32)[:, :1]
    bias[...] = jnp.where((row <= col) & (doc_k == doc_q), 0.0, NEGATIVE)
    cot[...] = cot_ref[...].astype(f32).T.astype(bf16)
    for at in halves:
        x[:, at] = lax.dot_general(
            wpool_ref[...], pooled[:, at], (((0,), (0,)), ((), ())), preferred_element_type=f32
        )
        z, rs = normed(x[:, at])
        z3[:, at] = z.astype(bf16)
        rs3[:, at] = rs
        a3[:, at] = (z * wide(ga_ref[...], SPAN)).astype(bf16)
        for n in range(3):
            rows = pl.ds(n * width, width)
            t[rows, at] = lax.dot_general(
                wqkv_ref[:, rows], a3[:, at], (((0,), (0,)), ((), ())), preferred_element_type=f32
            ).astype(bf16)
    for h in range(WORD_HEADS):
        k = t[pl.ds(width + h * head, head), :].T
        for n, at in enumerate(halves):
            seen = (n + 1) * SPAN
            keys = pl.ds(0, seen)
            q = t[pl.ds(h * head, head), at]
            s = dot(k[:seen], q) * scale + bias[keys, at]
            e = jnp.exp(s - jnp.max(s, 0, keepdims=True))
            w = e / jnp.sum(e, 0, keepdims=True)
            p[h, keys, at] = w
            o[pl.ds(h * head, head), at] = dot(t[pl.ds(2 * width + h * head, head), keys], w.astype(bf16)).astype(bf16)
    for at in halves:
        h3[:, at] = x[:, at] + lax.dot_general(
            wproj_ref[...], o[:, at], (((0,), (0,)), ((), ())), preferred_element_type=f32
        )
        z, rs = normed(h3[:, at])
        z4[:, at] = z.astype(bf16)
        rs4[:, at] = rs
        a4[:, at] = (z * wide(gb_ref[...], SPAN)).astype(bf16)
        for n in range(wup_ref.shape[1] // 256):
            rows = pl.ds(n * 256, 256)
            mm, gg = gelu_both(
                lax.dot_general(wup_ref[:, rows], a4[:, at], (((0,), (0,)), ((), ())), preferred_element_type=f32)
            )
            m[rows, at] = mm.astype(bf16)
            gp[rows, at] = gg.astype(bf16)
        out = h3[:, at] + lax.dot_general(
            wdown_ref[...], m[:, at], (((0,), (0,)), ((), ())), preferred_element_type=f32
        )
        out_ref[at, :] = out.T.astype(bf16)
        for n in range(wdown_ref.shape[0] // 256):
            rows = pl.ds(n * 256, 256)
            du[rows, at] = (dot(wdown_ref[rows, :], cot[:, at]) * gp[rows, at].astype(f32)).astype(bf16)
        dy = dot(wup_ref[...], du[:, at])
        z = z4[:, at].astype(f32)
        part = fold_lanes(dy * z)
        ggb_ref[...] = part if at is halves[0] else ggb_ref[...] + part
        dh3[:, at] = cot[:, at].astype(f32) + norm_back(dy, z, rs4[:, at], wide(gb_ref[...], SPAN))
        dh3b[:, at] = dh3[:, at].astype(bf16)
        do[:, at] = dot(wproj_ref[...], dh3b[:, at]).astype(bf16)
    gdown_ref[...] = dot_nt(m[...], cot[...]).astype(gdown_ref.dtype)
    gup_ref[...] = dot_nt(a4[...], du[...]).astype(gup_ref.dtype)
    gproj_ref[...] = dot_nt(o[...], dh3b[...]).astype(gproj_ref.dtype)
    for h in range(WORD_HEADS):
        q_rows = pl.ds(h * head, head)
        k_rows = pl.ds(width + h * head, head)
        v_rows = pl.ds(2 * width + h * head, head)
        v = t[v_rows, :].T
        for n in reversed(range(len(halves))):
            at = halves[n]
            seen = (n + 1) * SPAN
            keys = pl.ds(0, seen)
            w = p[h, keys, at]
            g = do[q_rows, at]
            dp = dot(v[:seen], g)
            ds = (w * (dp - jnp.sum(w * dp, 0, keepdims=True))).astype(bf16)
            dt[q_rows, at] = (dot(t[k_rows, keys], ds) * scale).astype(bf16)
            dk = dot_nt(t[q_rows, at], ds) * scale
            dv = dot_nt(g, w.astype(bf16))
            if n == len(halves) - 1:
                dtk[0] = dk
                dtk[1] = dv
            else:
                dtk[0, :, keys] += dk
                dtk[1, :, keys] += dv
        dt[k_rows, :] = dtk[0].astype(bf16)
        dt[v_rows, :] = dtk[1].astype(bf16)
    gqkv_ref[...] = dot_nt(a3[...], dt[...]).astype(gqkv_ref.dtype)
    for at in halves:
        dy = dot(wqkv_ref[...], dt[:, at])
        z = z3[:, at].astype(f32)
        part = fold_lanes(dy * z)
        gga_ref[...] = part if at is halves[0] else gga_ref[...] + part
        dx = dh3[:, at] + norm_back(dy, z, rs3[:, at], wide(ga_ref[...], SPAN))
        dh3b[:, at] = dx.astype(bf16)
        dpool_ref[:, at] = (dot(wpool_ref[...], dh3b[:, at]) / cnt_ref[:, at]).astype(bf16)
    gpool_ref[...] = dot_nt(pooled[...], dh3b[...]).astype(gpool_ref.dtype)


def word_layer(pool_sum, cnt, sep, cot, ga, gb, wpool, wqkv, wproj, wup, wdown, grad_type=f32):
    length, width = cot.shape
    inner = pool_sum.shape[0]
    hidden = wup.shape[1]
    vm = pltpu.VMEM
    return pl.pallas_call(
        word_kernel,
        out_shape=[
            jax.ShapeDtypeStruct((length, width), bf16),
            jax.ShapeDtypeStruct((inner, length), bf16),
            jax.ShapeDtypeStruct(wpool.shape, grad_type),
            jax.ShapeDtypeStruct(wqkv.shape, grad_type),
            jax.ShapeDtypeStruct(wproj.shape, grad_type),
            jax.ShapeDtypeStruct(wup.shape, grad_type),
            jax.ShapeDtypeStruct(wdown.shape, grad_type),
            jax.ShapeDtypeStruct((width, LANES), f32),
            jax.ShapeDtypeStruct((width, LANES), f32),
        ],
        scratch_shapes=[
            vm((inner, length), bf16), vm((width, length), f32), vm((width, length), bf16), vm((1, length), f32),
            vm((width, length), bf16), vm((3 * width, length), bf16), vm((WORD_HEADS, length, length), f32),
            vm((width, length), bf16), vm((width, length), f32), vm((width, length), bf16), vm((1, length), f32),
            vm((width, length), bf16), vm((hidden, length), bf16), vm((hidden, length), bf16),
            vm((length, length), f32), vm((width, length), bf16), vm((hidden, length), bf16),
            vm((width, length), f32), vm((width, length), bf16), vm((width, length), bf16),
            vm((3 * width, length), bf16), vm((2, width // WORD_HEADS, length), f32),
        ],
        compiler_params=pltpu.CompilerParams(vmem_limit_bytes=58 * 2**20),
        name="word_layer",
    )(pool_sum, cnt, sep, cot, ga, gb, wpool, wqkv, wproj, wup, wdown)


def gather_all(shards, counts):
    flat = jnp.concatenate([s.reshape(-1) for s in shards])
    packed = lax.all_gather(lax.all_gather(flat, "fsdp", axis=0), "dp", axis=0)
    wide_count, deep_count = packed.shape[:2]
    out, start = [], 0
    for s in shards:
        piece = packed[:, :, start : start + s.size]
        start += s.size
        if s.ndim == 1:
            out.append(piece[:, 0].reshape(-1))
        else:
            r, c = s.shape
            piece = piece.reshape(wide_count, deep_count, r, c).transpose(1, 2, 0, 3)
            out.append(piece.reshape(deep_count * r, wide_count * c))
    return out


def scatter_all(grads, shards):
    wide_count, deep_count = lax.axis_size("dp"), lax.axis_size("fsdp")
    pieces = []
    for g, s in zip(grads, shards):
        g = g.astype(bf16)
        if s.ndim == 1:
            g = jnp.broadcast_to(g.reshape(wide_count, 1, s.size), (wide_count, deep_count, s.size))
        else:
            r, c = s.shape
            g = g.reshape(deep_count, r, wide_count, c).transpose(2, 0, 1, 3)
        pieces.append(g.reshape(wide_count, deep_count, s.size))
    packed = jnp.concatenate(pieces, 2)
    packed = lax.psum_scatter(packed, "dp", scatter_dimension=0, tiled=True)
    packed = lax.psum_scatter(packed, "fsdp", scatter_dimension=1, tiled=True).reshape(-1)
    out, start = [], 0
    for s in shards:
        out.append(packed[start : start + s.size].reshape(s.shape).astype(f32))
        start += s.size
    return out


def shards(
    characters, counts, separators, cotangent, char_qkv, char_proj, char_up, char_down, char_gain_a, char_gain_b,
    pool_proj, word_qkv, word_proj, word_up, word_down, word_gain_a, word_gain_b,
):
    rows, length, letters, width = characters.shape
    char_shards = (char_qkv, char_proj, char_up, char_down, char_gain_a, char_gain_b)
    word_shards = (pool_proj, word_qkv, word_proj, word_up, word_down, word_gain_a, word_gain_b)
    cqkv, cproj, cup, cdown, cga, cgb = gather_all(char_shards, counts)
    wpool, wqkv, wproj, wup, wdown, wga, wgb = gather_all(word_shards, counts)
    x = characters.reshape(length * letters, width)
    tok = jnp.repeat(counts, letters, axis=1).reshape(length * letters // STEP, 1, STEP)
    cga, cgb, wga, wgb = (
        jnp.broadcast_to(g.astype(f32)[:, None], (g.shape[0], LANES)) for g in (cga, cgb, wga, wgb)
    )
    *saved, pool_sum = char_forward(x, tok, counts, cga, cgb, cqkv.T, cproj.T, cup.T, cdown.T, letters)
    word_out, dpool, gpool, gwqkv, gwproj, gwup, gwdown, gwga, gwgb = word_layer(
        pool_sum, counts.astype(f32), separators, cotangent.reshape(length, -1), wga, wgb, wpool, wqkv, wproj, wup, wdown
    )
    word_grads = scatter_all(
        (gpool, gwqkv, gwproj, gwup, gwdown, jnp.sum(gwga, 1), jnp.sum(gwgb, 1)), word_shards
    )
    char_grad, gcqkv, gcproj, gcup, gcdown, gcga, gcgb = char_backward(
        dpool, tok, cga, cgb, cqkv, cproj, cup, cdown, saved, letters
    )
    char_grads = scatter_all(
        (gcqkv, gcproj, gcup, gcdown, jnp.sum(gcga, 1), jnp.sum(gcgb, 1)), char_shards
    )
    return (word_out[None], char_grad.reshape(characters.shape), *char_grads, *word_grads)


def solution(mesh):
    rows = ("dp", "fsdp")
    matrix, vector = P("fsdp", "dp"), P("dp")
    data = (P(rows, None, None, None), P(rows, None), P(rows, None), P(rows, None, None))
    block = (matrix,) * 4 + (vector,) * 2
    word = (matrix,) * 5 + (vector,) * 2
    return jax.shard_map(
        shards,
        mesh=mesh,
        in_specs=data + block + word,
        out_specs=(data[3], data[0]) + block + word,
        check_vma=False,
    )
```

```python
import functools
import math

import jax
import jax.numpy as jnp
from jax import lax
from jax.experimental import pallas as pl
from jax.experimental.pallas import tpu as pltpu
from jax.sharding import PartitionSpec as P

CHAR_HEADS = 4
WORD_HEADS = 8
EPS = 1e-05
NEGATIVE = -1e30
LANES = 128
SPAN = 256
STEP = 512
GELU_A = 0.7978845608028654
GELU_B = 0.044715

bf16 = jnp.bfloat16
f32 = jnp.float32


def dot(a, b):
    return jnp.dot(a, b, preferred_element_type=f32)


def dot_nt(a, b):
    return lax.dot_general(a, b, (((1,), (1,)), ((), ())), preferred_element_type=f32)


def normed(v):
    c = v - jnp.mean(v, 0, keepdims=True)
    rs = lax.rsqrt(jnp.mean(c * c, 0, keepdims=True) + EPS)
    return c * rs, rs


def wide(g, n):
    return g if n == g.shape[1] else jnp.concatenate([g] * (n // g.shape[1]), 1)


def gelu_both(u):
    s = u * u
    t = jnp.tanh(u * (GELU_A + (GELU_A * GELU_B) * s))
    h = 0.5 * u
    r = 0.5 + 0.5 * t
    slope = r + h * (1.0 - t * t) * (GELU_A + (3.0 * GELU_A * GELU_B) * s)
    return u * r, slope


def lane_word(letters):
    return lax.broadcasted_iota(jnp.int32, (letters, LANES), 1) // letters


def pick_own(full, owner, letters):
    words = LANES // letters
    out = full[:letters]
    for w in range(1, words):
        out = jnp.where(owner == w, full[w * letters : (w + 1) * letters], out)
    return out


def own_blocks(letters):
    a = lax.broadcasted_iota(jnp.int32, (LANES, LANES), 0) // letters
    b = lax.broadcasted_iota(jnp.int32, (LANES, LANES), 1) // letters
    return jnp.where(a == b, 1.0, 0.0).astype(bf16)


def spread_own(compact, blocks, letters):
    return jnp.concatenate([compact] * (LANES // letters), 0) * blocks


def char_forward_kernel(
    letters, x_ref, tok_ref, cnt_ref, ga_ref, gb_ref, wqkv_ref, wproj_ref, wup_ref, wdown_ref,
    t_ref, o_ref, p_ref, z1_ref, rs1_ref, z2_ref, rs2_ref, m_ref, gp_ref, pool_ref,
):
    step = pl.program_id(0)
    width = x_ref.shape[1]
    head = width // CHAR_HEADS
    scale = head ** (-0.5)
    steps_per_block = LANES * letters // STEP
    owner = lane_word(letters)
    blocks = own_blocks(letters)
    key_slot = lax.broadcasted_iota(jnp.int32, (letters, LANES), 0)

    @pl.when(step % steps_per_block == 0)
    def _():
        pool_ref[...] = jnp.zeros_like(pool_ref)

    for part in range(STEP // SPAN):
        at = pl.ds(part * SPAN, SPAN)
        x = x_ref[at, :].astype(f32).T
        z1, rs1 = normed(x)
        z1_ref[0, :, at] = z1.astype(bf16)
        rs1_ref[0, :, at] = rs1
        a1 = (z1 * wide(ga_ref[...], SPAN)).astype(bf16)
        for n in range(3):
            rows = pl.ds(n * width, width)
            t_ref[0, rows, at] = dot(wqkv_ref[rows, :], a1).astype(bf16)
        for g in range(SPAN // LANES):
            lanes = pl.ds(part * SPAN + g * LANES, LANES)
            allowed = key_slot < tok_ref[0, :, lanes]
            for h in range(CHAR_HEADS):
                q = t_ref[0, pl.ds(h * head, head), lanes]
                k = t_ref[0, pl.ds(width + h * head, head), lanes]
                v = t_ref[0, pl.ds(2 * width + h * head, head), lanes]
                full = dot(k.T, q)
                s = jnp.where(allowed, pick_own(full, owner, letters) * scale, NEGATIVE)
                e = jnp.exp(s - jnp.max(s, 0, keepdims=True))
                p = e / jnp.sum(e, 0, keepdims=True)
                p_ref[0, pl.ds(h * letters, letters), lanes] = p
                o = dot(v, spread_own(p.astype(bf16), blocks, letters))
                o_ref[0, pl.ds(h * head, head), lanes] = o.astype(bf16)
        h1 = x + dot(wproj_ref[...], o_ref[0, :, at])
        z2, rs2 = normed(h1)
        z2_ref[0, :, at] = z2.astype(bf16)
        rs2_ref[0, :, at] = rs2
        a2 = (z2 * wide(gb_ref[...], SPAN)).astype(bf16)
        for n in range(wup_ref.shape[0] // 256):
            rows = pl.ds(n * 256, 256)
            m, gp = gelu_both(dot(wup_ref[rows, :], a2))
            m_ref[0, rows, at] = m.astype(bf16)
            gp_ref[0, rows, at] = gp.astype(bf16)
        h2 = h1 + dot(wdown_ref[...], m_ref[0, :, at])
        high = h2.astype(bf16)
        low = (h2 - high.astype(f32)).astype(bf16)
        row = lax.broadcasted_iota(jnp.int32, (SPAN, LANES), 0)
        word = lax.broadcasted_iota(jnp.int32, (SPAN, LANES), 1)
        first = (step % steps_per_block) * (STEP // letters) + part * (SPAN // letters)
        mine = (row // letters + first == word) & (row % letters < cnt_ref[...])
        gather = jnp.where(mine, 1.0, 0.0).astype(bf16)
        pool_ref[...] += dot(high, gather) + dot(low, gather)


def full_spec(a):
    nd = len(a.shape)
    return pl.BlockSpec(a.shape, lambda i: (0,) * nd)


def char_forward(x, tok, cnt, ga, gb, wqkv_t, wproj_t, wup_t, wdown_t, letters):
    tokens, width = x.shape
    steps = tokens // STEP
    hidden = wup_t.shape[0]
    per = LANES * letters // STEP

    def strip(rows, dtype=bf16):
        return (
            jax.ShapeDtypeStruct((steps, rows, STEP), dtype),
            pl.BlockSpec((1, rows, STEP), lambda i: (i, 0, 0)),
        )

    outs = [
        strip(3 * width), strip(width), strip(CHAR_HEADS * letters, f32), strip(width), strip(1, f32),
        strip(width), strip(1, f32), strip(hidden), strip(hidden),
        (jax.ShapeDtypeStruct((width, tokens // letters), f32), pl.BlockSpec((width, LANES), lambda i: (0, i // per))),
    ]
    return pl.pallas_call(
        functools.partial(char_forward_kernel, letters),
        grid=(steps,),
        in_specs=[
            pl.BlockSpec((STEP, width), lambda i: (i, 0)),
            pl.BlockSpec((1, 1, STEP), lambda i: (i, 0, 0)),
            pl.BlockSpec((1, LANES), lambda i: (0, i // per)),
        ] + [full_spec(a) for a in (ga, gb, wqkv_t, wproj_t, wup_t, wdown_t)],
        out_specs=[o[1] for o in outs],
        out_shape=[o[0] for o in outs],
        compiler_params=pltpu.CompilerParams(
            dimension_semantics=("arbitrary",), vmem_limit_bytes=56 * 2**20
        ),
        name="char_forward",
    )(x, tok, cnt, ga, gb, wqkv_t, wproj_t, wup_t, wdown_t)


def norm_back(dy, z, rs, gain):
    dz = dy * gain
    a = jnp.mean(dz, 0, keepdims=True)
    b = jnp.mean(dz * z, 0, keepdims=True)
    return rs * (dz - a - z * b)


def fold_lanes(v):
    out = v[:, :LANES]
    for n in range(1, v.shape[1] // LANES):
        out = out + v[:, n * LANES : (n + 1) * LANES]
    return out


def char_backward_kernel(
    letters, dp_ref, tok_ref, ga_ref, gb_ref, wqkv_ref, wproj_ref, wup_ref, wdown_ref,
    t_ref, o_ref, p_ref, z1_ref, rs1_ref, z2_ref, rs2_ref, m_ref, gp_ref,
    cg_ref, gqkv_ref, gproj_ref, gup_ref, gdown_ref, gga_ref, ggb_ref,
    dh2_ref, du_ref, dh1b_ref, do_ref, dt_ref,
):
    step = pl.program_id(0)
    width = cg_ref.shape[1]
    head = width // CHAR_HEADS
    scale = head ** (-0.5)
    steps_per_block = LANES * letters // STEP
    owner = lane_word(letters)
    blocks = own_blocks(letters)

    @pl.when(step == 0)
    def _():
        for ref in (gqkv_ref, gproj_ref, gup_ref, gdown_ref, gga_ref, ggb_ref):
            ref[...] = jnp.zeros_like(ref)

    for part in range(STEP // SPAN):
        at = pl.ds(part * SPAN, SPAN)
        word = lax.broadcasted_iota(jnp.int32, (LANES, SPAN), 0)
        col = lax.broadcasted_iota(jnp.int32, (LANES, SPAN), 1)
        first = (step % steps_per_block) * (STEP // letters) + part * (SPAN // letters)
        mine = (col // letters + first == word) & (col % letters < tok_ref[0, :, at])
        scatter = jnp.where(mine, 1.0, 0.0).astype(bf16)
        dh2 = dot(dp_ref[...], scatter)
        dh2b = dh2.astype(bf16)
        dh2_ref[:, at] = dh2b
        for n in range(wdown_ref.shape[0] // 256):
            rows = pl.ds(n * 256, 256)
            du_ref[rows, at] = (dot(wdown_ref[rows, :], dh2b) * gp_ref[0, rows, at].astype(f32)).astype(bf16)
        dy = dot(wup_ref[...], du_ref[:, at])
        z = z2_ref[0, :, at].astype(f32)
        ggb_ref[...] += fold_lanes(dy * z)
        dh1 = dh2 + norm_back(dy, z, rs2_ref[0, :, at], wide(gb_ref[...], SPAN))
        dh1b = dh1.astype(bf16)
        dh1b_ref[:, at] = dh1b
        do_ref[:, at] = dot(wproj_ref[...], dh1b).astype(bf16)
        for g in range(SPAN // LANES):
            lanes = pl.ds(part * SPAN + g * LANES, LANES)
            for h in range(CHAR_HEADS):
                q_rows = pl.ds(h * head, head)
                k_rows = pl.ds(width + h * head, head)
                v_rows = pl.ds(2 * width + h * head, head)
                q = t_ref[0, q_rows, lanes]
                k = t_ref[0, k_rows, lanes]
                v = t_ref[0, v_rows, lanes]
                do = do_ref[pl.ds(h * head, head), lanes]
                p = p_ref[0, pl.ds(h * letters, letters), lanes]
                dp = pick_own(dot(v.T, do), owner, letters)
                ds = p * (dp - jnp.sum(p * dp, 0, keepdims=True))
                pb = spread_own(p.astype(bf16), blocks, letters)
                dsb = spread_own(ds.astype(bf16), blocks, letters)
                dt_ref[q_rows, lanes] = (dot(k, dsb) * scale).astype(bf16)
                dt_ref[k_rows, lanes] = (dot_nt(q, dsb) * scale).astype(bf16)
                dt_ref[v_rows, lanes] = dot_nt(do, pb).astype(bf16)
        dy = dot(wqkv_ref[...], dt_ref[:, at])
        z = z1_ref[0, :, at].astype(f32)
        gga_ref[...] += fold_lanes(dy * z)
        dx = dh1 + norm_back(dy, z, rs1_ref[0, :, at], wide(ga_ref[...], SPAN))
        cg_ref[at, :] = dx.T.astype(bf16)
    gdown_ref[...] += dot_nt(m_ref[0], dh2_ref[...])
    gup_ref[...] += dot_nt(z2_ref[0], du_ref[...])
    gproj_ref[...] += dot_nt(o_ref[0], dh1b_ref[...])
    gqkv_ref[...] += dot_nt(z1_ref[0], dt_ref[...])

    @pl.when(step == pl.num_programs(0) - 1)
    def _():
        gup_ref[...] = gup_ref[...] * wide(gb_ref[...], gup_ref.shape[1])
        gqkv_ref[...] = gqkv_ref[...] * wide(ga_ref[...], gqkv_ref.shape[1])


def char_backward(dp, tok, ga, gb, wqkv, wproj, wup, wdown, saved, letters):
    t, o, p, z1, rs1, z2, rs2, m, gp = saved
    steps = t.shape[0]
    width = wqkv.shape[0]
    hidden = wup.shape[1]
    per = LANES * letters // STEP

    def whole(shape):
        return (jax.ShapeDtypeStruct(shape, f32), pl.BlockSpec(shape, lambda i: (0, 0)))

    outs = [
        (jax.ShapeDtypeStruct((steps * STEP, width), bf16), pl.BlockSpec((STEP, width), lambda i: (i, 0))),
        whole((width, 3 * width)), whole((width, width)), whole((width, hidden)), whole((hidden, width)),
        whole((width, LANES)), whole((width, LANES)),
    ]
    return pl.pallas_call(
        functools.partial(char_backward_kernel, letters),
        grid=(steps,),
        in_specs=[
            pl.BlockSpec((width, LANES), lambda i: (0, i // per)),
            pl.BlockSpec((1, 1, STEP), lambda i: (i, 0, 0)),
        ] + [full_spec(a) for a in (ga, gb, wqkv, wproj, wup, wdown)]
        + [pl.BlockSpec((1,) + s.shape[1:], lambda i: (i, 0, 0)) for s in saved],
        out_specs=[o[1] for o in outs],
        out_shape=[o[0] for o in outs],
        scratch_shapes=[
            pltpu.VMEM((width, STEP), bf16),
            pltpu.VMEM((hidden, STEP), bf16),
            pltpu.VMEM((width, STEP), bf16),
            pltpu.VMEM((width, STEP), bf16),
            pltpu.VMEM((3 * width, STEP), bf16),
        ],
        compiler_params=pltpu.CompilerParams(
            dimension_semantics=("arbitrary",), vmem_limit_bytes=56 * 2**20
        ),
        name="char_backward",
    )(dp, tok, ga, gb, wqkv, wproj, wup, wdown, *saved)


def word_gathered_kernel(
    pool_sum_ref, cnt_ref, sep_ref, cot_ref, ga_ref, gb_ref, wpool_t, all_ref,
    out_ref, dpool_ref, gpool_ref, gqkv_ref, gproj_ref, gup_ref, gdown_ref, gga_ref, ggb_ref,
    pooled, x, z3, rs3, a3, t, p, o, h3, z4, rs4, a4, m, gp, bias, cot, du, dh3, dh3b, do, dt, dtk,
    wqkv_t, wproj_t, wup_t, wdown_t, wqkv_ref, wproj_ref, wup_ref, wdown_ref, wpool_ref,
):
    unpack_word(all_ref, wqkv_t, wproj_t, wup_t, wdown_t, wqkv_ref, wproj_ref, wup_ref, wdown_ref)
    wpool_ref[...] = turned(wpool_t[...])
    width, length = x.shape
    head = width // WORD_HEADS
    scale = head ** (-0.5)
    halves = [pl.ds(n * SPAN, SPAN) for n in range(length // SPAN)]
    pooled[...] = (pool_sum_ref[...] / cnt_ref[...]).astype(bf16)
    row = lax.broadcasted_iota(jnp.int32, (length, length), 0)
    col = lax.broadcasted_iota(jnp.int32, (length, length), 1)
    tri = jnp.where(row <= col, 1.0, 0.0).astype(bf16)
    sep = jnp.broadcast_to(sep_ref[...].astype(f32).astype(bf16), (16, length))
    doc_q = dot(sep, tri)[:1]
    doc_k = lax.dot_general(tri, sep, (((0,), (1,)), ((), ())), preferred_element_type=f32)[:, :1]
    bias[...] = jnp.where((row <= col) & (doc_k == doc_q), 0.0, NEGATIVE)
    cot[...] = cot_ref[...].astype(f32).T.astype(bf16)
    for at in halves:
        x[:, at] = dot(wpool_t[...], pooled[:, at])
        z, rs = normed(x[:, at])
        z3[:, at] = z.astype(bf16)
        rs3[:, at] = rs
        a3[:, at] = (z * wide(ga_ref[...], SPAN)).astype(bf16)
        for n in range(3):
            rows = pl.ds(n * width, width)
            t[rows, at] = dot(wqkv_t[rows, :], a3[:, at]).astype(bf16)
    for h in range(WORD_HEADS):
        k = t[pl.ds(width + h * head, head), :].T
        for n, at in enumerate(halves):
            seen = (n + 1) * SPAN
            keys = pl.ds(0, seen)
            q = t[pl.ds(h * head, head), at]
            s = dot(k[:seen], q) * scale + bias[keys, at]
            e = jnp.exp(s - jnp.max(s, 0, keepdims=True))
            w = e / jnp.sum(e, 0, keepdims=True)
            p[h, keys, at] = w
            o[pl.ds(h * head, head), at] = dot(t[pl.ds(2 * width + h * head, head), keys], w.astype(bf16)).astype(bf16)
    for at in halves:
        h3[:, at] = x[:, at] + dot(wproj_t[...], o[:, at])
        z, rs = normed(h3[:, at])
        z4[:, at] = z.astype(bf16)
        rs4[:, at] = rs
        a4[:, at] = (z * wide(gb_ref[...], SPAN)).astype(bf16)
        for n in range(wup_ref.shape[1] // 256):
            rows = pl.ds(n * 256, 256)
            mm, gg = gelu_both(dot(wup_t[rows, :], a4[:, at]))
            m[rows, at] = mm.astype(bf16)
            gp[rows, at] = gg.astype(bf16)
        out = h3[:, at] + dot(wdown_t[...], m[:, at])
        out_ref[at, :] = out.T.astype(bf16)
        for n in range(wdown_ref.shape[0] // 256):
            rows = pl.ds(n * 256, 256)
            du[rows, at] = (dot(wdown_ref[rows, :], cot[:, at]) * gp[rows, at].astype(f32)).astype(bf16)
        dy = dot(wup_ref[...], du[:, at])
        z = z4[:, at].astype(f32)
        part = fold_lanes(dy * z)
        ggb_ref[...] = part if at is halves[0] else ggb_ref[...] + part
        dh3[:, at] = cot[:, at].astype(f32) + norm_back(dy, z, rs4[:, at], wide(gb_ref[...], SPAN))
        dh3b[:, at] = dh3[:, at].astype(bf16)
        do[:, at] = dot(wproj_ref[...], dh3b[:, at]).astype(bf16)
    gdown_ref[...] = dot_nt(m[...], cot[...]).astype(gdown_ref.dtype)
    gup_ref[...] = dot_nt(a4[...], du[...]).astype(gup_ref.dtype)
    gproj_ref[...] = dot_nt(o[...], dh3b[...]).astype(gproj_ref.dtype)
    for h in range(WORD_HEADS):
        q_rows = pl.ds(h * head, head)
        k_rows = pl.ds(width + h * head, head)
        v_rows = pl.ds(2 * width + h * head, head)
        v = t[v_rows, :].T
        for n in reversed(range(len(halves))):
            at = halves[n]
            seen = (n + 1) * SPAN
            keys = pl.ds(0, seen)
            w = p[h, keys, at]
            g = do[q_rows, at]
            dp = dot(v[:seen], g)
            ds = (w * (dp - jnp.sum(w * dp, 0, keepdims=True))).astype(bf16)
            dt[q_rows, at] = (dot(t[k_rows, keys], ds) * scale).astype(bf16)
            dk = dot_nt(t[q_rows, at], ds) * scale
            dv = dot_nt(g, w.astype(bf16))
            if n == len(halves) - 1:
                dtk[0] = dk
                dtk[1] = dv
            else:
                dtk[0, :, keys] += dk
                dtk[1, :, keys] += dv
        dt[k_rows, :] = dtk[0].astype(bf16)
        dt[v_rows, :] = dtk[1].astype(bf16)
    gqkv_ref[...] = dot_nt(a3[...], dt[...]).astype(gqkv_ref.dtype)
    for at in halves:
        dy = dot(wqkv_ref[...], dt[:, at])
        z = z3[:, at].astype(f32)
        part = fold_lanes(dy * z)
        gga_ref[...] = part if at is halves[0] else gga_ref[...] + part
        dx = dh3[:, at] + norm_back(dy, z, rs3[:, at], wide(ga_ref[...], SPAN))
        dh3b[:, at] = dx.astype(bf16)
        dpool_ref[:, at] = (dot(wpool_ref[...], dh3b[:, at]) / cnt_ref[:, at]).astype(bf16)
    gpool_ref[...] = dot_nt(pooled[...], dh3b[...]).astype(gpool_ref.dtype)


def word_gathered(pool_sum, cnt, sep, cot, ga, gb, pool_t, gathered, grad_type=f32):
    length, width = cot.shape
    inner = pool_sum.shape[0]
    nd, nz, rows, lanes = gathered.shape
    hidden = nd * lanes
    vm = pltpu.VMEM
    return pl.pallas_call(
        word_gathered_kernel,
        out_shape=[
            jax.ShapeDtypeStruct((length, width), bf16),
            jax.ShapeDtypeStruct((inner, length), bf16),
            jax.ShapeDtypeStruct((inner, width), grad_type),
            jax.ShapeDtypeStruct((width, 3 * width), grad_type),
            jax.ShapeDtypeStruct((width, width), grad_type),
            jax.ShapeDtypeStruct((width, hidden), grad_type),
            jax.ShapeDtypeStruct((hidden, width), grad_type),
            jax.ShapeDtypeStruct((width, LANES), f32),
            jax.ShapeDtypeStruct((width, LANES), f32),
        ],
        scratch_shapes=[
            vm((inner, length), bf16), vm((width, length), f32), vm((width, length), bf16), vm((1, length), f32),
            vm((width, length), bf16), vm((3 * width, length), bf16), vm((WORD_HEADS, length, length), f32),
            vm((width, length), bf16), vm((width, length), f32), vm((width, length), bf16), vm((1, length), f32),
            vm((width, length), bf16), vm((hidden, length), bf16), vm((hidden, length), bf16),
            vm((length, length), f32), vm((width, length), bf16), vm((hidden, length), bf16),
            vm((width, length), f32), vm((width, length), bf16), vm((width, length), bf16),
            vm((3 * width, length), bf16), vm((2, width // WORD_HEADS, length), f32),
            vm((3 * width, width), bf16), vm((width, width), bf16), vm((hidden, width), bf16), vm((width, hidden), bf16),
            vm((width, 3 * width), bf16), vm((width, width), bf16), vm((width, hidden), bf16), vm((hidden, width), bf16),
            vm((inner, width), bf16),
        ],
        compiler_params=pltpu.CompilerParams(vmem_limit_bytes=58 * 2**20),
        name="word_gathered",
    )(pool_sum, cnt, sep, cot, ga, gb, pool_t, gathered)


def word_kernel(
    pool_sum_ref, cnt_ref, sep_ref, cot_ref, ga_ref, gb_ref, wpool_ref, wqkv_ref, wproj_ref, wup_ref, wdown_ref,
    out_ref, dpool_ref, gpool_ref, gqkv_ref, gproj_ref, gup_ref, gdown_ref, gga_ref, ggb_ref,
    pooled, x, z3, rs3, a3, t, p, o, h3, z4, rs4, a4, m, gp, bias, cot, du, dh3, dh3b, do, dt, dtk,
):
    width, length = x.shape
    head = width // WORD_HEADS
    scale = head ** (-0.5)
    halves = [pl.ds(n * SPAN, SPAN) for n in range(length // SPAN)]
    pooled[...] = (pool_sum_ref[...] / cnt_ref[...]).astype(bf16)
    row = lax.broadcasted_iota(jnp.int32, (length, length), 0)
    col = lax.broadcasted_iota(jnp.int32, (length, length), 1)
    tri = jnp.where(row <= col, 1.0, 0.0).astype(bf16)
    sep = jnp.broadcast_to(sep_ref[...].astype(f32).astype(bf16), (16, length))
    doc_q = dot(sep, tri)[:1]
    doc_k = lax.dot_general(tri, sep, (((0,), (1,)), ((), ())), preferred_element_type=f32)[:, :1]
    bias[...] = jnp.where((row <= col) & (doc_k == doc_q), 0.0, NEGATIVE)
    cot[...] = cot_ref[...].astype(f32).T.astype(bf16)
    for at in halves:
        x[:, at] = lax.dot_general(
            wpool_ref[...], pooled[:, at], (((0,), (0,)), ((), ())), preferred_element_type=f32
        )
        z, rs = normed(x[:, at])
        z3[:, at] = z.astype(bf16)
        rs3[:, at] = rs
        a3[:, at] = (z * wide(ga_ref[...], SPAN)).astype(bf16)
        for n in range(3):
            rows = pl.ds(n * width, width)
            t[rows, at] = lax.dot_general(
                wqkv_ref[:, rows], a3[:, at], (((0,), (0,)), ((), ())), preferred_element_type=f32
            ).astype(bf16)
    for h in range(WORD_HEADS):
        k = t[pl.ds(width + h * head, head), :].T
        for n, at in enumerate(halves):
            seen = (n + 1) * SPAN
            keys = pl.ds(0, seen)
            q = t[pl.ds(h * head, head), at]
            s = dot(k[:seen], q) * scale + bias[keys, at]
            e = jnp.exp(s - jnp.max(s, 0, keepdims=True))
            w = e / jnp.sum(e, 0, keepdims=True)
            p[h, keys, at] = w
            o[pl.ds(h * head, head), at] = dot(t[pl.ds(2 * width + h * head, head), keys], w.astype(bf16)).astype(bf16)
    for at in halves:
        h3[:, at] = x[:, at] + lax.dot_general(
            wproj_ref[...], o[:, at], (((0,), (0,)), ((), ())), preferred_element_type=f32
        )
        z, rs = normed(h3[:, at])
        z4[:, at] = z.astype(bf16)
        rs4[:, at] = rs
        a4[:, at] = (z * wide(gb_ref[...], SPAN)).astype(bf16)
        for n in range(wup_ref.shape[1] // 256):
            rows = pl.ds(n * 256, 256)
            mm, gg = gelu_both(
                lax.dot_general(wup_ref[:, rows], a4[:, at], (((0,), (0,)), ((), ())), preferred_element_type=f32)
            )
            m[rows, at] = mm.astype(bf16)
            gp[rows, at] = gg.astype(bf16)
        out = h3[:, at] + lax.dot_general(
            wdown_ref[...], m[:, at], (((0,), (0,)), ((), ())), preferred_element_type=f32
        )
        out_ref[at, :] = out.T.astype(bf16)
        for n in range(wdown_ref.shape[0] // 256):
            rows = pl.ds(n * 256, 256)
            du[rows, at] = (dot(wdown_ref[rows, :], cot[:, at]) * gp[rows, at].astype(f32)).astype(bf16)
        dy = dot(wup_ref[...], du[:, at])
        z = z4[:, at].astype(f32)
        part = fold_lanes(dy * z)
        ggb_ref[...] = part if at is halves[0] else ggb_ref[...] + part
        dh3[:, at] = cot[:, at].astype(f32) + norm_back(dy, z, rs4[:, at], wide(gb_ref[...], SPAN))
        dh3b[:, at] = dh3[:, at].astype(bf16)
        do[:, at] = dot(wproj_ref[...], dh3b[:, at]).astype(bf16)
    gdown_ref[...] = dot_nt(m[...], cot[...]).astype(gdown_ref.dtype)
    gup_ref[...] = dot_nt(a4[...], du[...]).astype(gup_ref.dtype)
    gproj_ref[...] = dot_nt(o[...], dh3b[...]).astype(gproj_ref.dtype)
    for h in range(WORD_HEADS):
        q_rows = pl.ds(h * head, head)
        k_rows = pl.ds(width + h * head, head)
        v_rows = pl.ds(2 * width + h * head, head)
        v = t[v_rows, :].T
        for n in reversed(range(len(halves))):
            at = halves[n]
            seen = (n + 1) * SPAN
            keys = pl.ds(0, seen)
            w = p[h, keys, at]
            g = do[q_rows, at]
            dp = dot(v[:seen], g)
            ds = (w * (dp - jnp.sum(w * dp, 0, keepdims=True))).astype(bf16)
            dt[q_rows, at] = (dot(t[k_rows, keys], ds) * scale).astype(bf16)
            dk = dot_nt(t[q_rows, at], ds) * scale
            dv = dot_nt(g, w.astype(bf16))
            if n == len(halves) - 1:
                dtk[0] = dk
                dtk[1] = dv
            else:
                dtk[0, :, keys] += dk
                dtk[1, :, keys] += dv
        dt[k_rows, :] = dtk[0].astype(bf16)
        dt[v_rows, :] = dtk[1].astype(bf16)
    gqkv_ref[...] = dot_nt(a3[...], dt[...]).astype(gqkv_ref.dtype)
    for at in halves:
        dy = dot(wqkv_ref[...], dt[:, at])
        z = z3[:, at].astype(f32)
        part = fold_lanes(dy * z)
        gga_ref[...] = part if at is halves[0] else gga_ref[...] + part
        dx = dh3[:, at] + norm_back(dy, z, rs3[:, at], wide(ga_ref[...], SPAN))
        dh3b[:, at] = dx.astype(bf16)
        dpool_ref[:, at] = (dot(wpool_ref[...], dh3b[:, at]) / cnt_ref[:, at]).astype(bf16)
    gpool_ref[...] = dot_nt(pooled[...], dh3b[...]).astype(gpool_ref.dtype)


def word_layer(pool_sum, cnt, sep, cot, ga, gb, wpool, wqkv, wproj, wup, wdown, grad_type=f32):
    length, width = cot.shape
    inner = pool_sum.shape[0]
    hidden = wup.shape[1]
    vm = pltpu.VMEM
    return pl.pallas_call(
        word_kernel,
        out_shape=[
            jax.ShapeDtypeStruct((length, width), bf16),
            jax.ShapeDtypeStruct((inner, length), bf16),
            jax.ShapeDtypeStruct(wpool.shape, grad_type),
            jax.ShapeDtypeStruct(wqkv.shape, grad_type),
            jax.ShapeDtypeStruct(wproj.shape, grad_type),
            jax.ShapeDtypeStruct(wup.shape, grad_type),
            jax.ShapeDtypeStruct(wdown.shape, grad_type),
            jax.ShapeDtypeStruct((width, LANES), f32),
            jax.ShapeDtypeStruct((width, LANES), f32),
        ],
        scratch_shapes=[
            vm((inner, length), bf16), vm((width, length), f32), vm((width, length), bf16), vm((1, length), f32),
            vm((width, length), bf16), vm((3 * width, length), bf16), vm((WORD_HEADS, length, length), f32),
            vm((width, length), bf16), vm((width, length), f32), vm((width, length), bf16), vm((1, length), f32),
            vm((width, length), bf16), vm((hidden, length), bf16), vm((hidden, length), bf16),
            vm((length, length), f32), vm((width, length), bf16), vm((hidden, length), bf16),
            vm((width, length), f32), vm((width, length), bf16), vm((width, length), bf16),
            vm((3 * width, length), bf16), vm((2, width // WORD_HEADS, length), f32),
        ],
        compiler_params=pltpu.CompilerParams(vmem_limit_bytes=58 * 2**20),
        name="word_layer",
    )(pool_sum, cnt, sep, cot, ga, gb, wpool, wqkv, wproj, wup, wdown)


MESH = pl.DeviceIdType.MESH


def sides():
    chips = lax.axis_size("dp") // 2
    nx = math.isqrt(chips)
    return chips // nx, nx, lax.axis_size("fsdp")


def place():
    ny, nx, nz = sides()
    me = lax.axis_index("dp")
    return me // (2 * nx), (me // 2) % nx, me % 2, lax.axis_index("fsdp")


def device(y, x, c, z):
    return {"dp": (y * sides()[1] + x) * 2 + c, "fsdp": z}


def partners():
    ny, nx, nz = sides()
    y, x, c, z = place()
    found = [device(y, x, 1 - c, z)]
    found += [device(y, x, c, (z + k) % nz) for k in range(1, nz)]
    found += [device(y, (x + k) % nx, c, z) for k in range(1, nx)]
    found += [device((y + k) % ny, x, c, z) for k in range(1, ny)]
    return found


def greet():
    barrier = pltpu.get_barrier_semaphore()
    for other in partners():
        pl.semaphore_signal(barrier, inc=1, device_id=other, device_id_type=MESH)
    pl.semaphore_wait(barrier, len(partners()))


def gather_copies():
    ny, nx, nz = sides()
    return nz - 1 + 1 + 4 * (nx - 1) + 4 * (ny - 1)


def gather_stages(ref, sems):
    ny, nx, nz = sides()
    y, x, c, z = place()
    every = slice(None)
    half = ref.shape[4] // 2
    low, high = pl.ds(0, half), pl.ds(half, half)
    twin = device(y, x, 1 - c, z)
    plan = [[], [], [], []]
    plan[0] += [((y, x, c, z), device(y, x, c, (z + k) % nz)) for k in range(1, nz)]
    plan[1] += [((y, x, c, every, low), device(y, (x + k) % nx, c, z)) for k in range(1, nx)]
    plan[1] += [((y, x, c, every, high), device((y + k) % ny, x, c, z)) for k in range(1, ny)]
    plan[1] += [((y, x, c), twin)]
    plan[2] += [((y, every, c, every, low), device((y + k) % ny, x, c, z)) for k in range(1, ny)]
    plan[2] += [((every, x, c, every, high), device(y, (x + k) % nx, c, z)) for k in range(1, nx)]
    plan[2] += [((y, (x + k) % nx, c, every, low), twin) for k in range(1, nx)]
    plan[2] += [(((y + k) % ny, x, c, every, high), twin) for k in range(1, ny)]
    plan[3] += [(((y + k) % ny, every, c, every, low), twin) for k in range(1, ny)]
    plan[3] += [((every, (x + k) % nx, c, every, high), twin) for k in range(1, nx)]
    count = 0
    stages = []
    for part in plan:
        copies = []
        for where, other in part:
            copies.append(
                pltpu.make_async_remote_copy(
                    src_ref=ref.at[where], dst_ref=ref.at[where], send_sem=sems.at[0, count],
                    recv_sem=sems.at[1, count], device_id=other, device_id_type=MESH,
                )
            )
            count += 1
        stages.append(copies)
    return stages


def start_all(copies):
    for copy in copies:
        copy.start()


def arrive_all(copies):
    for copy in copies:
        copy.wait_recv()


def sent_all(stages):
    for copies in stages:
        for copy in copies:
            copy.wait_send()


def lanes_to(v, n):
    return v if v.shape[1] == n else jnp.concatenate([v, jnp.zeros((v.shape[0], n - v.shape[1]), v.dtype)], 1)


def turned(v):
    return v.astype(f32).T.astype(bf16)


def pack_char(slot, qkv, proj, up, down, pool, gains):
    r = up.shape[0]
    slot[pl.ds(0, r), :] = jnp.concatenate([qkv[...], proj[...]], 1)
    slot[pl.ds(r, r), :] = up[...]
    down_t = turned(lanes_to(down[...], LANES))[: down.shape[1]]
    slot[pl.ds(2 * r, r // 2), :] = down_t[:, :LANES]
    slot[pl.ds(2 * r + r // 2, r // 2), :] = down_t[:, LANES:]
    side = jnp.concatenate([gains[...], jnp.zeros((r - gains.shape[0], gains.shape[1]), f32)], 0).astype(bf16)
    slot[pl.ds(3 * r, r), :] = jnp.concatenate([pool[...], side], 1)


def pack_word(slot, qkv, proj, up, down):
    r = up.shape[0]
    slot[pl.ds(0, r), :] = jnp.concatenate([qkv[...], proj[...]], 1)
    slot[pl.ds(r, r), :] = up[...]
    down_t = turned(lanes_to(down[...], LANES))[: down.shape[1]]
    n = down_t.shape[1] // 2
    slot[pl.ds(2 * r, r // 2), :] = down_t[:, :n]
    slot[pl.ds(2 * r + r // 2, r // 2), :] = down_t[:, n:]


def unpack_char(all_ref, wqkv_t, wproj_t, wup_t, wdown_t, wqkv, wproj, wup, wdown, pool_t, cga, cgb, wga, wgb):
    ny, nx, nz = sides()
    r = all_ref.shape[4] // 4
    width = nz * r
    nd = ny * nx * 2
    a, b = wqkv_t.shape[0] // nd, wproj_t.shape[0] // nd
    n = wdown_t.shape[0] // nd
    deep = wdown_t.shape[1] // nz
    p = pool_t.shape[0] // nd
    gc = cga.shape[0] // nd
    for d in range(nd):
        at = (d // (2 * nx), (d // 2) % nx, d % 2)

        def column(row, rows):
            return all_ref[at + (slice(None), pl.ds(row, rows), slice(None))].reshape(nz * rows, LANES)

        t = turned(column(0, r))
        wqkv_t[pl.ds(d * a, a), :] = t[:a]
        wproj_t[pl.ds(d * b, b), :] = t[a:]
        up = column(r, r)
        wup[:, pl.ds(d * LANES, LANES)] = up
        wup_t[pl.ds(d * LANES, LANES), :] = turned(up)
        for z in range(nz):
            for s in range(2):
                wdown_t[pl.ds(d * n, n), pl.ds(z * deep + s * LANES, LANES)] = all_ref[
                    at + (z, pl.ds(2 * r + s * n, n), slice(None))
                ]
        t = column(3 * r, r).astype(f32).T
        pool_t[pl.ds(d * p, p), :] = t[:p].astype(bf16)
        one, two, three = (jnp.broadcast_to(t[p:, i : i + 1], (p, LANES)) for i in range(3))
        cga[pl.ds(d * gc, gc), :] = one[:gc]
        cgb[pl.ds(d * gc, gc), :] = one[gc:]
        wga[pl.ds(d * p, p), :] = two
        wgb[pl.ds(d * p, p), :] = three
    wqkv[...] = turned(wqkv_t[...])
    wproj[...] = turned(wproj_t[...])
    wdown[...] = turned(wdown_t[...])


def unpack_word(all_ref, wqkv_t, wproj_t, wup_t, wdown_t, wqkv, wproj, wup, wdown):
    nd, nz, rows, lanes = all_ref.shape
    r = rows // 3
    a, b = wqkv_t.shape[0] // nd, wproj_t.shape[0] // nd
    n = r // 2
    for d in range(nd):
        t = turned(all_ref[d, :, pl.ds(0, r), :].reshape(nz * r, lanes))
        wqkv_t[pl.ds(d * a, a), :] = t[:a]
        wproj_t[pl.ds(d * b, b), :] = t[a:]
        up = all_ref[d, :, pl.ds(r, r), :].reshape(nz * r, lanes)
        wup[:, pl.ds(d * lanes, lanes)] = up
        wup_t[pl.ds(d * lanes, lanes), :] = turned(up)
        for z in range(nz):
            for s in range(2):
                wdown_t[pl.ds(d * n, n), pl.ds((2 * z + s) * lanes, lanes)] = all_ref[
                    d, z, pl.ds(2 * r + s * n, n), :
                ]
    wqkv[...] = turned(wqkv_t[...])
    wproj[...] = turned(wproj_t[...])
    wdown[...] = turned(wdown_t[...])


def forward_gather_kernel(
    letters, x_ref, tok_ref, cnt_ref, s_qkv, s_proj, s_up, s_down, s_pool, s_gains, w_qkv, w_proj, w_up, w_down,
    t_ref, o_ref, p_ref, z1_ref, rs1_ref, z2_ref, rs2_ref, m_ref, gp_ref, pool_ref,
    word_all, wqkv, wproj, wup, wdown, pool_t, cga, cgb, wga, wgb,
    char_all, word_own, wqkv_t, wproj_t, wup_t, wdown_t, char_sems, word_sems, own_sem,
):
    step = pl.program_id(0)
    here = place()
    own = pltpu.make_async_copy(word_own, word_all.at[here], own_sem)

    @pl.when(step == 0)
    def _():
        greet()
        pack_char(char_all.at[here], s_qkv, s_proj, s_up, s_down, s_pool, s_gains)
        stages = gather_stages(char_all, char_sems)
        start_all(stages[0])
        pack_word(word_own, w_qkv, w_proj, w_up, w_down)
        own.start()
        for before, after in zip(stages, stages[1:]):
            arrive_all(before)
            start_all(after)
        arrive_all(stages[-1])
        own.wait()
        start_all(gather_stages(word_all, word_sems)[0])
        unpack_char(
            char_all, wqkv_t, wproj_t, wup_t, wdown_t, wqkv, wproj, wup, wdown, pool_t, cga, cgb, wga, wgb
        )
        sent_all(stages)

    for n, when in enumerate((4, 7, 11)):
        @pl.when(step == when)
        def _():
            stages = gather_stages(word_all, word_sems)
            arrive_all(stages[n])
            start_all(stages[n + 1])

    char_forward_kernel(
        letters, x_ref, tok_ref, cnt_ref, cga, cgb, wqkv_t, wproj_t, wup_t, wdown_t,
        t_ref, o_ref, p_ref, z1_ref, rs1_ref, z2_ref, rs2_ref, m_ref, gp_ref, pool_ref,
    )

    @pl.when(step == pl.num_programs(0) - 1)
    def _():
        stages = gather_stages(word_all, word_sems)
        arrive_all(stages[-1])
        sent_all(stages)


def forward_gather(x, tok, cnt, char_shards, word_shards, letters):
    tokens, width = x.shape
    steps = tokens // STEP
    nd, nz = lax.axis_size("dp"), lax.axis_size("fsdp")
    ny, nx, nz = sides()
    qkv, proj, up, down, pool, gains = char_shards
    hidden, outer = up.shape[1] * nd, pool.shape[1] * nd
    per = LANES * letters // STEP
    word_rows, word_lanes = 3 * word_shards[2].shape[0], word_shards[2].shape[1]
    char_rows = 4 * up.shape[0]

    def strip(rows, dtype=bf16):
        return (
            jax.ShapeDtypeStruct((steps, rows, STEP), dtype),
            pl.BlockSpec((1, rows, STEP), lambda i: (i, 0, 0)),
        )

    def whole(shape, dtype=bf16):
        return (jax.ShapeDtypeStruct(shape, dtype), pl.BlockSpec(shape, lambda i: (0, 0)))

    outs = [
        strip(3 * width), strip(width), strip(CHAR_HEADS * letters, f32), strip(width), strip(1, f32),
        strip(width), strip(1, f32), strip(hidden), strip(hidden),
        (jax.ShapeDtypeStruct((width, tokens // letters), f32), pl.BlockSpec((width, LANES), lambda i: (0, i // per))),
        (jax.ShapeDtypeStruct((ny, nx, 2, nz, word_rows, word_lanes), bf16), pl.BlockSpec(memory_space=pl.ANY)),
        whole((width, 3 * width)), whole((width, width)), whole((width, hidden)), whole((hidden, width)),
        whole((outer, width)), whole((width, LANES), f32), whole((width, LANES), f32),
        whole((outer, LANES), f32), whole((outer, LANES), f32),
    ]
    shards = (*char_shards, *word_shards)
    return pl.pallas_call(
        functools.partial(forward_gather_kernel, letters),
        grid=(steps,),
        in_specs=[
            pl.BlockSpec((STEP, width), lambda i: (i, 0)),
            pl.BlockSpec((1, 1, STEP), lambda i: (i, 0, 0)),
            pl.BlockSpec((1, LANES), lambda i: (0, i // per)),
        ] + [full_spec(a) for a in shards],
        out_specs=[o[1] for o in outs],
        out_shape=[o[0] for o in outs],
        scratch_shapes=[
            pltpu.VMEM((ny, nx, 2, nz, char_rows, LANES), bf16),
            pltpu.VMEM((word_rows, word_lanes), bf16),
            pltpu.VMEM((3 * width, width), bf16),
            pltpu.VMEM((width, width), bf16),
            pltpu.VMEM((hidden, width), bf16),
            pltpu.VMEM((width, hidden), bf16),
            pltpu.SemaphoreType.DMA((2, gather_copies())),
            pltpu.SemaphoreType.DMA((2, gather_copies())),
            pltpu.SemaphoreType.DMA,
        ],
        compiler_params=pltpu.CompilerParams(
            dimension_semantics=("arbitrary",), vmem_limit_bytes=56 * 2**20, collective_id=0, has_side_effects=True
        ),
        name="forward_gather",
    )(x, tok, cnt, *shards)


def gather_all(shards, counts):
    flat = jnp.concatenate([s.reshape(-1) for s in shards])
    packed = lax.all_gather(lax.all_gather(flat, "fsdp", axis=0), "dp", axis=0)
    wide_count, deep_count = packed.shape[:2]
    out, start = [], 0
    for s in shards:
        piece = packed[:, :, start : start + s.size]
        start += s.size
        if s.ndim == 1:
            out.append(piece[:, 0].reshape(-1))
        else:
            r, c = s.shape
            piece = piece.reshape(wide_count, deep_count, r, c).transpose(1, 2, 0, 3)
            out.append(piece.reshape(deep_count * r, wide_count * c))
    return out


def scatter_all(grads, shards):
    wide_count, deep_count = lax.axis_size("dp"), lax.axis_size("fsdp")
    pieces = []
    for g, s in zip(grads, shards):
        g = g.astype(bf16)
        if s.ndim == 1:
            g = jnp.broadcast_to(g.reshape(wide_count, 1, s.size), (wide_count, deep_count, s.size))
        else:
            r, c = s.shape
            g = g.reshape(deep_count, r, wide_count, c).transpose(2, 0, 1, 3)
        pieces.append(g.reshape(wide_count, deep_count, s.size))
    packed = jnp.concatenate(pieces, 2)
    packed = lax.psum_scatter(packed, "dp", scatter_dimension=0, tiled=True)
    packed = lax.psum_scatter(packed, "fsdp", scatter_dimension=1, tiled=True).reshape(-1)
    out, start = [], 0
    for s in shards:
        out.append(packed[start : start + s.size].reshape(s.shape).astype(f32))
        start += s.size
    return out


def shards_plain(
    characters, counts, separators, cotangent, char_qkv, char_proj, char_up, char_down, char_gain_a, char_gain_b,
    pool_proj, word_qkv, word_proj, word_up, word_down, word_gain_a, word_gain_b,
):
    rows, length, letters, width = characters.shape
    char_shards = (char_qkv, char_proj, char_up, char_down, char_gain_a, char_gain_b)
    word_shards = (pool_proj, word_qkv, word_proj, word_up, word_down, word_gain_a, word_gain_b)
    cqkv, cproj, cup, cdown, cga, cgb = gather_all(char_shards, counts)
    wpool, wqkv, wproj, wup, wdown, wga, wgb = gather_all(word_shards, counts)
    x = characters.reshape(length * letters, width)
    tok = jnp.repeat(counts, letters, axis=1).reshape(length * letters // STEP, 1, STEP)
    cga, cgb, wga, wgb = (
        jnp.broadcast_to(g.astype(f32)[:, None], (g.shape[0], LANES)) for g in (cga, cgb, wga, wgb)
    )
    *saved, pool_sum = char_forward(x, tok, counts, cga, cgb, cqkv.T, cproj.T, cup.T, cdown.T, letters)
    word_out, dpool, gpool, gwqkv, gwproj, gwup, gwdown, gwga, gwgb = word_layer(
        pool_sum, counts.astype(f32), separators, cotangent.reshape(length, -1), wga, wgb, wpool, wqkv, wproj, wup, wdown
    )
    word_grads = scatter_all(
        (gpool, gwqkv, gwproj, gwup, gwdown, jnp.sum(gwga, 1), jnp.sum(gwgb, 1)), word_shards
    )
    char_grad, gcqkv, gcproj, gcup, gcdown, gcga, gcgb = char_backward(
        dpool, tok, cga, cgb, cqkv, cproj, cup, cdown, saved, letters
    )
    char_grads = scatter_all(
        (gcqkv, gcproj, gcup, gcdown, jnp.sum(gcga, 1), jnp.sum(gcgb, 1)), char_shards
    )
    return (word_out[None], char_grad.reshape(characters.shape), *char_grads, *word_grads)


def shards_packed(
    characters, counts, separators, cotangent, char_qkv, char_proj, char_up, char_down, char_gain_a, char_gain_b,
    pool_proj, word_qkv, word_proj, word_up, word_down, word_gain_a, word_gain_b,
):
    rows, length, letters, width = characters.shape
    char_shards = (char_qkv, char_proj, char_up, char_down, char_gain_a, char_gain_b)
    word_shards = (pool_proj, word_qkv, word_proj, word_up, word_down, word_gain_a, word_gain_b)
    x = characters.reshape(length * letters, width)
    tok = jnp.repeat(counts, letters, axis=1).reshape(length * letters // STEP, 1, STEP)
    gains = jnp.concatenate([char_gain_a, char_gain_b, word_gain_a, word_gain_b]).astype(f32).reshape(3, -1)
    (
        *saved, pool_sum, word_all, cqkv, cproj, cup, cdown, pool_t, cga, cgb, wga, wgb
    ) = forward_gather(
        x, tok, counts, (char_qkv, char_proj, char_up, char_down, pool_proj, gains),
        (word_qkv, word_proj, word_up, word_down), letters,
    )
    word_all = word_all.reshape((-1,) + word_all.shape[3:])
    word_out, dpool, gpool, gwqkv, gwproj, gwup, gwdown, gwga, gwgb = word_gathered(
        pool_sum, counts.astype(f32), separators, cotangent.reshape(length, -1), wga, wgb, pool_t, word_all
    )
    word_grads = scatter_all(
        (gpool, gwqkv, gwproj, gwup, gwdown, jnp.sum(gwga, 1), jnp.sum(gwgb, 1)), word_shards
    )
    char_grad, gcqkv, gcproj, gcup, gcdown, gcga, gcgb = char_backward(
        dpool, tok, cga, cgb, cqkv, cproj, cup, cdown, saved, letters
    )
    char_grads = scatter_all(
        (gcqkv, gcproj, gcup, gcdown, jnp.sum(gcga, 1), jnp.sum(gcgb, 1)), char_shards
    )
    return (word_out[None], char_grad.reshape(characters.shape), *char_grads, *word_grads)


def shards(*arrays):
    char_qkv, char_proj, word_qkv, word_proj = arrays[4], arrays[5], arrays[11], arrays[12]
    tiles = (char_qkv.shape[1] + char_proj.shape[1]) // LANES, (word_qkv.shape[1] + word_proj.shape[1]) // LANES
    return (shards_packed if tiles == (1, 2) else shards_plain)(*arrays)


def solution(mesh):
    rows = ("dp", "fsdp")
    matrix, vector = P("fsdp", "dp"), P("dp")
    data = (P(rows, None, None, None), P(rows, None), P(rows, None), P(rows, None, None))
    block = (matrix,) * 4 + (vector,) * 2
    word = (matrix,) * 5 + (vector,) * 2
    return jax.shard_map(
        shards,
        mesh=mesh,
        in_specs=data + block + word,
        out_specs=(data[3], data[0]) + block + word,
        check_vma=False,
    )
```

```python
import functools
import math

import jax
import jax.numpy as jnp
from jax import lax
from jax.experimental import pallas as pl
from jax.experimental.pallas import tpu as pltpu
from jax.sharding import PartitionSpec as P

CHAR_HEADS = 4
WORD_HEADS = 8
EPS = 1e-05
NEGATIVE = -1e30
LANES = 128
SPAN = 256
STEP = 512
GELU_A = 0.7978845608028654
GELU_B = 0.044715

bf16 = jnp.bfloat16
f32 = jnp.float32


def dot(a, b):
    return jnp.dot(a, b, preferred_element_type=f32)


def dot_nt(a, b):
    return lax.dot_general(a, b, (((1,), (1,)), ((), ())), preferred_element_type=f32)


def normed(v):
    c = v - jnp.mean(v, 0, keepdims=True)
    rs = lax.rsqrt(jnp.mean(c * c, 0, keepdims=True) + EPS)
    return c * rs, rs


def wide(g, n):
    return g if n == g.shape[1] else jnp.concatenate([g] * (n // g.shape[1]), 1)


def gelu_both(u):
    s = u * u
    t = jnp.tanh(u * (GELU_A + (GELU_A * GELU_B) * s))
    h = 0.5 * u
    r = 0.5 + 0.5 * t
    slope = r + h * (1.0 - t * t) * (GELU_A + (3.0 * GELU_A * GELU_B) * s)
    return u * r, slope


def lane_word(letters):
    return lax.broadcasted_iota(jnp.int32, (letters, LANES), 1) // letters


def pick_own(full, owner, letters):
    words = LANES // letters
    out = full[:letters]
    for w in range(1, words):
        out = jnp.where(owner == w, full[w * letters : (w + 1) * letters], out)
    return out


def own_blocks(letters):
    a = lax.broadcasted_iota(jnp.int32, (LANES, LANES), 0) // letters
    b = lax.broadcasted_iota(jnp.int32, (LANES, LANES), 1) // letters
    return jnp.where(a == b, 1.0, 0.0).astype(bf16)


def spread_own(compact, blocks, letters):
    return jnp.concatenate([compact] * (LANES // letters), 0) * blocks


def char_forward_kernel(
    letters, x_ref, tok_ref, cnt_ref, ga_ref, gb_ref, wqkv_ref, wproj_ref, wup_ref, wdown_ref,
    t_ref, o_ref, p_ref, z1_ref, rs1_ref, z2_ref, rs2_ref, m_ref, gp_ref, pool_ref,
):
    step = pl.program_id(0)
    width = x_ref.shape[1]
    head = width // CHAR_HEADS
    scale = head ** (-0.5)
    steps_per_block = LANES * letters // STEP
    owner = lane_word(letters)
    blocks = own_blocks(letters)
    key_slot = lax.broadcasted_iota(jnp.int32, (letters, LANES), 0)

    @pl.when(step % steps_per_block == 0)
    def _():
        pool_ref[...] = jnp.zeros_like(pool_ref)

    for part in range(STEP // SPAN):
        at = pl.ds(part * SPAN, SPAN)
        x = x_ref[at, :].astype(f32).T
        z1, rs1 = normed(x)
        z1_ref[0, :, at] = z1.astype(bf16)
        rs1_ref[0, :, at] = rs1
        a1 = (z1 * wide(ga_ref[...], SPAN)).astype(bf16)
        for n in range(3):
            rows = pl.ds(n * width, width)
            t_ref[0, rows, at] = dot(wqkv_ref[rows, :], a1).astype(bf16)
        for g in range(SPAN // LANES):
            lanes = pl.ds(part * SPAN + g * LANES, LANES)
            allowed = key_slot < tok_ref[0, :, lanes]
            for h in range(CHAR_HEADS):
                q = t_ref[0, pl.ds(h * head, head), lanes]
                k = t_ref[0, pl.ds(width + h * head, head), lanes]
                v = t_ref[0, pl.ds(2 * width + h * head, head), lanes]
                full = dot(k.T, q)
                s = jnp.where(allowed, pick_own(full, owner, letters) * scale, NEGATIVE)
                e = jnp.exp(s - jnp.max(s, 0, keepdims=True))
                p = e / jnp.sum(e, 0, keepdims=True)
                p_ref[0, pl.ds(h * letters, letters), lanes] = p
                o = dot(v, spread_own(p.astype(bf16), blocks, letters))
                o_ref[0, pl.ds(h * head, head), lanes] = o.astype(bf16)
        h1 = x + dot(wproj_ref[...], o_ref[0, :, at])
        z2, rs2 = normed(h1)
        z2_ref[0, :, at] = z2.astype(bf16)
        rs2_ref[0, :, at] = rs2
        a2 = (z2 * wide(gb_ref[...], SPAN)).astype(bf16)
        for n in range(wup_ref.shape[0] // 256):
            rows = pl.ds(n * 256, 256)
            m, gp = gelu_both(dot(wup_ref[rows, :], a2))
            m_ref[0, rows, at] = m.astype(bf16)
            gp_ref[0, rows, at] = gp.astype(bf16)
        h2 = h1 + dot(wdown_ref[...], m_ref[0, :, at])
        high = h2.astype(bf16)
        low = (h2 - high.astype(f32)).astype(bf16)
        row = lax.broadcasted_iota(jnp.int32, (SPAN, LANES), 0)
        word = lax.broadcasted_iota(jnp.int32, (SPAN, LANES), 1)
        first = (step % steps_per_block) * (STEP // letters) + part * (SPAN // letters)
        mine = (row // letters + first == word) & (row % letters < cnt_ref[...])
        gather = jnp.where(mine, 1.0, 0.0).astype(bf16)
        pool_ref[...] += dot(high, gather) + dot(low, gather)


def full_spec(a):
    nd = len(a.shape)
    return pl.BlockSpec(a.shape, lambda i: (0,) * nd)


def char_forward(x, tok, cnt, ga, gb, wqkv_t, wproj_t, wup_t, wdown_t, letters):
    tokens, width = x.shape
    steps = tokens // STEP
    hidden = wup_t.shape[0]
    per = LANES * letters // STEP

    def strip(rows, dtype=bf16):
        return (
            jax.ShapeDtypeStruct((steps, rows, STEP), dtype),
            pl.BlockSpec((1, rows, STEP), lambda i: (i, 0, 0)),
        )

    outs = [
        strip(3 * width), strip(width), strip(CHAR_HEADS * letters, f32), strip(width), strip(1, f32),
        strip(width), strip(1, f32), strip(hidden), strip(hidden),
        (jax.ShapeDtypeStruct((width, tokens // letters), f32), pl.BlockSpec((width, LANES), lambda i: (0, i // per))),
    ]
    return pl.pallas_call(
        functools.partial(char_forward_kernel, letters),
        grid=(steps,),
        in_specs=[
            pl.BlockSpec((STEP, width), lambda i: (i, 0)),
            pl.BlockSpec((1, 1, STEP), lambda i: (i, 0, 0)),
            pl.BlockSpec((1, LANES), lambda i: (0, i // per)),
        ] + [full_spec(a) for a in (ga, gb, wqkv_t, wproj_t, wup_t, wdown_t)],
        out_specs=[o[1] for o in outs],
        out_shape=[o[0] for o in outs],
        compiler_params=pltpu.CompilerParams(
            dimension_semantics=("arbitrary",), vmem_limit_bytes=56 * 2**20
        ),
        name="char_forward",
    )(x, tok, cnt, ga, gb, wqkv_t, wproj_t, wup_t, wdown_t)


def norm_back(dy, z, rs, gain):
    dz = dy * gain
    a = jnp.mean(dz, 0, keepdims=True)
    b = jnp.mean(dz * z, 0, keepdims=True)
    return rs * (dz - a - z * b)


def fold_lanes(v):
    out = v[:, :LANES]
    for n in range(1, v.shape[1] // LANES):
        out = out + v[:, n * LANES : (n + 1) * LANES]
    return out


def char_backward_kernel(
    letters, dp_ref, tok_ref, ga_ref, gb_ref, wqkv_ref, wproj_ref, wup_ref, wdown_ref,
    t_ref, o_ref, p_ref, z1_ref, rs1_ref, z2_ref, rs2_ref, m_ref, gp_ref,
    cg_ref, gqkv_ref, gproj_ref, gup_ref, gdown_ref, gga_ref, ggb_ref,
    dh2_ref, du_ref, dh1b_ref, do_ref, dt_ref,
):
    step = pl.program_id(0)
    width = cg_ref.shape[1]
    head = width // CHAR_HEADS
    scale = head ** (-0.5)
    steps_per_block = LANES * letters // STEP
    owner = lane_word(letters)
    blocks = own_blocks(letters)

    @pl.when(step == 0)
    def _():
        for ref in (gqkv_ref, gproj_ref, gup_ref, gdown_ref, gga_ref, ggb_ref):
            ref[...] = jnp.zeros_like(ref)

    for part in range(STEP // SPAN):
        at = pl.ds(part * SPAN, SPAN)
        word = lax.broadcasted_iota(jnp.int32, (LANES, SPAN), 0)
        col = lax.broadcasted_iota(jnp.int32, (LANES, SPAN), 1)
        first = (step % steps_per_block) * (STEP // letters) + part * (SPAN // letters)
        mine = (col // letters + first == word) & (col % letters < tok_ref[0, :, at])
        scatter = jnp.where(mine, 1.0, 0.0).astype(bf16)
        dh2 = dot(dp_ref[...], scatter)
        dh2b = dh2.astype(bf16)
        dh2_ref[:, at] = dh2b
        for n in range(wdown_ref.shape[0] // 256):
            rows = pl.ds(n * 256, 256)
            du_ref[rows, at] = (dot(wdown_ref[rows, :], dh2b) * gp_ref[0, rows, at].astype(f32)).astype(bf16)
        dy = dot(wup_ref[...], du_ref[:, at])
        z = z2_ref[0, :, at].astype(f32)
        ggb_ref[...] += fold_lanes(dy * z)
        dh1 = dh2 + norm_back(dy, z, rs2_ref[0, :, at], wide(gb_ref[...], SPAN))
        dh1b = dh1.astype(bf16)
        dh1b_ref[:, at] = dh1b
        do_ref[:, at] = dot(wproj_ref[...], dh1b).astype(bf16)
        for g in range(SPAN // LANES):
            lanes = pl.ds(part * SPAN + g * LANES, LANES)
            for h in range(CHAR_HEADS):
                q_rows = pl.ds(h * head, head)
                k_rows = pl.ds(width + h * head, head)
                v_rows = pl.ds(2 * width + h * head, head)
                q = t_ref[0, q_rows, lanes]
                k = t_ref[0, k_rows, lanes]
                v = t_ref[0, v_rows, lanes]
                do = do_ref[pl.ds(h * head, head), lanes]
                p = p_ref[0, pl.ds(h * letters, letters), lanes]
                dp = pick_own(dot(v.T, do), owner, letters)
                ds = p * (dp - jnp.sum(p * dp, 0, keepdims=True))
                pb = spread_own(p.astype(bf16), blocks, letters)
                dsb = spread_own(ds.astype(bf16), blocks, letters)
                dt_ref[q_rows, lanes] = (dot(k, dsb) * scale).astype(bf16)
                dt_ref[k_rows, lanes] = (dot_nt(q, dsb) * scale).astype(bf16)
                dt_ref[v_rows, lanes] = dot_nt(do, pb).astype(bf16)
        dy = dot(wqkv_ref[...], dt_ref[:, at])
        z = z1_ref[0, :, at].astype(f32)
        gga_ref[...] += fold_lanes(dy * z)
        dx = dh1 + norm_back(dy, z, rs1_ref[0, :, at], wide(ga_ref[...], SPAN))
        cg_ref[at, :] = dx.T.astype(bf16)
    gdown_ref[...] += dot_nt(dh2_ref[...], m_ref[0])
    gup_ref[...] += dot_nt(z2_ref[0], du_ref[...])
    gproj_ref[...] += dot_nt(dh1b_ref[...], o_ref[0])
    gqkv_ref[...] += dot_nt(dt_ref[...], z1_ref[0])

    @pl.when(step == pl.num_programs(0) - 1)
    def _():
        gup_ref[...] = gup_ref[...] * wide(gb_ref[...], gup_ref.shape[1])
        gqkv_ref[...] = gqkv_ref[...] * ga_ref[...].T[:1]


def char_backward(dp, tok, ga, gb, wqkv, wproj, wup, wdown, saved, letters):
    t, o, p, z1, rs1, z2, rs2, m, gp = saved
    steps = t.shape[0]
    width = wqkv.shape[0]
    hidden = wup.shape[1]
    per = LANES * letters // STEP

    def whole(shape):
        return (jax.ShapeDtypeStruct(shape, f32), pl.BlockSpec(shape, lambda i: (0, 0)))

    outs = [
        (jax.ShapeDtypeStruct((steps * STEP, width), bf16), pl.BlockSpec((STEP, width), lambda i: (i, 0))),
        whole((3 * width, width)), whole((width, width)), whole((width, hidden)), whole((width, hidden)),
        whole((width, LANES)), whole((width, LANES)),
    ]
    return pl.pallas_call(
        functools.partial(char_backward_kernel, letters),
        grid=(steps,),
        in_specs=[
            pl.BlockSpec((width, LANES), lambda i: (0, i // per)),
            pl.BlockSpec((1, 1, STEP), lambda i: (i, 0, 0)),
        ] + [full_spec(a) for a in (ga, gb, wqkv, wproj, wup, wdown)]
        + [pl.BlockSpec((1,) + s.shape[1:], lambda i: (i, 0, 0)) for s in saved],
        out_specs=[o[1] for o in outs],
        out_shape=[o[0] for o in outs],
        scratch_shapes=[
            pltpu.VMEM((width, STEP), bf16),
            pltpu.VMEM((hidden, STEP), bf16),
            pltpu.VMEM((width, STEP), bf16),
            pltpu.VMEM((width, STEP), bf16),
            pltpu.VMEM((3 * width, STEP), bf16),
        ],
        compiler_params=pltpu.CompilerParams(
            dimension_semantics=("arbitrary",), vmem_limit_bytes=56 * 2**20
        ),
        name="char_backward",
    )(dp, tok, ga, gb, wqkv, wproj, wup, wdown, *saved)


def word_gathered_kernel(
    pool_sum_ref, cnt_ref, sep_ref, cot_ref, ga_ref, gb_ref, wpool_t, all_ref,
    out_ref, dpool_ref, gpool_ref, send_ref, gga_ref, ggb_ref,
    pooled, x, z3, rs3, a3, t, p, o, h3, z4, rs4, a4, m, gp, bias, cot, du, dh3, dh3b, do, dt, dtk,
    wqkv_t, wproj_t, wup_t, wdown_t, wqkv_ref, wproj_ref, wup_ref, wdown_ref, wpool_ref, gqkv_t, gproj_t,
):
    unpack_word(all_ref, wqkv_t, wproj_t, wup_t, wdown_t, wqkv_ref, wproj_ref, wup_ref, wdown_ref)
    wpool_ref[...] = turned(wpool_t[...])
    width, length = x.shape
    head = width // WORD_HEADS
    scale = head ** (-0.5)
    halves = [pl.ds(n * SPAN, SPAN) for n in range(length // SPAN)]
    pooled[...] = (pool_sum_ref[...] / cnt_ref[...]).astype(bf16)
    row = lax.broadcasted_iota(jnp.int32, (length, length), 0)
    col = lax.broadcasted_iota(jnp.int32, (length, length), 1)
    tri = jnp.where(row <= col, 1.0, 0.0).astype(bf16)
    sep = jnp.broadcast_to(sep_ref[...].astype(f32).astype(bf16), (16, length))
    doc_q = dot(sep, tri)[:1]
    doc_k = lax.dot_general(tri, sep, (((0,), (1,)), ((), ())), preferred_element_type=f32)[:, :1]
    bias[...] = jnp.where((row <= col) & (doc_k == doc_q), 0.0, NEGATIVE)
    cot[...] = cot_ref[...].astype(f32).T.astype(bf16)
    for at in halves:
        x[:, at] = dot(wpool_t[...], pooled[:, at])
        z, rs = normed(x[:, at])
        z3[:, at] = z.astype(bf16)
        rs3[:, at] = rs
        a3[:, at] = (z * wide(ga_ref[...], SPAN)).astype(bf16)
        for n in range(3):
            rows = pl.ds(n * width, width)
            t[rows, at] = dot(wqkv_t[rows, :], a3[:, at]).astype(bf16)
    for h in range(WORD_HEADS):
        k = t[pl.ds(width + h * head, head), :].T
        for n, at in enumerate(halves):
            seen = (n + 1) * SPAN
            keys = pl.ds(0, seen)
            q = t[pl.ds(h * head, head), at]
            s = dot(k[:seen], q) * scale + bias[keys, at]
            e = jnp.exp(s - jnp.max(s, 0, keepdims=True))
            w = e / jnp.sum(e, 0, keepdims=True)
            p[h, keys, at] = w
            o[pl.ds(h * head, head), at] = dot(t[pl.ds(2 * width + h * head, head), keys], w.astype(bf16)).astype(bf16)
    for at in halves:
        h3[:, at] = x[:, at] + dot(wproj_t[...], o[:, at])
        z, rs = normed(h3[:, at])
        z4[:, at] = z.astype(bf16)
        rs4[:, at] = rs
        a4[:, at] = (z * wide(gb_ref[...], SPAN)).astype(bf16)
        for n in range(wup_ref.shape[1] // 256):
            rows = pl.ds(n * 256, 256)
            mm, gg = gelu_both(dot(wup_t[rows, :], a4[:, at]))
            m[rows, at] = mm.astype(bf16)
            gp[rows, at] = gg.astype(bf16)
        out = h3[:, at] + dot(wdown_t[...], m[:, at])
        out_ref[at, :] = out.T.astype(bf16)
        for n in range(wdown_ref.shape[0] // 256):
            rows = pl.ds(n * 256, 256)
            du[rows, at] = (dot(wdown_ref[rows, :], cot[:, at]) * gp[rows, at].astype(f32)).astype(bf16)
        dy = dot(wup_ref[...], du[:, at])
        z = z4[:, at].astype(f32)
        part = fold_lanes(dy * z)
        ggb_ref[...] = part if at is halves[0] else ggb_ref[...] + part
        dh3[:, at] = cot[:, at].astype(f32) + norm_back(dy, z, rs4[:, at], wide(gb_ref[...], SPAN))
        dh3b[:, at] = dh3[:, at].astype(bf16)
        do[:, at] = dot(wproj_ref[...], dh3b[:, at]).astype(bf16)
    nd, nz, rows, lanes = send_ref.shape
    r = rows // 3
    n = r // 2
    for z in range(nz):
        for s in range(2):
            g = dot_nt(cot[...], m[pl.ds((2 * z + s) * lanes, lanes), :]).astype(bf16)
            for d in range(nd):
                send_ref[d, z, pl.ds(2 * r + s * n, n), :] = g[d * n : (d + 1) * n]
    for d in range(nd):
        g = dot_nt(a4[...], du[pl.ds(d * lanes, lanes), :]).astype(bf16)
        send_ref[d, :, pl.ds(r, r), :] = g.reshape(nz, r, lanes)
    gproj_t[...] = dot_nt(dh3b[...], o[...]).astype(bf16)
    for h in range(WORD_HEADS):
        q_rows = pl.ds(h * head, head)
        k_rows = pl.ds(width + h * head, head)
        v_rows = pl.ds(2 * width + h * head, head)
        v = t[v_rows, :].T
        for n in reversed(range(len(halves))):
            at = halves[n]
            seen = (n + 1) * SPAN
            keys = pl.ds(0, seen)
            w = p[h, keys, at]
            g = do[q_rows, at]
            dp = dot(v[:seen], g)
            ds = (w * (dp - jnp.sum(w * dp, 0, keepdims=True))).astype(bf16)
            dt[q_rows, at] = (dot(t[k_rows, keys], ds) * scale).astype(bf16)
            dk = dot_nt(t[q_rows, at], ds) * scale
            dv = dot_nt(g, w.astype(bf16))
            if n == len(halves) - 1:
                dtk[0] = dk
                dtk[1] = dv
            else:
                dtk[0, :, keys] += dk
                dtk[1, :, keys] += dv
        dt[k_rows, :] = dtk[0].astype(bf16)
        dt[v_rows, :] = dtk[1].astype(bf16)
    for n in range(3):
        part = pl.ds(n * width, width)
        gqkv_t[part, :] = dot_nt(dt[part, :], a3[...]).astype(bf16)
    a, b = gqkv_t.shape[0] // nd, gproj_t.shape[0] // nd
    for d in range(nd):
        g = turned(jnp.concatenate([gqkv_t[pl.ds(d * a, a), :], gproj_t[pl.ds(d * b, b), :]], 0))
        send_ref[d, :, pl.ds(0, r), :] = g.reshape(nz, r, lanes)
    for at in halves:
        dy = dot(wqkv_ref[...], dt[:, at])
        z = z3[:, at].astype(f32)
        part = fold_lanes(dy * z)
        gga_ref[...] = part if at is halves[0] else gga_ref[...] + part
        dx = dh3[:, at] + norm_back(dy, z, rs3[:, at], wide(ga_ref[...], SPAN))
        dh3b[:, at] = dx.astype(bf16)
        dpool_ref[:, at] = (dot(wpool_ref[...], dh3b[:, at]) / cnt_ref[:, at]).astype(bf16)
    gpool_ref[...] = dot_nt(dh3b[...], pooled[...])


def word_gathered(pool_sum, cnt, sep, cot, ga, gb, pool_t, gathered):
    length, width = cot.shape
    inner = pool_sum.shape[0]
    nd, nz, rows, lanes = gathered.shape
    hidden = nd * lanes
    vm = pltpu.VMEM
    return pl.pallas_call(
        word_gathered_kernel,
        out_shape=[
            jax.ShapeDtypeStruct((length, width), bf16),
            jax.ShapeDtypeStruct((inner, length), bf16),
            jax.ShapeDtypeStruct((width, inner), f32),
            jax.ShapeDtypeStruct(gathered.shape, bf16),
            jax.ShapeDtypeStruct((width, LANES), f32),
            jax.ShapeDtypeStruct((width, LANES), f32),
        ],
        scratch_shapes=[
            vm((inner, length), bf16), vm((width, length), f32), vm((width, length), bf16), vm((1, length), f32),
            vm((width, length), bf16), vm((3 * width, length), bf16), vm((WORD_HEADS, length, length), f32),
            vm((width, length), bf16), vm((width, length), f32), vm((width, length), bf16), vm((1, length), f32),
            vm((width, length), bf16), vm((hidden, length), bf16), vm((hidden, length), bf16),
            vm((length, length), f32), vm((width, length), bf16), vm((hidden, length), bf16),
            vm((width, length), f32), vm((width, length), bf16), vm((width, length), bf16),
            vm((3 * width, length), bf16), vm((2, width // WORD_HEADS, length), f32),
            vm((3 * width, width), bf16), vm((width, width), bf16), vm((hidden, width), bf16), vm((width, hidden), bf16),
            vm((width, 3 * width), bf16), vm((width, width), bf16), vm((width, hidden), bf16), vm((hidden, width), bf16),
            vm((inner, width), bf16), vm((3 * width, width), bf16), vm((width, width), bf16),
        ],
        compiler_params=pltpu.CompilerParams(vmem_limit_bytes=58 * 2**20),
        name="word_gathered",
    )(pool_sum, cnt, sep, cot, ga, gb, pool_t, gathered)


def word_kernel(
    pool_sum_ref, cnt_ref, sep_ref, cot_ref, ga_ref, gb_ref, wpool_ref, wqkv_ref, wproj_ref, wup_ref, wdown_ref,
    out_ref, dpool_ref, gpool_ref, gqkv_ref, gproj_ref, gup_ref, gdown_ref, gga_ref, ggb_ref,
    pooled, x, z3, rs3, a3, t, p, o, h3, z4, rs4, a4, m, gp, bias, cot, du, dh3, dh3b, do, dt, dtk,
):
    width, length = x.shape
    head = width // WORD_HEADS
    scale = head ** (-0.5)
    halves = [pl.ds(n * SPAN, SPAN) for n in range(length // SPAN)]
    pooled[...] = (pool_sum_ref[...] / cnt_ref[...]).astype(bf16)
    row = lax.broadcasted_iota(jnp.int32, (length, length), 0)
    col = lax.broadcasted_iota(jnp.int32, (length, length), 1)
    tri = jnp.where(row <= col, 1.0, 0.0).astype(bf16)
    sep = jnp.broadcast_to(sep_ref[...].astype(f32).astype(bf16), (16, length))
    doc_q = dot(sep, tri)[:1]
    doc_k = lax.dot_general(tri, sep, (((0,), (1,)), ((), ())), preferred_element_type=f32)[:, :1]
    bias[...] = jnp.where((row <= col) & (doc_k == doc_q), 0.0, NEGATIVE)
    cot[...] = cot_ref[...].astype(f32).T.astype(bf16)
    for at in halves:
        x[:, at] = lax.dot_general(
            wpool_ref[...], pooled[:, at], (((0,), (0,)), ((), ())), preferred_element_type=f32
        )
        z, rs = normed(x[:, at])
        z3[:, at] = z.astype(bf16)
        rs3[:, at] = rs
        a3[:, at] = (z * wide(ga_ref[...], SPAN)).astype(bf16)
        for n in range(3):
            rows = pl.ds(n * width, width)
            t[rows, at] = lax.dot_general(
                wqkv_ref[:, rows], a3[:, at], (((0,), (0,)), ((), ())), preferred_element_type=f32
            ).astype(bf16)
    for h in range(WORD_HEADS):
        k = t[pl.ds(width + h * head, head), :].T
        for n, at in enumerate(halves):
            seen = (n + 1) * SPAN
            keys = pl.ds(0, seen)
            q = t[pl.ds(h * head, head), at]
            s = dot(k[:seen], q) * scale + bias[keys, at]
            e = jnp.exp(s - jnp.max(s, 0, keepdims=True))
            w = e / jnp.sum(e, 0, keepdims=True)
            p[h, keys, at] = w
            o[pl.ds(h * head, head), at] = dot(t[pl.ds(2 * width + h * head, head), keys], w.astype(bf16)).astype(bf16)
    for at in halves:
        h3[:, at] = x[:, at] + lax.dot_general(
            wproj_ref[...], o[:, at], (((0,), (0,)), ((), ())), preferred_element_type=f32
        )
        z, rs = normed(h3[:, at])
        z4[:, at] = z.astype(bf16)
        rs4[:, at] = rs
        a4[:, at] = (z * wide(gb_ref[...], SPAN)).astype(bf16)
        for n in range(wup_ref.shape[1] // 256):
            rows = pl.ds(n * 256, 256)
            mm, gg = gelu_both(
                lax.dot_general(wup_ref[:, rows], a4[:, at], (((0,), (0,)), ((), ())), preferred_element_type=f32)
            )
            m[rows, at] = mm.astype(bf16)
            gp[rows, at] = gg.astype(bf16)
        out = h3[:, at] + lax.dot_general(
            wdown_ref[...], m[:, at], (((0,), (0,)), ((), ())), preferred_element_type=f32
        )
        out_ref[at, :] = out.T.astype(bf16)
        for n in range(wdown_ref.shape[0] // 256):
            rows = pl.ds(n * 256, 256)
            du[rows, at] = (dot(wdown_ref[rows, :], cot[:, at]) * gp[rows, at].astype(f32)).astype(bf16)
        dy = dot(wup_ref[...], du[:, at])
        z = z4[:, at].astype(f32)
        part = fold_lanes(dy * z)
        ggb_ref[...] = part if at is halves[0] else ggb_ref[...] + part
        dh3[:, at] = cot[:, at].astype(f32) + norm_back(dy, z, rs4[:, at], wide(gb_ref[...], SPAN))
        dh3b[:, at] = dh3[:, at].astype(bf16)
        do[:, at] = dot(wproj_ref[...], dh3b[:, at]).astype(bf16)
    gdown_ref[...] = dot_nt(m[...], cot[...]).astype(gdown_ref.dtype)
    gup_ref[...] = dot_nt(a4[...], du[...]).astype(gup_ref.dtype)
    gproj_ref[...] = dot_nt(o[...], dh3b[...]).astype(gproj_ref.dtype)
    for h in range(WORD_HEADS):
        q_rows = pl.ds(h * head, head)
        k_rows = pl.ds(width + h * head, head)
        v_rows = pl.ds(2 * width + h * head, head)
        v = t[v_rows, :].T
        for n in reversed(range(len(halves))):
            at = halves[n]
            seen = (n + 1) * SPAN
            keys = pl.ds(0, seen)
            w = p[h, keys, at]
            g = do[q_rows, at]
            dp = dot(v[:seen], g)
            ds = (w * (dp - jnp.sum(w * dp, 0, keepdims=True))).astype(bf16)
            dt[q_rows, at] = (dot(t[k_rows, keys], ds) * scale).astype(bf16)
            dk = dot_nt(t[q_rows, at], ds) * scale
            dv = dot_nt(g, w.astype(bf16))
            if n == len(halves) - 1:
                dtk[0] = dk
                dtk[1] = dv
            else:
                dtk[0, :, keys] += dk
                dtk[1, :, keys] += dv
        dt[k_rows, :] = dtk[0].astype(bf16)
        dt[v_rows, :] = dtk[1].astype(bf16)
    gqkv_ref[...] = dot_nt(a3[...], dt[...]).astype(gqkv_ref.dtype)
    for at in halves:
        dy = dot(wqkv_ref[...], dt[:, at])
        z = z3[:, at].astype(f32)
        part = fold_lanes(dy * z)
        gga_ref[...] = part if at is halves[0] else gga_ref[...] + part
        dx = dh3[:, at] + norm_back(dy, z, rs3[:, at], wide(ga_ref[...], SPAN))
        dh3b[:, at] = dx.astype(bf16)
        dpool_ref[:, at] = (dot(wpool_ref[...], dh3b[:, at]) / cnt_ref[:, at]).astype(bf16)
    gpool_ref[...] = dot_nt(pooled[...], dh3b[...]).astype(gpool_ref.dtype)


def word_layer(pool_sum, cnt, sep, cot, ga, gb, wpool, wqkv, wproj, wup, wdown, grad_type=f32):
    length, width = cot.shape
    inner = pool_sum.shape[0]
    hidden = wup.shape[1]
    vm = pltpu.VMEM
    return pl.pallas_call(
        word_kernel,
        out_shape=[
            jax.ShapeDtypeStruct((length, width), bf16),
            jax.ShapeDtypeStruct((inner, length), bf16),
            jax.ShapeDtypeStruct(wpool.shape, grad_type),
            jax.ShapeDtypeStruct(wqkv.shape, grad_type),
            jax.ShapeDtypeStruct(wproj.shape, grad_type),
            jax.ShapeDtypeStruct(wup.shape, grad_type),
            jax.ShapeDtypeStruct(wdown.shape, grad_type),
            jax.ShapeDtypeStruct((width, LANES), f32),
            jax.ShapeDtypeStruct((width, LANES), f32),
        ],
        scratch_shapes=[
            vm((inner, length), bf16), vm((width, length), f32), vm((width, length), bf16), vm((1, length), f32),
            vm((width, length), bf16), vm((3 * width, length), bf16), vm((WORD_HEADS, length, length), f32),
            vm((width, length), bf16), vm((width, length), f32), vm((width, length), bf16), vm((1, length), f32),
            vm((width, length), bf16), vm((hidden, length), bf16), vm((hidden, length), bf16),
            vm((length, length), f32), vm((width, length), bf16), vm((hidden, length), bf16),
            vm((width, length), f32), vm((width, length), bf16), vm((width, length), bf16),
            vm((3 * width, length), bf16), vm((2, width // WORD_HEADS, length), f32),
        ],
        compiler_params=pltpu.CompilerParams(vmem_limit_bytes=58 * 2**20),
        name="word_layer",
    )(pool_sum, cnt, sep, cot, ga, gb, wpool, wqkv, wproj, wup, wdown)


MESH = pl.DeviceIdType.MESH


def sides():
    chips = lax.axis_size("dp") // 2
    nx = math.isqrt(chips)
    return chips // nx, nx, lax.axis_size("fsdp")


def place():
    ny, nx, nz = sides()
    me = lax.axis_index("dp")
    return me // (2 * nx), (me // 2) % nx, me % 2, lax.axis_index("fsdp")


def device(y, x, c, z):
    return {"dp": (y * sides()[1] + x) * 2 + c, "fsdp": z}


def partners():
    ny, nx, nz = sides()
    y, x, c, z = place()
    found = [device(y, x, 1 - c, z)]
    found += [device(y, x, c, (z + k) % nz) for k in range(1, nz)]
    found += [device(y, (x + k) % nx, c, z) for k in range(1, nx)]
    found += [device((y + k) % ny, x, c, z) for k in range(1, ny)]
    return found


def greet():
    barrier = pltpu.get_barrier_semaphore()
    for other in partners():
        pl.semaphore_signal(barrier, inc=1, device_id=other, device_id_type=MESH)
    pl.semaphore_wait(barrier, len(partners()))


def remote(src, dst, sems, n, other):
    return pltpu.make_async_remote_copy(
        src_ref=src, dst_ref=dst, send_sem=sems.at[0, n], recv_sem=sems.at[1, n],
        device_id=other, device_id_type=MESH,
    )


def gather_copies():
    ny, nx, nz = sides()
    return nz - 1 + 1 + 4 * (nx - 1) + 4 * (ny - 1)


def gather_stages(ref, sems, wanted=(0, 1, 2, 3)):
    ny, nx, nz = sides()
    y, x, c, z = place()
    every = slice(None)
    half = ref.shape[4] // 2
    low, high = pl.ds(0, half), pl.ds(half, half)
    twin = device(y, x, 1 - c, z)
    plan = [[], [], [], []]
    plan[0] += [((y, x, c, z), device(y, x, c, (z + k) % nz)) for k in range(1, nz)]
    plan[1] += [((y, x, c, every, low), device(y, (x + k) % nx, c, z)) for k in range(1, nx)]
    plan[1] += [((y, x, c, every, high), device((y + k) % ny, x, c, z)) for k in range(1, ny)]
    plan[1] += [((y, x, c), twin)]
    plan[2] += [((y, every, c, every, low), device((y + k) % ny, x, c, z)) for k in range(1, ny)]
    plan[2] += [((every, x, c, every, high), device(y, (x + k) % nx, c, z)) for k in range(1, nx)]
    plan[2] += [((y, (x + k) % nx, c, every, low), twin) for k in range(1, nx)]
    plan[2] += [(((y + k) % ny, x, c, every, high), twin) for k in range(1, ny)]
    plan[3] += [(((y + k) % ny, every, c, every, low), twin) for k in range(1, ny)]
    plan[3] += [((every, (x + k) % nx, c, every, high), twin) for k in range(1, nx)]
    count = 0
    stages = []
    for n, part in enumerate(plan):
        copies = []
        for where, other in part:
            if n in wanted:
                copies.append(remote(ref.at[where], ref.at[where], sems, count, other))
            count += 1
        stages.append(copies)
    return stages


def start_all(copies):
    for copy in copies:
        copy.start()


def arrive_all(copies):
    for copy in copies:
        copy.wait_recv()


def sent_all(stages):
    for copies in stages:
        for copy in copies:
            copy.wait_send()


def lanes_to(v, n):
    return v if v.shape[1] == n else jnp.concatenate([v, jnp.zeros((v.shape[0], n - v.shape[1]), v.dtype)], 1)


def turned(v):
    return v.astype(f32).T.astype(bf16)


def pack_char(slot, qkv, proj, up, down, pool, gains):
    r = up.shape[0]
    slot[pl.ds(0, r), :] = jnp.concatenate([qkv[...], proj[...]], 1)
    slot[pl.ds(r, r), :] = up[...]
    down_t = turned(lanes_to(down[...], LANES))[: down.shape[1]]
    slot[pl.ds(2 * r, r // 2), :] = down_t[:, :LANES]
    slot[pl.ds(2 * r + r // 2, r // 2), :] = down_t[:, LANES:]
    side = jnp.concatenate([gains[...], jnp.zeros((r - gains.shape[0], gains.shape[1]), f32)], 0).astype(bf16)
    slot[pl.ds(3 * r, r), :] = jnp.concatenate([pool[...], side], 1)


def pack_word(slot, qkv, proj, up, down):
    r = up.shape[0]
    slot[pl.ds(0, r), :] = jnp.concatenate([qkv[...], proj[...]], 1)
    slot[pl.ds(r, r), :] = up[...]
    down_t = turned(lanes_to(down[...], LANES))[: down.shape[1]]
    n = down_t.shape[1] // 2
    slot[pl.ds(2 * r, r // 2), :] = down_t[:, :n]
    slot[pl.ds(2 * r + r // 2, r // 2), :] = down_t[:, n:]


def unpack_char(all_ref, wqkv_t, wproj_t, wup_t, wdown_t, wqkv, wproj, wup, wdown, pool_t, cga, cgb, wga, wgb):
    ny, nx, nz = sides()
    r = all_ref.shape[4] // 4
    width = nz * r
    nd = ny * nx * 2
    a, b = wqkv_t.shape[0] // nd, wproj_t.shape[0] // nd
    n = wdown_t.shape[0] // nd
    deep = wdown_t.shape[1] // nz
    p = pool_t.shape[0] // nd
    gc = cga.shape[0] // nd
    for d in range(nd):
        at = (d // (2 * nx), (d // 2) % nx, d % 2)

        def column(row, rows):
            return all_ref[at + (slice(None), pl.ds(row, rows), slice(None))].reshape(nz * rows, LANES)

        t = turned(column(0, r))
        wqkv_t[pl.ds(d * a, a), :] = t[:a]
        wproj_t[pl.ds(d * b, b), :] = t[a:]
        up = column(r, r)
        wup[:, pl.ds(d * LANES, LANES)] = up
        wup_t[pl.ds(d * LANES, LANES), :] = turned(up)
        for z in range(nz):
            for s in range(2):
                wdown_t[pl.ds(d * n, n), pl.ds(z * deep + s * LANES, LANES)] = all_ref[
                    at + (z, pl.ds(2 * r + s * n, n), slice(None))
                ]
        t = column(3 * r, r).astype(f32).T
        pool_t[pl.ds(d * p, p), :] = t[:p].astype(bf16)
        one, two, three = (jnp.broadcast_to(t[p:, i : i + 1], (p, LANES)) for i in range(3))
        cga[pl.ds(d * gc, gc), :] = one[:gc]
        cgb[pl.ds(d * gc, gc), :] = one[gc:]
        wga[pl.ds(d * p, p), :] = two
        wgb[pl.ds(d * p, p), :] = three
    wqkv[...] = turned(wqkv_t[...])
    wproj[...] = turned(wproj_t[...])
    wdown[...] = turned(wdown_t[...])


def unpack_word(all_ref, wqkv_t, wproj_t, wup_t, wdown_t, wqkv, wproj, wup, wdown):
    nd, nz, rows, lanes = all_ref.shape
    r = rows // 3
    a, b = wqkv_t.shape[0] // nd, wproj_t.shape[0] // nd
    n = r // 2
    for d in range(nd):
        t = turned(all_ref[d, :, pl.ds(0, r), :].reshape(nz * r, lanes))
        wqkv_t[pl.ds(d * a, a), :] = t[:a]
        wproj_t[pl.ds(d * b, b), :] = t[a:]
        up = all_ref[d, :, pl.ds(r, r), :].reshape(nz * r, lanes)
        wup[:, pl.ds(d * lanes, lanes)] = up
        wup_t[pl.ds(d * lanes, lanes), :] = turned(up)
        for z in range(nz):
            for s in range(2):
                wdown_t[pl.ds(d * n, n), pl.ds((2 * z + s) * lanes, lanes)] = all_ref[
                    d, z, pl.ds(2 * r + s * n, n), :
                ]
    wqkv[...] = turned(wqkv_t[...])
    wproj[...] = turned(wproj_t[...])
    wdown[...] = turned(wdown_t[...])


def forward_gather_kernel(
    letters, x_ref, tok_ref, cnt_ref, s_qkv, s_proj, s_up, s_down, s_pool, s_gains, w_qkv, w_proj, w_up, w_down,
    t_ref, o_ref, p_ref, z1_ref, rs1_ref, z2_ref, rs2_ref, m_ref, gp_ref, pool_ref,
    word_all, wqkv, wproj, wup, wdown, pool_t, cga, cgb, wga, wgb,
    char_all, word_own, wqkv_t, wproj_t, wup_t, wdown_t, char_sems, word_sems, own_sem,
):
    step = pl.program_id(0)
    here = place()
    own = pltpu.make_async_copy(word_own, word_all.at[here], own_sem)

    @pl.when(step == 0)
    def _():
        greet()
        pack_char(char_all.at[here], s_qkv, s_proj, s_up, s_down, s_pool, s_gains)
        stages = gather_stages(char_all, char_sems)
        start_all(stages[0])
        pack_word(word_own, w_qkv, w_proj, w_up, w_down)
        own.start()
        for before, after in zip(stages, stages[1:]):
            arrive_all(before)
            start_all(after)
        arrive_all(stages[-1])
        own.wait()
        start_all(gather_stages(word_all, word_sems, (0,))[0])
        unpack_char(
            char_all, wqkv_t, wproj_t, wup_t, wdown_t, wqkv, wproj, wup, wdown, pool_t, cga, cgb, wga, wgb
        )
        sent_all(stages)

    for n, when in enumerate((4, 7, 11)):
        @pl.when(step == when)
        def _():
            stages = gather_stages(word_all, word_sems, (n, n + 1))
            arrive_all(stages[n])
            start_all(stages[n + 1])

    char_forward_kernel(
        letters, x_ref, tok_ref, cnt_ref, cga, cgb, wqkv_t, wproj_t, wup_t, wdown_t,
        t_ref, o_ref, p_ref, z1_ref, rs1_ref, z2_ref, rs2_ref, m_ref, gp_ref, pool_ref,
    )

    @pl.when(step == pl.num_programs(0) - 1)
    def _():
        stages = gather_stages(word_all, word_sems)
        arrive_all(stages[-1])
        sent_all(stages)


def forward_gather(x, tok, cnt, char_shards, word_shards, letters):
    tokens, width = x.shape
    steps = tokens // STEP
    nd, nz = lax.axis_size("dp"), lax.axis_size("fsdp")
    ny, nx, nz = sides()
    qkv, proj, up, down, pool, gains = char_shards
    hidden, outer = up.shape[1] * nd, pool.shape[1] * nd
    per = LANES * letters // STEP
    word_rows, word_lanes = 3 * word_shards[2].shape[0], word_shards[2].shape[1]
    char_rows = 4 * up.shape[0]

    def strip(rows, dtype=bf16):
        return (
            jax.ShapeDtypeStruct((steps, rows, STEP), dtype),
            pl.BlockSpec((1, rows, STEP), lambda i: (i, 0, 0)),
        )

    def whole(shape, dtype=bf16):
        return (jax.ShapeDtypeStruct(shape, dtype), pl.BlockSpec(shape, lambda i: (0, 0)))

    outs = [
        strip(3 * width), strip(width), strip(CHAR_HEADS * letters, f32), strip(width), strip(1, f32),
        strip(width), strip(1, f32), strip(hidden), strip(hidden),
        (jax.ShapeDtypeStruct((width, tokens // letters), f32), pl.BlockSpec((width, LANES), lambda i: (0, i // per))),
        (jax.ShapeDtypeStruct((ny, nx, 2, nz, word_rows, word_lanes), bf16), pl.BlockSpec(memory_space=pl.ANY)),
        whole((width, 3 * width)), whole((width, width)), whole((width, hidden)), whole((hidden, width)),
        whole((outer, width)), whole((width, LANES), f32), whole((width, LANES), f32),
        whole((outer, LANES), f32), whole((outer, LANES), f32),
    ]
    shards = (*char_shards, *word_shards)
    return pl.pallas_call(
        functools.partial(forward_gather_kernel, letters),
        grid=(steps,),
        in_specs=[
            pl.BlockSpec((STEP, width), lambda i: (i, 0)),
            pl.BlockSpec((1, 1, STEP), lambda i: (i, 0, 0)),
            pl.BlockSpec((1, LANES), lambda i: (0, i // per)),
        ] + [full_spec(a) for a in shards],
        out_specs=[o[1] for o in outs],
        out_shape=[o[0] for o in outs],
        scratch_shapes=[
            pltpu.VMEM((ny, nx, 2, nz, char_rows, LANES), bf16),
            pltpu.VMEM((word_rows, word_lanes), bf16),
            pltpu.VMEM((3 * width, width), bf16),
            pltpu.VMEM((width, width), bf16),
            pltpu.VMEM((hidden, width), bf16),
            pltpu.VMEM((width, hidden), bf16),
            pltpu.SemaphoreType.DMA((2, gather_copies())),
            pltpu.SemaphoreType.DMA((2, gather_copies())),
            pltpu.SemaphoreType.DMA,
        ],
        compiler_params=pltpu.CompilerParams(
            dimension_semantics=("arbitrary",), vmem_limit_bytes=56 * 2**20, collective_id=0, has_side_effects=True
        ),
        name="forward_gather",
    )(x, tok, cnt, *shards)


def scatter_copies():
    ny, nx, nz = sides()
    return 1 + 2 * (nx - 1) + 2 * (ny - 1) + nz - 1


def scatter_scratch(rows, lanes):
    ny, nx, nz = sides()
    half = rows // 2
    shapes = (
        (ny, nx, nz, rows, lanes), (ny, nx, nz, rows, lanes), (nx - 1, ny, nz, half, lanes),
        (ny - 1, nx, nz, half, lanes), (ny - 1, nz, half, lanes), (nx - 1, nz, half, lanes), (nz - 1, rows, lanes),
    )
    return [pltpu.VMEM(shape, bf16) for shape in shapes] + [pltpu.SemaphoreType.DMA((2, scatter_copies()))]


def scatter_stage(n, send, work):
    acc, twin_in, one_low, one_high, two_low, two_high, last_in, sems = work
    ny, nx, nz = sides()
    y, x, c, z = place()
    half = acc.shape[3] // 2
    low, high, every = pl.ds(0, half), pl.ds(half, half), slice(None)
    plan = [[], [], [], []]
    plan[0] += [(send, (every, every, 1 - c), twin_in, device(y, x, 1 - c, z))]
    plan[1] += [
        (acc, (every, (x + k) % nx, every, low), one_low.at[k - 1], device(y, (x + k) % nx, c, z)) for k in range(1, nx)
    ]
    plan[1] += [
        (acc, ((y + k) % ny, every, every, high), one_high.at[k - 1], device((y + k) % ny, x, c, z)) for k in range(1, ny)
    ]
    plan[2] += [
        (acc, ((y + k) % ny, x, every, low), two_low.at[k - 1], device((y + k) % ny, x, c, z)) for k in range(1, ny)
    ]
    plan[2] += [
        (acc, (y, (x + k) % nx, every, high), two_high.at[k - 1], device(y, (x + k) % nx, c, z)) for k in range(1, nx)
    ]
    plan[3] += [(acc, (y, x, (z + k) % nz), last_in.at[k - 1], device(y, x, c, (z + k) % nz)) for k in range(1, nz)]
    first = sum(len(p) for p in plan[:n])
    return [remote(src.at[at], dst, sems, first + i, other) for i, (src, at, dst, other) in enumerate(plan[n])]


def scatter_sum(n, own, work, out):
    acc, twin_in, one_low, one_high, two_low, two_high, last_in, sems = work
    ny, nx, nz = sides()
    y, x, c, z = place()
    half = acc.shape[3] // 2
    low, high = pl.ds(0, half), pl.ds(half, half)
    if n == 0:
        for b in range(ny):
            for a in range(nx):
                for k in range(nz):
                    acc[b, a, k] = own(b, a, k) + twin_in[b, a, k]
    elif n == 1:
        for k in range(nz):
            for b in range(ny):
                acc[b, x, k, low] += sum(one_low[i, b, k] for i in range(nx - 1))
            for a in range(nx):
                acc[y, a, k, high] += sum(one_high[i, a, k] for i in range(ny - 1))
    elif n == 2:
        for k in range(nz):
            acc[y, x, k, low] += sum(two_low[i, k] for i in range(ny - 1))
            acc[y, x, k, high] += sum(two_high[i, k] for i in range(nx - 1))
    else:
        out[...] = acc[y, x, z].astype(f32) + sum(last_in[i].astype(f32) for i in range(nz - 1))


def pack_char_grads(slots, gqkv_t, gproj_t, gup, gdown_t, gpool_t, gga, ggb, gwga, gwgb):
    ny, nx, nz = sides()
    nd = ny * nx * 2
    r = slots.shape[4] // 4
    width = nz * r
    a, b, n, p = (g.shape[0] // nd for g in (gqkv_t, gproj_t, gdown_t, gpool_t))
    deep = gdown_t.shape[1] // nz
    gc = gga.shape[0] // nd
    spot = lax.broadcasted_iota(jnp.int32, (p, width), 1) % r
    char_a, char_b, word_a, word_b = (jnp.sum(g[...], 1, keepdims=True) for g in (gga, ggb, gwga, gwgb))
    every = slice(None)
    for d in range(nd):
        at = (d // (2 * nx), (d // 2) % nx, d % 2)
        t = jnp.concatenate([gqkv_t[pl.ds(d * a, a), :], gproj_t[pl.ds(d * b, b), :]], 0)
        slots[at + (every, pl.ds(0, r))] = t.T.astype(bf16).reshape(nz, r, LANES)
        slots[at + (every, pl.ds(r, r))] = gup[:, pl.ds(d * LANES, LANES)].astype(bf16).reshape(nz, r, LANES)
        for z in range(nz):
            for s in range(2):
                slots[at + (z, pl.ds(2 * r + s * n, n))] = gdown_t[
                    pl.ds(d * n, n), pl.ds(z * deep + s * LANES, LANES)
                ].astype(bf16)
        both = jnp.concatenate([char_a[d * gc : (d + 1) * gc], char_b[d * gc : (d + 1) * gc]], 0)
        side = jnp.where(spot == 0, both, 0.0)
        side = jnp.where(spot == 1, word_a[d * p : (d + 1) * p], side)
        side = jnp.where(spot == 2, word_b[d * p : (d + 1) * p], side)
        t = jnp.concatenate([gpool_t[pl.ds(d * p, p), :], side], 0)
        slots[at + (every, pl.ds(3 * r, r))] = t.T.astype(bf16).reshape(nz, r, LANES)


def finish_kernel(
    char_ref, word_ref, cqkv, cproj, cup, cdown, cga, cgb, pool, wqkv, wproj, wup, wdown, wga, wgb
):
    r = cup.shape[0]
    n = cqkv.shape[1]
    cqkv[...] = char_ref[pl.ds(0, r), :n]
    cproj[...] = char_ref[pl.ds(0, r), n:]
    cup[...] = char_ref[pl.ds(r, r), :]
    down_t = jnp.concatenate([char_ref[pl.ds(2 * r, r // 2), :], char_ref[pl.ds(2 * r + r // 2, r // 2), :]], 1)
    cdown[...] = down_t.T
    p = pool.shape[1]
    pool[...] = char_ref[pl.ds(3 * r, r), :p]
    gc = cga.shape[1]
    side = char_ref[pl.ds(3 * r, 8), :]
    cga[...] = side[0:1, p : p + gc]
    cgb[...] = side[0:1, p + gc :]
    wga[...] = side[1:2, p:]
    wgb[...] = side[2:3, p:]
    r = wup.shape[0]
    n = wqkv.shape[1]
    wqkv[...] = word_ref[pl.ds(0, r), :n]
    wproj[...] = word_ref[pl.ds(0, r), n:]
    wup[...] = word_ref[pl.ds(r, r), :]
    down_t = jnp.concatenate([word_ref[pl.ds(2 * r, r // 2), :], word_ref[pl.ds(2 * r + r // 2, r // 2), :]], 1)
    wdown[...] = down_t.T


def finish(char_sum, word_sum, like):
    shapes = [jax.ShapeDtypeStruct(s.shape if s.ndim == 2 else (1, s.shape[0]), f32) for s in like]
    outs = pl.pallas_call(finish_kernel, out_shape=shapes, name="finish")(char_sum, word_sum)
    return [o.reshape(s.shape) for o, s in zip(outs, like)]


def backward_scatter_kernel(
    letters, dp_ref, tok_ref, ga_ref, gb_ref, wqkv_ref, wproj_ref, wup_ref, wdown_ref,
    word_send, gpool_t, gwga, gwgb,
    t_ref, o_ref, p_ref, z1_ref, rs1_ref, z2_ref, rs2_ref, m_ref, gp_ref,
    cg_ref, char_out, word_out,
    dh2_ref, du_ref, dh1b_ref, do_ref, dt_ref, gqkv_ref, gproj_ref, gup_ref, gdown_ref, gga_ref, ggb_ref,
    own_sem, char_send, *work,
):
    step = pl.program_id(0)
    y, x, c, z = place()
    word_work, char_work = work[: len(work) // 2], work[len(work) // 2 :]
    word_acc = word_work[0]
    own = pltpu.make_async_copy(word_send.at[:, :, c], word_acc, own_sem)

    @pl.when(step == 0)
    def _():
        greet()
        own.start()
        start_all(scatter_stage(0, word_send, word_work))

    for n, when in enumerate((2, 5, 8, 11)):
        @pl.when(step == when)
        def _():
            arrive_all(scatter_stage(n, word_send, word_work))
            if n == 0:
                own.wait()
            scatter_sum(n, lambda b, a, k: word_acc[b, a, k], word_work, word_out)
            if n < 3:
                start_all(scatter_stage(n + 1, word_send, word_work))

    char_backward_kernel(
        letters, dp_ref, tok_ref, ga_ref, gb_ref, wqkv_ref, wproj_ref, wup_ref, wdown_ref,
        t_ref, o_ref, p_ref, z1_ref, rs1_ref, z2_ref, rs2_ref, m_ref, gp_ref,
        cg_ref, gqkv_ref, gproj_ref, gup_ref, gdown_ref, gga_ref, ggb_ref,
        dh2_ref, du_ref, dh1b_ref, do_ref, dt_ref,
    )

    @pl.when(step == pl.num_programs(0) - 1)
    def _():
        pack_char_grads(char_send, gqkv_ref, gproj_ref, gup_ref, gdown_ref, gpool_t, gga_ref, ggb_ref, gwga, gwgb)
        for n in range(4):
            copies = scatter_stage(n, char_send, char_work)
            start_all(copies)
            arrive_all(copies)
            scatter_sum(n, lambda b, a, k: char_send[b, a, c, k], char_work, char_out)
        for n in range(4):
            sent_all([scatter_stage(n, char_send, char_work), scatter_stage(n, word_send, word_work)])


def backward_scatter(dp, tok, ga, gb, weights, word_send, gpool_t, gwga, gwgb, saved, letters):
    wqkv, wproj, wup, wdown = weights
    t = saved[0]
    steps = t.shape[0]
    width = wqkv.shape[0]
    hidden = wup.shape[1]
    per = LANES * letters // STEP
    ny, nx, nz = sides()
    char_rows = 4 * width // nz
    word_rows, word_lanes = word_send.shape[4:]

    def whole(shape):
        return (jax.ShapeDtypeStruct(shape, f32), pl.BlockSpec(shape, lambda i: (0, 0)))

    outs = [
        (jax.ShapeDtypeStruct((steps * STEP, width), bf16), pl.BlockSpec((STEP, width), lambda i: (i, 0))),
        whole((char_rows, LANES)), whole((word_rows, word_lanes)),
    ]
    return pl.pallas_call(
        functools.partial(backward_scatter_kernel, letters),
        grid=(steps,),
        in_specs=[
            pl.BlockSpec((width, LANES), lambda i: (0, i // per)),
            pl.BlockSpec((1, 1, STEP), lambda i: (i, 0, 0)),
        ] + [full_spec(a) for a in (ga, gb, *weights)] + [pl.BlockSpec(memory_space=pl.ANY)]
        + [full_spec(a) for a in (gpool_t, gwga, gwgb)]
        + [pl.BlockSpec((1,) + s.shape[1:], lambda i: (i, 0, 0)) for s in saved],
        out_specs=[o[1] for o in outs],
        out_shape=[o[0] for o in outs],
        scratch_shapes=[
            pltpu.VMEM((width, STEP), bf16),
            pltpu.VMEM((hidden, STEP), bf16),
            pltpu.VMEM((width, STEP), bf16),
            pltpu.VMEM((width, STEP), bf16),
            pltpu.VMEM((3 * width, STEP), bf16),
            pltpu.VMEM((3 * width, width), f32),
            pltpu.VMEM((width, width), f32),
            pltpu.VMEM((width, hidden), f32),
            pltpu.VMEM((width, hidden), f32),
            pltpu.VMEM((width, LANES), f32),
            pltpu.VMEM((width, LANES), f32),
            pltpu.SemaphoreType.DMA,
            pltpu.VMEM((ny, nx, 2, nz, char_rows, LANES), bf16),
        ] + scatter_scratch(word_rows, word_lanes) + scatter_scratch(char_rows, LANES),
        compiler_params=pltpu.CompilerParams(
            dimension_semantics=("arbitrary",), vmem_limit_bytes=58 * 2**20, collective_id=1, has_side_effects=True
        ),
        name="backward_scatter",
    )(dp, tok, ga, gb, *weights, word_send, gpool_t, gwga, gwgb, *saved)


def gather_all(shards, counts):
    flat = jnp.concatenate([s.reshape(-1) for s in shards])
    packed = lax.all_gather(lax.all_gather(flat, "fsdp", axis=0), "dp", axis=0)
    wide_count, deep_count = packed.shape[:2]
    out, start = [], 0
    for s in shards:
        piece = packed[:, :, start : start + s.size]
        start += s.size
        if s.ndim == 1:
            out.append(piece[:, 0].reshape(-1))
        else:
            r, c = s.shape
            piece = piece.reshape(wide_count, deep_count, r, c).transpose(1, 2, 0, 3)
            out.append(piece.reshape(deep_count * r, wide_count * c))
    return out


def scatter_all(grads, shards):
    wide_count, deep_count = lax.axis_size("dp"), lax.axis_size("fsdp")
    pieces = []
    for g, s in zip(grads, shards):
        g = g.astype(bf16)
        if s.ndim == 1:
            g = jnp.broadcast_to(g.reshape(wide_count, 1, s.size), (wide_count, deep_count, s.size))
        else:
            r, c = s.shape
            g = g.reshape(deep_count, r, wide_count, c).transpose(2, 0, 1, 3)
        pieces.append(g.reshape(wide_count, deep_count, s.size))
    packed = jnp.concatenate(pieces, 2)
    packed = lax.psum_scatter(packed, "dp", scatter_dimension=0, tiled=True)
    packed = lax.psum_scatter(packed, "fsdp", scatter_dimension=1, tiled=True).reshape(-1)
    out, start = [], 0
    for s in shards:
        out.append(packed[start : start + s.size].reshape(s.shape).astype(f32))
        start += s.size
    return out


def shards_plain(
    characters, counts, separators, cotangent, char_qkv, char_proj, char_up, char_down, char_gain_a, char_gain_b,
    pool_proj, word_qkv, word_proj, word_up, word_down, word_gain_a, word_gain_b,
):
    rows, length, letters, width = characters.shape
    char_shards = (char_qkv, char_proj, char_up, char_down, char_gain_a, char_gain_b)
    word_shards = (pool_proj, word_qkv, word_proj, word_up, word_down, word_gain_a, word_gain_b)
    cqkv, cproj, cup, cdown, cga, cgb = gather_all(char_shards, counts)
    wpool, wqkv, wproj, wup, wdown, wga, wgb = gather_all(word_shards, counts)
    x = characters.reshape(length * letters, width)
    tok = jnp.repeat(counts, letters, axis=1).reshape(length * letters // STEP, 1, STEP)
    cga, cgb, wga, wgb = (
        jnp.broadcast_to(g.astype(f32)[:, None], (g.shape[0], LANES)) for g in (cga, cgb, wga, wgb)
    )
    *saved, pool_sum = char_forward(x, tok, counts, cga, cgb, cqkv.T, cproj.T, cup.T, cdown.T, letters)
    word_out, dpool, gpool, gwqkv, gwproj, gwup, gwdown, gwga, gwgb = word_layer(
        pool_sum, counts.astype(f32), separators, cotangent.reshape(length, -1), wga, wgb, wpool, wqkv, wproj, wup, wdown
    )
    word_grads = scatter_all(
        (gpool, gwqkv, gwproj, gwup, gwdown, jnp.sum(gwga, 1), jnp.sum(gwgb, 1)), word_shards
    )
    char_grad, gcqkv, gcproj, gcup, gcdown, gcga, gcgb = char_backward(
        dpool, tok, cga, cgb, cqkv, cproj, cup, cdown, saved, letters
    )
    char_grads = scatter_all(
        (gcqkv, gcproj, gcup, gcdown, jnp.sum(gcga, 1), jnp.sum(gcgb, 1)), char_shards
    )
    return (word_out[None], char_grad.reshape(characters.shape), *char_grads, *word_grads)


def shards_packed(
    characters, counts, separators, cotangent, char_qkv, char_proj, char_up, char_down, char_gain_a, char_gain_b,
    pool_proj, word_qkv, word_proj, word_up, word_down, word_gain_a, word_gain_b,
):
    rows, length, letters, width = characters.shape
    x = characters.reshape(length * letters, width)
    tok = jnp.repeat(counts, letters, axis=1).reshape(length * letters // STEP, 1, STEP)
    gains = jnp.concatenate([char_gain_a, char_gain_b, word_gain_a, word_gain_b]).astype(f32).reshape(3, -1)
    (
        *saved, pool_sum, word_all, cqkv, cproj, cup, cdown, pool_t, cga, cgb, wga, wgb
    ) = forward_gather(
        x, tok, counts, (char_qkv, char_proj, char_up, char_down, pool_proj, gains),
        (word_qkv, word_proj, word_up, word_down), letters,
    )
    word_out, dpool, gpool_t, word_send, gwga, gwgb = word_gathered(
        pool_sum, counts.astype(f32), separators, cotangent.reshape(length, -1), wga, wgb, pool_t,
        word_all.reshape((-1,) + word_all.shape[3:]),
    )
    char_grad, char_sum, word_sum = backward_scatter(
        dpool, tok, cga, cgb, (cqkv, cproj, cup, cdown), word_send.reshape(word_all.shape), gpool_t, gwga, gwgb,
        saved, letters,
    )
    like = (
        char_qkv, char_proj, char_up, char_down, char_gain_a, char_gain_b,
        pool_proj, word_qkv, word_proj, word_up, word_down, word_gain_a, word_gain_b,
    )
    return (word_out[None], char_grad.reshape(characters.shape), *finish(char_sum, word_sum, like))


def shards(*arrays):
    char_qkv, char_proj, word_qkv, word_proj = arrays[4], arrays[5], arrays[11], arrays[12]
    tiles = (char_qkv.shape[1] + char_proj.shape[1]) // LANES, (word_qkv.shape[1] + word_proj.shape[1]) // LANES
    return (shards_packed if tiles == (1, 2) else shards_plain)(*arrays)


def solution(mesh):
    rows = ("dp", "fsdp")
    matrix, vector = P("fsdp", "dp"), P("dp")
    data = (P(rows, None, None, None), P(rows, None), P(rows, None), P(rows, None, None))
    block = (matrix,) * 4 + (vector,) * 2
    word = (matrix,) * 5 + (vector,) * 2
    return jax.shard_map(
        shards,
        mesh=mesh,
        in_specs=data + block + word,
        out_specs=(data[3], data[0]) + block + word,
        check_vma=False,
    )
```

```python
import functools
import math

import jax
import jax.numpy as jnp
from jax import lax
from jax.experimental import pallas as pl
from jax.experimental.pallas import tpu as pltpu
from jax.sharding import PartitionSpec as P

CHAR_HEADS = 4
WORD_HEADS = 8
EPS = 1e-05
NEGATIVE = -1e30
LANES = 128
SPAN = 256
STEP = 512
BATCH = 1024
VMEM_BYTES = 60 * 2**20
GELU_A = 0.7978845608028654
GELU_B = 0.044715

bf16 = jnp.bfloat16
f32 = jnp.float32


def dot(a, b):
    return jnp.dot(a, b, preferred_element_type=f32)


def dot_nt(a, b):
    return lax.dot_general(a, b, (((1,), (1,)), ((), ())), preferred_element_type=f32)


def normed(v):
    c = v - jnp.mean(v, 0, keepdims=True)
    rs = lax.rsqrt(jnp.mean(c * c, 0, keepdims=True) + EPS)
    return c * rs, rs


def wide(g, n):
    return g if n == g.shape[1] else jnp.concatenate([g] * (n // g.shape[1]), 1)


def gelu_both(u):
    s = u * u
    t = jnp.tanh(u * (GELU_A + (GELU_A * GELU_B) * s))
    h = 0.5 * u
    r = 0.5 + 0.5 * t
    slope = r + h * (1.0 - t * t) * (GELU_A + (3.0 * GELU_A * GELU_B) * s)
    return u * r, slope


def lane_word(letters):
    return lax.broadcasted_iota(jnp.int32, (letters, LANES), 1) // letters


def pick_own(full, owner, letters):
    words = LANES // letters
    out = full[:letters]
    for w in range(1, words):
        out = jnp.where(owner == w, full[w * letters : (w + 1) * letters], out)
    return out


def own_blocks(letters):
    a = lax.broadcasted_iota(jnp.int32, (LANES, LANES), 0) // letters
    b = lax.broadcasted_iota(jnp.int32, (LANES, LANES), 1) // letters
    return jnp.where(a == b, 1.0, 0.0).astype(bf16)


def spread_own(compact, blocks, letters):
    return jnp.concatenate([compact] * (LANES // letters), 0) * blocks


def char_forward_kernel(
    letters, x_ref, tok_ref, cnt_ref, ga_ref, gb_ref, wqkv_ref, wproj_ref, wup_ref, wdown_ref,
    t_ref, o_ref, p_ref, z1_ref, rs1_ref, z2_ref, rs2_ref, m_ref, gp_ref, pool_ref,
):
    step = pl.program_id(0)
    width = x_ref.shape[1]
    head = width // CHAR_HEADS
    scale = head ** (-0.5)
    steps_per_block = LANES * letters // STEP
    owner = lane_word(letters)
    blocks = own_blocks(letters)
    key_slot = lax.broadcasted_iota(jnp.int32, (letters, LANES), 0)

    @pl.when(step % steps_per_block == 0)
    def _():
        pool_ref[...] = jnp.zeros_like(pool_ref)

    for part in range(STEP // SPAN):
        at = pl.ds(part * SPAN, SPAN)
        x = x_ref[at, :].astype(f32).T
        z1, rs1 = normed(x)
        z1_ref[0, :, at] = z1.astype(bf16)
        rs1_ref[0, :, at] = rs1
        a1 = (z1 * wide(ga_ref[...], SPAN)).astype(bf16)
        for n in range(3):
            rows = pl.ds(n * width, width)
            t_ref[0, rows, at] = dot(wqkv_ref[rows, :], a1).astype(bf16)
        for g in range(SPAN // LANES):
            lanes = pl.ds(part * SPAN + g * LANES, LANES)
            allowed = key_slot < tok_ref[0, :, lanes]
            for h in range(CHAR_HEADS):
                q = t_ref[0, pl.ds(h * head, head), lanes]
                k = t_ref[0, pl.ds(width + h * head, head), lanes]
                v = t_ref[0, pl.ds(2 * width + h * head, head), lanes]
                full = dot(k.T, q)
                s = jnp.where(allowed, pick_own(full, owner, letters) * scale, NEGATIVE)
                e = jnp.exp(s - jnp.max(s, 0, keepdims=True))
                p = e / jnp.sum(e, 0, keepdims=True)
                p_ref[0, pl.ds(h * letters, letters), lanes] = p
                o = dot(v, spread_own(p.astype(bf16), blocks, letters))
                o_ref[0, pl.ds(h * head, head), lanes] = o.astype(bf16)
        h1 = x + dot(wproj_ref[...], o_ref[0, :, at])
        z2, rs2 = normed(h1)
        z2_ref[0, :, at] = z2.astype(bf16)
        rs2_ref[0, :, at] = rs2
        a2 = (z2 * wide(gb_ref[...], SPAN)).astype(bf16)
        for n in range(wup_ref.shape[0] // 256):
            rows = pl.ds(n * 256, 256)
            m, gp = gelu_both(dot(wup_ref[rows, :], a2))
            m_ref[0, rows, at] = m.astype(bf16)
            gp_ref[0, rows, at] = gp.astype(bf16)
        h2 = h1 + dot(wdown_ref[...], m_ref[0, :, at])
        high = h2.astype(bf16)
        low = (h2 - high.astype(f32)).astype(bf16)
        row = lax.broadcasted_iota(jnp.int32, (SPAN, LANES), 0)
        word = lax.broadcasted_iota(jnp.int32, (SPAN, LANES), 1)
        first = (step % steps_per_block) * (STEP // letters) + part * (SPAN // letters)
        mine = (row // letters + first == word) & (row % letters < cnt_ref[...])
        gather = jnp.where(mine, 1.0, 0.0).astype(bf16)
        pool_ref[...] += dot(high, gather) + dot(low, gather)


def full_spec(a):
    nd = len(a.shape)
    return pl.BlockSpec(a.shape, lambda i: (0,) * nd)


def char_forward(x, tok, cnt, ga, gb, wqkv_t, wproj_t, wup_t, wdown_t, letters):
    tokens, width = x.shape
    steps = tokens // STEP
    hidden = wup_t.shape[0]
    per = LANES * letters // STEP

    def strip(rows, dtype=bf16):
        return (
            jax.ShapeDtypeStruct((steps, rows, STEP), dtype),
            pl.BlockSpec((1, rows, STEP), lambda i: (i, 0, 0)),
        )

    outs = [
        strip(3 * width), strip(width), strip(CHAR_HEADS * letters, f32), strip(width), strip(1, f32),
        strip(width), strip(1, f32), strip(hidden), strip(hidden),
        (jax.ShapeDtypeStruct((width, tokens // letters), f32), pl.BlockSpec((width, LANES), lambda i: (0, i // per))),
    ]
    return pl.pallas_call(
        functools.partial(char_forward_kernel, letters),
        grid=(steps,),
        in_specs=[
            pl.BlockSpec((STEP, width), lambda i: (i, 0)),
            pl.BlockSpec((1, 1, STEP), lambda i: (i, 0, 0)),
            pl.BlockSpec((1, LANES), lambda i: (0, i // per)),
        ] + [full_spec(a) for a in (ga, gb, wqkv_t, wproj_t, wup_t, wdown_t)],
        out_specs=[o[1] for o in outs],
        out_shape=[o[0] for o in outs],
        compiler_params=pltpu.CompilerParams(
            dimension_semantics=("arbitrary",), vmem_limit_bytes=56 * 2**20
        ),
        name="char_forward",
    )(x, tok, cnt, ga, gb, wqkv_t, wproj_t, wup_t, wdown_t)


def norm_back(dy, z, rs, gain):
    dz = dy * gain
    a = jnp.mean(dz, 0, keepdims=True)
    b = jnp.mean(dz * z, 0, keepdims=True)
    return rs * (dz - a - z * b)


def fold_lanes(v):
    out = v[:, :LANES]
    for n in range(1, v.shape[1] // LANES):
        out = out + v[:, n * LANES : (n + 1) * LANES]
    return out


def char_backward_kernel(
    letters, dp_ref, tok_ref, ga_ref, gb_ref, wqkv_ref, wproj_ref, wup_ref, wdown_ref,
    t_ref, o_ref, p_ref, z1_ref, rs1_ref, z2_ref, rs2_ref, m_ref, gp_ref,
    cg_ref, gqkv_ref, gproj_ref, gup_ref, gdown_ref, gga_ref, ggb_ref,
    dh2_ref, du_ref, dh1b_ref, do_ref, dt_ref,
):
    step = pl.program_id(0)
    width = cg_ref.shape[1]
    head = width // CHAR_HEADS
    scale = head ** (-0.5)
    steps_per_block = LANES * letters // STEP
    owner = lane_word(letters)
    blocks = own_blocks(letters)

    @pl.when(step == 0)
    def _():
        for ref in (gqkv_ref, gproj_ref, gup_ref, gdown_ref, gga_ref, ggb_ref):
            ref[...] = jnp.zeros_like(ref)

    for part in range(STEP // SPAN):
        at = pl.ds(part * SPAN, SPAN)
        word = lax.broadcasted_iota(jnp.int32, (LANES, SPAN), 0)
        col = lax.broadcasted_iota(jnp.int32, (LANES, SPAN), 1)
        first = (step % steps_per_block) * (STEP // letters) + part * (SPAN // letters)
        mine = (col // letters + first == word) & (col % letters < tok_ref[0, :, at])
        scatter = jnp.where(mine, 1.0, 0.0).astype(bf16)
        dh2 = dot(dp_ref[...], scatter)
        dh2b = dh2.astype(bf16)
        dh2_ref[:, at] = dh2b
        for n in range(wdown_ref.shape[0] // 256):
            rows = pl.ds(n * 256, 256)
            du_ref[rows, at] = (dot(wdown_ref[rows, :], dh2b) * gp_ref[0, rows, at].astype(f32)).astype(bf16)
        dy = dot(wup_ref[...], du_ref[:, at])
        z = z2_ref[0, :, at].astype(f32)
        ggb_ref[...] += fold_lanes(dy * z)
        dh1 = dh2 + norm_back(dy, z, rs2_ref[0, :, at], wide(gb_ref[...], SPAN))
        dh1b = dh1.astype(bf16)
        dh1b_ref[:, at] = dh1b
        do_ref[:, at] = dot(wproj_ref[...], dh1b).astype(bf16)
        for g in range(SPAN // LANES):
            lanes = pl.ds(part * SPAN + g * LANES, LANES)
            for h in range(CHAR_HEADS):
                q_rows = pl.ds(h * head, head)
                k_rows = pl.ds(width + h * head, head)
                v_rows = pl.ds(2 * width + h * head, head)
                q = t_ref[0, q_rows, lanes]
                k = t_ref[0, k_rows, lanes]
                v = t_ref[0, v_rows, lanes]
                do = do_ref[pl.ds(h * head, head), lanes]
                p = p_ref[0, pl.ds(h * letters, letters), lanes]
                dp = pick_own(dot(v.T, do), owner, letters)
                ds = p * (dp - jnp.sum(p * dp, 0, keepdims=True))
                pb = spread_own(p.astype(bf16), blocks, letters)
                dsb = spread_own(ds.astype(bf16), blocks, letters)
                dt_ref[q_rows, lanes] = (dot(k, dsb) * scale).astype(bf16)
                dt_ref[k_rows, lanes] = (dot_nt(q, dsb) * scale).astype(bf16)
                dt_ref[v_rows, lanes] = dot_nt(do, pb).astype(bf16)
        dy = dot(wqkv_ref[...], dt_ref[:, at])
        z = z1_ref[0, :, at].astype(f32)
        gga_ref[...] += fold_lanes(dy * z)
        dx = dh1 + norm_back(dy, z, rs1_ref[0, :, at], wide(ga_ref[...], SPAN))
        cg_ref[at, :] = dx.T.astype(bf16)
    gdown_ref[...] += dot_nt(dh2_ref[...], m_ref[0])
    gup_ref[...] += dot_nt(z2_ref[0], du_ref[...])
    gproj_ref[...] += dot_nt(dh1b_ref[...], o_ref[0])
    gqkv_ref[...] += dot_nt(dt_ref[...], z1_ref[0])

    @pl.when(step == pl.num_programs(0) - 1)
    def _():
        gup_ref[...] = gup_ref[...] * wide(gb_ref[...], gup_ref.shape[1])
        gqkv_ref[...] = gqkv_ref[...] * ga_ref[...].T[:1]


def char_backward(dp, tok, ga, gb, wqkv, wproj, wup, wdown, saved, letters):
    t, o, p, z1, rs1, z2, rs2, m, gp = saved
    steps = t.shape[0]
    width = wqkv.shape[0]
    hidden = wup.shape[1]
    per = LANES * letters // STEP

    def whole(shape):
        return (jax.ShapeDtypeStruct(shape, f32), pl.BlockSpec(shape, lambda i: (0, 0)))

    outs = [
        (jax.ShapeDtypeStruct((steps * STEP, width), bf16), pl.BlockSpec((STEP, width), lambda i: (i, 0))),
        whole((3 * width, width)), whole((width, width)), whole((width, hidden)), whole((width, hidden)),
        whole((width, LANES)), whole((width, LANES)),
    ]
    return pl.pallas_call(
        functools.partial(char_backward_kernel, letters),
        grid=(steps,),
        in_specs=[
            pl.BlockSpec((width, LANES), lambda i: (0, i // per)),
            pl.BlockSpec((1, 1, STEP), lambda i: (i, 0, 0)),
        ] + [full_spec(a) for a in (ga, gb, wqkv, wproj, wup, wdown)]
        + [pl.BlockSpec((1,) + s.shape[1:], lambda i: (i, 0, 0)) for s in saved],
        out_specs=[o[1] for o in outs],
        out_shape=[o[0] for o in outs],
        scratch_shapes=[
            pltpu.VMEM((width, STEP), bf16),
            pltpu.VMEM((hidden, STEP), bf16),
            pltpu.VMEM((width, STEP), bf16),
            pltpu.VMEM((width, STEP), bf16),
            pltpu.VMEM((3 * width, STEP), bf16),
        ],
        compiler_params=pltpu.CompilerParams(
            dimension_semantics=("arbitrary",), vmem_limit_bytes=56 * 2**20
        ),
        name="char_backward",
    )(dp, tok, ga, gb, wqkv, wproj, wup, wdown, *saved)


def word_kernel(
    pool_sum_ref, cnt_ref, sep_ref, cot_ref, ga_ref, gb_ref, wpool_ref, wqkv_ref, wproj_ref, wup_ref, wdown_ref,
    out_ref, dpool_ref, gpool_ref, gqkv_ref, gproj_ref, gup_ref, gdown_ref, gga_ref, ggb_ref,
    pooled, x, z3, rs3, a3, t, p, o, h3, z4, rs4, a4, m, gp, bias, cot, du, dh3, dh3b, do, dt, dtk,
):
    width, length = x.shape
    head = width // WORD_HEADS
    scale = head ** (-0.5)
    halves = [pl.ds(n * SPAN, SPAN) for n in range(length // SPAN)]
    pooled[...] = (pool_sum_ref[...] / cnt_ref[...]).astype(bf16)
    row = lax.broadcasted_iota(jnp.int32, (length, length), 0)
    col = lax.broadcasted_iota(jnp.int32, (length, length), 1)
    tri = jnp.where(row <= col, 1.0, 0.0).astype(bf16)
    sep = jnp.broadcast_to(sep_ref[...].astype(f32).astype(bf16), (16, length))
    doc_q = dot(sep, tri)[:1]
    doc_k = lax.dot_general(tri, sep, (((0,), (1,)), ((), ())), preferred_element_type=f32)[:, :1]
    bias[...] = jnp.where((row <= col) & (doc_k == doc_q), 0.0, NEGATIVE)
    cot[...] = cot_ref[...].astype(f32).T.astype(bf16)
    for at in halves:
        x[:, at] = lax.dot_general(
            wpool_ref[...], pooled[:, at], (((0,), (0,)), ((), ())), preferred_element_type=f32
        )
        z, rs = normed(x[:, at])
        z3[:, at] = z.astype(bf16)
        rs3[:, at] = rs
        a3[:, at] = (z * wide(ga_ref[...], SPAN)).astype(bf16)
        for n in range(3):
            rows = pl.ds(n * width, width)
            t[rows, at] = lax.dot_general(
                wqkv_ref[:, rows], a3[:, at], (((0,), (0,)), ((), ())), preferred_element_type=f32
            ).astype(bf16)
    for h in range(WORD_HEADS):
        k = t[pl.ds(width + h * head, head), :].T
        for n, at in enumerate(halves):
            seen = (n + 1) * SPAN
            keys = pl.ds(0, seen)
            q = t[pl.ds(h * head, head), at]
            s = dot(k[:seen], q) * scale + bias[keys, at]
            e = jnp.exp(s - jnp.max(s, 0, keepdims=True))
            w = e / jnp.sum(e, 0, keepdims=True)
            p[h, keys, at] = w
            o[pl.ds(h * head, head), at] = dot(t[pl.ds(2 * width + h * head, head), keys], w.astype(bf16)).astype(bf16)
    for at in halves:
        h3[:, at] = x[:, at] + lax.dot_general(
            wproj_ref[...], o[:, at], (((0,), (0,)), ((), ())), preferred_element_type=f32
        )
        z, rs = normed(h3[:, at])
        z4[:, at] = z.astype(bf16)
        rs4[:, at] = rs
        a4[:, at] = (z * wide(gb_ref[...], SPAN)).astype(bf16)
        for n in range(wup_ref.shape[1] // 256):
            rows = pl.ds(n * 256, 256)
            mm, gg = gelu_both(
                lax.dot_general(wup_ref[:, rows], a4[:, at], (((0,), (0,)), ((), ())), preferred_element_type=f32)
            )
            m[rows, at] = mm.astype(bf16)
            gp[rows, at] = gg.astype(bf16)
        out = h3[:, at] + lax.dot_general(
            wdown_ref[...], m[:, at], (((0,), (0,)), ((), ())), preferred_element_type=f32
        )
        out_ref[at, :] = out.T.astype(bf16)
        for n in range(wdown_ref.shape[0] // 256):
            rows = pl.ds(n * 256, 256)
            du[rows, at] = (dot(wdown_ref[rows, :], cot[:, at]) * gp[rows, at].astype(f32)).astype(bf16)
        dy = dot(wup_ref[...], du[:, at])
        z = z4[:, at].astype(f32)
        part = fold_lanes(dy * z)
        ggb_ref[...] = part if at is halves[0] else ggb_ref[...] + part
        dh3[:, at] = cot[:, at].astype(f32) + norm_back(dy, z, rs4[:, at], wide(gb_ref[...], SPAN))
        dh3b[:, at] = dh3[:, at].astype(bf16)
        do[:, at] = dot(wproj_ref[...], dh3b[:, at]).astype(bf16)
    gdown_ref[...] = dot_nt(m[...], cot[...]).astype(gdown_ref.dtype)
    gup_ref[...] = dot_nt(a4[...], du[...]).astype(gup_ref.dtype)
    gproj_ref[...] = dot_nt(o[...], dh3b[...]).astype(gproj_ref.dtype)
    for h in range(WORD_HEADS):
        q_rows = pl.ds(h * head, head)
        k_rows = pl.ds(width + h * head, head)
        v_rows = pl.ds(2 * width + h * head, head)
        v = t[v_rows, :].T
        for n in reversed(range(len(halves))):
            at = halves[n]
            seen = (n + 1) * SPAN
            keys = pl.ds(0, seen)
            w = p[h, keys, at]
            g = do[q_rows, at]
            dp = dot(v[:seen], g)
            ds = (w * (dp - jnp.sum(w * dp, 0, keepdims=True))).astype(bf16)
            dt[q_rows, at] = (dot(t[k_rows, keys], ds) * scale).astype(bf16)
            dk = dot_nt(t[q_rows, at], ds) * scale
            dv = dot_nt(g, w.astype(bf16))
            if n == len(halves) - 1:
                dtk[0] = dk
                dtk[1] = dv
            else:
                dtk[0, :, keys] += dk
                dtk[1, :, keys] += dv
        dt[k_rows, :] = dtk[0].astype(bf16)
        dt[v_rows, :] = dtk[1].astype(bf16)
    gqkv_ref[...] = dot_nt(a3[...], dt[...]).astype(gqkv_ref.dtype)
    for at in halves:
        dy = dot(wqkv_ref[...], dt[:, at])
        z = z3[:, at].astype(f32)
        part = fold_lanes(dy * z)
        gga_ref[...] = part if at is halves[0] else gga_ref[...] + part
        dx = dh3[:, at] + norm_back(dy, z, rs3[:, at], wide(ga_ref[...], SPAN))
        dh3b[:, at] = dx.astype(bf16)
        dpool_ref[:, at] = (dot(wpool_ref[...], dh3b[:, at]) / cnt_ref[:, at]).astype(bf16)
    gpool_ref[...] = dot_nt(pooled[...], dh3b[...]).astype(gpool_ref.dtype)


def word_layer(pool_sum, cnt, sep, cot, ga, gb, wpool, wqkv, wproj, wup, wdown, grad_type=f32):
    length, width = cot.shape
    inner = pool_sum.shape[0]
    hidden = wup.shape[1]
    vm = pltpu.VMEM
    return pl.pallas_call(
        word_kernel,
        out_shape=[
            jax.ShapeDtypeStruct((length, width), bf16),
            jax.ShapeDtypeStruct((inner, length), bf16),
            jax.ShapeDtypeStruct(wpool.shape, grad_type),
            jax.ShapeDtypeStruct(wqkv.shape, grad_type),
            jax.ShapeDtypeStruct(wproj.shape, grad_type),
            jax.ShapeDtypeStruct(wup.shape, grad_type),
            jax.ShapeDtypeStruct(wdown.shape, grad_type),
            jax.ShapeDtypeStruct((width, LANES), f32),
            jax.ShapeDtypeStruct((width, LANES), f32),
        ],
        scratch_shapes=[
            vm((inner, length), bf16), vm((width, length), f32), vm((width, length), bf16), vm((1, length), f32),
            vm((width, length), bf16), vm((3 * width, length), bf16), vm((WORD_HEADS, length, length), f32),
            vm((width, length), bf16), vm((width, length), f32), vm((width, length), bf16), vm((1, length), f32),
            vm((width, length), bf16), vm((hidden, length), bf16), vm((hidden, length), bf16),
            vm((length, length), f32), vm((width, length), bf16), vm((hidden, length), bf16),
            vm((width, length), f32), vm((width, length), bf16), vm((width, length), bf16),
            vm((3 * width, length), bf16), vm((2, width // WORD_HEADS, length), f32),
        ],
        compiler_params=pltpu.CompilerParams(vmem_limit_bytes=58 * 2**20),
        name="word_layer",
    )(pool_sum, cnt, sep, cot, ga, gb, wpool, wqkv, wproj, wup, wdown)


MESH = pl.DeviceIdType.MESH


def sides():
    chips = lax.axis_size("dp") // 2
    nx = math.isqrt(chips)
    return chips // nx, nx, lax.axis_size("fsdp")


def place():
    ny, nx, nz = sides()
    me = lax.axis_index("dp")
    return me // (2 * nx), (me // 2) % nx, me % 2, lax.axis_index("fsdp")


def device(y, x, c, z):
    return {"dp": (y * sides()[1] + x) * 2 + c, "fsdp": z}


def partners():
    ny, nx, nz = sides()
    y, x, c, z = place()
    found = [device(y, x, 1 - c, z)]
    found += [device(y, x, c, (z + k) % nz) for k in range(1, nz)]
    found += [device(y, (x + k) % nx, c, z) for k in range(1, nx)]
    found += [device((y + k) % ny, x, c, z) for k in range(1, ny)]
    return found


def greet():
    barrier = pltpu.get_barrier_semaphore()
    for other in partners():
        pl.semaphore_signal(barrier, inc=1, device_id=other, device_id_type=MESH)
    pl.semaphore_wait(barrier, len(partners()))


def remote(src, dst, sems, n, other):
    return pltpu.make_async_remote_copy(
        src_ref=src, dst_ref=dst, send_sem=sems.at[0, n], recv_sem=sems.at[1, n],
        device_id=other, device_id_type=MESH,
    )


def gather_copies():
    ny, nx, nz = sides()
    return nz - 1 + 1 + 4 * (nx - 1) + 4 * (ny - 1)


def gather_stages(ref, sems, wanted=(0, 1, 2, 3)):
    ny, nx, nz = sides()
    y, x, c, z = place()
    every = slice(None)
    half = ref.shape[4] // 2
    low, high = pl.ds(0, half), pl.ds(half, half)
    twin = device(y, x, 1 - c, z)
    plan = [[], [], [], []]
    plan[0] += [((y, x, c, z), device(y, x, c, (z + k) % nz)) for k in range(1, nz)]
    plan[1] += [((y, x, c, every, low), device(y, (x + k) % nx, c, z)) for k in range(1, nx)]
    plan[1] += [((y, x, c, every, high), device((y + k) % ny, x, c, z)) for k in range(1, ny)]
    plan[1] += [((y, x, c), twin)]
    plan[2] += [((y, every, c, every, low), device((y + k) % ny, x, c, z)) for k in range(1, ny)]
    plan[2] += [((every, x, c, every, high), device(y, (x + k) % nx, c, z)) for k in range(1, nx)]
    plan[2] += [((y, (x + k) % nx, c, every, low), twin) for k in range(1, nx)]
    plan[2] += [(((y + k) % ny, x, c, every, high), twin) for k in range(1, ny)]
    plan[3] += [(((y + k) % ny, every, c, every, low), twin) for k in range(1, ny)]
    plan[3] += [((every, (x + k) % nx, c, every, high), twin) for k in range(1, nx)]
    count = 0
    stages = []
    for n, part in enumerate(plan):
        copies = []
        for where, other in part:
            if n in wanted:
                copies.append(remote(ref.at[where], ref.at[where], sems, count, other))
            count += 1
        stages.append(copies)
    return stages


def start_all(copies):
    for copy in copies:
        copy.start()


def arrive_all(copies):
    for copy in copies:
        copy.wait_recv()


def sent_all(stages):
    for copies in stages:
        for copy in copies:
            copy.wait_send()


def lanes_to(v, n):
    return v if v.shape[1] == n else jnp.concatenate([v, jnp.zeros((v.shape[0], n - v.shape[1]), v.dtype)], 1)


def turned(v):
    return v.astype(f32).T.astype(bf16)


def scatter_copies():
    ny, nx, nz = sides()
    return 1 + 2 * (nx - 1) + 2 * (ny - 1) + nz - 1


def scatter_scratch(rows, lanes):
    ny, nx, nz = sides()
    half = rows // 2
    shapes = (
        (ny, nx, nz, rows, lanes), (ny, nx, nz, rows, lanes), (nx - 1, ny, nz, half, lanes),
        (ny - 1, nx, nz, half, lanes), (ny - 1, nz, half, lanes), (nx - 1, nz, half, lanes), (nz - 1, rows, lanes),
    )
    return [pltpu.VMEM(shape, bf16) for shape in shapes] + [pltpu.SemaphoreType.DMA((2, scatter_copies()))]


def scatter_stage(n, send, work):
    acc, twin_in, one_low, one_high, two_low, two_high, last_in, sems = work
    ny, nx, nz = sides()
    y, x, c, z = place()
    half = acc.shape[3] // 2
    low, high, every = pl.ds(0, half), pl.ds(half, half), slice(None)
    plan = [[], [], [], []]
    plan[0] += [(send, (every, every, 1 - c), twin_in, device(y, x, 1 - c, z))]
    plan[1] += [
        (acc, (every, (x + k) % nx, every, low), one_low.at[k - 1], device(y, (x + k) % nx, c, z)) for k in range(1, nx)
    ]
    plan[1] += [
        (acc, ((y + k) % ny, every, every, high), one_high.at[k - 1], device((y + k) % ny, x, c, z)) for k in range(1, ny)
    ]
    plan[2] += [
        (acc, ((y + k) % ny, x, every, low), two_low.at[k - 1], device((y + k) % ny, x, c, z)) for k in range(1, ny)
    ]
    plan[2] += [
        (acc, (y, (x + k) % nx, every, high), two_high.at[k - 1], device(y, (x + k) % nx, c, z)) for k in range(1, nx)
    ]
    plan[3] += [(acc, (y, x, (z + k) % nz), last_in.at[k - 1], device(y, x, c, (z + k) % nz)) for k in range(1, nz)]
    first = sum(len(p) for p in plan[:n])
    return [remote(src.at[at], dst, sems, first + i, other) for i, (src, at, dst, other) in enumerate(plan[n])]


def scatter_sum(n, own, work, out):
    acc, twin_in, one_low, one_high, two_low, two_high, last_in, sems = work
    ny, nx, nz = sides()
    y, x, c, z = place()
    half = acc.shape[3] // 2
    low, high = pl.ds(0, half), pl.ds(half, half)
    if n == 0:
        for b in range(ny):
            for a in range(nx):
                for k in range(nz):
                    acc[b, a, k] = own(b, a, k) + twin_in[b, a, k]
    elif n == 1:
        for k in range(nz):
            for b in range(ny):
                acc[b, x, k, low] += sum(one_low[i, b, k] for i in range(nx - 1))
            for a in range(nx):
                acc[y, a, k, high] += sum(one_high[i, a, k] for i in range(ny - 1))
    elif n == 2:
        for k in range(nz):
            acc[y, x, k, low] += sum(two_low[i, k] for i in range(ny - 1))
            acc[y, x, k, high] += sum(two_high[i, k] for i in range(nx - 1))
    else:
        out[...] = acc[y, x, z].astype(f32) + sum(last_in[i].astype(f32) for i in range(nz - 1))


def word_gathered_kernel(
    pool_sum_ref, cnt_ref, sep_ref, cot_ref, ga_ref, gb_ref, wpool_t, all0, all1, all2,
    out_ref, dpool_ref, gpool_ref, send0, send1, send2, gga_ref, ggb_ref,
    pooled, x, z3, rs3, a3, t, p, o, h3, z4, rs4, a4, m, gp, bias, cot, du, dh3, dh3b, do, dt, dtk,
    wqkv_t, wproj_t, wup_t, wdown_t, wqkv_ref, wproj_ref, wup_ref, wdown_ref, wpool_ref, gqkv_t, gproj_t,
):
    unpack_words(all0, all1, all2, wqkv_t, wproj_t, wup_t, wdown_t, wqkv_ref, wproj_ref, wup_ref, wdown_ref)
    wpool_ref[...] = turned(wpool_t[...])
    width, length = x.shape
    head = width // WORD_HEADS
    scale = head ** (-0.5)
    halves = [pl.ds(n * SPAN, SPAN) for n in range(length // SPAN)]
    pooled[...] = (pool_sum_ref[...] / cnt_ref[...]).astype(bf16)
    row = lax.broadcasted_iota(jnp.int32, (length, length), 0)
    col = lax.broadcasted_iota(jnp.int32, (length, length), 1)
    tri = jnp.where(row <= col, 1.0, 0.0).astype(bf16)
    sep = jnp.broadcast_to(sep_ref[...].astype(f32).astype(bf16), (16, length))
    doc_q = dot(sep, tri)[:1]
    doc_k = lax.dot_general(tri, sep, (((0,), (1,)), ((), ())), preferred_element_type=f32)[:, :1]
    bias[...] = jnp.where((row <= col) & (doc_k == doc_q), 0.0, NEGATIVE)
    cot[...] = cot_ref[...].astype(f32).T.astype(bf16)
    for at in halves:
        x[:, at] = dot(wpool_t[...], pooled[:, at])
        z, rs = normed(x[:, at])
        z3[:, at] = z.astype(bf16)
        rs3[:, at] = rs
        a3[:, at] = (z * wide(ga_ref[...], SPAN)).astype(bf16)
        for n in range(3):
            rows = pl.ds(n * width, width)
            t[rows, at] = dot(wqkv_t[rows, :], a3[:, at]).astype(bf16)
    for h in range(WORD_HEADS):
        k = t[pl.ds(width + h * head, head), :].T
        for n, at in enumerate(halves):
            seen = (n + 1) * SPAN
            keys = pl.ds(0, seen)
            q = t[pl.ds(h * head, head), at]
            s = dot(k[:seen], q) * scale + bias[keys, at]
            e = jnp.exp(s - jnp.max(s, 0, keepdims=True))
            w = e / jnp.sum(e, 0, keepdims=True)
            p[h, keys, at] = w
            o[pl.ds(h * head, head), at] = dot(t[pl.ds(2 * width + h * head, head), keys], w.astype(bf16)).astype(bf16)
    for at in halves:
        h3[:, at] = x[:, at] + dot(wproj_t[...], o[:, at])
        z, rs = normed(h3[:, at])
        z4[:, at] = z.astype(bf16)
        rs4[:, at] = rs
        a4[:, at] = (z * wide(gb_ref[...], SPAN)).astype(bf16)
        for n in range(wup_ref.shape[1] // 256):
            rows = pl.ds(n * 256, 256)
            mm, gg = gelu_both(dot(wup_t[rows, :], a4[:, at]))
            m[rows, at] = mm.astype(bf16)
            gp[rows, at] = gg.astype(bf16)
        out = h3[:, at] + dot(wdown_t[...], m[:, at])
        out_ref[at, :] = out.T.astype(bf16)
        for n in range(wdown_ref.shape[0] // 256):
            rows = pl.ds(n * 256, 256)
            du[rows, at] = (dot(wdown_ref[rows, :], cot[:, at]) * gp[rows, at].astype(f32)).astype(bf16)
        dy = dot(wup_ref[...], du[:, at])
        z = z4[:, at].astype(f32)
        part = fold_lanes(dy * z)
        ggb_ref[...] = part if at is halves[0] else ggb_ref[...] + part
        dh3[:, at] = cot[:, at].astype(f32) + norm_back(dy, z, rs4[:, at], wide(gb_ref[...], SPAN))
        dh3b[:, at] = dh3[:, at].astype(bf16)
        do[:, at] = dot(wproj_ref[...], dh3b[:, at]).astype(bf16)
    nd, nz, r, lanes = send0.shape
    n = cot.shape[0] // nd
    deep = m.shape[0] // nz
    for z in range(nz):
        for i in range(deep // lanes):
            g = dot_nt(cot[...], m[pl.ds(z * deep + i * lanes, lanes), :]).astype(bf16)
            for d in range(nd):
                send2[d, z, pl.ds(i * n, n), :] = g[d * n : (d + 1) * n]
    for d in range(nd):
        g = dot_nt(a4[...], du[pl.ds(d * lanes, lanes), :]).astype(bf16)
        send1[d] = g.reshape(nz, r, lanes)
    gproj_t[...] = dot_nt(dh3b[...], o[...]).astype(bf16)
    for h in range(WORD_HEADS):
        q_rows = pl.ds(h * head, head)
        k_rows = pl.ds(width + h * head, head)
        v_rows = pl.ds(2 * width + h * head, head)
        v = t[v_rows, :].T
        for n in reversed(range(len(halves))):
            at = halves[n]
            seen = (n + 1) * SPAN
            keys = pl.ds(0, seen)
            w = p[h, keys, at]
            g = do[q_rows, at]
            dp = dot(v[:seen], g)
            ds = (w * (dp - jnp.sum(w * dp, 0, keepdims=True))).astype(bf16)
            dt[q_rows, at] = (dot(t[k_rows, keys], ds) * scale).astype(bf16)
            dk = dot_nt(t[q_rows, at], ds) * scale
            dv = dot_nt(g, w.astype(bf16))
            if n == len(halves) - 1:
                dtk[0] = dk
                dtk[1] = dv
            else:
                dtk[0, :, keys] += dk
                dtk[1, :, keys] += dv
        dt[k_rows, :] = dtk[0].astype(bf16)
        dt[v_rows, :] = dtk[1].astype(bf16)
    for n in range(3):
        part = pl.ds(n * width, width)
        gqkv_t[part, :] = dot_nt(dt[part, :], a3[...]).astype(bf16)
    a, b = gqkv_t.shape[0] // nd, gproj_t.shape[0] // nd
    for d in range(nd):
        g = turned(jnp.concatenate([gqkv_t[pl.ds(d * a, a), :], gproj_t[pl.ds(d * b, b), :]], 0))
        send0[d] = g.reshape(nz, r, lanes)
    for at in halves:
        dy = dot(wqkv_ref[...], dt[:, at])
        z = z3[:, at].astype(f32)
        part = fold_lanes(dy * z)
        gga_ref[...] = part if at is halves[0] else gga_ref[...] + part
        dx = dh3[:, at] + norm_back(dy, z, rs3[:, at], wide(ga_ref[...], SPAN))
        dh3b[:, at] = dx.astype(bf16)
        dpool_ref[:, at] = (dot(wpool_ref[...], dh3b[:, at]) / cnt_ref[:, at]).astype(bf16)
    gpool_ref[...] = dot_nt(dh3b[...], pooled[...])


def word_gathered(pool_sum, cnt, sep, cot, ga, gb, pool_t, *gathered):
    length, width = cot.shape
    inner = pool_sum.shape[0]
    nd, nz, r, lanes = gathered[0].shape
    hidden = nd * lanes
    vm = pltpu.VMEM
    return pl.pallas_call(
        word_gathered_kernel,
        out_shape=[
            jax.ShapeDtypeStruct((length, width), bf16),
            jax.ShapeDtypeStruct((inner, length), bf16),
            jax.ShapeDtypeStruct((width, inner), f32),
            *(jax.ShapeDtypeStruct(g.shape, bf16) for g in gathered),
            jax.ShapeDtypeStruct((width, LANES), f32),
            jax.ShapeDtypeStruct((width, LANES), f32),
        ],
        scratch_shapes=[
            vm((inner, length), bf16), vm((width, length), f32), vm((width, length), bf16), vm((1, length), f32),
            vm((width, length), bf16), vm((3 * width, length), bf16), vm((WORD_HEADS, length, length), f32),
            vm((width, length), bf16), vm((width, length), f32), vm((width, length), bf16), vm((1, length), f32),
            vm((width, length), bf16), vm((hidden, length), bf16), vm((hidden, length), bf16),
            vm((length, length), f32), vm((width, length), bf16), vm((hidden, length), bf16),
            vm((width, length), f32), vm((width, length), bf16), vm((width, length), bf16),
            vm((3 * width, length), bf16), vm((2, width // WORD_HEADS, length), f32),
            vm((3 * width, width), bf16), vm((width, width), bf16), vm((hidden, width), bf16), vm((width, hidden), bf16),
            vm((width, 3 * width), bf16), vm((width, width), bf16), vm((width, hidden), bf16), vm((hidden, width), bf16),
            vm((inner, width), bf16), vm((3 * width, width), bf16), vm((width, width), bf16),
        ],
        compiler_params=pltpu.CompilerParams(vmem_limit_bytes=58 * 2**20),
        name="word_gathered",
    )(pool_sum, cnt, sep, cot, ga, gb, pool_t, *gathered)


def gelu_gate(u, s):
    t = jnp.tanh(u * (GELU_A + (GELU_A * GELU_B) * s))
    return 0.5 + 0.5 * t


def gelu(u):
    return u * gelu_gate(u, u * u)


def gelu_pair(u):
    s = u * u
    r = gelu_gate(u, s)
    m = u * r
    return m, r + (m - m * r) * (2.0 * GELU_A + (6.0 * GELU_A * GELU_B) * s)


def shift_of(letters):
    return letters.bit_length() - 1


def twin_owner(letters):
    lane = lax.broadcasted_iota(jnp.int32, (letters, 2 * LANES), 1)
    return lax.shift_right_logical(lane & (LANES - 1), shift_of(letters))


def twin_mask(letters):
    bits = shift_of(letters)
    a = lax.shift_right_logical(lax.broadcasted_iota(jnp.int32, (LANES, 2 * LANES), 0), bits)
    b = lax.shift_right_logical(lax.broadcasted_iota(jnp.int32, (LANES, 2 * LANES), 1) & (LANES - 1), bits)
    return jnp.where(a == b, 1.0, 0.0).astype(bf16)


def twin_blocks(v):
    half = v.shape[0] // 2
    none = jnp.zeros((half, v.shape[1]), v.dtype)
    return jnp.concatenate([jnp.concatenate([v[:half], none], 1), jnp.concatenate([none, v[half:]], 1)], 0)


def stacked(v):
    return jnp.concatenate([v[:, :LANES], v[:, LANES:]], 0)


def char_units():
    for g in range(BATCH // LANES):
        for h in range(CHAR_HEADS // 2):
            yield h, pl.ds(g * LANES, LANES), pl.ds(2 * g * LANES, 2 * LANES)


def word_of(step, letters, per, shape, axis):
    token = lax.broadcasted_iota(jnp.int32, shape, axis)
    word = lax.broadcasted_iota(jnp.int32, shape, 1 - axis)
    first = (step % per) * (BATCH // letters)
    return lax.shift_right_logical(token, shift_of(letters)) + first == word, token & (letters - 1)


def forward_first(s, x_ref, rs1_ref, x_all, z1_all):
    x = x_ref[...].astype(f32).T
    x_all[s] = x.astype(bf16)
    z1, rs1 = normed(x)
    z1_all[s] = z1.astype(bf16)
    rs1_ref[s] = rs1


def forward_attention(s, letters, tok_ref, ga_ref, wqkv_t, wproj_t, t_ref, o_ref, p_ref, z1_ref, x_all, z1_all, h1_all):
    width = o_ref.shape[1]
    pair = 2 * (width // CHAR_HEADS)
    scale = (width // CHAR_HEADS) ** (-0.5)
    owner, blocks = twin_owner(letters), twin_mask(letters)
    key_slot = lax.broadcasted_iota(jnp.int32, (letters, 2 * LANES), 0)
    z1 = z1_all[s]
    z1_ref[0] = z1
    a1 = (z1.astype(f32) * wide(ga_ref[...], BATCH)).astype(bf16)
    t_ref[0] = dot(wqkv_t[...], a1).astype(bf16)
    units = list(char_units())
    scores = []
    for h, lanes, lanes2 in units:
        q = twin_blocks(t_ref[0, pl.ds(h * pair, pair), lanes])
        k = t_ref[0, pl.ds(width + h * pair, pair), lanes].T
        scores.append(pick_own(dot(k, q), owner, letters))
    probs = []
    for (h, lanes, lanes2), score in zip(units, scores):
        counts = tok_ref[0, :, lanes]
        allowed = key_slot < jnp.concatenate([counts, counts], 1)
        score = jnp.where(allowed, score * scale, NEGATIVE)
        e = jnp.exp(score - jnp.max(score, 0, keepdims=True))
        p = e / jnp.sum(e, 0, keepdims=True)
        p_ref[0, pl.ds(h * letters, letters), lanes2] = p
        probs.append(p)
    for (h, lanes, lanes2), p in zip(units, probs):
        v = twin_blocks(t_ref[0, pl.ds(2 * width + h * pair, pair), lanes])
        o = dot(v, stacked(spread_own(p.astype(bf16), blocks, letters)))
        o_ref[0, pl.ds(h * pair, pair), lanes] = o.astype(bf16)
    h1_all[s] = x_all[s].astype(f32) + dot(wproj_t[...], o_ref[0])


def forward_feed(s, letters, per, cnt_ref, gb_ref, wup_t, wdown_t, z2_ref, rs2_ref, u_ref, pool_ref, h1_all, m_ref):
    h1 = h1_all[s]
    z2, rs2 = normed(h1)
    z2_ref[0] = z2.astype(bf16)
    rs2_ref[0] = rs2
    a2 = (z2 * wide(gb_ref[...], BATCH)).astype(bf16)
    for n in range(wup_t.shape[0] // 256):
        rows = pl.ds(n * 256, 256)
        u = dot(wup_t[rows, :], a2)
        u_ref[0, rows, :] = u.astype(bf16)
        m_ref[rows, :] = gelu(u).astype(bf16)
    h2 = h1 + dot(wdown_t[...], m_ref[...])
    high = h2.astype(bf16)
    low = (h2 - high.astype(f32)).astype(bf16)
    mine, slot = word_of(s, letters, per, (BATCH, LANES), 0)
    gather = jnp.where(mine & (slot < cnt_ref[...]), 1.0, 0.0).astype(bf16)
    part = dot(high, gather) + dot(low, gather)

    @pl.when(s % per == 0)
    def _():
        pool_ref[...] = part

    @pl.when(s % per != 0)
    def _():
        pool_ref[...] += part


def backward_feed(
    s, letters, per, dp_ref, tok_ref, gb_ref, wup, wdown, z2_ref, rs2_ref, u_ref, gup, gdown_t, dh1_all, m_ref, du_ref
):
    mine, slot = word_of(s, letters, per, (LANES, BATCH), 1)
    scatter = jnp.where(mine & (slot < tok_ref[0]), 1.0, 0.0).astype(bf16)
    dh2 = dot(dp_ref[...], scatter)
    dh2b = dh2.astype(bf16)
    for n in range(wdown.shape[0] // 256):
        rows = pl.ds(n * 256, 256)
        m, slope = gelu_pair(u_ref[0, rows, :].astype(f32))
        m_ref[rows, :] = m.astype(bf16)
        du_ref[rows, :] = (dot(wdown[rows, :], dh2b) * slope).astype(bf16)
    dy = dot(wup[...], du_ref[...])
    z = z2_ref[0].astype(f32)
    dh1 = dh2 + norm_back(dy, z, rs2_ref[0], wide(gb_ref[...], BATCH))
    dh1_all[s] = dh1.astype(bf16)
    down = dot_nt(dh2b, m_ref[...])
    up = dot_nt(z2_ref[0], du_ref[...])

    @pl.when(s == 0)
    def _():
        gdown_t[...] = down
        gup[...] = up

    @pl.when(s != 0)
    def _():
        gdown_t[...] += down
        gup[...] += up


def backward_attention(s, letters, wproj, t_ref, o_ref, p_ref, z1_ref, gqkv_t, gproj_t, dh1_all, dt_all, do_ref):
    width = wproj.shape[0]
    pair = 2 * (width // CHAR_HEADS)
    scale = (width // CHAR_HEADS) ** (-0.5)
    owner, blocks = twin_owner(letters), twin_mask(letters)
    dh1b = dh1_all[s]
    do_ref[...] = dot(wproj[...], dh1b).astype(bf16)
    units = list(char_units())
    grads = []
    for h, lanes, lanes2 in units:
        v = t_ref[0, pl.ds(2 * width + h * pair, pair), lanes].T
        grads.append(pick_own(dot(v, twin_blocks(do_ref[pl.ds(h * pair, pair), lanes])), owner, letters))
    spread = []
    for (h, lanes, lanes2), dp in zip(units, grads):
        p = p_ref[0, pl.ds(h * letters, letters), lanes2]
        ds = p * (dp - jnp.sum(p * dp, 0, keepdims=True))
        spread.append((spread_own(p.astype(bf16), blocks, letters), spread_own(ds.astype(bf16), blocks, letters)))
    for (h, lanes, lanes2), (pb, dsb) in zip(units, spread):
        q_rows = pl.ds(h * pair, pair)
        k_rows = pl.ds(width + h * pair, pair)
        v_rows = pl.ds(2 * width + h * pair, pair)
        q = twin_blocks(t_ref[0, q_rows, lanes])
        k = twin_blocks(t_ref[0, k_rows, lanes])
        do = twin_blocks(do_ref[q_rows, lanes])
        dt_all[s, q_rows, lanes] = (dot(k, stacked(dsb)) * scale).astype(bf16)
        dt_all[s, k_rows, lanes] = (dot_nt(q, dsb) * scale).astype(bf16)
        dt_all[s, v_rows, lanes] = dot_nt(do, pb).astype(bf16)
    proj = dot_nt(dh1b, o_ref[0])
    qkv = dot_nt(dt_all[s], z1_ref[0])

    @pl.when(s == 0)
    def _():
        gproj_t[...] = proj
        gqkv_t[...] = qkv

    @pl.when(s != 0)
    def _():
        gproj_t[...] += proj
        gqkv_t[...] += qkv


def backward_last(s, ga_ref, wqkv, z1_ref, rs1_ref, cg_ref, dh1_all, dt_all):
    dy = dot(wqkv[...], dt_all[s])
    z = z1_ref[0].astype(f32)
    dx = dh1_all[s].astype(f32) + norm_back(dy, z, rs1_ref[0], wide(ga_ref[...], BATCH))
    cg_ref[...] = dx.T.astype(bf16)


def pack_first(slot, qkv, proj_t, gains):
    r = qkv.shape[0]
    slot[pl.ds(0, r), :] = jnp.concatenate([qkv[...], turned(lanes_to(proj_t[...], LANES))[:r]], 1)
    none = jnp.zeros((slot.shape[0] - r - gains.shape[0], LANES), f32)
    slot[pl.ds(r, slot.shape[0] - r), :] = jnp.concatenate([gains[...], none], 0).astype(bf16)


def pack_second(slot, up, down_t, pool):
    r, n = up.shape[0], down_t.shape[0]
    slot[pl.ds(0, r), :] = up[...]
    for i in range(down_t.shape[1] // LANES):
        slot[pl.ds(r + i * n, n), :] = down_t[:, pl.ds(i * LANES, LANES)]
    slot[pl.ds(2 * r, r), :] = lanes_to(pool[...], LANES)


def pack_words(slots, qkv_t, proj_t, up, down_t):
    slots[0] = turned(jnp.concatenate([qkv_t[...], proj_t[...]], 0))
    slots[1] = up[...]
    n, lanes = down_t.shape[0], up.shape[1]
    for i in range(down_t.shape[1] // lanes):
        slots[2, pl.ds(i * n, n), :] = down_t[:, pl.ds(i * lanes, lanes)]


def seats():
    ny, nx, nz = sides()
    for d in range(2 * ny * nx):
        yield d, (d // (2 * nx), (d // 2) % nx, d % 2)


def unpack_first(ref, wqkv_t, wproj_t, wqkv, wproj, cga, cgb, wga, wgb):
    ny, nx, nz = sides()
    nd = 2 * ny * nx
    r = wqkv.shape[0] // nz
    a, b, gc, gw = wqkv_t.shape[0] // nd, wproj_t.shape[0] // nd, cga.shape[0] // nd, wga.shape[0] // nd
    for d, at in seats():
        t = turned(ref[at + (slice(None), pl.ds(0, r))].reshape(nz * r, LANES))
        wqkv_t[pl.ds(d * a, a), :] = t[:a]
        wproj_t[pl.ds(d * b, b), :] = t[a:]
        g = ref[at + (0, pl.ds(r, 16))].astype(f32).T
        one, two = (jnp.broadcast_to(g[:, i : i + 1], (LANES, LANES)) for i in range(2))
        cga[pl.ds(d * gc, gc), :] = one[:gc]
        cgb[pl.ds(d * gc, gc), :] = one[gc : 2 * gc]
        wga[pl.ds(d * gw, gw), :] = one[2 * gc : 2 * gc + gw]
        wgb[pl.ds(d * gw, gw), :] = two[:gw]
    wqkv[...] = turned(wqkv_t[...])
    wproj[...] = turned(wproj_t[...])


def unpack_second(ref, wup_t, wdown_t, wup, wdown, pool_t):
    ny, nx, nz = sides()
    nd = 2 * ny * nx
    r, n, p = wup.shape[0] // nz, wdown_t.shape[0] // nd, pool_t.shape[0] // nd
    deep = wdown_t.shape[1] // nz
    for d, at in seats():
        up = ref[at + (slice(None), pl.ds(0, r))].reshape(nz * r, LANES)
        wup[:, pl.ds(d * LANES, LANES)] = up
        wup_t[pl.ds(d * LANES, LANES), :] = turned(up)
        for z in range(nz):
            for i in range(deep // LANES):
                wdown_t[pl.ds(d * n, n), pl.ds(z * deep + i * LANES, LANES)] = ref[at + (z, pl.ds(r + i * n, n))]
        t = turned(ref[at + (slice(None), pl.ds(2 * r, r))].reshape(nz * r, LANES))
        pool_t[pl.ds(d * p, p), :] = t[:p]
    wdown[...] = turned(wdown_t[...])


def unpack_words(first, second, third, wqkv_t, wproj_t, wup_t, wdown_t, wqkv, wproj, wup, wdown):
    nd, nz, r, lanes = first.shape
    a, b, n = wqkv_t.shape[0] // nd, wproj_t.shape[0] // nd, wdown_t.shape[0] // nd
    deep = wdown_t.shape[1] // nz
    for d in range(nd):
        t = turned(first[d].reshape(nz * r, lanes))
        wqkv_t[pl.ds(d * a, a), :] = t[:a]
        wproj_t[pl.ds(d * b, b), :] = t[a:]
        up = second[d].reshape(nz * r, lanes)
        wup[:, pl.ds(d * lanes, lanes)] = up
        wup_t[pl.ds(d * lanes, lanes), :] = turned(up)
        for z in range(nz):
            for i in range(deep // lanes):
                wdown_t[pl.ds(d * n, n), pl.ds(z * deep + i * lanes, lanes)] = third[d, z, pl.ds(i * n, n), :]
    wqkv[...] = turned(wqkv_t[...])
    wproj[...] = turned(wproj_t[...])
    wdown[...] = turned(wdown_t[...])


def pack_first_grads(slots, gqkv_t, gproj_t, ga, wqkv_t, gup, wup, gwga, gwgb):
    ny, nx, nz = sides()
    nd = 2 * ny * nx
    width = gqkv_t.shape[1]
    r = width // nz
    tail = slots.shape[4] - r
    a, b, gc, gw = gqkv_t.shape[0] // nd, gproj_t.shape[0] // nd, width // nd, gwga.shape[0] // nd
    char_a = jnp.sum(gqkv_t[...] * wqkv_t[...].astype(f32), 0, keepdims=True)
    char_a = jnp.broadcast_to(char_a, (8, width)).T[:, :1]
    char_b = jnp.sum(gup[...] * wup[...].astype(f32), 1, keepdims=True)
    word_a, word_b = (jnp.sum(g[...], 1, keepdims=True) for g in (gwga, gwgb))
    gain = ga[...].T[:1]
    spot = lax.broadcasted_iota(jnp.int32, (LANES, nz * tail), 1) % tail
    none = jnp.zeros((LANES - gw, 1), f32)
    for d, at in seats():
        t = jnp.concatenate([gqkv_t[pl.ds(d * a, a), :] * gain, gproj_t[pl.ds(d * b, b), :]], 0)
        slots[at + (slice(None), pl.ds(0, r))] = t.T.astype(bf16).reshape(nz, r, LANES)
        char, word = slice(d * gc, (d + 1) * gc), slice(d * gw, (d + 1) * gw)
        one = jnp.concatenate([char_a[char], char_b[char], word_a[word]], 0)
        two = jnp.concatenate([word_b[word], none], 0)
        side = jnp.where(spot == 0, one, jnp.where(spot == 1, two, 0.0))
        slots[at + (slice(None), pl.ds(r, tail))] = side.T.astype(bf16).reshape(nz, tail, LANES)


def pack_second_grads(slots, gup, gdown_t, gb, gpool_t):
    ny, nx, nz = sides()
    nd = 2 * ny * nx
    width = gup.shape[0]
    r, n, p = width // nz, gdown_t.shape[0] // nd, gpool_t.shape[0] // nd
    deep = gdown_t.shape[1] // nz
    none = jnp.zeros((LANES - p, width), f32)
    for d, at in seats():
        up = gup[:, pl.ds(d * LANES, LANES)] * gb[...]
        slots[at + (slice(None), pl.ds(0, r))] = up.astype(bf16).reshape(nz, r, LANES)
        for z in range(nz):
            for i in range(deep // LANES):
                slots[at + (z, pl.ds(r + i * n, n))] = gdown_t[
                    pl.ds(d * n, n), pl.ds(z * deep + i * LANES, LANES)
                ].astype(bf16)
        t = jnp.concatenate([gpool_t[pl.ds(d * p, p), :], none], 0)
        slots[at + (slice(None), pl.ds(2 * r, r))] = t.T.astype(bf16).reshape(nz, r, LANES)


GATHER_PLAN = {
    "first": (0, 3, 5, 7, 8),
    "second": (2, 6, 8, 10, 14),
    0: (5, 9, 11, 13, 16),
    1: (8, 13, 14, 17, 19),
    2: (10, 17, 18, 20, 22),
}
SCATTER_PLAN = {
    0: (0, 1, 3, 4, 6),
    1: (1, 3, 5, 6, 8),
    2: (2, 5, 7, 8, 10),
    "second": (8, 10, 12, 13, 15),
    "first": (16, 18, 20, 22, 23),
}


def planned(plan, event, steps):
    when = plan[event]
    return [(at // 8) * steps + (at % 8) * steps // 8 for at in when]


def forward_gather_kernel(
    letters, steps, x_ref, tok_ref, cnt_ref, s_qkv, s_proj, s_gains, s_up, s_down, s_pool, w_qkv, w_proj, w_up, w_down,
    t_ref, o_ref, p_ref, z1_ref, rs1_ref, z2_ref, rs2_ref, u_ref, pool_ref, word0, word1, word2,
    wqkv_t, wqkv, wproj, wup, wdown, pool_t, cga, cgb, wga, wgb,
    first_all, second_all, word_own, wproj_t, wup_t, wdown_t, x_all, z1_all, h1_all, m_ref,
    first_sems, second_sems, word_sems0, word_sems1, word_sems2, own_sems,
):
    step = pl.program_id(0)
    here = place()
    words = (word0, word1, word2)
    per = LANES * letters // BATCH
    streams = {
        "first": (first_all, first_sems), "second": (second_all, second_sems),
        0: (word0, word_sems0), 1: (word1, word_sems1), 2: (word2, word_sems2),
    }
    own = [pltpu.make_async_copy(word_own.at[n], words[n].at[here], own_sems.at[n]) for n in range(3)]

    for name, (ref, sems) in streams.items():
        for n, when in enumerate(planned(GATHER_PLAN, name, steps)):
            @pl.when(step == when)
            def _():
                if n == 0:
                    if name == "first":
                        greet()
                        pack_first(first_all.at[here], s_qkv, s_proj, s_gains)
                        start_all(gather_stages(ref, sems, (0,))[0])
                        pack_second(second_all.at[here], s_up, s_down, s_pool)
                        pack_words(word_own, w_qkv, w_proj, w_up, w_down)
                        start_all(own)
                    else:
                        if name != "second":
                            own[name].wait()
                        start_all(gather_stages(ref, sems, (0,))[0])
                else:
                    stages = gather_stages(ref, sems, (n - 1, n))
                    arrive_all(stages[n - 1])
                    if n < 4:
                        start_all(stages[n])
                    elif name == "first":
                        unpack_first(first_all, wqkv_t, wproj_t, wqkv, wproj, cga, cgb, wga, wgb)
                    elif name == "second":
                        unpack_second(second_all, wup_t, wdown_t, wup, wdown, pool_t)

    @pl.when(step < steps)
    def _():
        forward_first(step, x_ref, rs1_ref, x_all, z1_all)

    @pl.when((step >= steps) & (step < 2 * steps))
    def _():
        forward_attention(
            step - steps, letters, tok_ref, cga, wqkv_t, wproj_t, t_ref, o_ref, p_ref, z1_ref, x_all, z1_all, h1_all
        )

    @pl.when(step >= 2 * steps)
    def _():
        forward_feed(
            step - 2 * steps, letters, per, cnt_ref, cgb, wup_t, wdown_t, z2_ref, rs2_ref, u_ref, pool_ref, h1_all, m_ref
        )

    @pl.when(step == 3 * steps - 1)
    def _():
        for ref, sems in streams.values():
            sent_all(gather_stages(ref, sems))


def phase_map(phase, steps, per=1):
    return lambda i: jnp.clip(i - phase * steps, 0, steps - 1) // per


def forward_gather(x, tok, cnt, first_shards, second_shards, word_shards, letters):
    tokens, width = x.shape
    steps = tokens // BATCH
    ny, nx, nz = sides()
    nd = 2 * ny * nx
    hidden, outer = second_shards[0].shape[1] * nd, second_shards[2].shape[1] * nd
    r = width // nz
    per = LANES * letters // BATCH
    word_rows, word_lanes = word_shards[2].shape

    def strip(phase, rows, lanes=BATCH, dtype=bf16):
        where = phase_map(phase, steps)
        return (
            jax.ShapeDtypeStruct((steps, rows, lanes), dtype),
            pl.BlockSpec((1, rows, lanes), lambda i: (where(i), 0, 0)),
        )

    def whole(shape, dtype=bf16):
        return (jax.ShapeDtypeStruct(shape, dtype), pl.BlockSpec(shape, lambda i: (0,) * len(shape)))

    pooled = phase_map(2, steps, per)
    gathered = (
        jax.ShapeDtypeStruct((ny, nx, 2, nz, word_rows, word_lanes), bf16), pl.BlockSpec(memory_space=pl.ANY)
    )
    outs = [
        strip(1, 3 * width), strip(1, width), strip(1, CHAR_HEADS // 2 * letters, 2 * BATCH, f32), strip(1, width),
        whole((steps, 1, BATCH), f32), strip(2, width), strip(2, 1, BATCH, f32), strip(2, hidden),
        (
            jax.ShapeDtypeStruct((width, tokens // letters), f32),
            pl.BlockSpec((width, LANES), lambda i: (0, pooled(i))),
        ),
        gathered, gathered, gathered,
        whole((3 * width, width)), whole((width, 3 * width)), whole((width, width)), whole((width, hidden)),
        whole((hidden, width)), whole((outer, width)), whole((width, LANES), f32), whole((width, LANES), f32),
        whole((outer, LANES), f32), whole((outer, LANES), f32),
    ]
    shards = (*first_shards, *second_shards, *word_shards)
    at0, at1 = phase_map(0, steps), phase_map(1, steps)
    sems = pltpu.SemaphoreType.DMA((2, gather_copies()))
    return pl.pallas_call(
        functools.partial(forward_gather_kernel, letters, steps),
        grid=(3 * steps,),
        in_specs=[
            pl.BlockSpec((BATCH, width), lambda i: (at0(i), 0)),
            pl.BlockSpec((1, 1, BATCH), lambda i: (at1(i), 0, 0)),
            pl.BlockSpec((1, LANES), lambda i: (0, pooled(i))),
        ] + [full_spec(a) for a in shards],
        out_specs=[o[1] for o in outs],
        out_shape=[o[0] for o in outs],
        scratch_shapes=[
            pltpu.VMEM((ny, nx, 2, nz, r + 32, LANES), bf16),
            pltpu.VMEM((ny, nx, 2, nz, 3 * r, LANES), bf16),
            pltpu.VMEM((3, word_rows, word_lanes), bf16),
            pltpu.VMEM((width, width), bf16),
            pltpu.VMEM((hidden, width), bf16),
            pltpu.VMEM((width, hidden), bf16),
            pltpu.VMEM((steps, width, BATCH), bf16),
            pltpu.VMEM((steps, width, BATCH), bf16),
            pltpu.VMEM((steps, width, BATCH), f32),
            pltpu.VMEM((hidden, BATCH), bf16),
            sems, sems, sems, sems, sems,
            pltpu.SemaphoreType.DMA((3,)),
        ],
        compiler_params=pltpu.CompilerParams(
            dimension_semantics=("arbitrary",), vmem_limit_bytes=VMEM_BYTES, collective_id=0, has_side_effects=True
        ),
        name="forward_gather",
    )(x, tok, cnt, *shards)


def backward_scatter_kernel(
    letters, steps, dp_ref, tok_ref, ga_ref, gb_ref, wqkv_t, wqkv, wproj, wup, wdown, send0, send1, send2,
    gpool_t, gwga, gwgb, t_ref, o_ref, p_ref, z1_ref, rs1_ref, z2_ref, rs2_ref, u_ref,
    cg_ref, first_sum, second_sum, word_sum,
    gqkv_t, gproj_t, gup, gdown_t, dh1_all, dt_all, do_ref, m_ref, du_ref, first_send, second_send, own_sems, *work,
):
    step = pl.program_id(0)
    y, x, c, z = place()
    per = LANES * letters // BATCH
    size = len(work) // 5
    work = [work[n * size : (n + 1) * size] for n in range(5)]
    sends = (send0, send1, send2)
    streams = {n: (sends[n], work[n], word_sum.at[n]) for n in range(3)}
    streams["second"] = (second_send, work[3], second_sum)
    streams["first"] = (first_send, work[4], first_sum)
    own = [pltpu.make_async_copy(sends[n].at[:, :, c], work[n][0], own_sems.at[n]) for n in range(3)]

    @pl.when(step == 0)
    def _():
        greet()
        start_all(own)

    for name, (send, scratch, total) in streams.items():
        acc = scratch[0]
        for n, when in enumerate(planned(SCATTER_PLAN, name, steps)):
            @pl.when(step == when)
            def _():
                if n == 0:
                    if name == "second":
                        pack_second_grads(second_send, gup, gdown_t, gb_ref, gpool_t)
                    elif name == "first":
                        pack_first_grads(first_send, gqkv_t, gproj_t, ga_ref, wqkv_t, gup, wup, gwga, gwgb)
                else:
                    arrive_all(scatter_stage(n - 1, send, scratch))
                    if n == 1 and name in (0, 1, 2):
                        own[name].wait()
                        mine = lambda b, a, k: acc[b, a, k]
                    else:
                        mine = lambda b, a, k: send[b, a, c, k]
                    scatter_sum(n - 1, mine, scratch, total)
                if n < 4:
                    start_all(scatter_stage(n, send, scratch))

    @pl.when(step < steps)
    def _():
        backward_feed(
            step, letters, per, dp_ref, tok_ref, gb_ref, wup, wdown, z2_ref, rs2_ref, u_ref,
            gup, gdown_t, dh1_all, m_ref, du_ref,
        )

    @pl.when((step >= steps) & (step < 2 * steps))
    def _():
        backward_attention(
            step - steps, letters, wproj, t_ref, o_ref, p_ref, z1_ref, gqkv_t, gproj_t, dh1_all, dt_all, do_ref
        )

    @pl.when(step >= 2 * steps)
    def _():
        backward_last(step - 2 * steps, ga_ref, wqkv, z1_ref, rs1_ref, cg_ref, dh1_all, dt_all)

    @pl.when(step == 3 * steps - 1)
    def _():
        for send, scratch, total in streams.values():
            sent_all([scatter_stage(n, send, scratch) for n in range(4)])


def backward_scatter(dp, tok, ga, gb, weights, sends, gpool_t, gwga, gwgb, saved, letters):
    wqkv_t, wqkv, wproj, wup, wdown = weights
    t, o, p, z1, rs1, z2, rs2, u = saved
    steps = t.shape[0]
    width, hidden = wup.shape
    per = LANES * letters // BATCH
    ny, nx, nz = sides()
    r = width // nz
    word_rows, word_lanes = sends[0].shape[4:]
    at = [phase_map(n, steps) for n in range(3)]
    words = phase_map(0, steps, per)

    def strip(a, where):
        return pl.BlockSpec((1,) + a.shape[1:], lambda i: (where(i), 0, 0))

    def whole(shape):
        return (jax.ShapeDtypeStruct(shape, f32), pl.BlockSpec(shape, lambda i: (0,) * len(shape)))

    def once(a):
        return pl.BlockSpec(a.shape, lambda i: (0,) * a.ndim, pipeline_mode=pl.Buffered(1))

    outs = [
        (jax.ShapeDtypeStruct((steps * BATCH, width), bf16), pl.BlockSpec((BATCH, width), lambda i: (at[2](i), 0))),
        whole((r + 32, LANES)), whole((3 * r, LANES)), whole((3, word_rows, word_lanes)),
    ]
    either = lambda i: jnp.where(i < 2 * steps, at[1](i), at[2](i))
    saved_specs = [
        strip(t, at[1]), strip(o, at[1]), strip(p, at[1]), strip(z1, either), strip(rs1, at[2]),
        strip(z2, at[0]), strip(rs2, at[0]), strip(u, at[0]),
    ]
    return pl.pallas_call(
        functools.partial(backward_scatter_kernel, letters, steps),
        grid=(3 * steps,),
        in_specs=[
            pl.BlockSpec((width, LANES), lambda i: (0, words(i))),
            pl.BlockSpec((1, 1, BATCH), lambda i: (at[0](i), 0, 0)),
        ] + [once(a) for a in (ga, gb, *weights)] + [pl.BlockSpec(memory_space=pl.ANY)] * 3
        + [once(a) for a in (gpool_t, gwga, gwgb)] + saved_specs,
        out_specs=[o[1] for o in outs],
        out_shape=[o[0] for o in outs],
        scratch_shapes=[
            pltpu.VMEM((3 * width, width), f32),
            pltpu.VMEM((width, width), f32),
            pltpu.VMEM((width, hidden), f32),
            pltpu.VMEM((width, hidden), f32),
            pltpu.VMEM((steps, width, BATCH), bf16),
            pltpu.VMEM((steps, 3 * width, BATCH), bf16),
            pltpu.VMEM((width, BATCH), bf16),
            pltpu.VMEM((hidden, BATCH), bf16),
            pltpu.VMEM((hidden, BATCH), bf16),
            pltpu.VMEM((ny, nx, 2, nz, r + 32, LANES), bf16),
            pltpu.VMEM((ny, nx, 2, nz, 3 * r, LANES), bf16),
            pltpu.SemaphoreType.DMA((3,)),
        ] + 3 * scatter_scratch(word_rows, word_lanes) + scatter_scratch(3 * r, LANES) + scatter_scratch(r + 32, LANES),
        compiler_params=pltpu.CompilerParams(
            dimension_semantics=("arbitrary",), vmem_limit_bytes=VMEM_BYTES, collective_id=1, has_side_effects=True
        ),
        name="backward_scatter",
    )(dp, tok, ga, gb, *weights, *sends, gpool_t, gwga, gwgb, *saved)


def finish_kernel(
    first, second, words, grad_in, cqkv, cproj_t, cup, cdown_t, cga, cgb, pool, wqkv_t, wproj_t, wup, wdown_t, wga, wgb,
    grad_out,
):
    grad_out[...] = grad_in[...]

    @pl.when(pl.program_id(0) == 0)
    def _():
        r, n, gc, gw = cup.shape[0], cqkv.shape[1], cga.shape[1], wga.shape[1]
        cqkv[...] = first[pl.ds(0, r), :n]
        cproj_t[...] = first[pl.ds(0, r), :].T[n:]
        side = first[pl.ds(r, 8), :]
        cga[...] = side[0:1, :gc]
        cgb[...] = side[0:1, gc : 2 * gc]
        wga[...] = side[0:1, 2 * gc : 2 * gc + gw]
        wgb[...] = side[1:2, :gw]
        cup[...] = second[pl.ds(0, r), :]
        n = cdown_t.shape[0]
        for i in range(cdown_t.shape[1] // LANES):
            cdown_t[:, pl.ds(i * LANES, LANES)] = second[pl.ds(r + i * n, n), :]
        pool[...] = second[pl.ds(2 * r, r), : pool.shape[1]]
        t = words[0].T
        n = wqkv_t.shape[0]
        wqkv_t[...] = t[:n]
        wproj_t[...] = t[n:]
        wup[...] = words[1]
        n, lanes = wdown_t.shape[0], wup.shape[1]
        for i in range(wdown_t.shape[1] // lanes):
            wdown_t[:, pl.ds(i * lanes, lanes)] = words[2, pl.ds(i * n, n), :]


def finish(first, second, words, grad, shapes):
    steps = 8
    moved = pl.BlockSpec((grad.shape[0] // steps, grad.shape[1]), lambda i: (i, 0))
    shapes = [jax.ShapeDtypeStruct(s, f32) for s in shapes]
    return pl.pallas_call(
        finish_kernel,
        grid=(steps,),
        in_specs=[full_spec(a) for a in (first, second, words)] + [moved],
        out_specs=[full_spec(a) for a in shapes] + [moved],
        out_shape=shapes + [jax.ShapeDtypeStruct(grad.shape, grad.dtype)],
        name="finish",
    )(first, second, words, grad)


def gather_all(shards, counts):
    flat = jnp.concatenate([s.reshape(-1) for s in shards])
    packed = lax.all_gather(lax.all_gather(flat, "fsdp", axis=0), "dp", axis=0)
    wide_count, deep_count = packed.shape[:2]
    out, start = [], 0
    for s in shards:
        piece = packed[:, :, start : start + s.size]
        start += s.size
        if s.ndim == 1:
            out.append(piece[:, 0].reshape(-1))
        else:
            r, c = s.shape
            piece = piece.reshape(wide_count, deep_count, r, c).transpose(1, 2, 0, 3)
            out.append(piece.reshape(deep_count * r, wide_count * c))
    return out


def scatter_all(grads, shards):
    wide_count, deep_count = lax.axis_size("dp"), lax.axis_size("fsdp")
    pieces = []
    for g, s in zip(grads, shards):
        g = g.astype(bf16)
        if s.ndim == 1:
            g = jnp.broadcast_to(g.reshape(wide_count, 1, s.size), (wide_count, deep_count, s.size))
        else:
            r, c = s.shape
            g = g.reshape(deep_count, r, wide_count, c).transpose(2, 0, 1, 3)
        pieces.append(g.reshape(wide_count, deep_count, s.size))
    packed = jnp.concatenate(pieces, 2)
    packed = lax.psum_scatter(packed, "dp", scatter_dimension=0, tiled=True)
    packed = lax.psum_scatter(packed, "fsdp", scatter_dimension=1, tiled=True).reshape(-1)
    out, start = [], 0
    for s in shards:
        out.append(packed[start : start + s.size].reshape(s.shape).astype(f32))
        start += s.size
    return out


def shards_plain(
    characters, counts, separators, cotangent, char_qkv, char_proj, char_up, char_down, char_gain_a, char_gain_b,
    pool_proj, word_qkv, word_proj, word_up, word_down, word_gain_a, word_gain_b,
):
    rows, length, letters, width = characters.shape
    char_shards = (char_qkv, char_proj, char_up, char_down, char_gain_a, char_gain_b)
    word_shards = (pool_proj, word_qkv, word_proj, word_up, word_down, word_gain_a, word_gain_b)
    cqkv, cproj, cup, cdown, cga, cgb = gather_all(char_shards, counts)
    wpool, wqkv, wproj, wup, wdown, wga, wgb = gather_all(word_shards, counts)
    x = characters.reshape(length * letters, width)
    tok = jnp.repeat(counts, letters, axis=1).reshape(length * letters // STEP, 1, STEP)
    cga, cgb, wga, wgb = (
        jnp.broadcast_to(g.astype(f32)[:, None], (g.shape[0], LANES)) for g in (cga, cgb, wga, wgb)
    )
    *saved, pool_sum = char_forward(x, tok, counts, cga, cgb, cqkv.T, cproj.T, cup.T, cdown.T, letters)
    word_out, dpool, gpool, gwqkv, gwproj, gwup, gwdown, gwga, gwgb = word_layer(
        pool_sum, counts.astype(f32), separators, cotangent.reshape(length, -1), wga, wgb, wpool, wqkv, wproj, wup, wdown
    )
    word_grads = scatter_all(
        (gpool, gwqkv, gwproj, gwup, gwdown, jnp.sum(gwga, 1), jnp.sum(gwgb, 1)), word_shards
    )
    char_grad, gcqkv, gcproj, gcup, gcdown, gcga, gcgb = char_backward(
        dpool, tok, cga, cgb, cqkv, cproj, cup, cdown, saved, letters
    )
    char_grads = scatter_all(
        (gcqkv, gcproj, gcup, gcdown, jnp.sum(gcga, 1), jnp.sum(gcgb, 1)), char_shards
    )
    return (word_out[None], char_grad.reshape(characters.shape), *char_grads, *word_grads)


def shards_packed(
    characters, counts, separators, cotangent, char_qkv, char_proj, char_up, char_down, char_gain_a, char_gain_b,
    pool_proj, word_qkv, word_proj, word_up, word_down, word_gain_a, word_gain_b,
):
    rows, length, letters, width = characters.shape
    x = characters.reshape(length * letters, width)
    tok = jnp.repeat(counts, letters, axis=1).reshape(length * letters // BATCH, 1, BATCH)
    gains = jnp.concatenate([char_gain_a, char_gain_b, word_gain_a, word_gain_b]).astype(f32)
    gains = jnp.pad(gains, (0, 2 * LANES - gains.shape[0])).reshape(2, LANES)
    (
        *saved, pool_sum, word0, word1, word2, wqkv_t, wqkv, wproj, wup, wdown, pool_t, cga, cgb, wga, wgb
    ) = forward_gather(
        x, tok, counts, (char_qkv, char_proj.T, gains), (char_up, char_down.T, pool_proj),
        (word_qkv.T, word_proj.T, word_up, word_down.T), letters,
    )
    shape = word0.shape
    flat = (-1,) + shape[3:]
    word_out, dpool, gpool_t, *sends, gwga, gwgb = word_gathered(
        pool_sum, counts.astype(f32), separators, cotangent.reshape(length, -1), wga, wgb, pool_t,
        *(w.reshape(flat) for w in (word0, word1, word2)),
    )
    char_grad, first, second, words = backward_scatter(
        dpool, tok, cga, cgb, (wqkv_t, wqkv, wproj, wup, wdown), [s.reshape(shape) for s in sends],
        gpool_t, gwga, gwgb, saved, letters,
    )
    shapes = [
        s.shape if s.ndim == 2 else (1, s.shape[0])
        for s in (
            char_qkv, char_proj.T, char_up, char_down.T, char_gain_a, char_gain_b,
            pool_proj, word_qkv.T, word_proj.T, word_up, word_down.T, word_gain_a, word_gain_b,
        )
    ]
    (
        cqkv, cproj_t, cup, cdown_t, cgain_a, cgain_b, pool, gqkv_t, gproj_t, gup, gdown_t, wgain_a, wgain_b, char_grad
    ) = finish(first, second, words, char_grad, shapes)
    return (
        word_out[None], char_grad.reshape(characters.shape), cqkv, cproj_t.T, cup, cdown_t.T, cgain_a[0], cgain_b[0],
        pool, gqkv_t.T, gproj_t.T, gup, gdown_t.T, wgain_a[0], wgain_b[0],
    )


def shards(*arrays):
    char_qkv, char_proj, word_qkv, word_proj = arrays[4], arrays[5], arrays[11], arrays[12]
    tiles = (char_qkv.shape[1] + char_proj.shape[1]) // LANES, (word_qkv.shape[1] + word_proj.shape[1]) // LANES
    return (shards_packed if tiles == (1, 2) else shards_plain)(*arrays)


def solution(mesh):
    rows = ("dp", "fsdp")
    matrix, vector = P("fsdp", "dp"), P("dp")
    data = (P(rows, None, None, None), P(rows, None), P(rows, None), P(rows, None, None))
    block = (matrix,) * 4 + (vector,) * 2
    word = (matrix,) * 5 + (vector,) * 2
    return jax.shard_map(
        shards,
        mesh=mesh,
        in_specs=data + block + word,
        out_specs=(data[3], data[0]) + block + word,
        check_vma=False,
    )
```

```python
import functools
import math

import jax
import jax.numpy as jnp
from jax import lax
from jax.experimental import pallas as pl
from jax.experimental.pallas import tpu as pltpu
from jax.sharding import PartitionSpec as P

CHAR_HEADS = 4
WORD_HEADS = 8
EPS = 1e-05
NEGATIVE = -1e30
LANES = 128
SPAN = 256
STEP = 512
BATCH = 1024
VMEM_BYTES = 60 * 2**20
GELU_A = 0.7978845608028654
GELU_B = 0.044715

bf16 = jnp.bfloat16
f32 = jnp.float32


def dot(a, b):
    return jnp.dot(a, b, preferred_element_type=f32)


def dot_nt(a, b):
    return lax.dot_general(a, b, (((1,), (1,)), ((), ())), preferred_element_type=f32)


def normed(v):
    c = v - jnp.mean(v, 0, keepdims=True)
    rs = lax.rsqrt(jnp.mean(c * c, 0, keepdims=True) + EPS)
    return c * rs, rs


def wide(g, n):
    return g if n == g.shape[1] else jnp.concatenate([g] * (n // g.shape[1]), 1)


def gelu_both(u):
    s = u * u
    t = jnp.tanh(u * (GELU_A + (GELU_A * GELU_B) * s))
    h = 0.5 * u
    r = 0.5 + 0.5 * t
    slope = r + h * (1.0 - t * t) * (GELU_A + (3.0 * GELU_A * GELU_B) * s)
    return u * r, slope


def lane_word(letters):
    return lax.broadcasted_iota(jnp.int32, (letters, LANES), 1) // letters


def pick_own(full, owner, letters):
    words = LANES // letters
    out = full[:letters]
    for w in range(1, words):
        out = jnp.where(owner == w, full[w * letters : (w + 1) * letters], out)
    return out


def own_blocks(letters):
    a = lax.broadcasted_iota(jnp.int32, (LANES, LANES), 0) // letters
    b = lax.broadcasted_iota(jnp.int32, (LANES, LANES), 1) // letters
    return jnp.where(a == b, 1.0, 0.0).astype(bf16)


def spread_own(compact, blocks, letters):
    return jnp.concatenate([compact] * (LANES // letters), 0) * blocks


def char_forward_kernel(
    letters, x_ref, tok_ref, cnt_ref, ga_ref, gb_ref, wqkv_ref, wproj_ref, wup_ref, wdown_ref,
    t_ref, o_ref, p_ref, z1_ref, rs1_ref, z2_ref, rs2_ref, m_ref, gp_ref, pool_ref,
):
    step = pl.program_id(0)
    width = x_ref.shape[1]
    head = width // CHAR_HEADS
    scale = head ** (-0.5)
    steps_per_block = LANES * letters // STEP
    owner = lane_word(letters)
    blocks = own_blocks(letters)
    key_slot = lax.broadcasted_iota(jnp.int32, (letters, LANES), 0)

    @pl.when(step % steps_per_block == 0)
    def _():
        pool_ref[...] = jnp.zeros_like(pool_ref)

    for part in range(STEP // SPAN):
        at = pl.ds(part * SPAN, SPAN)
        x = x_ref[at, :].astype(f32).T
        z1, rs1 = normed(x)
        z1_ref[0, :, at] = z1.astype(bf16)
        rs1_ref[0, :, at] = rs1
        a1 = (z1 * wide(ga_ref[...], SPAN)).astype(bf16)
        for n in range(3):
            rows = pl.ds(n * width, width)
            t_ref[0, rows, at] = dot(wqkv_ref[rows, :], a1).astype(bf16)
        for g in range(SPAN // LANES):
            lanes = pl.ds(part * SPAN + g * LANES, LANES)
            allowed = key_slot < tok_ref[0, :, lanes]
            for h in range(CHAR_HEADS):
                q = t_ref[0, pl.ds(h * head, head), lanes]
                k = t_ref[0, pl.ds(width + h * head, head), lanes]
                v = t_ref[0, pl.ds(2 * width + h * head, head), lanes]
                full = dot(k.T, q)
                s = jnp.where(allowed, pick_own(full, owner, letters) * scale, NEGATIVE)
                e = jnp.exp(s - jnp.max(s, 0, keepdims=True))
                p = e / jnp.sum(e, 0, keepdims=True)
                p_ref[0, pl.ds(h * letters, letters), lanes] = p
                o = dot(v, spread_own(p.astype(bf16), blocks, letters))
                o_ref[0, pl.ds(h * head, head), lanes] = o.astype(bf16)
        h1 = x + dot(wproj_ref[...], o_ref[0, :, at])
        z2, rs2 = normed(h1)
        z2_ref[0, :, at] = z2.astype(bf16)
        rs2_ref[0, :, at] = rs2
        a2 = (z2 * wide(gb_ref[...], SPAN)).astype(bf16)
        for n in range(wup_ref.shape[0] // 256):
            rows = pl.ds(n * 256, 256)
            m, gp = gelu_both(dot(wup_ref[rows, :], a2))
            m_ref[0, rows, at] = m.astype(bf16)
            gp_ref[0, rows, at] = gp.astype(bf16)
        h2 = h1 + dot(wdown_ref[...], m_ref[0, :, at])
        high = h2.astype(bf16)
        low = (h2 - high.astype(f32)).astype(bf16)
        row = lax.broadcasted_iota(jnp.int32, (SPAN, LANES), 0)
        word = lax.broadcasted_iota(jnp.int32, (SPAN, LANES), 1)
        first = (step % steps_per_block) * (STEP // letters) + part * (SPAN // letters)
        mine = (row // letters + first == word) & (row % letters < cnt_ref[...])
        gather = jnp.where(mine, 1.0, 0.0).astype(bf16)
        pool_ref[...] += dot(high, gather) + dot(low, gather)


def full_spec(a):
    nd = len(a.shape)
    return pl.BlockSpec(a.shape, lambda i: (0,) * nd)


def char_forward(x, tok, cnt, ga, gb, wqkv_t, wproj_t, wup_t, wdown_t, letters):
    tokens, width = x.shape
    steps = tokens // STEP
    hidden = wup_t.shape[0]
    per = LANES * letters // STEP

    def strip(rows, dtype=bf16):
        return (
            jax.ShapeDtypeStruct((steps, rows, STEP), dtype),
            pl.BlockSpec((1, rows, STEP), lambda i: (i, 0, 0)),
        )

    outs = [
        strip(3 * width), strip(width), strip(CHAR_HEADS * letters, f32), strip(width), strip(1, f32),
        strip(width), strip(1, f32), strip(hidden), strip(hidden),
        (jax.ShapeDtypeStruct((width, tokens // letters), f32), pl.BlockSpec((width, LANES), lambda i: (0, i // per))),
    ]
    return pl.pallas_call(
        functools.partial(char_forward_kernel, letters),
        grid=(steps,),
        in_specs=[
            pl.BlockSpec((STEP, width), lambda i: (i, 0)),
            pl.BlockSpec((1, 1, STEP), lambda i: (i, 0, 0)),
            pl.BlockSpec((1, LANES), lambda i: (0, i // per)),
        ] + [full_spec(a) for a in (ga, gb, wqkv_t, wproj_t, wup_t, wdown_t)],
        out_specs=[o[1] for o in outs],
        out_shape=[o[0] for o in outs],
        compiler_params=pltpu.CompilerParams(
            dimension_semantics=("arbitrary",), vmem_limit_bytes=56 * 2**20
        ),
        name="char_forward",
    )(x, tok, cnt, ga, gb, wqkv_t, wproj_t, wup_t, wdown_t)


def norm_back(dy, z, rs, gain):
    dz = dy * gain
    a = jnp.mean(dz, 0, keepdims=True)
    b = jnp.mean(dz * z, 0, keepdims=True)
    return rs * (dz - a - z * b)


def fold_lanes(v):
    out = v[:, :LANES]
    for n in range(1, v.shape[1] // LANES):
        out = out + v[:, n * LANES : (n + 1) * LANES]
    return out


def char_backward_kernel(
    letters, dp_ref, tok_ref, ga_ref, gb_ref, wqkv_ref, wproj_ref, wup_ref, wdown_ref,
    t_ref, o_ref, p_ref, z1_ref, rs1_ref, z2_ref, rs2_ref, m_ref, gp_ref,
    cg_ref, gqkv_ref, gproj_ref, gup_ref, gdown_ref, gga_ref, ggb_ref,
    dh2_ref, du_ref, dh1b_ref, do_ref, dt_ref,
):
    step = pl.program_id(0)
    width = cg_ref.shape[1]
    head = width // CHAR_HEADS
    scale = head ** (-0.5)
    steps_per_block = LANES * letters // STEP
    owner = lane_word(letters)
    blocks = own_blocks(letters)

    @pl.when(step == 0)
    def _():
        for ref in (gqkv_ref, gproj_ref, gup_ref, gdown_ref, gga_ref, ggb_ref):
            ref[...] = jnp.zeros_like(ref)

    for part in range(STEP // SPAN):
        at = pl.ds(part * SPAN, SPAN)
        word = lax.broadcasted_iota(jnp.int32, (LANES, SPAN), 0)
        col = lax.broadcasted_iota(jnp.int32, (LANES, SPAN), 1)
        first = (step % steps_per_block) * (STEP // letters) + part * (SPAN // letters)
        mine = (col // letters + first == word) & (col % letters < tok_ref[0, :, at])
        scatter = jnp.where(mine, 1.0, 0.0).astype(bf16)
        dh2 = dot(dp_ref[...], scatter)
        dh2b = dh2.astype(bf16)
        dh2_ref[:, at] = dh2b
        for n in range(wdown_ref.shape[0] // 256):
            rows = pl.ds(n * 256, 256)
            du_ref[rows, at] = (dot(wdown_ref[rows, :], dh2b) * gp_ref[0, rows, at].astype(f32)).astype(bf16)
        dy = dot(wup_ref[...], du_ref[:, at])
        z = z2_ref[0, :, at].astype(f32)
        ggb_ref[...] += fold_lanes(dy * z)
        dh1 = dh2 + norm_back(dy, z, rs2_ref[0, :, at], wide(gb_ref[...], SPAN))
        dh1b = dh1.astype(bf16)
        dh1b_ref[:, at] = dh1b
        do_ref[:, at] = dot(wproj_ref[...], dh1b).astype(bf16)
        for g in range(SPAN // LANES):
            lanes = pl.ds(part * SPAN + g * LANES, LANES)
            for h in range(CHAR_HEADS):
                q_rows = pl.ds(h * head, head)
                k_rows = pl.ds(width + h * head, head)
                v_rows = pl.ds(2 * width + h * head, head)
                q = t_ref[0, q_rows, lanes]
                k = t_ref[0, k_rows, lanes]
                v = t_ref[0, v_rows, lanes]
                do = do_ref[pl.ds(h * head, head), lanes]
                p = p_ref[0, pl.ds(h * letters, letters), lanes]
                dp = pick_own(dot(v.T, do), owner, letters)
                ds = p * (dp - jnp.sum(p * dp, 0, keepdims=True))
                pb = spread_own(p.astype(bf16), blocks, letters)
                dsb = spread_own(ds.astype(bf16), blocks, letters)
                dt_ref[q_rows, lanes] = (dot(k, dsb) * scale).astype(bf16)
                dt_ref[k_rows, lanes] = (dot_nt(q, dsb) * scale).astype(bf16)
                dt_ref[v_rows, lanes] = dot_nt(do, pb).astype(bf16)
        dy = dot(wqkv_ref[...], dt_ref[:, at])
        z = z1_ref[0, :, at].astype(f32)
        gga_ref[...] += fold_lanes(dy * z)
        dx = dh1 + norm_back(dy, z, rs1_ref[0, :, at], wide(ga_ref[...], SPAN))
        cg_ref[at, :] = dx.T.astype(bf16)
    gdown_ref[...] += dot_nt(dh2_ref[...], m_ref[0])
    gup_ref[...] += dot_nt(z2_ref[0], du_ref[...])
    gproj_ref[...] += dot_nt(dh1b_ref[...], o_ref[0])
    gqkv_ref[...] += dot_nt(dt_ref[...], z1_ref[0])

    @pl.when(step == pl.num_programs(0) - 1)
    def _():
        gup_ref[...] = gup_ref[...] * wide(gb_ref[...], gup_ref.shape[1])
        gqkv_ref[...] = gqkv_ref[...] * ga_ref[...].T[:1]


def char_backward(dp, tok, ga, gb, wqkv, wproj, wup, wdown, saved, letters):
    t, o, p, z1, rs1, z2, rs2, m, gp = saved
    steps = t.shape[0]
    width = wqkv.shape[0]
    hidden = wup.shape[1]
    per = LANES * letters // STEP

    def whole(shape):
        return (jax.ShapeDtypeStruct(shape, f32), pl.BlockSpec(shape, lambda i: (0, 0)))

    outs = [
        (jax.ShapeDtypeStruct((steps * STEP, width), bf16), pl.BlockSpec((STEP, width), lambda i: (i, 0))),
        whole((3 * width, width)), whole((width, width)), whole((width, hidden)), whole((width, hidden)),
        whole((width, LANES)), whole((width, LANES)),
    ]
    return pl.pallas_call(
        functools.partial(char_backward_kernel, letters),
        grid=(steps,),
        in_specs=[
            pl.BlockSpec((width, LANES), lambda i: (0, i // per)),
            pl.BlockSpec((1, 1, STEP), lambda i: (i, 0, 0)),
        ] + [full_spec(a) for a in (ga, gb, wqkv, wproj, wup, wdown)]
        + [pl.BlockSpec((1,) + s.shape[1:], lambda i: (i, 0, 0)) for s in saved],
        out_specs=[o[1] for o in outs],
        out_shape=[o[0] for o in outs],
        scratch_shapes=[
            pltpu.VMEM((width, STEP), bf16),
            pltpu.VMEM((hidden, STEP), bf16),
            pltpu.VMEM((width, STEP), bf16),
            pltpu.VMEM((width, STEP), bf16),
            pltpu.VMEM((3 * width, STEP), bf16),
        ],
        compiler_params=pltpu.CompilerParams(
            dimension_semantics=("arbitrary",), vmem_limit_bytes=56 * 2**20
        ),
        name="char_backward",
    )(dp, tok, ga, gb, wqkv, wproj, wup, wdown, *saved)


def word_kernel(
    pool_sum_ref, cnt_ref, sep_ref, cot_ref, ga_ref, gb_ref, wpool_ref, wqkv_ref, wproj_ref, wup_ref, wdown_ref,
    out_ref, dpool_ref, gpool_ref, gqkv_ref, gproj_ref, gup_ref, gdown_ref, gga_ref, ggb_ref,
    pooled, x, z3, rs3, a3, t, p, o, h3, z4, rs4, a4, m, gp, bias, cot, du, dh3, dh3b, do, dt, dtk,
):
    width, length = x.shape
    head = width // WORD_HEADS
    scale = head ** (-0.5)
    halves = [pl.ds(n * SPAN, SPAN) for n in range(length // SPAN)]
    pooled[...] = (pool_sum_ref[...] / cnt_ref[...]).astype(bf16)
    row = lax.broadcasted_iota(jnp.int32, (length, length), 0)
    col = lax.broadcasted_iota(jnp.int32, (length, length), 1)
    tri = jnp.where(row <= col, 1.0, 0.0).astype(bf16)
    sep = jnp.broadcast_to(sep_ref[...].astype(f32).astype(bf16), (16, length))
    doc_q = dot(sep, tri)[:1]
    doc_k = lax.dot_general(tri, sep, (((0,), (1,)), ((), ())), preferred_element_type=f32)[:, :1]
    bias[...] = jnp.where((row <= col) & (doc_k == doc_q), 0.0, NEGATIVE)
    cot[...] = cot_ref[...].astype(f32).T.astype(bf16)
    for at in halves:
        x[:, at] = lax.dot_general(
            wpool_ref[...], pooled[:, at], (((0,), (0,)), ((), ())), preferred_element_type=f32
        )
        z, rs = normed(x[:, at])
        z3[:, at] = z.astype(bf16)
        rs3[:, at] = rs
        a3[:, at] = (z * wide(ga_ref[...], SPAN)).astype(bf16)
        for n in range(3):
            rows = pl.ds(n * width, width)
            t[rows, at] = lax.dot_general(
                wqkv_ref[:, rows], a3[:, at], (((0,), (0,)), ((), ())), preferred_element_type=f32
            ).astype(bf16)
    for h in range(WORD_HEADS):
        k = t[pl.ds(width + h * head, head), :].T
        for n, at in enumerate(halves):
            seen = (n + 1) * SPAN
            keys = pl.ds(0, seen)
            q = t[pl.ds(h * head, head), at]
            s = dot(k[:seen], q) * scale + bias[keys, at]
            e = jnp.exp(s - jnp.max(s, 0, keepdims=True))
            w = e / jnp.sum(e, 0, keepdims=True)
            p[h, keys, at] = w
            o[pl.ds(h * head, head), at] = dot(t[pl.ds(2 * width + h * head, head), keys], w.astype(bf16)).astype(bf16)
    for at in halves:
        h3[:, at] = x[:, at] + lax.dot_general(
            wproj_ref[...], o[:, at], (((0,), (0,)), ((), ())), preferred_element_type=f32
        )
        z, rs = normed(h3[:, at])
        z4[:, at] = z.astype(bf16)
        rs4[:, at] = rs
        a4[:, at] = (z * wide(gb_ref[...], SPAN)).astype(bf16)
        for n in range(wup_ref.shape[1] // 256):
            rows = pl.ds(n * 256, 256)
            mm, gg = gelu_both(
                lax.dot_general(wup_ref[:, rows], a4[:, at], (((0,), (0,)), ((), ())), preferred_element_type=f32)
            )
            m[rows, at] = mm.astype(bf16)
            gp[rows, at] = gg.astype(bf16)
        out = h3[:, at] + lax.dot_general(
            wdown_ref[...], m[:, at], (((0,), (0,)), ((), ())), preferred_element_type=f32
        )
        out_ref[at, :] = out.T.astype(bf16)
        for n in range(wdown_ref.shape[0] // 256):
            rows = pl.ds(n * 256, 256)
            du[rows, at] = (dot(wdown_ref[rows, :], cot[:, at]) * gp[rows, at].astype(f32)).astype(bf16)
        dy = dot(wup_ref[...], du[:, at])
        z = z4[:, at].astype(f32)
        part = fold_lanes(dy * z)
        ggb_ref[...] = part if at is halves[0] else ggb_ref[...] + part
        dh3[:, at] = cot[:, at].astype(f32) + norm_back(dy, z, rs4[:, at], wide(gb_ref[...], SPAN))
        dh3b[:, at] = dh3[:, at].astype(bf16)
        do[:, at] = dot(wproj_ref[...], dh3b[:, at]).astype(bf16)
    gdown_ref[...] = dot_nt(m[...], cot[...]).astype(gdown_ref.dtype)
    gup_ref[...] = dot_nt(a4[...], du[...]).astype(gup_ref.dtype)
    gproj_ref[...] = dot_nt(o[...], dh3b[...]).astype(gproj_ref.dtype)
    for h in range(WORD_HEADS):
        q_rows = pl.ds(h * head, head)
        k_rows = pl.ds(width + h * head, head)
        v_rows = pl.ds(2 * width + h * head, head)
        v = t[v_rows, :].T
        for n in reversed(range(len(halves))):
            at = halves[n]
            seen = (n + 1) * SPAN
            keys = pl.ds(0, seen)
            w = p[h, keys, at]
            g = do[q_rows, at]
            dp = dot(v[:seen], g)
            ds = (w * (dp - jnp.sum(w * dp, 0, keepdims=True))).astype(bf16)
            dt[q_rows, at] = (dot(t[k_rows, keys], ds) * scale).astype(bf16)
            dk = dot_nt(t[q_rows, at], ds) * scale
            dv = dot_nt(g, w.astype(bf16))
            if n == len(halves) - 1:
                dtk[0] = dk
                dtk[1] = dv
            else:
                dtk[0, :, keys] += dk
                dtk[1, :, keys] += dv
        dt[k_rows, :] = dtk[0].astype(bf16)
        dt[v_rows, :] = dtk[1].astype(bf16)
    gqkv_ref[...] = dot_nt(a3[...], dt[...]).astype(gqkv_ref.dtype)
    for at in halves:
        dy = dot(wqkv_ref[...], dt[:, at])
        z = z3[:, at].astype(f32)
        part = fold_lanes(dy * z)
        gga_ref[...] = part if at is halves[0] else gga_ref[...] + part
        dx = dh3[:, at] + norm_back(dy, z, rs3[:, at], wide(ga_ref[...], SPAN))
        dh3b[:, at] = dx.astype(bf16)
        dpool_ref[:, at] = (dot(wpool_ref[...], dh3b[:, at]) / cnt_ref[:, at]).astype(bf16)
    gpool_ref[...] = dot_nt(pooled[...], dh3b[...]).astype(gpool_ref.dtype)


def word_layer(pool_sum, cnt, sep, cot, ga, gb, wpool, wqkv, wproj, wup, wdown, grad_type=f32):
    length, width = cot.shape
    inner = pool_sum.shape[0]
    hidden = wup.shape[1]
    vm = pltpu.VMEM
    return pl.pallas_call(
        word_kernel,
        out_shape=[
            jax.ShapeDtypeStruct((length, width), bf16),
            jax.ShapeDtypeStruct((inner, length), bf16),
            jax.ShapeDtypeStruct(wpool.shape, grad_type),
            jax.ShapeDtypeStruct(wqkv.shape, grad_type),
            jax.ShapeDtypeStruct(wproj.shape, grad_type),
            jax.ShapeDtypeStruct(wup.shape, grad_type),
            jax.ShapeDtypeStruct(wdown.shape, grad_type),
            jax.ShapeDtypeStruct((width, LANES), f32),
            jax.ShapeDtypeStruct((width, LANES), f32),
        ],
        scratch_shapes=[
            vm((inner, length), bf16), vm((width, length), f32), vm((width, length), bf16), vm((1, length), f32),
            vm((width, length), bf16), vm((3 * width, length), bf16), vm((WORD_HEADS, length, length), f32),
            vm((width, length), bf16), vm((width, length), f32), vm((width, length), bf16), vm((1, length), f32),
            vm((width, length), bf16), vm((hidden, length), bf16), vm((hidden, length), bf16),
            vm((length, length), f32), vm((width, length), bf16), vm((hidden, length), bf16),
            vm((width, length), f32), vm((width, length), bf16), vm((width, length), bf16),
            vm((3 * width, length), bf16), vm((2, width // WORD_HEADS, length), f32),
        ],
        compiler_params=pltpu.CompilerParams(vmem_limit_bytes=58 * 2**20),
        name="word_layer",
    )(pool_sum, cnt, sep, cot, ga, gb, wpool, wqkv, wproj, wup, wdown)


MESH = pl.DeviceIdType.MESH


def sides():
    chips = lax.axis_size("dp") // 2
    nx = math.isqrt(chips)
    return chips // nx, nx, lax.axis_size("fsdp")


def place():
    ny, nx, nz = sides()
    me = lax.axis_index("dp")
    return me // (2 * nx), (me // 2) % nx, me % 2, lax.axis_index("fsdp")


def device(y, x, c, z):
    return {"dp": (y * sides()[1] + x) * 2 + c, "fsdp": z}


def others():
    ny, nx, nz = sides()
    y, x, c, z = place()
    return [((y + j) % ny, (x + i) % nx) for j in range(ny) for i in range(nx) if j + i > 0]


def partners():
    ny, nx, nz = sides()
    y, x, c, z = place()
    found = [device(y, x, 1 - c, z)]
    found += [device(y, x, c, (z + k) % nz) for k in range(1, nz)]
    return found + [device(j, i, c, z) for j, i in others()]


def greet():
    barrier = pltpu.get_barrier_semaphore()
    for other in partners():
        pl.semaphore_signal(barrier, inc=1, device_id=other, device_id_type=MESH)


def greeted():
    pl.semaphore_wait(pltpu.get_barrier_semaphore(), len(partners()))


def remote(src, dst, sems, n, other):
    return pltpu.make_async_remote_copy(
        src_ref=src, dst_ref=dst, send_sem=sems.at[0, n], recv_sem=sems.at[1, n],
        device_id=other, device_id_type=MESH,
    )


def gather_copies():
    ny, nx, nz = sides()
    return nz - 1 + 1 + 4 * (nx - 1) + 4 * (ny - 1)


def gather_stages(ref, sems, wanted=(0, 1, 2, 3)):
    ny, nx, nz = sides()
    y, x, c, z = place()
    every = slice(None)
    half = ref.shape[4] // 2
    low, high = pl.ds(0, half), pl.ds(half, half)
    twin = device(y, x, 1 - c, z)
    plan = [[], [], [], []]
    plan[0] += [((y, x, c, z), device(y, x, c, (z + k) % nz)) for k in range(1, nz)]
    plan[1] += [((y, x, c, every, low), device(y, (x + k) % nx, c, z)) for k in range(1, nx)]
    plan[1] += [((y, x, c, every, high), device((y + k) % ny, x, c, z)) for k in range(1, ny)]
    plan[1] += [((y, x, c), twin)]
    plan[2] += [((y, every, c, every, low), device((y + k) % ny, x, c, z)) for k in range(1, ny)]
    plan[2] += [((every, x, c, every, high), device(y, (x + k) % nx, c, z)) for k in range(1, nx)]
    plan[2] += [((y, (x + k) % nx, c, every, low), twin) for k in range(1, nx)]
    plan[2] += [(((y + k) % ny, x, c, every, high), twin) for k in range(1, ny)]
    plan[3] += [(((y + k) % ny, every, c, every, low), twin) for k in range(1, ny)]
    plan[3] += [((every, (x + k) % nx, c, every, high), twin) for k in range(1, nx)]
    count = 0
    stages = []
    for n, part in enumerate(plan):
        copies = []
        for where, other in part:
            if n in wanted:
                copies.append(remote(ref.at[where], ref.at[where], sems, count, other))
            count += 1
        stages.append(copies)
    return stages


def gather_direct(ref, sems, wanted=(0, 1, 2)):
    ny, nx, nz = sides()
    y, x, c, z = place()
    twin = device(y, x, 1 - c, z)
    plan = [[((y, x, c, z), device(y, x, c, (z + k) % nz)) for k in range(1, nz)]]
    plan += [[((y, x, c), device(j, i, c, z)) for j, i in others()] + [((y, x, c), twin)]]
    plan += [[((j, i, c), twin) for j, i in others()]]
    count, stages = 0, []
    for n, part in enumerate(plan):
        copies = []
        for where, other in part:
            if n in wanted:
                copies.append(remote(ref.at[where], ref.at[where], sems, count, other))
            count += 1
        stages.append(copies)
    return stages


def start_all(copies):
    for copy in copies:
        copy.start()


def arrive_all(copies):
    for copy in copies:
        copy.wait_recv()


def sent_all(stages):
    for copies in stages:
        for copy in copies:
            copy.wait_send()


def lanes_to(v, n):
    return v if v.shape[1] == n else jnp.concatenate([v, jnp.zeros((v.shape[0], n - v.shape[1]), v.dtype)], 1)


def turned(v):
    return v.astype(f32).T.astype(bf16)


def scatter_copies():
    ny, nx, nz = sides()
    return 1 + 2 * (nx - 1) + 2 * (ny - 1) + nz - 1


def scatter_scratch(rows, lanes):
    ny, nx, nz = sides()
    half = rows // 2
    shapes = (
        (ny, nx, nz, rows, lanes), (ny, nx, nz, rows, lanes), (nx - 1, ny, nz, half, lanes),
        (ny - 1, nx, nz, half, lanes), (ny - 1, nz, half, lanes), (nx - 1, nz, half, lanes), (nz - 1, rows, lanes),
    )
    return [pltpu.VMEM(shape, bf16) for shape in shapes] + [pltpu.SemaphoreType.DMA((2, scatter_copies()))]


def scatter_stage(n, send, work):
    acc, twin_in, one_low, one_high, two_low, two_high, last_in, sems = work
    ny, nx, nz = sides()
    y, x, c, z = place()
    half = acc.shape[3] // 2
    low, high, every = pl.ds(0, half), pl.ds(half, half), slice(None)
    plan = [[], [], [], []]
    plan[0] += [(send, (every, every, 1 - c), twin_in, device(y, x, 1 - c, z))]
    plan[1] += [
        (acc, (every, (x + k) % nx, every, low), one_low.at[k - 1], device(y, (x + k) % nx, c, z)) for k in range(1, nx)
    ]
    plan[1] += [
        (acc, ((y + k) % ny, every, every, high), one_high.at[k - 1], device((y + k) % ny, x, c, z)) for k in range(1, ny)
    ]
    plan[2] += [
        (acc, ((y + k) % ny, x, every, low), two_low.at[k - 1], device((y + k) % ny, x, c, z)) for k in range(1, ny)
    ]
    plan[2] += [
        (acc, (y, (x + k) % nx, every, high), two_high.at[k - 1], device(y, (x + k) % nx, c, z)) for k in range(1, nx)
    ]
    plan[3] += [(acc, (y, x, (z + k) % nz), last_in.at[k - 1], device(y, x, c, (z + k) % nz)) for k in range(1, nz)]
    first = sum(len(p) for p in plan[:n])
    return [remote(src.at[at], dst, sems, first + i, other) for i, (src, at, dst, other) in enumerate(plan[n])]


def direct_scratch(rows, lanes):
    ny, nx, nz = sides()
    shapes = (
        (ny, nx, nz, rows, lanes), (ny, nx, nz, rows, lanes), (ny * nx - 1, nz, rows, lanes), (nz - 1, rows, lanes)
    )
    count = 1 + ny * nx - 1 + nz - 1
    return [pltpu.VMEM(shape, bf16) for shape in shapes] + [pltpu.SemaphoreType.DMA((2, count))]


def direct_stage(n, send, work):
    acc, twin_in, near_in, last_in, sems = work
    ny, nx, nz = sides()
    y, x, c, z = place()
    if n == 0:
        return [remote(send.at[:, :, 1 - c], twin_in, sems, 0, device(y, x, 1 - c, z))]
    if n == 1:
        return [
            remote(acc.at[j, i], near_in.at[k], sems, 1 + k, device(j, i, c, z)) for k, (j, i) in enumerate(others())
        ]
    return [
        remote(acc.at[y, x, (z + k) % nz], last_in.at[k - 1], sems, ny * nx + k - 1, device(y, x, c, (z + k) % nz))
        for k in range(1, nz)
    ]


def direct_sum(n, own, work, out):
    acc, twin_in, near_in, last_in, sems = work
    ny, nx, nz = sides()
    y, x, c, z = place()
    if n == 0:
        for b in range(ny):
            for a in range(nx):
                for k in range(nz):
                    acc[b, a, k] = own(b, a, k) + twin_in[b, a, k]
    elif n == 1:
        for k in range(nz):
            total = acc[y, x, k].astype(f32) + sum(near_in[i, k].astype(f32) for i in range(ny * nx - 1))
            acc[y, x, k] = total.astype(bf16)
    else:
        out[...] = acc[y, x, z].astype(f32) + sum(last_in[i].astype(f32) for i in range(nz - 1))


def scatter_sum(n, own, work, out):
    acc, twin_in, one_low, one_high, two_low, two_high, last_in, sems = work
    ny, nx, nz = sides()
    y, x, c, z = place()
    half = acc.shape[3] // 2
    low, high = pl.ds(0, half), pl.ds(half, half)
    if n == 0:
        for b in range(ny):
            for a in range(nx):
                for k in range(nz):
                    acc[b, a, k] = own(b, a, k) + twin_in[b, a, k]
    elif n == 1:
        for k in range(nz):
            for b in range(ny):
                acc[b, x, k, low] += sum(one_low[i, b, k] for i in range(nx - 1))
            for a in range(nx):
                acc[y, a, k, high] += sum(one_high[i, a, k] for i in range(ny - 1))
    elif n == 2:
        for k in range(nz):
            acc[y, x, k, low] += sum(two_low[i, k] for i in range(ny - 1))
            acc[y, x, k, high] += sum(two_high[i, k] for i in range(nx - 1))
    else:
        out[...] = acc[y, x, z].astype(f32) + sum(last_in[i].astype(f32) for i in range(nz - 1))


def gelu_twice(u):
    s = u * u
    t = jnp.tanh(u * (GELU_A + (GELU_A * GELU_B) * s))
    a = 1.0 + t
    m = u * a
    return m, a + m * ((1.0 - t) * (GELU_A + (3.0 * GELU_A * GELU_B) * s))


def shift_of(letters):
    return letters.bit_length() - 1


def twin_owner(letters):
    lane = lax.broadcasted_iota(jnp.int32, (letters, 2 * LANES), 1)
    return lax.shift_right_logical(lane & (LANES - 1), shift_of(letters))


def twin_mask(letters):
    bits = shift_of(letters)
    a = lax.shift_right_logical(lax.broadcasted_iota(jnp.int32, (LANES, 2 * LANES), 0), bits)
    b = lax.shift_right_logical(lax.broadcasted_iota(jnp.int32, (LANES, 2 * LANES), 1) & (LANES - 1), bits)
    return jnp.where(a == b, 1.0, 0.0).astype(bf16)


def twin_blocks(v):
    half = v.shape[0] // 2
    none = jnp.zeros((half, v.shape[1]), v.dtype)
    return jnp.concatenate([jnp.concatenate([v[:half], none], 1), jnp.concatenate([none, v[half:]], 1)], 0)


def stacked(v):
    return jnp.concatenate([v[:, :LANES], v[:, LANES:]], 0)


def char_units():
    for g in range(BATCH // LANES):
        for h in range(CHAR_HEADS // 2):
            yield h, pl.ds(g * LANES, LANES), pl.ds(2 * g * LANES, 2 * LANES)


def word_of(step, letters, per, shape, axis):
    token = lax.broadcasted_iota(jnp.int32, shape, axis)
    word = lax.broadcasted_iota(jnp.int32, shape, 1 - axis)
    first = (step % per) * (BATCH // letters)
    return lax.shift_right_logical(token, shift_of(letters)) + first == word, token & (letters - 1)


def forward_first(s, letters, per, x_ref, cnt_ref, tok_ref, rs1_ref, x_all, z1_all):
    mine, slot = word_of(s, letters, per, (LANES, BATCH), 1)
    counts = jnp.broadcast_to(cnt_ref[...].astype(f32), (16, LANES)).astype(bf16)
    tok_ref[s] = dot(counts, jnp.where(mine, 1.0, 0.0).astype(bf16))[:1].astype(jnp.int32)
    x = x_ref[...].astype(f32).T
    x_all[s] = x.astype(bf16)
    z1, rs1 = normed(x)
    z1_all[s] = z1.astype(bf16)
    rs1_ref[s] = rs1


def forward_attention(s, letters, tok_ref, ga_ref, wqkv_t, wproj_t, t_ref, o_ref, p_ref, z1_ref, x_all, z1_all, h1_all):
    width = o_ref.shape[1]
    pair = 2 * (width // CHAR_HEADS)
    scale = (width // CHAR_HEADS) ** (-0.5)
    owner, blocks = twin_owner(letters), twin_mask(letters)
    key_slot = lax.broadcasted_iota(jnp.int32, (letters, 2 * LANES), 0)
    z1 = z1_all[s]
    z1_ref[0] = z1
    a1 = (z1.astype(f32) * wide(ga_ref[...], BATCH)).astype(bf16)
    t_ref[0] = dot(wqkv_t[...], a1).astype(bf16)
    units = list(char_units())
    scores = []
    for h, lanes, lanes2 in units:
        q = twin_blocks(t_ref[0, pl.ds(h * pair, pair), lanes])
        k = t_ref[0, pl.ds(width + h * pair, pair), lanes].T
        scores.append(pick_own(dot(k, q), owner, letters))
    probs = []
    for (h, lanes, lanes2), score in zip(units, scores):
        counts = tok_ref[s, :, lanes]
        allowed = key_slot < jnp.concatenate([counts, counts], 1)
        score = jnp.where(allowed, score * scale, NEGATIVE)
        e = jnp.exp(score - jnp.max(score, 0, keepdims=True))
        p = e / jnp.sum(e, 0, keepdims=True)
        p_ref[0, pl.ds(h * letters, letters), lanes2] = p
        probs.append(p)
    for (h, lanes, lanes2), p in zip(units, probs):
        v = twin_blocks(t_ref[0, pl.ds(2 * width + h * pair, pair), lanes])
        o = dot(v, stacked(spread_own(p.astype(bf16), blocks, letters)))
        o_ref[0, pl.ds(h * pair, pair), lanes] = o.astype(bf16)
    h1_all[s] = x_all[s].astype(f32) + dot(wproj_t[...], o_ref[0])


def forward_feed(s, letters, per, cnt_ref, gb_ref, wup_t, wdown_t, z2_ref, rs2_ref, m_ref, slope_ref, pool_ref, h1_all):
    h1 = h1_all[s]
    z2, rs2 = normed(h1)
    z2_ref[0] = z2.astype(bf16)
    rs2_ref[0] = rs2
    a2 = (z2 * wide(gb_ref[...], BATCH)).astype(bf16)
    for n in range(wup_t.shape[0] // 256):
        rows = pl.ds(n * 256, 256)
        m, slope = gelu_twice(dot(wup_t[rows, :], a2))
        m_ref[0, rows, :] = m.astype(bf16)
        slope_ref[0, rows, :] = slope.astype(bf16)
    h2 = h1 + dot(wdown_t[...], m_ref[0])
    high = h2.astype(bf16)
    low = (h2 - high.astype(f32)).astype(bf16)
    mine, slot = word_of(s, letters, per, (BATCH, LANES), 0)
    gather = jnp.where(mine & (slot < cnt_ref[...]), 1.0, 0.0).astype(bf16)
    part = dot(high, gather) + dot(low, gather)

    @pl.when(s % per == 0)
    def _():
        pool_ref[...] = part

    @pl.when(s % per != 0)
    def _():
        pool_ref[...] += part


def backward_feed(
    s, letters, per, dp_ref, tok_ref, gb_ref, wup, wdown, z2_ref, rs2_ref, m_ref, slope_ref, gup, gdown_t, dh1_all, du_ref
):
    mine, slot = word_of(s, letters, per, (LANES, BATCH), 1)
    scatter = jnp.where(mine & (slot < tok_ref[0]), 1.0, 0.0).astype(bf16)
    dh2 = dot(dp_ref[...], scatter)
    dh2b = dh2.astype(bf16)
    for n in range(wdown.shape[0] // 256):
        rows = pl.ds(n * 256, 256)
        du_ref[rows, :] = (dot(wdown[rows, :], dh2b) * slope_ref[0, rows, :].astype(f32)).astype(bf16)
    dy = dot(wup[...], du_ref[...])
    z = z2_ref[0].astype(f32)
    dh1 = dh2 + norm_back(dy, z, rs2_ref[0], wide(gb_ref[...], BATCH))
    dh1_all[s] = dh1.astype(bf16)
    down = dot_nt(dh2b, m_ref[0])
    up = dot_nt(z2_ref[0], du_ref[...])

    @pl.when(s == 0)
    def _():
        gdown_t[...] = down
        gup[...] = up

    @pl.when(s != 0)
    def _():
        gdown_t[...] += down
        gup[...] += up


def backward_attention(s, letters, wproj, t_ref, o_ref, p_ref, z1_ref, gqkv_t, gproj_t, dh1_all, dt_all, do_ref):
    width = wproj.shape[0]
    pair = 2 * (width // CHAR_HEADS)
    scale = (width // CHAR_HEADS) ** (-0.5)
    owner, blocks = twin_owner(letters), twin_mask(letters)
    dh1b = dh1_all[s]
    do_ref[...] = dot(wproj[...], dh1b).astype(bf16)
    units = list(char_units())
    grads = []
    for h, lanes, lanes2 in units:
        v = t_ref[0, pl.ds(2 * width + h * pair, pair), lanes].T
        grads.append(pick_own(dot(v, twin_blocks(do_ref[pl.ds(h * pair, pair), lanes])), owner, letters))
    spread = []
    for (h, lanes, lanes2), dp in zip(units, grads):
        p = p_ref[0, pl.ds(h * letters, letters), lanes2]
        ds = p * (dp - jnp.sum(p * dp, 0, keepdims=True))
        spread.append((spread_own(p.astype(bf16), blocks, letters), spread_own(ds.astype(bf16), blocks, letters)))
    for (h, lanes, lanes2), (pb, dsb) in zip(units, spread):
        q_rows = pl.ds(h * pair, pair)
        k_rows = pl.ds(width + h * pair, pair)
        v_rows = pl.ds(2 * width + h * pair, pair)
        q = twin_blocks(t_ref[0, q_rows, lanes])
        k = twin_blocks(t_ref[0, k_rows, lanes])
        do = twin_blocks(do_ref[q_rows, lanes])
        dt_all[s, q_rows, lanes] = (dot(k, stacked(dsb)) * scale).astype(bf16)
        dt_all[s, k_rows, lanes] = (dot_nt(q, dsb) * scale).astype(bf16)
        dt_all[s, v_rows, lanes] = dot_nt(do, pb).astype(bf16)
    proj = dot_nt(dh1b, o_ref[0])
    qkv = dot_nt(dt_all[s], z1_ref[0])

    @pl.when(s == 0)
    def _():
        gproj_t[...] = proj
        gqkv_t[...] = qkv

    @pl.when(s != 0)
    def _():
        gproj_t[...] += proj
        gqkv_t[...] += qkv


def backward_last(s, ga_ref, wqkv, z1_ref, rs1_ref, cg_ref, dh1_all, dt_all):
    dy = dot(wqkv[...], dt_all[s])
    z = z1_ref[0].astype(f32)
    dx = dh1_all[s].astype(f32) + norm_back(dy, z, rs1_ref[0], wide(ga_ref[...], BATCH))
    cg_ref[...] = dx.T.astype(bf16)


def pack_first(slot, qkv, proj_t, gains):
    r = qkv.shape[0]
    slot[pl.ds(0, r), :] = jnp.concatenate([qkv[...], turned(lanes_to(proj_t[...], LANES))[:r]], 1)
    none = jnp.zeros((slot.shape[0] - r - gains.shape[0], LANES), f32)
    slot[pl.ds(r, slot.shape[0] - r), :] = jnp.concatenate([gains[...], none], 0).astype(bf16)


def pack_second(slot, up, down_t, pool):
    r, n = up.shape[0], down_t.shape[0]
    slot[pl.ds(0, r), :] = up[...]
    for i in range(down_t.shape[1] // LANES):
        slot[pl.ds(r + i * n, n), :] = down_t[:, pl.ds(i * LANES, LANES)]
    slot[pl.ds(2 * r, r), :] = lanes_to(pool[...], LANES)


def pack_words(slots, qkv_t, proj_t, up, down_t):
    slots[0] = turned(jnp.concatenate([qkv_t[...], proj_t[...]], 0))
    slots[1] = up[...]
    n, lanes = down_t.shape[0], up.shape[1]
    for i in range(down_t.shape[1] // lanes):
        slots[2, pl.ds(i * n, n), :] = down_t[:, pl.ds(i * lanes, lanes)]


def seats():
    ny, nx, nz = sides()
    for d in range(2 * ny * nx):
        yield d, (d // (2 * nx), (d // 2) % nx, d % 2)


def unpack_first(ref, wqkv_t, wproj_t, wqkv, wproj, cga, cgb, wga, wgb):
    ny, nx, nz = sides()
    nd = 2 * ny * nx
    r = wqkv.shape[0] // nz
    a, b, gc, gw = wqkv_t.shape[0] // nd, wproj_t.shape[0] // nd, cga.shape[0] // nd, wga.shape[0] // nd
    for d, at in seats():
        t = turned(ref[at + (slice(None), pl.ds(0, r))].reshape(nz * r, LANES))
        wqkv_t[pl.ds(d * a, a), :] = t[:a]
        wproj_t[pl.ds(d * b, b), :] = t[a:]
        g = ref[at + (0, pl.ds(r, 16))].astype(f32).T
        one, two = (jnp.broadcast_to(g[:, i : i + 1], (LANES, LANES)) for i in range(2))
        cga[pl.ds(d * gc, gc), :] = one[:gc]
        cgb[pl.ds(d * gc, gc), :] = one[gc : 2 * gc]
        wga[pl.ds(d * gw, gw), :] = one[2 * gc : 2 * gc + gw]
        wgb[pl.ds(d * gw, gw), :] = two[:gw]
    wqkv[...] = turned(wqkv_t[...])
    wproj[...] = turned(wproj_t[...])


def unpack_second(ref, wup_t, wdown_t, wup, wdown, pool_t):
    ny, nx, nz = sides()
    nd = 2 * ny * nx
    r, n, p = wup.shape[0] // nz, wdown_t.shape[0] // nd, pool_t.shape[0] // nd
    deep = wdown_t.shape[1] // nz
    for d, at in seats():
        up = ref[at + (slice(None), pl.ds(0, r))].reshape(nz * r, LANES)
        wup[:, pl.ds(d * LANES, LANES)] = up
        wup_t[pl.ds(d * LANES, LANES), :] = turned(up)
        for z in range(nz):
            for i in range(deep // LANES):
                wdown_t[pl.ds(d * n, n), pl.ds(z * deep + i * LANES, LANES)] = ref[at + (z, pl.ds(r + i * n, n))] * 0.5
        t = turned(ref[at + (slice(None), pl.ds(2 * r, r))].reshape(nz * r, LANES))
        pool_t[pl.ds(d * p, p), :] = t[:p]
    wdown[...] = turned(wdown_t[...])


def pack_first_grads(slots, gqkv_t, gproj_t, ga, wqkv_t, gup, wup, gwga, gwgb):
    ny, nx, nz = sides()
    nd = 2 * ny * nx
    width = gqkv_t.shape[1]
    r = width // nz
    tail = slots.shape[4] - r
    a, b, gc, gw = gqkv_t.shape[0] // nd, gproj_t.shape[0] // nd, width // nd, gwga.shape[0] // nd
    char_a = jnp.sum(gqkv_t[...] * wqkv_t[...].astype(f32), 0, keepdims=True)
    char_a = jnp.broadcast_to(char_a, (8, width)).T[:, :1]
    char_b = jnp.sum(gup[...] * wup[...].astype(f32), 1, keepdims=True)
    word_a, word_b = (jnp.sum(g[...], 1, keepdims=True) for g in (gwga, gwgb))
    gain = ga[...].T[:1]
    spot = lax.broadcasted_iota(jnp.int32, (LANES, nz * tail), 1) % tail
    none = jnp.zeros((LANES - gw, 1), f32)
    for d, at in seats():
        t = jnp.concatenate([gqkv_t[pl.ds(d * a, a), :] * gain, gproj_t[pl.ds(d * b, b), :]], 0)
        slots[at + (slice(None), pl.ds(0, r))] = t.T.astype(bf16).reshape(nz, r, LANES)
        char, word = slice(d * gc, (d + 1) * gc), slice(d * gw, (d + 1) * gw)
        one = jnp.concatenate([char_a[char], char_b[char], word_a[word]], 0)
        two = jnp.concatenate([word_b[word], none], 0)
        side = jnp.where(spot == 0, one, jnp.where(spot == 1, two, 0.0))
        slots[at + (slice(None), pl.ds(r, tail))] = side.T.astype(bf16).reshape(nz, tail, LANES)


def pack_second_grads(slots, gup, gdown_t, gb, gpool_t):
    ny, nx, nz = sides()
    nd = 2 * ny * nx
    width = gup.shape[0]
    r, n, p = width // nz, gdown_t.shape[0] // nd, gpool_t.shape[0] // nd
    deep = gdown_t.shape[1] // nz
    none = jnp.zeros((LANES - p, width), f32)
    for d, at in seats():
        up = gup[:, pl.ds(d * LANES, LANES)] * gb[...]
        slots[at + (slice(None), pl.ds(0, r))] = up.astype(bf16).reshape(nz, r, LANES)
        for z in range(nz):
            for i in range(deep // LANES):
                down = gdown_t[pl.ds(d * n, n), pl.ds(z * deep + i * LANES, LANES)] * 0.5
                slots[at + (z, pl.ds(r + i * n, n))] = down.astype(bf16)
        t = jnp.concatenate([gpool_t[pl.ds(d * p, p), :], none], 0)
        slots[at + (slice(None), pl.ds(2 * r, r))] = t.T.astype(bf16).reshape(nz, r, LANES)


def unpack_mixed(ref, qkv_t, proj_t):
    nd, nz, r, lanes = ref.shape
    a, b = qkv_t.shape[0] // nd, proj_t.shape[0] // nd
    for d in range(nd):
        t = turned(ref[d].reshape(nz * r, lanes))
        qkv_t[pl.ds(d * a, a), :] = t[:a]
        proj_t[pl.ds(d * b, b), :] = t[a:]


def unpack_up(ref, up_t, up):
    nd, nz, r, lanes = ref.shape
    for d in range(nd):
        piece = ref[d].reshape(nz * r, lanes)
        up[:, pl.ds(d * lanes, lanes)] = piece
        up_t[pl.ds(d * lanes, lanes), :] = turned(piece)


def unpack_down(ref, down_t):
    nd, nz, r, lanes = ref.shape
    n, deep = down_t.shape[0] // nd, down_t.shape[1] // nz
    for d in range(nd):
        for z in range(nz):
            for i in range(deep // lanes):
                down_t[pl.ds(d * n, n), pl.ds(z * deep + i * lanes, lanes)] = ref[d, z, pl.ds(i * n, n), :] * 0.5


def word_gathered_kernel(
    pool_sum_ref, cnt_ref, sep_ref, cot_ref, ga_ref, gb_ref, wpool_t, far0, far1, far2,
    out_ref, dpool_ref, gpool_ref, gone0, gone1, gone2, gga_ref, ggb_ref,
    pooled, x, z3, rs3, a3, t, p, o, h3, z4, rs4, a4, m, slope, bias, cot, du, dh3, dh3b, do, dt, dtk,
    wqkv_t, wproj_t, wup_t, wdown_t, wqkv, wproj, wup, wdown, wpool, gqkv_t, gproj_t,
    all0, all1, all2, send0, send1, send2, in_sems, out_sems,
):
    width, length = x.shape
    head = width // WORD_HEADS
    scale = head ** (-0.5)
    nd, nz, r, lanes = send0.shape
    halves = [pl.ds(n * SPAN, SPAN) for n in range(length // SPAN)]
    fetch = [pltpu.make_async_copy(a, b, in_sems.at[n]) for n, (a, b) in enumerate(((far0, all0), (far1, all1), (far2, all2)))]
    leave = [pltpu.make_async_copy(a, b, out_sems.at[n]) for n, (a, b) in enumerate(((send0, gone0), (send1, gone1), (send2, gone2)))]
    start_all(fetch)
    pooled[...] = (pool_sum_ref[...] / cnt_ref[...]).astype(bf16)
    row = lax.broadcasted_iota(jnp.int32, (length, length), 0)
    col = lax.broadcasted_iota(jnp.int32, (length, length), 1)
    tri = jnp.where(row <= col, 1.0, 0.0).astype(bf16)
    sep = jnp.broadcast_to(sep_ref[...].astype(f32).astype(bf16), (16, length))
    doc_q = dot(sep, tri)[:1]
    doc_k = jnp.broadcast_to(doc_q, (8, length)).T[:, :1]
    bias[...] = jnp.where((row <= col) & (doc_k == doc_q), 0.0, NEGATIVE)
    cot[...] = turned(cot_ref[...])
    x[...] = dot(wpool_t[...], pooled[...])
    z, rs = normed(x[...])
    z3[...] = z.astype(bf16)
    rs3[...] = rs
    a3[...] = (z * wide(ga_ref[...], length)).astype(bf16)
    fetch[0].wait()
    unpack_mixed(all0, wqkv_t, wproj_t)
    t[...] = dot(wqkv_t[...], a3[...]).astype(bf16)
    for h in range(WORD_HEADS):
        k = t[pl.ds(width + h * head, head), :].T
        for n, at in enumerate(halves):
            seen = (n + 1) * SPAN
            keys = pl.ds(0, seen)
            q = t[pl.ds(h * head, head), at]
            s = dot(k[:seen], q) * scale + bias[keys, at]
            e = jnp.exp(s - jnp.max(s, 0, keepdims=True))
            w = e * (1.0 / jnp.sum(e, 0, keepdims=True))
            p[h, keys, at] = w
            o[pl.ds(h * head, head), at] = dot(t[pl.ds(2 * width + h * head, head), keys], w.astype(bf16)).astype(bf16)
    fetch[1].wait()
    unpack_up(all1, wup_t, wup)
    h3[...] = x[...] + dot(wproj_t[...], o[...])
    z, rs = normed(h3[...])
    z4[...] = z.astype(bf16)
    rs4[...] = rs
    a4[...] = (z * wide(gb_ref[...], length)).astype(bf16)
    for n in range(wup_t.shape[0] // 256):
        rows = pl.ds(n * 256, 256)
        mm, gg = gelu_twice(dot(wup_t[rows, :], a4[...]))
        m[rows, :] = mm.astype(bf16)
        slope[rows, :] = gg.astype(bf16)
    fetch[2].wait()
    unpack_down(all2, wdown_t)
    wdown[...] = turned(wdown_t[...])
    for n in range(wdown.shape[0] // 256):
        rows = pl.ds(n * 256, 256)
        du[rows, :] = (dot(wdown[rows, :], cot[...]) * slope[rows, :].astype(f32)).astype(bf16)
    out = h3[...] + dot(wdown_t[...], m[...])
    out_ref[...] = out.T.astype(bf16)
    dy = dot(wup[...], du[...])
    z = z4[...].astype(f32)
    ggb_ref[...] = fold_lanes(dy * z)
    dh3[...] = cot[...].astype(f32) + norm_back(dy, z, rs4[...], wide(gb_ref[...], length))
    dh3b[...] = dh3[...].astype(bf16)
    wproj[...] = turned(wproj_t[...])
    do[...] = dot(wproj[...], dh3b[...]).astype(bf16)
    n = width // nd
    deep = m.shape[0] // nz
    for z in range(nz):
        for i in range(deep // lanes):
            g = (dot_nt(cot[...], m[pl.ds(z * deep + i * lanes, lanes), :]) * 0.5).astype(bf16)
            for d in range(nd):
                send2[d, z, pl.ds(i * n, n), :] = g[d * n : (d + 1) * n]
    leave[2].start()
    for d in range(nd):
        g = dot_nt(a4[...], du[pl.ds(d * lanes, lanes), :]).astype(bf16)
        send1[d] = g.reshape(nz, r, lanes)
    leave[1].start()
    gproj_t[...] = dot_nt(dh3b[...], o[...]).astype(bf16)
    for h in range(WORD_HEADS):
        q_rows = pl.ds(h * head, head)
        k_rows = pl.ds(width + h * head, head)
        v_rows = pl.ds(2 * width + h * head, head)
        v = t[v_rows, :].T
        for n in reversed(range(len(halves))):
            at = halves[n]
            seen = (n + 1) * SPAN
            keys = pl.ds(0, seen)
            w = p[h, keys, at]
            g = do[q_rows, at]
            dp = dot(v[:seen], g)
            ds = (w * (dp - jnp.sum(w * dp, 0, keepdims=True))).astype(bf16)
            dt[q_rows, at] = (dot(t[k_rows, keys], ds) * scale).astype(bf16)
            dk = dot_nt(t[q_rows, at], ds) * scale
            dv = dot_nt(g, w.astype(bf16))
            if n == len(halves) - 1:
                dtk[0] = dk
                dtk[1] = dv
            else:
                dtk[0, :, keys] += dk
                dtk[1, :, keys] += dv
        dt[k_rows, :] = dtk[0].astype(bf16)
        dt[v_rows, :] = dtk[1].astype(bf16)
    for n in range(3):
        part = pl.ds(n * width, width)
        gqkv_t[part, :] = dot_nt(dt[part, :], a3[...]).astype(bf16)
    a, b = gqkv_t.shape[0] // nd, gproj_t.shape[0] // nd
    for d in range(nd):
        g = turned(jnp.concatenate([gqkv_t[pl.ds(d * a, a), :], gproj_t[pl.ds(d * b, b), :]], 0))
        send0[d] = g.reshape(nz, r, lanes)
    leave[0].start()
    wqkv[...] = turned(wqkv_t[...])
    dy = dot(wqkv[...], dt[...])
    z = z3[...].astype(f32)
    gga_ref[...] = fold_lanes(dy * z)
    dx = dh3[...] + norm_back(dy, z, rs3[...], wide(ga_ref[...], length))
    dh3b[...] = dx.astype(bf16)
    wpool[...] = turned(wpool_t[...])
    dpool_ref[...] = (dot(wpool[...], dh3b[...]) / cnt_ref[...]).astype(bf16)
    gpool_ref[...] = dot_nt(dh3b[...], pooled[...])
    for copy in leave:
        copy.wait()


def word_gathered(pool_sum, cnt, sep, cot, ga, gb, pool_t, *gathered):
    length, width = cot.shape
    inner = pool_sum.shape[0]
    nd, nz, r, lanes = gathered[0].shape
    hidden = nd * lanes
    vm = pltpu.VMEM
    near, far = pl.BlockSpec(memory_space=pltpu.VMEM), pl.BlockSpec(memory_space=pl.ANY)
    return pl.pallas_call(
        word_gathered_kernel,
        in_specs=[near] * 7 + [far] * 3,
        out_specs=[near] * 3 + [far] * 3 + [near] * 2,
        out_shape=[
            jax.ShapeDtypeStruct((length, width), bf16),
            jax.ShapeDtypeStruct((inner, length), bf16),
            jax.ShapeDtypeStruct((width, inner), f32),
            *(jax.ShapeDtypeStruct(g.shape, bf16) for g in gathered),
            jax.ShapeDtypeStruct((width, LANES), f32),
            jax.ShapeDtypeStruct((width, LANES), f32),
        ],
        scratch_shapes=[
            vm((inner, length), bf16), vm((width, length), f32), vm((width, length), bf16), vm((1, length), f32),
            vm((width, length), bf16), vm((3 * width, length), bf16), vm((WORD_HEADS, length, length), f32),
            vm((width, length), bf16), vm((width, length), f32), vm((width, length), bf16), vm((1, length), f32),
            vm((width, length), bf16), vm((hidden, length), bf16), vm((hidden, length), bf16),
            vm((length, length), f32), vm((width, length), bf16), vm((hidden, length), bf16),
            vm((width, length), f32), vm((width, length), bf16), vm((width, length), bf16),
            vm((3 * width, length), bf16), vm((2, width // WORD_HEADS, length), f32),
            vm((3 * width, width), bf16), vm((width, width), bf16), vm((hidden, width), bf16), vm((width, hidden), bf16),
            vm((width, 3 * width), bf16), vm((width, width), bf16), vm((width, hidden), bf16), vm((hidden, width), bf16),
            vm((inner, width), bf16), vm((3 * width, width), bf16), vm((width, width), bf16),
        ] + [vm(g.shape, bf16) for g in gathered] * 2 + [pltpu.SemaphoreType.DMA((3,)), pltpu.SemaphoreType.DMA((3,))],
        compiler_params=pltpu.CompilerParams(vmem_limit_bytes=VMEM_BYTES),
        name="word_gathered",
    )(pool_sum, cnt, sep, cot, ga, gb, pool_t, *gathered)


GATHER_PLAN = {
    "first": (1, 3, 6, 8),
    "second": (3, 6, 9, 11, 13),
    0: (6, 11, 14, 17, 19),
    1: (9, 14, 17, 20, 22),
    2: (11, 17, 20, 22, 23),
}
SCATTER_PLAN = {
    0: (1, 2, 4, 6, 8),
    1: (2, 5, 7, 9, 11),
    2: (3, 8, 10, 12, 15),
    "second": (8, 11, 13, 15, 17),
    "first": (16, 18, 20, 23),
}


def planned(plan, event, steps):
    when = plan[event]
    return [(at // 8) * steps + (at % 8) * steps // 8 for at in when]


def forward_gather_kernel(
    letters, steps, x_ref, cnt_ref, s_qkv, s_proj, s_gains, s_up, s_down, s_pool, w_qkv, w_proj, w_up, w_down,
    tok_ref, t_ref, o_ref, p_ref, z1_ref, rs1_ref, z2_ref, rs2_ref, m_ref, slope_ref, pool_ref, word0, word1, word2,
    wqkv_t, wqkv, wproj, wup, wdown, pool_t, cga, cgb, wga, wgb,
    first_all, second_all, word_own, wproj_t, wup_t, wdown_t, x_all, z1_all, h1_all,
    first_sems, second_sems, word_sems0, word_sems1, word_sems2, own_sems,
):
    step = pl.program_id(0)
    here = place()
    words = (word0, word1, word2)
    per = LANES * letters // BATCH
    streams = {
        "first": (first_all, first_sems), "second": (second_all, second_sems),
        0: (word0, word_sems0), 1: (word1, word_sems1), 2: (word2, word_sems2),
    }
    own = [pltpu.make_async_copy(word_own.at[n], words[n].at[here], own_sems.at[n]) for n in range(3)]

    def stages_of(name, wanted):
        return (gather_direct if name == "first" else gather_stages)(*streams[name], wanted)

    @pl.when(step == 0)
    def _():
        greet()
        pack_first(first_all.at[here], s_qkv, s_proj, s_gains)
        pack_second(second_all.at[here], s_up, s_down, s_pool)
        pack_words(word_own, w_qkv, w_proj, w_up, w_down)
        start_all(own)

    @pl.when(step == 1)
    def _():
        greeted()

    for name in streams:
        events = planned(GATHER_PLAN, name, steps)
        for n, when in enumerate(events):
            @pl.when(step == when)
            def _():
                if n > 0:
                    arrive_all(stages_of(name, (n - 1,))[n - 1])
                elif name in (0, 1, 2):
                    own[name].wait()
                if n < len(events) - 1:
                    start_all(stages_of(name, (n,))[n])
                elif name == "first":
                    unpack_first(first_all, wqkv_t, wproj_t, wqkv, wproj, cga, cgb, wga, wgb)
                elif name == "second":
                    unpack_second(second_all, wup_t, wdown_t, wup, wdown, pool_t)

    @pl.when(step < steps)
    def _():
        forward_first(step, letters, per, x_ref, cnt_ref, tok_ref, rs1_ref, x_all, z1_all)

    @pl.when((step >= steps) & (step < 2 * steps))
    def _():
        forward_attention(
            step - steps, letters, tok_ref, cga, wqkv_t, wproj_t, t_ref, o_ref, p_ref, z1_ref, x_all, z1_all, h1_all
        )

    @pl.when(step >= 2 * steps)
    def _():
        forward_feed(
            step - 2 * steps, letters, per, cnt_ref, cgb, wup_t, wdown_t, z2_ref, rs2_ref, m_ref, slope_ref, pool_ref, h1_all
        )

    @pl.when(step == 3 * steps - 1)
    def _():
        for name in streams:
            sent_all(stages_of(name, (0, 1, 2, 3)))


def phase_map(phase, steps, per=1):
    return lambda i: jnp.clip(i - phase * steps, 0, steps - 1) // per


def forward_gather(x, cnt, first_shards, second_shards, word_shards, letters):
    tokens, width = x.shape
    steps = tokens // BATCH
    ny, nx, nz = sides()
    nd = 2 * ny * nx
    hidden, outer = second_shards[0].shape[1] * nd, second_shards[2].shape[1] * nd
    r = width // nz
    per = LANES * letters // BATCH
    word_rows, word_lanes = word_shards[2].shape

    def strip(phase, rows, lanes=BATCH, dtype=bf16):
        where = phase_map(phase, steps)
        return (
            jax.ShapeDtypeStruct((steps, rows, lanes), dtype),
            pl.BlockSpec((1, rows, lanes), lambda i: (where(i), 0, 0)),
        )

    def whole(shape, dtype=bf16):
        return (jax.ShapeDtypeStruct(shape, dtype), pl.BlockSpec(shape, lambda i: (0,) * len(shape)))

    pooled = phase_map(2, steps, per)
    gathered = (
        jax.ShapeDtypeStruct((ny, nx, 2, nz, word_rows, word_lanes), bf16), pl.BlockSpec(memory_space=pl.ANY)
    )
    outs = [
        whole((steps, 1, BATCH), jnp.int32), strip(1, 3 * width), strip(1, width), strip(1, CHAR_HEADS // 2 * letters, 2 * BATCH, f32), strip(1, width),
        whole((steps, 1, BATCH), f32), strip(2, width), strip(2, 1, BATCH, f32), strip(2, hidden), strip(2, hidden),
        (
            jax.ShapeDtypeStruct((width, tokens // letters), f32),
            pl.BlockSpec((width, LANES), lambda i: (0, pooled(i))),
        ),
        gathered, gathered, gathered,
        whole((3 * width, width)), whole((width, 3 * width)), whole((width, width)), whole((width, hidden)),
        whole((hidden, width)), whole((outer, width)), whole((width, LANES), f32), whole((width, LANES), f32),
        whole((outer, LANES), f32), whole((outer, LANES), f32),
    ]
    shards = (*first_shards, *second_shards, *word_shards)
    at0 = phase_map(0, steps)
    sems = pltpu.SemaphoreType.DMA((2, gather_copies()))
    return pl.pallas_call(
        functools.partial(forward_gather_kernel, letters, steps),
        grid=(3 * steps,),
        in_specs=[
            pl.BlockSpec((BATCH, width), lambda i: (at0(i), 0)),
            pl.BlockSpec((1, LANES), lambda i: (0, (i % steps) // per)),
        ] + [full_spec(a) for a in shards],
        out_specs=[o[1] for o in outs],
        out_shape=[o[0] for o in outs],
        scratch_shapes=[
            pltpu.VMEM((ny, nx, 2, nz, r + 16, LANES), bf16),
            pltpu.VMEM((ny, nx, 2, nz, 3 * r, LANES), bf16),
            pltpu.VMEM((3, word_rows, word_lanes), bf16),
            pltpu.VMEM((width, width), bf16),
            pltpu.VMEM((hidden, width), bf16),
            pltpu.VMEM((width, hidden), bf16),
            pltpu.VMEM((steps, width, BATCH), bf16),
            pltpu.VMEM((steps, width, BATCH), bf16),
            pltpu.VMEM((steps, width, BATCH), f32),
            pltpu.SemaphoreType.DMA((2, nz - 1 + 2 * ny * nx - 1)), sems, sems, sems, sems,
            pltpu.SemaphoreType.DMA((3,)),
        ],
        compiler_params=pltpu.CompilerParams(
            dimension_semantics=("arbitrary",), vmem_limit_bytes=VMEM_BYTES, collective_id=0, has_side_effects=True
        ),
        name="forward_gather",
    )(x, cnt, *shards)


def backward_scatter_kernel(
    letters, steps, dp_ref, tok_ref, ga_ref, gb_ref, wqkv_t, wqkv, wproj, wup, wdown, send0, send1, send2,
    gpool_t, gwga, gwgb, t_ref, o_ref, p_ref, z1_ref, rs1_ref, z2_ref, rs2_ref, m_ref, slope_ref,
    cg_ref, first_sum, second_sum, word_sum,
    gqkv_t, gproj_t, gup, gdown_t, dh1_all, dt_all, do_ref, du_ref, first_send, second_send, own_sems, *work,
):
    step = pl.program_id(0)
    y, x, c, z = place()
    per = LANES * letters // BATCH
    size = (len(work) - 5) // 4
    work = [work[n * size : (n + 1) * size] for n in range(5)]
    sends = (send0, send1, send2)
    streams = {n: (sends[n], work[n], word_sum.at[n]) for n in range(3)}
    streams["second"] = (second_send, work[3], second_sum)
    streams["first"] = (first_send, work[4], first_sum)
    own = [pltpu.make_async_copy(sends[n].at[:, :, c], work[n][0], own_sems.at[n]) for n in range(3)]

    @pl.when(step == 0)
    def _():
        greet()
        start_all(own)

    @pl.when(step == 1)
    def _():
        greeted()

    for name, (send, scratch, total) in streams.items():
        acc = scratch[0]
        stage, add = (direct_stage, direct_sum) if name == "first" else (scatter_stage, scatter_sum)
        events = planned(SCATTER_PLAN, name, steps)
        for n, when in enumerate(events):
            @pl.when(step == when)
            def _():
                if n == 0:
                    if name == "second":
                        pack_second_grads(second_send, gup, gdown_t, gb_ref, gpool_t)
                    elif name == "first":
                        pack_first_grads(first_send, gqkv_t, gproj_t, ga_ref, wqkv_t, gup, wup, gwga, gwgb)
                else:
                    arrive_all(stage(n - 1, send, scratch))
                    if n == 1 and name in (0, 1, 2):
                        own[name].wait()
                        mine = lambda b, a, k: acc[b, a, k]
                    else:
                        mine = lambda b, a, k: send[b, a, c, k]
                    add(n - 1, mine, scratch, total)
                if n < len(events) - 1:
                    start_all(stage(n, send, scratch))

    @pl.when(step < steps)
    def _():
        backward_feed(
            step, letters, per, dp_ref, tok_ref, gb_ref, wup, wdown, z2_ref, rs2_ref, m_ref, slope_ref,
            gup, gdown_t, dh1_all, du_ref,
        )

    @pl.when((step >= steps) & (step < 2 * steps))
    def _():
        backward_attention(
            step - steps, letters, wproj, t_ref, o_ref, p_ref, z1_ref, gqkv_t, gproj_t, dh1_all, dt_all, do_ref
        )

    @pl.when(step >= 2 * steps)
    def _():
        backward_last(step - 2 * steps, ga_ref, wqkv, z1_ref, rs1_ref, cg_ref, dh1_all, dt_all)

    @pl.when(step == 3 * steps - 1)
    def _():
        for name, (send, scratch, total) in streams.items():
            if name == "first":
                sent_all([direct_stage(n, send, scratch) for n in range(3)])
            else:
                sent_all([scatter_stage(n, send, scratch) for n in range(4)])


def backward_scatter(dp, tok, ga, gb, weights, sends, gpool_t, gwga, gwgb, saved, letters):
    wqkv_t, wqkv, wproj, wup, wdown = weights
    t, o, p, z1, rs1, z2, rs2, m, slope = saved
    steps = t.shape[0]
    width, hidden = wup.shape
    per = LANES * letters // BATCH
    ny, nx, nz = sides()
    r = width // nz
    word_rows, word_lanes = sends[0].shape[4:]
    at = [phase_map(n, steps) for n in range(3)]
    words = phase_map(0, steps, per)

    def strip(a, where):
        return pl.BlockSpec((1,) + a.shape[1:], lambda i: (where(i), 0, 0))

    def whole(shape):
        return (jax.ShapeDtypeStruct(shape, f32), pl.BlockSpec(shape, lambda i: (0,) * len(shape)))

    def once(a):
        return pl.BlockSpec(a.shape, lambda i: (0,) * a.ndim, pipeline_mode=pl.Buffered(1))

    outs = [
        (jax.ShapeDtypeStruct((steps * BATCH, width), bf16), pl.BlockSpec((BATCH, width), lambda i: (at[2](i), 0))),
        whole((r + 16, LANES)), whole((3 * r, LANES)), whole((3, word_rows, word_lanes)),
    ]
    either = lambda i: jnp.where(i < 2 * steps, at[1](i), at[2](i))
    saved_specs = [
        strip(t, at[1]), strip(o, at[1]), strip(p, at[1]), strip(z1, either), strip(rs1, at[2]),
        strip(z2, at[0]), strip(rs2, at[0]), strip(m, at[0]), strip(slope, at[0]),
    ]
    return pl.pallas_call(
        functools.partial(backward_scatter_kernel, letters, steps),
        grid=(3 * steps,),
        in_specs=[
            pl.BlockSpec((width, LANES), lambda i: (0, words(i))),
            pl.BlockSpec((1, 1, BATCH), lambda i: (at[0](i), 0, 0)),
        ] + [once(a) for a in (ga, gb, *weights)] + [pl.BlockSpec(memory_space=pl.ANY)] * 3
        + [once(a) for a in (gpool_t, gwga, gwgb)] + saved_specs,
        out_specs=[o[1] for o in outs],
        out_shape=[o[0] for o in outs],
        scratch_shapes=[
            pltpu.VMEM((3 * width, width), f32),
            pltpu.VMEM((width, width), f32),
            pltpu.VMEM((width, hidden), f32),
            pltpu.VMEM((width, hidden), f32),
            pltpu.VMEM((steps, width, BATCH), bf16),
            pltpu.VMEM((steps, 3 * width, BATCH), bf16),
            pltpu.VMEM((width, BATCH), bf16),
            pltpu.VMEM((hidden, BATCH), bf16),
            pltpu.VMEM((ny, nx, 2, nz, r + 16, LANES), bf16),
            pltpu.VMEM((ny, nx, 2, nz, 3 * r, LANES), bf16),
            pltpu.SemaphoreType.DMA((3,)),
        ] + 3 * scatter_scratch(word_rows, word_lanes) + scatter_scratch(3 * r, LANES) + direct_scratch(r + 16, LANES),
        compiler_params=pltpu.CompilerParams(
            dimension_semantics=("arbitrary",), vmem_limit_bytes=VMEM_BYTES, collective_id=1, has_side_effects=True
        ),
        name="backward_scatter",
    )(dp, tok, ga, gb, *weights, *sends, gpool_t, gwga, gwgb, *saved)


def finish_kernel(
    first, second, words, grad_in, cqkv, cproj_t, cup, cdown_t, cga, cgb, pool, wqkv_t, wproj_t, wup, wdown_t, wga, wgb,
    grad_out,
):
    grad_out[...] = grad_in[...]

    @pl.when(pl.program_id(0) == 0)
    def _():
        r, n, gc, gw = cup.shape[0], cqkv.shape[1], cga.shape[1], wga.shape[1]
        cqkv[...] = first[pl.ds(0, r), :n]
        cproj_t[...] = first[pl.ds(0, r), :].T[n:]
        side = first[pl.ds(r, 8), :]
        cga[...] = side[0:1, :gc]
        cgb[...] = side[0:1, gc : 2 * gc]
        wga[...] = side[0:1, 2 * gc : 2 * gc + gw]
        wgb[...] = side[1:2, :gw]
        cup[...] = second[pl.ds(0, r), :]
        n = cdown_t.shape[0]
        for i in range(cdown_t.shape[1] // LANES):
            cdown_t[:, pl.ds(i * LANES, LANES)] = second[pl.ds(r + i * n, n), :]
        pool[...] = second[pl.ds(2 * r, r), : pool.shape[1]]
        t = words[0].T
        n = wqkv_t.shape[0]
        wqkv_t[...] = t[:n]
        wproj_t[...] = t[n:]
        wup[...] = words[1]
        n, lanes = wdown_t.shape[0], wup.shape[1]
        for i in range(wdown_t.shape[1] // lanes):
            wdown_t[:, pl.ds(i * lanes, lanes)] = words[2, pl.ds(i * n, n), :]


def finish(first, second, words, grad, shapes):
    steps = 8
    moved = pl.BlockSpec((grad.shape[0] // steps, grad.shape[1]), lambda i: (i, 0))
    shapes = [jax.ShapeDtypeStruct(s, f32) for s in shapes]
    return pl.pallas_call(
        finish_kernel,
        grid=(steps,),
        in_specs=[full_spec(a) for a in (first, second, words)] + [moved],
        out_specs=[full_spec(a) for a in shapes] + [moved],
        out_shape=shapes + [jax.ShapeDtypeStruct(grad.shape, grad.dtype)],
        name="finish",
    )(first, second, words, grad)


def gather_all(shards, counts):
    flat = jnp.concatenate([s.reshape(-1) for s in shards])
    packed = lax.all_gather(lax.all_gather(flat, "fsdp", axis=0), "dp", axis=0)
    wide_count, deep_count = packed.shape[:2]
    out, start = [], 0
    for s in shards:
        piece = packed[:, :, start : start + s.size]
        start += s.size
        if s.ndim == 1:
            out.append(piece[:, 0].reshape(-1))
        else:
            r, c = s.shape
            piece = piece.reshape(wide_count, deep_count, r, c).transpose(1, 2, 0, 3)
            out.append(piece.reshape(deep_count * r, wide_count * c))
    return out


def scatter_all(grads, shards):
    wide_count, deep_count = lax.axis_size("dp"), lax.axis_size("fsdp")
    pieces = []
    for g, s in zip(grads, shards):
        g = g.astype(bf16)
        if s.ndim == 1:
            g = jnp.broadcast_to(g.reshape(wide_count, 1, s.size), (wide_count, deep_count, s.size))
        else:
            r, c = s.shape
            g = g.reshape(deep_count, r, wide_count, c).transpose(2, 0, 1, 3)
        pieces.append(g.reshape(wide_count, deep_count, s.size))
    packed = jnp.concatenate(pieces, 2)
    packed = lax.psum_scatter(packed, "dp", scatter_dimension=0, tiled=True)
    packed = lax.psum_scatter(packed, "fsdp", scatter_dimension=1, tiled=True).reshape(-1)
    out, start = [], 0
    for s in shards:
        out.append(packed[start : start + s.size].reshape(s.shape).astype(f32))
        start += s.size
    return out


def shards_plain(
    characters, counts, separators, cotangent, char_qkv, char_proj, char_up, char_down, char_gain_a, char_gain_b,
    pool_proj, word_qkv, word_proj, word_up, word_down, word_gain_a, word_gain_b,
):
    rows, length, letters, width = characters.shape
    char_shards = (char_qkv, char_proj, char_up, char_down, char_gain_a, char_gain_b)
    word_shards = (pool_proj, word_qkv, word_proj, word_up, word_down, word_gain_a, word_gain_b)
    cqkv, cproj, cup, cdown, cga, cgb = gather_all(char_shards, counts)
    wpool, wqkv, wproj, wup, wdown, wga, wgb = gather_all(word_shards, counts)
    x = characters.reshape(length * letters, width)
    tok = jnp.repeat(counts, letters, axis=1).reshape(length * letters // STEP, 1, STEP)
    cga, cgb, wga, wgb = (
        jnp.broadcast_to(g.astype(f32)[:, None], (g.shape[0], LANES)) for g in (cga, cgb, wga, wgb)
    )
    *saved, pool_sum = char_forward(x, tok, counts, cga, cgb, cqkv.T, cproj.T, cup.T, cdown.T, letters)
    word_out, dpool, gpool, gwqkv, gwproj, gwup, gwdown, gwga, gwgb = word_layer(
        pool_sum, counts.astype(f32), separators, cotangent.reshape(length, -1), wga, wgb, wpool, wqkv, wproj, wup, wdown
    )
    word_grads = scatter_all(
        (gpool, gwqkv, gwproj, gwup, gwdown, jnp.sum(gwga, 1), jnp.sum(gwgb, 1)), word_shards
    )
    char_grad, gcqkv, gcproj, gcup, gcdown, gcga, gcgb = char_backward(
        dpool, tok, cga, cgb, cqkv, cproj, cup, cdown, saved, letters
    )
    char_grads = scatter_all(
        (gcqkv, gcproj, gcup, gcdown, jnp.sum(gcga, 1), jnp.sum(gcgb, 1)), char_shards
    )
    return (word_out[None], char_grad.reshape(characters.shape), *char_grads, *word_grads)


def shards_packed(
    characters, counts, separators, cotangent, char_qkv, char_proj, char_up, char_down, char_gain_a, char_gain_b,
    pool_proj, word_qkv, word_proj, word_up, word_down, word_gain_a, word_gain_b,
):
    rows, length, letters, width = characters.shape
    x = characters.reshape(length * letters, width)
    gains = jnp.concatenate([char_gain_a, char_gain_b, word_gain_a, word_gain_b]).astype(f32)
    gains = jnp.pad(gains, (0, 2 * LANES - gains.shape[0])).reshape(2, LANES)
    (
        tok, *saved, pool_sum, word0, word1, word2, wqkv_t, wqkv, wproj, wup, wdown, pool_t, cga, cgb, wga, wgb
    ) = forward_gather(
        x, counts, (char_qkv, char_proj.T, gains), (char_up, char_down.T, pool_proj),
        (word_qkv.T, word_proj.T, word_up, word_down.T), letters,
    )
    shape = word0.shape
    flat = (-1,) + shape[3:]
    word_out, dpool, gpool_t, *sends, gwga, gwgb = word_gathered(
        pool_sum, counts.astype(f32), separators, cotangent.reshape(length, -1), wga, wgb, pool_t,
        *(w.reshape(flat) for w in (word0, word1, word2)),
    )
    char_grad, first, second, words = backward_scatter(
        dpool, tok, cga, cgb, (wqkv_t, wqkv, wproj, wup, wdown), [s.reshape(shape) for s in sends],
        gpool_t, gwga, gwgb, saved, letters,
    )
    shapes = [
        s.shape if s.ndim == 2 else (1, s.shape[0])
        for s in (
            char_qkv, char_proj.T, char_up, char_down.T, char_gain_a, char_gain_b,
            pool_proj, word_qkv.T, word_proj.T, word_up, word_down.T, word_gain_a, word_gain_b,
        )
    ]
    (
        cqkv, cproj_t, cup, cdown_t, cgain_a, cgain_b, pool, gqkv_t, gproj_t, gup, gdown_t, wgain_a, wgain_b, char_grad
    ) = finish(first, second, words, char_grad, shapes)
    return (
        word_out[None], char_grad.reshape(characters.shape), cqkv, cproj_t.T, cup, cdown_t.T, cgain_a[0], cgain_b[0],
        pool, gqkv_t.T, gproj_t.T, gup, gdown_t.T, wgain_a[0], wgain_b[0],
    )


def shards(*arrays):
    char_qkv, char_proj, word_qkv, word_proj = arrays[4], arrays[5], arrays[11], arrays[12]
    tiles = (char_qkv.shape[1] + char_proj.shape[1]) // LANES, (word_qkv.shape[1] + word_proj.shape[1]) // LANES
    return (shards_packed if tiles == (1, 2) else shards_plain)(*arrays)


def solution(mesh):
    rows = ("dp", "fsdp")
    matrix, vector = P("fsdp", "dp"), P("dp")
    data = (P(rows, None, None, None), P(rows, None), P(rows, None), P(rows, None, None))
    block = (matrix,) * 4 + (vector,) * 2
    word = (matrix,) * 5 + (vector,) * 2
    return jax.shard_map(
        shards,
        mesh=mesh,
        in_specs=data + block + word,
        out_specs=(data[3], data[0]) + block + word,
        check_vma=False,
    )
```

```python
import functools
import math

import jax
import jax.numpy as jnp
from jax import lax
from jax.experimental import pallas as pl
from jax.experimental.pallas import tpu as pltpu
from jax.sharding import PartitionSpec as P

CHAR_HEADS = 4
WORD_HEADS = 8
EPS = 1e-05
NEGATIVE = -1e30
LANES = 128
SPAN = 256
STEP = 512
BATCH = 1024
VMEM_BYTES = 60 * 2**20
GELU_A = 0.7978845608028654
GELU_B = 0.044715

bf16 = jnp.bfloat16
f32 = jnp.float32


def dot(a, b):
    return jnp.dot(a, b, preferred_element_type=f32)


def dot_nt(a, b):
    return lax.dot_general(a, b, (((1,), (1,)), ((), ())), preferred_element_type=f32)


def normed(v):
    c = v - jnp.mean(v, 0, keepdims=True)
    rs = lax.rsqrt(jnp.mean(c * c, 0, keepdims=True) + EPS)
    return c * rs, rs


def wide(g, n):
    return g if n == g.shape[1] else jnp.concatenate([g] * (n // g.shape[1]), 1)


def gelu_both(u):
    s = u * u
    t = jnp.tanh(u * (GELU_A + (GELU_A * GELU_B) * s))
    h = 0.5 * u
    r = 0.5 + 0.5 * t
    slope = r + h * (1.0 - t * t) * (GELU_A + (3.0 * GELU_A * GELU_B) * s)
    return u * r, slope


def lane_word(letters):
    return lax.broadcasted_iota(jnp.int32, (letters, LANES), 1) // letters


def pick_own(full, owner, letters):
    words = LANES // letters
    out = full[:letters]
    for w in range(1, words):
        out = jnp.where(owner == w, full[w * letters : (w + 1) * letters], out)
    return out


def own_blocks(letters):
    a = lax.broadcasted_iota(jnp.int32, (LANES, LANES), 0) // letters
    b = lax.broadcasted_iota(jnp.int32, (LANES, LANES), 1) // letters
    return jnp.where(a == b, 1.0, 0.0).astype(bf16)


def spread_own(compact, blocks, letters):
    return jnp.concatenate([compact] * (LANES // letters), 0) * blocks


def char_forward_kernel(
    letters, x_ref, tok_ref, cnt_ref, ga_ref, gb_ref, wqkv_ref, wproj_ref, wup_ref, wdown_ref,
    t_ref, o_ref, p_ref, z1_ref, rs1_ref, z2_ref, rs2_ref, m_ref, gp_ref, pool_ref,
):
    step = pl.program_id(0)
    width = x_ref.shape[1]
    head = width // CHAR_HEADS
    scale = head ** (-0.5)
    steps_per_block = LANES * letters // STEP
    owner = lane_word(letters)
    blocks = own_blocks(letters)
    key_slot = lax.broadcasted_iota(jnp.int32, (letters, LANES), 0)

    @pl.when(step % steps_per_block == 0)
    def _():
        pool_ref[...] = jnp.zeros_like(pool_ref)

    for part in range(STEP // SPAN):
        at = pl.ds(part * SPAN, SPAN)
        x = x_ref[at, :].astype(f32).T
        z1, rs1 = normed(x)
        z1_ref[0, :, at] = z1.astype(bf16)
        rs1_ref[0, :, at] = rs1
        a1 = (z1 * wide(ga_ref[...], SPAN)).astype(bf16)
        for n in range(3):
            rows = pl.ds(n * width, width)
            t_ref[0, rows, at] = dot(wqkv_ref[rows, :], a1).astype(bf16)
        for g in range(SPAN // LANES):
            lanes = pl.ds(part * SPAN + g * LANES, LANES)
            allowed = key_slot < tok_ref[0, :, lanes]
            for h in range(CHAR_HEADS):
                q = t_ref[0, pl.ds(h * head, head), lanes]
                k = t_ref[0, pl.ds(width + h * head, head), lanes]
                v = t_ref[0, pl.ds(2 * width + h * head, head), lanes]
                full = dot(k.T, q)
                s = jnp.where(allowed, pick_own(full, owner, letters) * scale, NEGATIVE)
                e = jnp.exp(s - jnp.max(s, 0, keepdims=True))
                p = e / jnp.sum(e, 0, keepdims=True)
                p_ref[0, pl.ds(h * letters, letters), lanes] = p
                o = dot(v, spread_own(p.astype(bf16), blocks, letters))
                o_ref[0, pl.ds(h * head, head), lanes] = o.astype(bf16)
        h1 = x + dot(wproj_ref[...], o_ref[0, :, at])
        z2, rs2 = normed(h1)
        z2_ref[0, :, at] = z2.astype(bf16)
        rs2_ref[0, :, at] = rs2
        a2 = (z2 * wide(gb_ref[...], SPAN)).astype(bf16)
        for n in range(wup_ref.shape[0] // 256):
            rows = pl.ds(n * 256, 256)
            m, gp = gelu_both(dot(wup_ref[rows, :], a2))
            m_ref[0, rows, at] = m.astype(bf16)
            gp_ref[0, rows, at] = gp.astype(bf16)
        h2 = h1 + dot(wdown_ref[...], m_ref[0, :, at])
        high = h2.astype(bf16)
        low = (h2 - high.astype(f32)).astype(bf16)
        row = lax.broadcasted_iota(jnp.int32, (SPAN, LANES), 0)
        word = lax.broadcasted_iota(jnp.int32, (SPAN, LANES), 1)
        first = (step % steps_per_block) * (STEP // letters) + part * (SPAN // letters)
        mine = (row // letters + first == word) & (row % letters < cnt_ref[...])
        gather = jnp.where(mine, 1.0, 0.0).astype(bf16)
        pool_ref[...] += dot(high, gather) + dot(low, gather)


def full_spec(a):
    nd = len(a.shape)
    return pl.BlockSpec(a.shape, lambda i: (0,) * nd)


def char_forward(x, tok, cnt, ga, gb, wqkv_t, wproj_t, wup_t, wdown_t, letters):
    tokens, width = x.shape
    steps = tokens // STEP
    hidden = wup_t.shape[0]
    per = LANES * letters // STEP

    def strip(rows, dtype=bf16):
        return (
            jax.ShapeDtypeStruct((steps, rows, STEP), dtype),
            pl.BlockSpec((1, rows, STEP), lambda i: (i, 0, 0)),
        )

    outs = [
        strip(3 * width), strip(width), strip(CHAR_HEADS * letters, f32), strip(width), strip(1, f32),
        strip(width), strip(1, f32), strip(hidden), strip(hidden),
        (jax.ShapeDtypeStruct((width, tokens // letters), f32), pl.BlockSpec((width, LANES), lambda i: (0, i // per))),
    ]
    return pl.pallas_call(
        functools.partial(char_forward_kernel, letters),
        grid=(steps,),
        in_specs=[
            pl.BlockSpec((STEP, width), lambda i: (i, 0)),
            pl.BlockSpec((1, 1, STEP), lambda i: (i, 0, 0)),
            pl.BlockSpec((1, LANES), lambda i: (0, i // per)),
        ] + [full_spec(a) for a in (ga, gb, wqkv_t, wproj_t, wup_t, wdown_t)],
        out_specs=[o[1] for o in outs],
        out_shape=[o[0] for o in outs],
        compiler_params=pltpu.CompilerParams(
            dimension_semantics=("arbitrary",), vmem_limit_bytes=56 * 2**20
        ),
        name="char_forward",
    )(x, tok, cnt, ga, gb, wqkv_t, wproj_t, wup_t, wdown_t)


def norm_back(dy, z, rs, gain):
    dz = dy * gain
    a = jnp.mean(dz, 0, keepdims=True)
    b = jnp.mean(dz * z, 0, keepdims=True)
    return rs * (dz - a - z * b)


def fold_lanes(v):
    out = v[:, :LANES]
    for n in range(1, v.shape[1] // LANES):
        out = out + v[:, n * LANES : (n + 1) * LANES]
    return out


def char_backward_kernel(
    letters, dp_ref, tok_ref, ga_ref, gb_ref, wqkv_ref, wproj_ref, wup_ref, wdown_ref,
    t_ref, o_ref, p_ref, z1_ref, rs1_ref, z2_ref, rs2_ref, m_ref, gp_ref,
    cg_ref, gqkv_ref, gproj_ref, gup_ref, gdown_ref, gga_ref, ggb_ref,
    dh2_ref, du_ref, dh1b_ref, do_ref, dt_ref,
):
    step = pl.program_id(0)
    width = cg_ref.shape[1]
    head = width // CHAR_HEADS
    scale = head ** (-0.5)
    steps_per_block = LANES * letters // STEP
    owner = lane_word(letters)
    blocks = own_blocks(letters)

    @pl.when(step == 0)
    def _():
        for ref in (gqkv_ref, gproj_ref, gup_ref, gdown_ref, gga_ref, ggb_ref):
            ref[...] = jnp.zeros_like(ref)

    for part in range(STEP // SPAN):
        at = pl.ds(part * SPAN, SPAN)
        word = lax.broadcasted_iota(jnp.int32, (LANES, SPAN), 0)
        col = lax.broadcasted_iota(jnp.int32, (LANES, SPAN), 1)
        first = (step % steps_per_block) * (STEP // letters) + part * (SPAN // letters)
        mine = (col // letters + first == word) & (col % letters < tok_ref[0, :, at])
        scatter = jnp.where(mine, 1.0, 0.0).astype(bf16)
        dh2 = dot(dp_ref[...], scatter)
        dh2b = dh2.astype(bf16)
        dh2_ref[:, at] = dh2b
        for n in range(wdown_ref.shape[0] // 256):
            rows = pl.ds(n * 256, 256)
            du_ref[rows, at] = (dot(wdown_ref[rows, :], dh2b) * gp_ref[0, rows, at].astype(f32)).astype(bf16)
        dy = dot(wup_ref[...], du_ref[:, at])
        z = z2_ref[0, :, at].astype(f32)
        ggb_ref[...] += fold_lanes(dy * z)
        dh1 = dh2 + norm_back(dy, z, rs2_ref[0, :, at], wide(gb_ref[...], SPAN))
        dh1b = dh1.astype(bf16)
        dh1b_ref[:, at] = dh1b
        do_ref[:, at] = dot(wproj_ref[...], dh1b).astype(bf16)
        for g in range(SPAN // LANES):
            lanes = pl.ds(part * SPAN + g * LANES, LANES)
            for h in range(CHAR_HEADS):
                q_rows = pl.ds(h * head, head)
                k_rows = pl.ds(width + h * head, head)
                v_rows = pl.ds(2 * width + h * head, head)
                q = t_ref[0, q_rows, lanes]
                k = t_ref[0, k_rows, lanes]
                v = t_ref[0, v_rows, lanes]
                do = do_ref[pl.ds(h * head, head), lanes]
                p = p_ref[0, pl.ds(h * letters, letters), lanes]
                dp = pick_own(dot(v.T, do), owner, letters)
                ds = p * (dp - jnp.sum(p * dp, 0, keepdims=True))
                pb = spread_own(p.astype(bf16), blocks, letters)
                dsb = spread_own(ds.astype(bf16), blocks, letters)
                dt_ref[q_rows, lanes] = (dot(k, dsb) * scale).astype(bf16)
                dt_ref[k_rows, lanes] = (dot_nt(q, dsb) * scale).astype(bf16)
                dt_ref[v_rows, lanes] = dot_nt(do, pb).astype(bf16)
        dy = dot(wqkv_ref[...], dt_ref[:, at])
        z = z1_ref[0, :, at].astype(f32)
        gga_ref[...] += fold_lanes(dy * z)
        dx = dh1 + norm_back(dy, z, rs1_ref[0, :, at], wide(ga_ref[...], SPAN))
        cg_ref[at, :] = dx.T.astype(bf16)
    gdown_ref[...] += dot_nt(dh2_ref[...], m_ref[0])
    gup_ref[...] += dot_nt(z2_ref[0], du_ref[...])
    gproj_ref[...] += dot_nt(dh1b_ref[...], o_ref[0])
    gqkv_ref[...] += dot_nt(dt_ref[...], z1_ref[0])

    @pl.when(step == pl.num_programs(0) - 1)
    def _():
        gup_ref[...] = gup_ref[...] * wide(gb_ref[...], gup_ref.shape[1])
        gqkv_ref[...] = gqkv_ref[...] * ga_ref[...].T[:1]


def char_backward(dp, tok, ga, gb, wqkv, wproj, wup, wdown, saved, letters):
    t, o, p, z1, rs1, z2, rs2, m, gp = saved
    steps = t.shape[0]
    width = wqkv.shape[0]
    hidden = wup.shape[1]
    per = LANES * letters // STEP

    def whole(shape):
        return (jax.ShapeDtypeStruct(shape, f32), pl.BlockSpec(shape, lambda i: (0, 0)))

    outs = [
        (jax.ShapeDtypeStruct((steps * STEP, width), bf16), pl.BlockSpec((STEP, width), lambda i: (i, 0))),
        whole((3 * width, width)), whole((width, width)), whole((width, hidden)), whole((width, hidden)),
        whole((width, LANES)), whole((width, LANES)),
    ]
    return pl.pallas_call(
        functools.partial(char_backward_kernel, letters),
        grid=(steps,),
        in_specs=[
            pl.BlockSpec((width, LANES), lambda i: (0, i // per)),
            pl.BlockSpec((1, 1, STEP), lambda i: (i, 0, 0)),
        ] + [full_spec(a) for a in (ga, gb, wqkv, wproj, wup, wdown)]
        + [pl.BlockSpec((1,) + s.shape[1:], lambda i: (i, 0, 0)) for s in saved],
        out_specs=[o[1] for o in outs],
        out_shape=[o[0] for o in outs],
        scratch_shapes=[
            pltpu.VMEM((width, STEP), bf16),
            pltpu.VMEM((hidden, STEP), bf16),
            pltpu.VMEM((width, STEP), bf16),
            pltpu.VMEM((width, STEP), bf16),
            pltpu.VMEM((3 * width, STEP), bf16),
        ],
        compiler_params=pltpu.CompilerParams(
            dimension_semantics=("arbitrary",), vmem_limit_bytes=56 * 2**20
        ),
        name="char_backward",
    )(dp, tok, ga, gb, wqkv, wproj, wup, wdown, *saved)


def word_kernel(
    pool_sum_ref, cnt_ref, sep_ref, cot_ref, ga_ref, gb_ref, wpool_ref, wqkv_ref, wproj_ref, wup_ref, wdown_ref,
    out_ref, dpool_ref, gpool_ref, gqkv_ref, gproj_ref, gup_ref, gdown_ref, gga_ref, ggb_ref,
    pooled, x, z3, rs3, a3, t, p, o, h3, z4, rs4, a4, m, gp, bias, cot, du, dh3, dh3b, do, dt, dtk,
):
    width, length = x.shape
    head = width // WORD_HEADS
    scale = head ** (-0.5)
    halves = [pl.ds(n * SPAN, SPAN) for n in range(length // SPAN)]
    pooled[...] = (pool_sum_ref[...] / cnt_ref[...]).astype(bf16)
    row = lax.broadcasted_iota(jnp.int32, (length, length), 0)
    col = lax.broadcasted_iota(jnp.int32, (length, length), 1)
    tri = jnp.where(row <= col, 1.0, 0.0).astype(bf16)
    sep = jnp.broadcast_to(sep_ref[...].astype(f32).astype(bf16), (16, length))
    doc_q = dot(sep, tri)[:1]
    doc_k = lax.dot_general(tri, sep, (((0,), (1,)), ((), ())), preferred_element_type=f32)[:, :1]
    bias[...] = jnp.where((row <= col) & (doc_k == doc_q), 0.0, NEGATIVE)
    cot[...] = cot_ref[...].astype(f32).T.astype(bf16)
    for at in halves:
        x[:, at] = lax.dot_general(
            wpool_ref[...], pooled[:, at], (((0,), (0,)), ((), ())), preferred_element_type=f32
        )
        z, rs = normed(x[:, at])
        z3[:, at] = z.astype(bf16)
        rs3[:, at] = rs
        a3[:, at] = (z * wide(ga_ref[...], SPAN)).astype(bf16)
        for n in range(3):
            rows = pl.ds(n * width, width)
            t[rows, at] = lax.dot_general(
                wqkv_ref[:, rows], a3[:, at], (((0,), (0,)), ((), ())), preferred_element_type=f32
            ).astype(bf16)
    for h in range(WORD_HEADS):
        k = t[pl.ds(width + h * head, head), :].T
        for n, at in enumerate(halves):
            seen = (n + 1) * SPAN
            keys = pl.ds(0, seen)
            q = t[pl.ds(h * head, head), at]
            s = dot(k[:seen], q) * scale + bias[keys, at]
            e = jnp.exp(s - jnp.max(s, 0, keepdims=True))
            w = e / jnp.sum(e, 0, keepdims=True)
            p[h, keys, at] = w
            o[pl.ds(h * head, head), at] = dot(t[pl.ds(2 * width + h * head, head), keys], w.astype(bf16)).astype(bf16)
    for at in halves:
        h3[:, at] = x[:, at] + lax.dot_general(
            wproj_ref[...], o[:, at], (((0,), (0,)), ((), ())), preferred_element_type=f32
        )
        z, rs = normed(h3[:, at])
        z4[:, at] = z.astype(bf16)
        rs4[:, at] = rs
        a4[:, at] = (z * wide(gb_ref[...], SPAN)).astype(bf16)
        for n in range(wup_ref.shape[1] // 256):
            rows = pl.ds(n * 256, 256)
            mm, gg = gelu_both(
                lax.dot_general(wup_ref[:, rows], a4[:, at], (((0,), (0,)), ((), ())), preferred_element_type=f32)
            )
            m[rows, at] = mm.astype(bf16)
            gp[rows, at] = gg.astype(bf16)
        out = h3[:, at] + lax.dot_general(
            wdown_ref[...], m[:, at], (((0,), (0,)), ((), ())), preferred_element_type=f32
        )
        out_ref[at, :] = out.T.astype(bf16)
        for n in range(wdown_ref.shape[0] // 256):
            rows = pl.ds(n * 256, 256)
            du[rows, at] = (dot(wdown_ref[rows, :], cot[:, at]) * gp[rows, at].astype(f32)).astype(bf16)
        dy = dot(wup_ref[...], du[:, at])
        z = z4[:, at].astype(f32)
        part = fold_lanes(dy * z)
        ggb_ref[...] = part if at is halves[0] else ggb_ref[...] + part
        dh3[:, at] = cot[:, at].astype(f32) + norm_back(dy, z, rs4[:, at], wide(gb_ref[...], SPAN))
        dh3b[:, at] = dh3[:, at].astype(bf16)
        do[:, at] = dot(wproj_ref[...], dh3b[:, at]).astype(bf16)
    gdown_ref[...] = dot_nt(m[...], cot[...]).astype(gdown_ref.dtype)
    gup_ref[...] = dot_nt(a4[...], du[...]).astype(gup_ref.dtype)
    gproj_ref[...] = dot_nt(o[...], dh3b[...]).astype(gproj_ref.dtype)
    for h in range(WORD_HEADS):
        q_rows = pl.ds(h * head, head)
        k_rows = pl.ds(width + h * head, head)
        v_rows = pl.ds(2 * width + h * head, head)
        v = t[v_rows, :].T
        for n in reversed(range(len(halves))):
            at = halves[n]
            seen = (n + 1) * SPAN
            keys = pl.ds(0, seen)
            w = p[h, keys, at]
            g = do[q_rows, at]
            dp = dot(v[:seen], g)
            ds = (w * (dp - jnp.sum(w * dp, 0, keepdims=True))).astype(bf16)
            dt[q_rows, at] = (dot(t[k_rows, keys], ds) * scale).astype(bf16)
            dk = dot_nt(t[q_rows, at], ds) * scale
            dv = dot_nt(g, w.astype(bf16))
            if n == len(halves) - 1:
                dtk[0] = dk
                dtk[1] = dv
            else:
                dtk[0, :, keys] += dk
                dtk[1, :, keys] += dv
        dt[k_rows, :] = dtk[0].astype(bf16)
        dt[v_rows, :] = dtk[1].astype(bf16)
    gqkv_ref[...] = dot_nt(a3[...], dt[...]).astype(gqkv_ref.dtype)
    for at in halves:
        dy = dot(wqkv_ref[...], dt[:, at])
        z = z3[:, at].astype(f32)
        part = fold_lanes(dy * z)
        gga_ref[...] = part if at is halves[0] else gga_ref[...] + part
        dx = dh3[:, at] + norm_back(dy, z, rs3[:, at], wide(ga_ref[...], SPAN))
        dh3b[:, at] = dx.astype(bf16)
        dpool_ref[:, at] = (dot(wpool_ref[...], dh3b[:, at]) / cnt_ref[:, at]).astype(bf16)
    gpool_ref[...] = dot_nt(pooled[...], dh3b[...]).astype(gpool_ref.dtype)


def word_layer(pool_sum, cnt, sep, cot, ga, gb, wpool, wqkv, wproj, wup, wdown, grad_type=f32):
    length, width = cot.shape
    inner = pool_sum.shape[0]
    hidden = wup.shape[1]
    vm = pltpu.VMEM
    return pl.pallas_call(
        word_kernel,
        out_shape=[
            jax.ShapeDtypeStruct((length, width), bf16),
            jax.ShapeDtypeStruct((inner, length), bf16),
            jax.ShapeDtypeStruct(wpool.shape, grad_type),
            jax.ShapeDtypeStruct(wqkv.shape, grad_type),
            jax.ShapeDtypeStruct(wproj.shape, grad_type),
            jax.ShapeDtypeStruct(wup.shape, grad_type),
            jax.ShapeDtypeStruct(wdown.shape, grad_type),
            jax.ShapeDtypeStruct((width, LANES), f32),
            jax.ShapeDtypeStruct((width, LANES), f32),
        ],
        scratch_shapes=[
            vm((inner, length), bf16), vm((width, length), f32), vm((width, length), bf16), vm((1, length), f32),
            vm((width, length), bf16), vm((3 * width, length), bf16), vm((WORD_HEADS, length, length), f32),
            vm((width, length), bf16), vm((width, length), f32), vm((width, length), bf16), vm((1, length), f32),
            vm((width, length), bf16), vm((hidden, length), bf16), vm((hidden, length), bf16),
            vm((length, length), f32), vm((width, length), bf16), vm((hidden, length), bf16),
            vm((width, length), f32), vm((width, length), bf16), vm((width, length), bf16),
            vm((3 * width, length), bf16), vm((2, width // WORD_HEADS, length), f32),
        ],
        compiler_params=pltpu.CompilerParams(vmem_limit_bytes=58 * 2**20),
        name="word_layer",
    )(pool_sum, cnt, sep, cot, ga, gb, wpool, wqkv, wproj, wup, wdown)


MESH = pl.DeviceIdType.MESH


def sides():
    chips = lax.axis_size("dp") // 2
    nx = math.isqrt(chips)
    return chips // nx, nx, lax.axis_size("fsdp")


def place():
    ny, nx, nz = sides()
    me = lax.axis_index("dp")
    return me // (2 * nx), (me // 2) % nx, me % 2, lax.axis_index("fsdp")


def device(y, x, c, z):
    return {"dp": (y * sides()[1] + x) * 2 + c, "fsdp": z}


def others():
    ny, nx, nz = sides()
    y, x, c, z = place()
    return [((y + j) % ny, (x + i) % nx) for j in range(ny) for i in range(nx) if j + i > 0]


def partners():
    ny, nx, nz = sides()
    y, x, c, z = place()
    found = [device(y, x, 1 - c, z)]
    found += [device(y, x, c, (z + k) % nz) for k in range(1, nz)]
    return found + [device(j, i, c, z) for j, i in others()]


def greet():
    barrier = pltpu.get_barrier_semaphore()
    for other in partners():
        pl.semaphore_signal(barrier, inc=1, device_id=other, device_id_type=MESH)


def greeted():
    pl.semaphore_wait(pltpu.get_barrier_semaphore(), len(partners()))


def remote(src, dst, sems, n, other):
    return pltpu.make_async_remote_copy(
        src_ref=src, dst_ref=dst, send_sem=sems.at[0, n], recv_sem=sems.at[1, n],
        device_id=other, device_id_type=MESH,
    )


def gather_copies():
    ny, nx, nz = sides()
    return nz - 1 + 1 + 4 * (nx - 1) + 4 * (ny - 1)


def gather_stages(ref, sems, wanted=(0, 1, 2, 3)):
    ny, nx, nz = sides()
    y, x, c, z = place()
    every = slice(None)
    half = ref.shape[4] // 2
    low, high = pl.ds(0, half), pl.ds(half, half)
    twin = device(y, x, 1 - c, z)
    plan = [[], [], [], []]
    plan[0] += [((y, x, c, z), device(y, x, c, (z + k) % nz)) for k in range(1, nz)]
    plan[1] += [((y, x, c, every, low), device(y, (x + k) % nx, c, z)) for k in range(1, nx)]
    plan[1] += [((y, x, c, every, high), device((y + k) % ny, x, c, z)) for k in range(1, ny)]
    plan[1] += [((y, x, c), twin)]
    plan[2] += [((y, every, c, every, low), device((y + k) % ny, x, c, z)) for k in range(1, ny)]
    plan[2] += [((every, x, c, every, high), device(y, (x + k) % nx, c, z)) for k in range(1, nx)]
    plan[2] += [((y, (x + k) % nx, c, every, low), twin) for k in range(1, nx)]
    plan[2] += [(((y + k) % ny, x, c, every, high), twin) for k in range(1, ny)]
    plan[3] += [(((y + k) % ny, every, c, every, low), twin) for k in range(1, ny)]
    plan[3] += [((every, (x + k) % nx, c, every, high), twin) for k in range(1, nx)]
    count = 0
    stages = []
    for n, part in enumerate(plan):
        copies = []
        for where, other in part:
            if n in wanted:
                copies.append(remote(ref.at[where], ref.at[where], sems, count, other))
            count += 1
        stages.append(copies)
    return stages


def gather_direct(ref, sems, wanted=(0, 1, 2)):
    ny, nx, nz = sides()
    y, x, c, z = place()
    twin = device(y, x, 1 - c, z)
    plan = [[((y, x, c, z), device(y, x, c, (z + k) % nz)) for k in range(1, nz)]]
    plan += [[((y, x, c), device(j, i, c, z)) for j, i in others()] + [((y, x, c), twin)]]
    plan += [[((j, i, c), twin) for j, i in others()]]
    count, stages = 0, []
    for n, part in enumerate(plan):
        copies = []
        for where, other in part:
            if n in wanted:
                copies.append(remote(ref.at[where], ref.at[where], sems, count, other))
            count += 1
        stages.append(copies)
    return stages


def start_all(copies):
    for copy in copies:
        copy.start()


def arrive_all(copies):
    for copy in copies:
        copy.wait_recv()


def sent_all(stages):
    for copies in stages:
        for copy in copies:
            copy.wait_send()


def lanes_to(v, n):
    return v if v.shape[1] == n else jnp.concatenate([v, jnp.zeros((v.shape[0], n - v.shape[1]), v.dtype)], 1)


def turned(v):
    return v.astype(f32).T.astype(bf16)


def scatter_copies():
    ny, nx, nz = sides()
    return 1 + 2 * (nx - 1) + 2 * (ny - 1) + nz - 1


def scatter_scratch(rows, lanes):
    ny, nx, nz = sides()
    half = rows // 2
    shapes = (
        (ny, nx, nz, rows, lanes), (ny, nx, nz, rows, lanes), (nx - 1, ny, nz, half, lanes),
        (ny - 1, nx, nz, half, lanes), (ny - 1, nz, half, lanes), (nx - 1, nz, half, lanes), (nz - 1, rows, lanes),
    )
    return [pltpu.VMEM(shape, bf16) for shape in shapes] + [pltpu.SemaphoreType.DMA((2, scatter_copies()))]


def scatter_stage(n, send, work):
    acc, twin_in, one_low, one_high, two_low, two_high, last_in, sems = work
    ny, nx, nz = sides()
    y, x, c, z = place()
    half = acc.shape[3] // 2
    low, high, every = pl.ds(0, half), pl.ds(half, half), slice(None)
    plan = [[], [], [], []]
    plan[0] += [(send, (every, every, 1 - c), twin_in, device(y, x, 1 - c, z))]
    plan[1] += [
        (acc, (every, (x + k) % nx, every, low), one_low.at[k - 1], device(y, (x + k) % nx, c, z)) for k in range(1, nx)
    ]
    plan[1] += [
        (acc, ((y + k) % ny, every, every, high), one_high.at[k - 1], device((y + k) % ny, x, c, z)) for k in range(1, ny)
    ]
    plan[2] += [
        (acc, ((y + k) % ny, x, every, low), two_low.at[k - 1], device((y + k) % ny, x, c, z)) for k in range(1, ny)
    ]
    plan[2] += [
        (acc, (y, (x + k) % nx, every, high), two_high.at[k - 1], device(y, (x + k) % nx, c, z)) for k in range(1, nx)
    ]
    plan[3] += [(acc, (y, x, (z + k) % nz), last_in.at[k - 1], device(y, x, c, (z + k) % nz)) for k in range(1, nz)]
    first = sum(len(p) for p in plan[:n])
    return [remote(src.at[at], dst, sems, first + i, other) for i, (src, at, dst, other) in enumerate(plan[n])]


def direct_scratch(rows, lanes):
    ny, nx, nz = sides()
    shapes = (
        (ny, nx, nz, rows, lanes), (ny, nx, nz, rows, lanes), (ny * nx - 1, nz, rows, lanes), (nz - 1, rows, lanes)
    )
    count = 1 + ny * nx - 1 + nz - 1
    return [pltpu.VMEM(shape, bf16) for shape in shapes] + [pltpu.SemaphoreType.DMA((2, count))]


def direct_stage(n, send, work):
    acc, twin_in, near_in, last_in, sems = work
    ny, nx, nz = sides()
    y, x, c, z = place()
    if n == 0:
        return [remote(send.at[:, :, 1 - c], twin_in, sems, 0, device(y, x, 1 - c, z))]
    if n == 1:
        return [
            remote(acc.at[j, i], near_in.at[k], sems, 1 + k, device(j, i, c, z)) for k, (j, i) in enumerate(others())
        ]
    return [
        remote(acc.at[y, x, (z + k) % nz], last_in.at[k - 1], sems, ny * nx + k - 1, device(y, x, c, (z + k) % nz))
        for k in range(1, nz)
    ]


def direct_sum(n, own, work, out):
    acc, twin_in, near_in, last_in, sems = work
    ny, nx, nz = sides()
    y, x, c, z = place()
    if n == 0:
        for b in range(ny):
            for a in range(nx):
                for k in range(nz):
                    acc[b, a, k] = own(b, a, k) + twin_in[b, a, k]
    elif n == 1:
        for k in range(nz):
            total = acc[y, x, k].astype(f32) + sum(near_in[i, k].astype(f32) for i in range(ny * nx - 1))
            acc[y, x, k] = total.astype(bf16)
    else:
        out[...] = acc[y, x, z].astype(f32) + sum(last_in[i].astype(f32) for i in range(nz - 1))


def scatter_sum(n, own, work, out):
    acc, twin_in, one_low, one_high, two_low, two_high, last_in, sems = work
    ny, nx, nz = sides()
    y, x, c, z = place()
    half = acc.shape[3] // 2
    low, high = pl.ds(0, half), pl.ds(half, half)
    if n == 0:
        for b in range(ny):
            for a in range(nx):
                for k in range(nz):
                    acc[b, a, k] = own(b, a, k) + twin_in[b, a, k]
    elif n == 1:
        for k in range(nz):
            for b in range(ny):
                acc[b, x, k, low] += sum(one_low[i, b, k] for i in range(nx - 1))
            for a in range(nx):
                acc[y, a, k, high] += sum(one_high[i, a, k] for i in range(ny - 1))
    elif n == 2:
        for k in range(nz):
            acc[y, x, k, low] += sum(two_low[i, k] for i in range(ny - 1))
            acc[y, x, k, high] += sum(two_high[i, k] for i in range(nx - 1))
    else:
        out[...] = acc[y, x, z].astype(f32) + sum(last_in[i].astype(f32) for i in range(nz - 1))


def gelu_twice(u):
    s = u * u
    t = jnp.tanh(u * (GELU_A + (GELU_A * GELU_B) * s))
    a = 1.0 + t
    m = u * a
    return m, a + m * ((1.0 - t) * (GELU_A + (3.0 * GELU_A * GELU_B) * s))


def shift_of(letters):
    return letters.bit_length() - 1


def twin_owner(letters):
    lane = lax.broadcasted_iota(jnp.int32, (letters, 2 * LANES), 1)
    return lax.shift_right_logical(lane & (LANES - 1), shift_of(letters))


def twin_mask(letters):
    bits = shift_of(letters)
    a = lax.shift_right_logical(lax.broadcasted_iota(jnp.int32, (LANES, 2 * LANES), 0), bits)
    b = lax.shift_right_logical(lax.broadcasted_iota(jnp.int32, (LANES, 2 * LANES), 1) & (LANES - 1), bits)
    return jnp.where(a == b, 1.0, 0.0).astype(bf16)


def twin_blocks(v):
    half = v.shape[0] // 2
    none = jnp.zeros((half, v.shape[1]), v.dtype)
    return jnp.concatenate([jnp.concatenate([v[:half], none], 1), jnp.concatenate([none, v[half:]], 1)], 0)


def stacked(v):
    return jnp.concatenate([v[:, :LANES], v[:, LANES:]], 0)


def char_units():
    for g in range(BATCH // LANES):
        for h in range(CHAR_HEADS // 2):
            yield h, pl.ds(g * LANES, LANES), pl.ds(2 * g * LANES, 2 * LANES)


def patterns(near, far, letters):
    words, tokens = near.shape
    bits = shift_of(letters)
    word = lax.broadcasted_iota(jnp.int32, (words, tokens), 0)
    token = lax.shift_right_logical(lax.broadcasted_iota(jnp.int32, (words, tokens), 1), bits)
    near[...] = jnp.where(word == token, 1.0, 0.0).astype(bf16)
    if far is not None:
        token = lax.shift_right_logical(lax.broadcasted_iota(jnp.int32, far.shape, 0), bits)
        word = lax.broadcasted_iota(jnp.int32, far.shape, 1)
        far[...] = jnp.where(word == token, 1.0, 0.0).astype(bf16)


def own_words(s, per, v):
    words = LANES // per
    out = v[:, :words]
    for i in range(1, per):
        out = jnp.where(s % per == i, v[:, i * words : (i + 1) * words], out)
    return out


def valid_tokens(letters, counts):
    slot = lax.broadcasted_iota(jnp.int32, counts.shape, 1) & (letters - 1)
    return jnp.where(slot < counts, 1.0, 0.0)


def forward_first(s, per, x_ref, cnt_ref, tok_ref, rs1_ref, x_all, z1_all, near):
    counts = jnp.broadcast_to(own_words(s, per, cnt_ref[...].astype(f32)), (16, near.shape[0])).astype(bf16)
    tok_ref[s] = dot(counts, near[...])[:1].astype(jnp.int32)
    x = x_ref[...].astype(f32).T
    x_all[s] = x.astype(bf16)
    z1, rs1 = normed(x)
    z1_all[s] = z1.astype(bf16)
    rs1_ref[s] = rs1


def forward_attention(s, letters, tok_ref, ga_ref, wqkv_t, wproj_t, t_ref, o_ref, p_ref, z1_ref, x_all, z1_all, h1_all, j):
    width = o_ref.shape[1]
    pair = 2 * (width // CHAR_HEADS)
    scale = (width // CHAR_HEADS) ** (-0.5)
    owner, blocks = twin_owner(letters), twin_mask(letters)
    key_slot = lax.broadcasted_iota(jnp.int32, (letters, 2 * LANES), 0)
    z1 = z1_all[s]
    z1_ref[j] = z1
    a1 = (z1.astype(f32) * wide(ga_ref[...], BATCH)).astype(bf16)
    t_ref[j] = dot(wqkv_t[...], a1).astype(bf16)
    units = list(char_units())
    scores = []
    for h, lanes, lanes2 in units:
        q = twin_blocks(t_ref[j, pl.ds(h * pair, pair), lanes])
        k = t_ref[j, pl.ds(width + h * pair, pair), lanes].T
        scores.append(pick_own(dot(k, q), owner, letters))
    probs = []
    for (h, lanes, lanes2), score in zip(units, scores):
        counts = tok_ref[s, :, lanes]
        allowed = key_slot < jnp.concatenate([counts, counts], 1)
        score = jnp.where(allowed, score * scale, NEGATIVE)
        e = jnp.exp(score - jnp.max(score, 0, keepdims=True))
        p = e / jnp.sum(e, 0, keepdims=True)
        p_ref[j, pl.ds(h * letters, letters), lanes2] = p
        probs.append(p)
    for (h, lanes, lanes2), p in zip(units, probs):
        v = twin_blocks(t_ref[j, pl.ds(2 * width + h * pair, pair), lanes])
        o = dot(v, stacked(spread_own(p.astype(bf16), blocks, letters)))
        o_ref[j, pl.ds(h * pair, pair), lanes] = o.astype(bf16)
    h1_all[s] = x_all[s].astype(f32) + dot(wproj_t[...], o_ref[j])


def forward_feed(
    s, letters, per, tok_ref, gb_ref, wup_t, wdown_t, z2_ref, rs2_ref, m_ref, slope_ref, pool_ref, h1_all, far, a2_ref
):
    z2, rs2 = normed(h1_all[s])
    z2_ref[0] = z2.astype(bf16)
    rs2_ref[0] = rs2
    a2_ref[...] = (z2 * wide(gb_ref[...], BATCH)).astype(bf16)
    valid = valid_tokens(letters, tok_ref[s])
    strips = [
        (pl.ds(at, SPAN), pl.ds(n * 256, 256)) for at in range(0, BATCH, SPAN) for n in range(wup_t.shape[0] // 256)
    ]

    def close(cols):
        h2 = h1_all[s, :, cols] + dot(wdown_t[...], m_ref[0, :, cols])
        kept = (h2 * valid[:, cols.start : cols.start + cols.size]).astype(bf16)
        return dot(kept, far[cols, :])

    part = 0.0
    ahead = dot(wup_t[strips[0][1], :], a2_ref[:, strips[0][0]])
    for i, (cols, rows) in enumerate(strips):
        u = ahead
        if i + 1 < len(strips):
            ahead = dot(wup_t[strips[i + 1][1], :], a2_ref[:, strips[i + 1][0]])
        if rows.start == 0 and cols.start > 0:
            part += close(pl.ds(cols.start - SPAN, SPAN))
        m, slope = gelu_twice(u)
        m_ref[0, rows, cols] = m.astype(bf16)
        slope_ref[0, rows, cols] = slope.astype(bf16)
    part += close(pl.ds(BATCH - SPAN, SPAN))
    words = LANES // per
    for i in range(per):
        moved = part if i == 0 else pltpu.roll(part, i * words, 1)

        @pl.when(s % per == i)
        def _():
            pool_ref[...] = moved if i == 0 else pool_ref[...] + moved


def backward_feed(
    s, letters, per, dp_ref, tok_ref, gb_ref, wup, wdown, z2_ref, rs2_ref, m_ref, slope_ref, gup, gdown_t, dh1_all, spare
):
    deep = spare.shape[1]
    word = lax.broadcasted_iota(jnp.int32, (LANES, BATCH), 0) - (s % per) * (BATCH // letters)
    token = lax.broadcasted_iota(jnp.int32, (LANES, BATCH), 1)
    mine = lax.shift_right_logical(token, shift_of(letters)) == word
    scatter = jnp.where(mine & ((token & (letters - 1)) < tok_ref[0]), 1.0, 0.0).astype(bf16)
    dh2 = dot(dp_ref[...], scatter)
    dh2b = dh2.astype(bf16)
    for n in range(wdown.shape[0] // 256):
        rows = pl.ds(n * 256, 256)
        du = (dot(wdown[rows, :], dh2b) * slope_ref[0, rows, :].astype(f32)).astype(bf16)
        spare[n * 256 // deep, pl.ds(n * 256 % deep, 256), :] = du
    pieces = []
    for n in range(0, wdown.shape[0], deep):
        size = min(deep, wdown.shape[0] - n)
        pieces.append((pl.ds(n, size), (n // deep, pl.ds(0, size))))
    dy = sum(dot(wup[:, cols], spare[at]) for cols, at in pieces)
    z = z2_ref[0].astype(f32)
    dh1 = dh2 + norm_back(dy, z, rs2_ref[0], wide(gb_ref[...], BATCH))
    dh1_all[s] = dh1.astype(bf16)

    @pl.when(s == 0)
    def _():
        gdown_t[...] = jnp.zeros_like(gdown_t)
        gup[...] = jnp.zeros_like(gup)

    gdown_t[...] += dot_nt(dh2b, m_ref[0])
    for cols, at in pieces:
        gup[:, cols] += dot_nt(z2_ref[0], spare[at])


def backward_attention(s, letters, wproj, t_ref, o_ref, p_ref, z1_ref, gqkv_t, gproj_t, dh1_all, dt_all, do_ref, j):
    width = wproj.shape[0]
    pair = 2 * (width // CHAR_HEADS)
    scale = (width // CHAR_HEADS) ** (-0.5)
    owner, blocks = twin_owner(letters), twin_mask(letters)
    dh1b = dh1_all[s]
    do_ref[...] = dot(wproj[...], dh1b).astype(bf16)
    units = list(char_units())
    grads = []
    for h, lanes, lanes2 in units:
        v = t_ref[j, pl.ds(2 * width + h * pair, pair), lanes].T
        grads.append(pick_own(dot(v, twin_blocks(do_ref[pl.ds(h * pair, pair), lanes])), owner, letters))
    spread = []
    for (h, lanes, lanes2), dp in zip(units, grads):
        p = p_ref[j, pl.ds(h * letters, letters), lanes2]
        ds = p * (dp - jnp.sum(p * dp, 0, keepdims=True))
        spread.append((spread_own(p.astype(bf16), blocks, letters), spread_own(ds.astype(bf16), blocks, letters)))
    for (h, lanes, lanes2), (pb, dsb) in zip(units, spread):
        q_rows = pl.ds(h * pair, pair)
        k_rows = pl.ds(width + h * pair, pair)
        v_rows = pl.ds(2 * width + h * pair, pair)
        q = twin_blocks(t_ref[j, q_rows, lanes])
        k = twin_blocks(t_ref[j, k_rows, lanes])
        do = twin_blocks(do_ref[q_rows, lanes])
        dt_all[s, q_rows, lanes] = (dot(k, stacked(dsb)) * scale).astype(bf16)
        dt_all[s, k_rows, lanes] = (dot_nt(q, dsb) * scale).astype(bf16)
        dt_all[s, v_rows, lanes] = dot_nt(do, pb).astype(bf16)

    @pl.when(s == 0)
    def _():
        gproj_t[...] = jnp.zeros_like(gproj_t)
        gqkv_t[...] = jnp.zeros_like(gqkv_t)

    gproj_t[...] += dot_nt(dh1b, o_ref[j])
    gqkv_t[...] += dot_nt(dt_all[s], z1_ref[j])


def backward_last(s, ga_ref, wqkv, z1_ref, rs1_ref, cg_ref, dh1_all, dt_all, j):
    dy = dot(wqkv[...], dt_all[s])
    z = z1_ref[j].astype(f32)
    dx = dh1_all[s].astype(f32) + norm_back(dy, z, rs1_ref[j], wide(ga_ref[...], BATCH))
    cg_ref[pl.ds(j * BATCH, BATCH), :] = dx.T.astype(bf16)


def pack_first(slot, qkv, proj_t, gains):
    r = qkv.shape[0]
    slot[pl.ds(0, r), :] = jnp.concatenate([qkv[...], turned(lanes_to(proj_t[...], LANES))[:r]], 1)
    none = jnp.zeros((slot.shape[0] - r - gains.shape[0], LANES), f32)
    slot[pl.ds(r, slot.shape[0] - r), :] = jnp.concatenate([gains[...], none], 0).astype(bf16)


def pack_second(slot, up, down_t, pool):
    r, n = up.shape[0], down_t.shape[0]
    slot[pl.ds(0, r), :] = up[...]
    for i in range(down_t.shape[1] // LANES):
        slot[pl.ds(r + i * n, n), :] = down_t[:, pl.ds(i * LANES, LANES)]
    slot[pl.ds(2 * r, r), :] = lanes_to(pool[...], LANES)


def pack_words(slots, qkv_t, proj_t, up, down_t):
    slots[0] = turned(jnp.concatenate([qkv_t[...], proj_t[...]], 0))
    slots[1] = up[...]
    n, lanes = down_t.shape[0], up.shape[1]
    for i in range(down_t.shape[1] // lanes):
        slots[2, pl.ds(i * n, n), :] = down_t[:, pl.ds(i * lanes, lanes)]


def seats():
    ny, nx, nz = sides()
    for d in range(2 * ny * nx):
        yield d, (d // (2 * nx), (d // 2) % nx, d % 2)


def unpack_first(ref, wqkv_t, wproj_t, wqkv, wproj, cga, cgb, wga, wgb):
    ny, nx, nz = sides()
    nd = 2 * ny * nx
    r = wqkv.shape[0] // nz
    a, b, gc, gw = wqkv_t.shape[0] // nd, wproj_t.shape[0] // nd, cga.shape[0] // nd, wga.shape[0] // nd
    for d, at in seats():
        t = turned(ref[at + (slice(None), pl.ds(0, r))].reshape(nz * r, LANES))
        wqkv_t[pl.ds(d * a, a), :] = t[:a]
        wproj_t[pl.ds(d * b, b), :] = t[a:]
        g = ref[at + (0, pl.ds(r, 16))].astype(f32).T
        one, two = (jnp.broadcast_to(g[:, i : i + 1], (LANES, LANES)) for i in range(2))
        cga[pl.ds(d * gc, gc), :] = one[:gc]
        cgb[pl.ds(d * gc, gc), :] = one[gc : 2 * gc]
        wga[pl.ds(d * gw, gw), :] = one[2 * gc : 2 * gc + gw]
        wgb[pl.ds(d * gw, gw), :] = two[:gw]
    wqkv[...] = turned(wqkv_t[...])
    wproj[...] = turned(wproj_t[...])


def unpack_second(ref, wup_t, wdown_t, wup, wdown, pool_t):
    ny, nx, nz = sides()
    nd = 2 * ny * nx
    r, n, p = wup.shape[0] // nz, wdown_t.shape[0] // nd, pool_t.shape[0] // nd
    deep = wdown_t.shape[1] // nz
    for d, at in seats():
        up = ref[at + (slice(None), pl.ds(0, r))].reshape(nz * r, LANES)
        wup[:, pl.ds(d * LANES, LANES)] = up
        wup_t[pl.ds(d * LANES, LANES), :] = turned(up)
        for z in range(nz):
            for i in range(deep // LANES):
                wdown_t[pl.ds(d * n, n), pl.ds(z * deep + i * LANES, LANES)] = ref[at + (z, pl.ds(r + i * n, n))] * 0.5
        t = turned(ref[at + (slice(None), pl.ds(2 * r, r))].reshape(nz * r, LANES))
        pool_t[pl.ds(d * p, p), :] = t[:p]
    wdown[...] = turned(wdown_t[...])


def pack_first_grads(slots, gqkv_t, gproj_t, ga, wqkv_t, gup, wup, gwga, gwgb):
    ny, nx, nz = sides()
    nd = 2 * ny * nx
    width = gqkv_t.shape[1]
    r = width // nz
    tail = slots.shape[4] - r
    a, b, gc, gw = gqkv_t.shape[0] // nd, gproj_t.shape[0] // nd, width // nd, gwga.shape[1] // nd
    char_a = jnp.sum(gqkv_t[...] * wqkv_t[...].astype(f32), 0, keepdims=True)
    char_a = jnp.broadcast_to(char_a, (8, width)).T[:, :1]
    char_b = jnp.sum(gup[...] * wup[...].astype(f32), 1, keepdims=True)
    word_a, word_b = (g[...].T[:, :1] for g in (gwga, gwgb))
    gain = ga[...].T[:1]
    spot = lax.broadcasted_iota(jnp.int32, (LANES, nz * tail), 1) % tail
    none = jnp.zeros((LANES - gw, 1), f32)
    for d, at in seats():
        t = jnp.concatenate([gqkv_t[pl.ds(d * a, a), :] * gain, gproj_t[pl.ds(d * b, b), :]], 0)
        slots[at + (slice(None), pl.ds(0, r))] = t.T.astype(bf16).reshape(nz, r, LANES)
        char, word = slice(d * gc, (d + 1) * gc), slice(d * gw, (d + 1) * gw)
        one = jnp.concatenate([char_a[char], char_b[char], word_a[word]], 0)
        two = jnp.concatenate([word_b[word], none], 0)
        side = jnp.where(spot == 0, one, jnp.where(spot == 1, two, 0.0))
        slots[at + (slice(None), pl.ds(r, tail))] = side.T.astype(bf16).reshape(nz, tail, LANES)


def pack_second_grads(slots, gup, gdown_t, gb, gpool_t):
    ny, nx, nz = sides()
    nd = 2 * ny * nx
    width = gup.shape[0]
    r, n, p = width // nz, gdown_t.shape[0] // nd, gpool_t.shape[0] // nd
    deep = gdown_t.shape[1] // nz
    none = jnp.zeros((LANES - p, width), f32)
    for d, at in seats():
        up = gup[:, pl.ds(d * LANES, LANES)] * gb[...]
        slots[at + (slice(None), pl.ds(0, r))] = up.astype(bf16).reshape(nz, r, LANES)
        for z in range(nz):
            for i in range(deep // LANES):
                down = gdown_t[pl.ds(d * n, n), pl.ds(z * deep + i * LANES, LANES)] * 0.5
                slots[at + (z, pl.ds(r + i * n, n))] = down.astype(bf16)
        t = jnp.concatenate([gpool_t[pl.ds(d * p, p), :].astype(f32), none], 0)
        slots[at + (slice(None), pl.ds(2 * r, r))] = t.T.astype(bf16).reshape(nz, r, LANES)


def unpack_mixed(ref, qkv_t, proj_t):
    nd, nz, r, lanes = ref.shape
    a, b = qkv_t.shape[0] // nd, proj_t.shape[0] // nd
    for d in range(nd):
        t = turned(ref[d].reshape(nz * r, lanes))
        qkv_t[pl.ds(d * a, a), :] = t[:a]
        proj_t[pl.ds(d * b, b), :] = t[a:]


def unpack_up(ref, up_t, up):
    nd, nz, r, lanes = ref.shape
    for d in range(nd):
        piece = ref[d].reshape(nz * r, lanes)
        up[:, pl.ds(d * lanes, lanes)] = piece
        up_t[pl.ds(d * lanes, lanes), :] = turned(piece)


def unpack_down(ref, down_t):
    nd, nz, r, lanes = ref.shape
    n, deep = down_t.shape[0] // nd, down_t.shape[1] // nz
    for d in range(nd):
        for z in range(nz):
            for i in range(deep // lanes):
                down_t[pl.ds(d * n, n), pl.ds(z * deep + i * lanes, lanes)] = ref[d, z, pl.ds(i * n, n), :] * 0.5


def word_gathered_kernel(
    pool_sum_ref, cnt_ref, sep_ref, cot_ref, ga_ref, gb_ref, wpool_t, far0, far1, far2,
    out_ref, dpool_ref, gpool_ref, gone0, gone1, gone2, gga_ref, ggb_ref,
    pooled, x, z3, rs3, a3, t, p, o, h3, z4, rs4, a4, m, slope, bias, cot, du, dh3, dh3b, do, dt, dtk,
    wqkv_t, wproj_t, wup_t, wdown_t, wqkv, wproj, wup, wdown, wpool, gqkv_t, gproj_t,
    all0, all1, all2, send0, send1, send2, in_sems, out_sems,
):
    width, length = x.shape
    head = width // WORD_HEADS
    scale = head ** (-0.5)
    nd, nz, r, lanes = send0.shape
    halves = [pl.ds(n * SPAN, SPAN) for n in range(length // SPAN)]
    fetch = [pltpu.make_async_copy(a, b, in_sems.at[n]) for n, (a, b) in enumerate(((far0, all0), (far1, all1), (far2, all2)))]
    leave = [pltpu.make_async_copy(a, b, out_sems.at[n]) for n, (a, b) in enumerate(((send0, gone0), (send1, gone1), (send2, gone2)))]
    start_all(fetch)
    counts = cnt_ref[...].astype(f32)
    pooled[...] = (pool_sum_ref[...] / counts).astype(bf16)
    row = lax.broadcasted_iota(jnp.int32, (length, length), 0)
    col = lax.broadcasted_iota(jnp.int32, (length, length), 1)
    tri = jnp.where(row <= col, 1.0, 0.0).astype(bf16)
    sep = jnp.broadcast_to(sep_ref[...].astype(f32).astype(bf16), (16, length))
    doc_q = dot(sep, tri)[:1]
    doc_k = jnp.broadcast_to(doc_q, (8, length)).T[:, :1]
    bias[...] = jnp.where((row <= col) & (doc_k == doc_q), 0.0, NEGATIVE)
    cot[...] = turned(cot_ref[...])
    x[...] = dot(wpool_t[...], pooled[...])
    z, rs = normed(x[...])
    z3[...] = z.astype(bf16)
    rs3[...] = rs
    a3[...] = (z * wide(ga_ref[...], length)).astype(bf16)
    fetch[0].wait()
    unpack_mixed(all0, wqkv_t, wproj_t)
    t[...] = dot(wqkv_t[...], a3[...]).astype(bf16)
    units = [(h, n) for h in range(WORD_HEADS) for n in range(len(halves))]

    def score(h, n):
        k = t[pl.ds(width + h * head, head), pl.ds(0, (n + 1) * SPAN)].T
        return dot(k, t[pl.ds(h * head, head), halves[n]])

    def mix(h, n, w):
        keys = pl.ds(0, (n + 1) * SPAN)
        o[pl.ds(h * head, head), halves[n]] = dot(t[pl.ds(2 * width + h * head, head), keys], w).astype(bf16)

    ahead, behind = score(*units[0]), None
    for i, (h, n) in enumerate(units):
        s = ahead
        if i + 1 < len(units):
            ahead = score(*units[i + 1])
        keys = pl.ds(0, (n + 1) * SPAN)
        s = s * scale + bias[keys, halves[n]]
        e = jnp.exp(s - jnp.max(s, 0, keepdims=True))
        w = e * (1.0 / jnp.sum(e, 0, keepdims=True))
        p[h, keys, halves[n]] = w
        if behind is not None:
            mix(*behind)
        behind = (h, n, w.astype(bf16))
    mix(*behind)
    fetch[1].wait()
    unpack_up(all1, wup_t, wup)
    h3[...] = x[...] + dot(wproj_t[...], o[...])
    z, rs = normed(h3[...])
    z4[...] = z.astype(bf16)
    rs4[...] = rs
    a4[...] = (z * wide(gb_ref[...], length)).astype(bf16)
    for n in range(wup_t.shape[0] // 256):
        rows = pl.ds(n * 256, 256)
        mm, gg = gelu_twice(dot(wup_t[rows, :], a4[...]))
        m[rows, :] = mm.astype(bf16)
        slope[rows, :] = gg.astype(bf16)
    fetch[2].wait()
    unpack_down(all2, wdown_t)
    wdown[...] = turned(wdown_t[...])
    for n in range(wdown.shape[0] // 256):
        rows = pl.ds(n * 256, 256)
        du[rows, :] = (dot(wdown[rows, :], cot[...]) * slope[rows, :].astype(f32)).astype(bf16)
    out = h3[...] + dot(wdown_t[...], m[...])
    out_ref[...] = out.T.astype(bf16)
    dy = dot(wup[...], du[...])
    z = z4[...].astype(f32)
    ggb_ref[...] = jnp.broadcast_to(jnp.sum(fold_lanes(dy * z).T, 0, keepdims=True), ggb_ref.shape)
    dh3[...] = cot[...].astype(f32) + norm_back(dy, z, rs4[...], wide(gb_ref[...], length))
    dh3b[...] = dh3[...].astype(bf16)
    wproj[...] = turned(wproj_t[...])
    do[...] = dot(wproj[...], dh3b[...]).astype(bf16)
    n = width // nd
    deep = m.shape[0] // nz
    for z in range(nz):
        for i in range(deep // lanes):
            g = (dot_nt(cot[...], m[pl.ds(z * deep + i * lanes, lanes), :]) * 0.5).astype(bf16)
            for d in range(nd):
                send2[d, z, pl.ds(i * n, n), :] = g[d * n : (d + 1) * n]
    leave[2].start()
    for d in range(nd):
        g = dot_nt(a4[...], du[pl.ds(d * lanes, lanes), :]).astype(bf16)
        send1[d] = g.reshape(nz, r, lanes)
    leave[1].start()
    gproj_t[...] = dot_nt(dh3b[...], o[...]).astype(bf16)
    last = len(halves) - 1
    units = [(h, n) for h in range(WORD_HEADS) for n in reversed(range(len(halves)))]

    def rows_of(kind, h):
        return pl.ds(kind * width + h * head, head)

    def upstream(h, n):
        return dot(t[rows_of(2, h), pl.ds(0, (n + 1) * SPAN)].T, do[rows_of(0, h), halves[n]])

    def spread(h, n, ds, w):
        keys, at = pl.ds(0, (n + 1) * SPAN), halves[n]
        dt[rows_of(0, h), at] = (dot(t[rows_of(1, h), keys], ds) * scale).astype(bf16)
        dk = dot_nt(t[rows_of(0, h), at], ds) * scale
        dv = dot_nt(do[rows_of(0, h), at], w)
        if n == last:
            dtk[0] = dk
            dtk[1] = dv
        else:
            dtk[0, :, keys] += dk
            dtk[1, :, keys] += dv
        if n == 0:
            dt[rows_of(1, h), :] = dtk[0].astype(bf16)
            dt[rows_of(2, h), :] = dtk[1].astype(bf16)

    ahead, behind = upstream(*units[0]), None
    for i, (h, n) in enumerate(units):
        dp = ahead
        if i + 1 < len(units):
            ahead = upstream(*units[i + 1])
        w = p[h, pl.ds(0, (n + 1) * SPAN), halves[n]]
        ds = (w * (dp - jnp.sum(w * dp, 0, keepdims=True))).astype(bf16)
        if behind is not None:
            spread(*behind)
        behind = (h, n, ds, w.astype(bf16))
    spread(*behind)
    for n in range(3):
        part = pl.ds(n * width, width)
        gqkv_t[part, :] = dot_nt(dt[part, :], a3[...]).astype(bf16)
    a, b = gqkv_t.shape[0] // nd, gproj_t.shape[0] // nd
    for d in range(nd):
        g = turned(jnp.concatenate([gqkv_t[pl.ds(d * a, a), :], gproj_t[pl.ds(d * b, b), :]], 0))
        send0[d] = g.reshape(nz, r, lanes)
    leave[0].start()
    wqkv[...] = turned(wqkv_t[...])
    dy = dot(wqkv[...], dt[...])
    z = z3[...].astype(f32)
    gga_ref[...] = jnp.broadcast_to(jnp.sum(fold_lanes(dy * z).T, 0, keepdims=True), gga_ref.shape)
    dx = dh3[...] + norm_back(dy, z, rs3[...], wide(ga_ref[...], length))
    dh3b[...] = dx.astype(bf16)
    wpool[...] = turned(wpool_t[...])
    dpool_ref[...] = (dot(wpool[...], dh3b[...]) / counts).astype(bf16)
    gpool_ref[...] = dot_nt(dh3b[...], pooled[...]).astype(bf16)
    for copy in leave:
        copy.wait()


def word_gathered(pool_sum, cnt, sep, cot, ga, gb, pool_t, *gathered):
    length, width = cot.shape
    inner = pool_sum.shape[0]
    nd, nz, r, lanes = gathered[0].shape
    hidden = nd * lanes
    vm = pltpu.VMEM
    near, far = pl.BlockSpec(memory_space=pltpu.VMEM), pl.BlockSpec(memory_space=pl.ANY)
    return pl.pallas_call(
        word_gathered_kernel,
        in_specs=[near] * 7 + [far] * 3,
        out_specs=[near] * 3 + [far] * 3 + [near] * 2,
        out_shape=[
            jax.ShapeDtypeStruct((length, width), bf16),
            jax.ShapeDtypeStruct((inner, length), bf16),
            jax.ShapeDtypeStruct((width, inner), bf16),
            *(jax.ShapeDtypeStruct(g.shape, bf16) for g in gathered),
            jax.ShapeDtypeStruct((8, width), f32),
            jax.ShapeDtypeStruct((8, width), f32),
        ],
        scratch_shapes=[
            vm((inner, length), bf16), vm((width, length), f32), vm((width, length), bf16), vm((1, length), f32),
            vm((width, length), bf16), vm((3 * width, length), bf16), vm((WORD_HEADS, length, length), f32),
            vm((width, length), bf16), vm((width, length), f32), vm((width, length), bf16), vm((1, length), f32),
            vm((width, length), bf16), vm((hidden, length), bf16), vm((hidden, length), bf16),
            vm((length, length), f32), vm((width, length), bf16), vm((hidden, length), bf16),
            vm((width, length), f32), vm((width, length), bf16), vm((width, length), bf16),
            vm((3 * width, length), bf16), vm((2, width // WORD_HEADS, length), f32),
            vm((3 * width, width), bf16), vm((width, width), bf16), vm((hidden, width), bf16), vm((width, hidden), bf16),
            vm((width, 3 * width), bf16), vm((width, width), bf16), vm((width, hidden), bf16), vm((hidden, width), bf16),
            vm((inner, width), bf16), vm((3 * width, width), bf16), vm((width, width), bf16),
        ] + [vm(g.shape, bf16) for g in gathered] * 2 + [pltpu.SemaphoreType.DMA((3,)), pltpu.SemaphoreType.DMA((3,))],
        compiler_params=pltpu.CompilerParams(vmem_limit_bytes=VMEM_BYTES),
        name="word_gathered",
    )(pool_sum, cnt, sep, cot, ga, gb, pool_t, *gathered)


GATHER_PLAN = {
    "first": (1, 3, 6, 8),
    "second": (3, 6, 9, 13, 15),
    0: (6, 11, 14, 17, 19),
    1: (9, 14, 17, 20, 22),
    2: (11, 17, 20, 22, 24),
}
SCATTER_PLAN = {
    0: (1, 2, 4, 6, 8),
    1: (2, 5, 7, 9, 11),
    2: (3, 8, 10, 12, 15),
    "second": (8, 11, 13, 15, 17),
    "first": (16, 18, 20, 24),
}
FORWARD_HALVES = (1, 2, 1)
BACKWARD_HALVES = (1, 1, 1)


def planned(plan, event, steps):
    return [(at // 8) * steps + (at % 8) * steps // 8 for at in plan[event]]


def starts(halves, steps):
    ends = [0]
    for h in halves:
        ends.append(ends[-1] + steps // h)
    return ends


def step_of(tick, halves, steps):
    phase = min(tick // steps, 2)
    inside = tick - phase * steps
    return starts(halves, steps)[phase] + inside // halves[phase], inside % halves[phase]


def forward_gather_kernel(
    letters, steps, x_ref, cnt_ref, s_qkv, s_proj, s_gains, s_up, s_down, s_pool, w_qkv, w_proj, w_up, w_down,
    tok_ref, t_ref, o_ref, p_ref, z1_ref, rs1_ref, z2_ref, rs2_ref, m_ref, slope_ref, pool_ref, word0, word1, word2,
    wqkv_t, wqkv, wproj, wup, wdown, pool_t, cga, cgb, wga, wgb,
    first_all, second_all, word_own, wproj_t, wup_t, wdown_t, x_all, z1_all, h1_all, near, far, a2_ref,
    first_sems, second_sems, word_sems0, word_sems1, word_sems2, own_sems,
):
    step = pl.program_id(0)
    here = place()
    words = (word0, word1, word2)
    per = LANES * letters // BATCH
    streams = {
        "first": (first_all, first_sems), "second": (second_all, second_sems),
        0: (word0, word_sems0), 1: (word1, word_sems1), 2: (word2, word_sems2),
    }
    own = [pltpu.make_async_copy(word_own.at[n], words[n].at[here], own_sems.at[n]) for n in range(3)]

    def stages_of(name, wanted):
        return (gather_direct if name == "first" else gather_stages)(*streams[name], wanted)

    @pl.when(step == 0)
    def _():
        greet()
        patterns(near, far, letters)
        pack_first(first_all.at[here], s_qkv, s_proj, s_gains)

    @pl.when(step == 1)
    def _():
        greeted()

    def advance(half):
        for name in streams:
            events = planned(GATHER_PLAN, name, steps)
            for n, when in enumerate(events):
                if when == 3 * steps or step_of(when, FORWARD_HALVES, steps)[1] != half:
                    continue

                @pl.when(step == step_of(when, FORWARD_HALVES, steps)[0])
                def _():
                    if n > 0:
                        arrive_all(stages_of(name, (n - 1,))[n - 1])
                    elif name in (0, 1, 2):
                        own[name].wait()
                    if n < len(events) - 1:
                        start_all(stages_of(name, (n,))[n])
                        if name == "first" and n == 0:
                            pack_second(second_all.at[here], s_up, s_down, s_pool)
                            pack_words(word_own, w_qkv, w_proj, w_up, w_down)
                            start_all(own)
                    elif name == "first":
                        unpack_first(first_all, wqkv_t, wproj_t, wqkv, wproj, cga, cgb, wga, wgb)
                    elif name == "second":
                        unpack_second(second_all, wup_t, wdown_t, wup, wdown, pool_t)

    advance(0)
    _, one, two, end = starts(FORWARD_HALVES, steps)

    @pl.when(step < steps)
    def _():
        forward_first(step, per, x_ref, cnt_ref, tok_ref, rs1_ref, x_all, z1_all, near)

    @pl.when((step >= one) & (step < two))
    def _():
        for j in range(FORWARD_HALVES[1]):
            if j > 0:
                advance(j)
            forward_attention(
                (step - one) * FORWARD_HALVES[1] + j, letters, tok_ref, cga, wqkv_t, wproj_t, t_ref, o_ref, p_ref, z1_ref,
                x_all, z1_all, h1_all, j,
            )

    @pl.when(step >= two)
    def _():
        forward_feed(
            step - two, letters, per, tok_ref, cgb, wup_t, wdown_t, z2_ref, rs2_ref, m_ref, slope_ref, pool_ref,
            h1_all, far, a2_ref,
        )

    @pl.when(step == end - 1)
    def _():
        for name in streams:
            if planned(GATHER_PLAN, name, steps)[-1] == 3 * steps:
                arrive_all(stages_of(name, (3,))[3])
            sent_all(stages_of(name, (0, 1, 2, 3)))


def phase_map(phase, halves, steps, per=1):
    first = starts(halves, steps)[phase]
    return lambda i: jnp.clip(i - first, 0, steps // halves[phase] - 1) // per


def forward_gather(x, cnt, first_shards, second_shards, word_shards, letters):
    tokens, width = x.shape
    steps = tokens // BATCH
    ny, nx, nz = sides()
    nd = 2 * ny * nx
    hidden, outer = second_shards[0].shape[1] * nd, second_shards[2].shape[1] * nd
    r = width // nz
    per = LANES * letters // BATCH
    word_rows, word_lanes = word_shards[2].shape

    def strip(phase, rows, lanes=BATCH, dtype=bf16):
        where, many = phase_map(phase, FORWARD_HALVES, steps), FORWARD_HALVES[phase]
        return (
            jax.ShapeDtypeStruct((steps, rows, lanes), dtype),
            pl.BlockSpec((many, rows, lanes), lambda i: (where(i), 0, 0)),
        )

    def whole(shape, dtype=bf16):
        return (jax.ShapeDtypeStruct(shape, dtype), pl.BlockSpec(shape, lambda i: (0,) * len(shape)))

    pooled = phase_map(2, FORWARD_HALVES, steps, per)
    gathered = (
        jax.ShapeDtypeStruct((ny, nx, 2, nz, word_rows, word_lanes), bf16), pl.BlockSpec(memory_space=pl.ANY)
    )
    outs = [
        whole((steps, 1, BATCH), jnp.int32), strip(1, 3 * width), strip(1, width), strip(1, CHAR_HEADS // 2 * letters, 2 * BATCH, f32), strip(1, width),
        whole((steps, 1, BATCH), f32), strip(2, width), strip(2, 1, BATCH, f32), strip(2, hidden), strip(2, hidden),
        (
            jax.ShapeDtypeStruct((width, tokens // letters), f32),
            pl.BlockSpec((width, LANES), lambda i: (0, pooled(i))),
        ),
        gathered, gathered, gathered,
        whole((3 * width, width)), whole((width, 3 * width)), whole((width, width)), whole((width, hidden)),
        whole((hidden, width)), whole((outer, width)), whole((width, LANES), f32), whole((width, LANES), f32),
        whole((outer, LANES), f32), whole((outer, LANES), f32),
    ]
    shards = (*first_shards, *second_shards, *word_shards)
    at0 = phase_map(0, FORWARD_HALVES, steps)
    sems = pltpu.SemaphoreType.DMA((2, gather_copies()))
    return pl.pallas_call(
        functools.partial(forward_gather_kernel, letters, steps),
        grid=(starts(FORWARD_HALVES, steps)[3],),
        in_specs=[
            pl.BlockSpec((BATCH, width), lambda i: (at0(i), 0)),
            pl.BlockSpec((1, LANES), lambda i: (0, at0(i) // per)),
        ] + [full_spec(a) for a in shards],
        out_specs=[o[1] for o in outs],
        out_shape=[o[0] for o in outs],
        scratch_shapes=[
            pltpu.VMEM((ny, nx, 2, nz, r + 16, LANES), bf16),
            pltpu.VMEM((ny, nx, 2, nz, 3 * r, LANES), bf16),
            pltpu.VMEM((3, word_rows, word_lanes), bf16),
            pltpu.VMEM((width, width), bf16),
            pltpu.VMEM((hidden, width), bf16),
            pltpu.VMEM((width, hidden), bf16),
            pltpu.VMEM((steps, width, BATCH), bf16),
            pltpu.VMEM((steps, width, BATCH), bf16),
            pltpu.VMEM((steps, width, BATCH), f32),
            pltpu.VMEM((BATCH // letters, BATCH), bf16),
            pltpu.VMEM((BATCH, LANES), bf16),
            pltpu.VMEM((width, BATCH), bf16),
            pltpu.SemaphoreType.DMA((2, nz - 1 + 2 * ny * nx - 1)), sems, sems, sems, sems,
            pltpu.SemaphoreType.DMA((3,)),
        ],
        compiler_params=pltpu.CompilerParams(
            dimension_semantics=("arbitrary",), vmem_limit_bytes=VMEM_BYTES, collective_id=0, has_side_effects=True
        ),
        name="forward_gather",
    )(x, cnt, *shards)


def backward_scatter_kernel(
    letters, steps, dp_ref, tok_ref, ga_ref, gb_ref, wqkv_t, wqkv, wproj, wup, wdown, send0, send1, send2,
    gpool_t, gwga, gwgb, t_ref, o_ref, p_ref, z1_ref, rs1_ref, z2_ref, rs2_ref, m_ref, slope_ref,
    cg_ref, first_sum, second_sum, word_sum,
    gqkv_t, gproj_t, gup, gdown_t, dh1_all, dt_all, do_ref, first_send, second_send, own_sems, *work,
):
    step = pl.program_id(0)
    y, x, c, z = place()
    per = LANES * letters // BATCH
    size = (len(work) - 5) // 4
    work = [work[n * size : (n + 1) * size] for n in range(5)]
    sends = (send0, send1, send2)
    streams = {n: (sends[n], work[n], word_sum.at[n]) for n in range(3)}
    streams["second"] = (second_send, work[3], second_sum)
    streams["first"] = (first_send, work[4], first_sum)
    own = [pltpu.make_async_copy(sends[n].at[:, :, c], work[n][0], own_sems.at[n]) for n in range(3)]

    @pl.when(step == 0)
    def _():
        greet()
        start_all(own)

    @pl.when(step == 1)
    def _():
        greeted()

    def advance(half):
        for name, (send, scratch, total) in streams.items():
            acc = scratch[0]
            stage, add = (direct_stage, direct_sum) if name == "first" else (scatter_stage, scatter_sum)
            events = planned(SCATTER_PLAN, name, steps)
            for n, when in enumerate(events):
                if when == 3 * steps or step_of(when, BACKWARD_HALVES, steps)[1] != half:
                    continue

                @pl.when(step == step_of(when, BACKWARD_HALVES, steps)[0])
                def _():
                    if n == 0:
                        if name == "second":
                            pack_second_grads(second_send, gup, gdown_t, gb_ref, gpool_t)
                        elif name == "first":
                            pack_first_grads(first_send, gqkv_t, gproj_t, ga_ref, wqkv_t, gup, wup, gwga, gwgb)
                    else:
                        arrive_all(stage(n - 1, send, scratch))
                        if n == 1 and name in (0, 1, 2):
                            own[name].wait()
                            mine = lambda b, a, k: acc[b, a, k]
                        else:
                            mine = lambda b, a, k: send[b, a, c, k]
                        add(n - 1, mine, scratch, total)
                    if n < len(events) - 1:
                        start_all(stage(n, send, scratch))

    advance(0)
    _, one, two, end = starts(BACKWARD_HALVES, steps)

    @pl.when(step < steps)
    def _():
        backward_feed(
            step, letters, per, dp_ref, tok_ref, gb_ref, wup, wdown, z2_ref, rs2_ref, m_ref, slope_ref,
            gup, gdown_t, dh1_all, dt_all,
        )

    @pl.when((step >= one) & (step < two))
    def _():
        for j in range(BACKWARD_HALVES[1]):
            if j > 0:
                advance(j)
            backward_attention(
                (step - one) * BACKWARD_HALVES[1] + j, letters, wproj, t_ref, o_ref, p_ref, z1_ref, gqkv_t, gproj_t,
                dh1_all, dt_all, do_ref, j,
            )

    @pl.when(step >= two)
    def _():
        for j in range(BACKWARD_HALVES[2]):
            if j > 0:
                advance(j)
            backward_last((step - two) * BACKWARD_HALVES[2] + j, ga_ref, wqkv, z1_ref, rs1_ref, cg_ref, dh1_all, dt_all, j)

    @pl.when(step == end - 1)
    def _():
        for name, (send, scratch, total) in streams.items():
            if name == "first":
                arrive_all(direct_stage(2, send, scratch))
                direct_sum(2, None, scratch, total)
                sent_all([direct_stage(n, send, scratch) for n in range(3)])
            else:
                sent_all([scatter_stage(n, send, scratch) for n in range(4)])


def backward_scatter(dp, tok, ga, gb, weights, sends, gpool_t, gwga, gwgb, saved, letters):
    wqkv_t, wqkv, wproj, wup, wdown = weights
    t, o, p, z1, rs1, z2, rs2, m, slope = saved
    steps = t.shape[0]
    width, hidden = wup.shape
    per = LANES * letters // BATCH
    ny, nx, nz = sides()
    r = width // nz
    word_rows, word_lanes = sends[0].shape[4:]
    at = [phase_map(n, BACKWARD_HALVES, steps) for n in range(3)]
    words = phase_map(0, BACKWARD_HALVES, steps, per)

    def strip(a, where, many):
        return pl.BlockSpec((many,) + a.shape[1:], lambda i: (where(i), 0, 0))

    def whole(shape):
        return (jax.ShapeDtypeStruct(shape, f32), pl.BlockSpec(shape, lambda i: (0,) * len(shape)))

    def once(a):
        return pl.BlockSpec(a.shape, lambda i: (0,) * a.ndim, pipeline_mode=pl.Buffered(1))

    outs = [
        (jax.ShapeDtypeStruct((steps * BATCH, width), bf16), pl.BlockSpec((BACKWARD_HALVES[2] * BATCH, width), lambda i: (at[2](i), 0))),
        whole((r + 16, LANES)), whole((3 * r, LANES)), whole((3, word_rows, word_lanes)),
    ]
    _, one, two, end = starts(BACKWARD_HALVES, steps)
    either = lambda i: jnp.where(i < two, at[1](i), at[2](i))
    lots = BACKWARD_HALVES[1]
    saved_specs = [
        strip(t, at[1], lots), strip(o, at[1], lots), strip(p, at[1], lots), strip(z1, either, lots),
        strip(rs1, at[2], lots), strip(z2, at[0], 1), strip(rs2, at[0], 1), strip(m, at[0], 1), strip(slope, at[0], 1),
    ]
    return pl.pallas_call(
        functools.partial(backward_scatter_kernel, letters, steps),
        grid=(end,),
        in_specs=[
            pl.BlockSpec((width, LANES), lambda i: (0, words(i))),
            pl.BlockSpec((1, 1, BATCH), lambda i: (at[0](i), 0, 0)),
        ] + [once(a) for a in (ga, gb, *weights)] + [pl.BlockSpec(memory_space=pl.ANY)] * 3
        + [once(a) for a in (gpool_t, gwga, gwgb)] + saved_specs,
        out_specs=[o[1] for o in outs],
        out_shape=[o[0] for o in outs],
        scratch_shapes=[
            pltpu.VMEM((3 * width, width), f32),
            pltpu.VMEM((width, width), f32),
            pltpu.VMEM((width, hidden), f32),
            pltpu.VMEM((width, hidden), f32),
            pltpu.VMEM((steps, width, BATCH), bf16),
            pltpu.VMEM((steps, 3 * width, BATCH), bf16),
            pltpu.VMEM((width, BATCH), bf16),
            pltpu.VMEM((ny, nx, 2, nz, r + 16, LANES), bf16),
            pltpu.VMEM((ny, nx, 2, nz, 3 * r, LANES), bf16),
            pltpu.SemaphoreType.DMA((3,)),
        ] + 3 * scatter_scratch(word_rows, word_lanes) + scatter_scratch(3 * r, LANES) + direct_scratch(r + 16, LANES),
        compiler_params=pltpu.CompilerParams(
            dimension_semantics=("arbitrary",), vmem_limit_bytes=VMEM_BYTES, collective_id=1, has_side_effects=True
        ),
        name="backward_scatter",
    )(dp, tok, ga, gb, *weights, *sends, gpool_t, gwga, gwgb, *saved)


def finish_kernel(
    first, second, words, grad_in, cqkv, cproj_t, cup, cdown_t, cga, cgb, pool, wqkv_t, wproj_t, wup, wdown_t, wga, wgb,
    grad_out,
):
    grad_out[...] = grad_in[...]

    @pl.when(pl.program_id(0) == 0)
    def _():
        r, n, gc, gw = cup.shape[0], cqkv.shape[1], cga.shape[1], wga.shape[1]
        cqkv[...] = first[pl.ds(0, r), :n]
        cproj_t[...] = first[pl.ds(0, r), :].T[n:]
        side = first[pl.ds(r, 8), :]
        cga[...] = side[0:1, :gc]
        cgb[...] = side[0:1, gc : 2 * gc]
        wga[...] = side[0:1, 2 * gc : 2 * gc + gw]
        wgb[...] = side[1:2, :gw]
        cup[...] = second[pl.ds(0, r), :]
        n = cdown_t.shape[0]
        for i in range(cdown_t.shape[1] // LANES):
            cdown_t[:, pl.ds(i * LANES, LANES)] = second[pl.ds(r + i * n, n), :]
        pool[...] = second[pl.ds(2 * r, r), : pool.shape[1]]
        t = words[0].T
        n = wqkv_t.shape[0]
        wqkv_t[...] = t[:n]
        wproj_t[...] = t[n:]
        wup[...] = words[1]
        n, lanes = wdown_t.shape[0], wup.shape[1]
        for i in range(wdown_t.shape[1] // lanes):
            wdown_t[:, pl.ds(i * lanes, lanes)] = words[2, pl.ds(i * n, n), :]


def finish(first, second, words, grad, shapes):
    steps = 4
    moved = pl.BlockSpec((grad.shape[0] // steps, grad.shape[1]), lambda i: (i, 0))
    shapes = [jax.ShapeDtypeStruct(s, f32) for s in shapes]
    return pl.pallas_call(
        finish_kernel,
        grid=(steps,),
        in_specs=[full_spec(a) for a in (first, second, words)] + [moved],
        out_specs=[full_spec(a) for a in shapes] + [moved],
        out_shape=shapes + [jax.ShapeDtypeStruct(grad.shape, grad.dtype)],
        name="finish",
    )(first, second, words, grad)


def gather_all(shards, counts):
    flat = jnp.concatenate([s.reshape(-1) for s in shards])
    packed = lax.all_gather(lax.all_gather(flat, "fsdp", axis=0), "dp", axis=0)
    wide_count, deep_count = packed.shape[:2]
    out, start = [], 0
    for s in shards:
        piece = packed[:, :, start : start + s.size]
        start += s.size
        if s.ndim == 1:
            out.append(piece[:, 0].reshape(-1))
        else:
            r, c = s.shape
            piece = piece.reshape(wide_count, deep_count, r, c).transpose(1, 2, 0, 3)
            out.append(piece.reshape(deep_count * r, wide_count * c))
    return out


def scatter_all(grads, shards):
    wide_count, deep_count = lax.axis_size("dp"), lax.axis_size("fsdp")
    pieces = []
    for g, s in zip(grads, shards):
        g = g.astype(bf16)
        if s.ndim == 1:
            g = jnp.broadcast_to(g.reshape(wide_count, 1, s.size), (wide_count, deep_count, s.size))
        else:
            r, c = s.shape
            g = g.reshape(deep_count, r, wide_count, c).transpose(2, 0, 1, 3)
        pieces.append(g.reshape(wide_count, deep_count, s.size))
    packed = jnp.concatenate(pieces, 2)
    packed = lax.psum_scatter(packed, "dp", scatter_dimension=0, tiled=True)
    packed = lax.psum_scatter(packed, "fsdp", scatter_dimension=1, tiled=True).reshape(-1)
    out, start = [], 0
    for s in shards:
        out.append(packed[start : start + s.size].reshape(s.shape).astype(f32))
        start += s.size
    return out


def shards_plain(
    characters, counts, separators, cotangent, char_qkv, char_proj, char_up, char_down, char_gain_a, char_gain_b,
    pool_proj, word_qkv, word_proj, word_up, word_down, word_gain_a, word_gain_b,
):
    rows, length, letters, width = characters.shape
    char_shards = (char_qkv, char_proj, char_up, char_down, char_gain_a, char_gain_b)
    word_shards = (pool_proj, word_qkv, word_proj, word_up, word_down, word_gain_a, word_gain_b)
    cqkv, cproj, cup, cdown, cga, cgb = gather_all(char_shards, counts)
    wpool, wqkv, wproj, wup, wdown, wga, wgb = gather_all(word_shards, counts)
    x = characters.reshape(length * letters, width)
    tok = jnp.repeat(counts, letters, axis=1).reshape(length * letters // STEP, 1, STEP)
    cga, cgb, wga, wgb = (
        jnp.broadcast_to(g.astype(f32)[:, None], (g.shape[0], LANES)) for g in (cga, cgb, wga, wgb)
    )
    *saved, pool_sum = char_forward(x, tok, counts, cga, cgb, cqkv.T, cproj.T, cup.T, cdown.T, letters)
    word_out, dpool, gpool, gwqkv, gwproj, gwup, gwdown, gwga, gwgb = word_layer(
        pool_sum, counts.astype(f32), separators, cotangent.reshape(length, -1), wga, wgb, wpool, wqkv, wproj, wup, wdown
    )
    word_grads = scatter_all(
        (gpool, gwqkv, gwproj, gwup, gwdown, jnp.sum(gwga, 1), jnp.sum(gwgb, 1)), word_shards
    )
    char_grad, gcqkv, gcproj, gcup, gcdown, gcga, gcgb = char_backward(
        dpool, tok, cga, cgb, cqkv, cproj, cup, cdown, saved, letters
    )
    char_grads = scatter_all(
        (gcqkv, gcproj, gcup, gcdown, jnp.sum(gcga, 1), jnp.sum(gcgb, 1)), char_shards
    )
    return (word_out[None], char_grad.reshape(characters.shape), *char_grads, *word_grads)


def shards_packed(
    characters, counts, separators, cotangent, char_qkv, char_proj, char_up, char_down, char_gain_a, char_gain_b,
    pool_proj, word_qkv, word_proj, word_up, word_down, word_gain_a, word_gain_b,
):
    rows, length, letters, width = characters.shape
    x = characters.reshape(length * letters, width)
    gains = jnp.concatenate([char_gain_a, char_gain_b, word_gain_a, word_gain_b]).astype(f32)
    gains = jnp.pad(gains, (0, 2 * LANES - gains.shape[0])).reshape(2, LANES)
    (
        tok, *saved, pool_sum, word0, word1, word2, wqkv_t, wqkv, wproj, wup, wdown, pool_t, cga, cgb, wga, wgb
    ) = forward_gather(
        x, counts, (char_qkv, char_proj.T, gains), (char_up, char_down.T, pool_proj),
        (word_qkv.T, word_proj.T, word_up, word_down.T), letters,
    )
    shape = word0.shape
    flat = (-1,) + shape[3:]
    word_out, dpool, gpool_t, *sends, gwga, gwgb = word_gathered(
        pool_sum, counts, separators, cotangent.reshape(length, -1), wga, wgb, pool_t,
        *(w.reshape(flat) for w in (word0, word1, word2)),
    )
    char_grad, first, second, words = backward_scatter(
        dpool, tok, cga, cgb, (wqkv_t, wqkv, wproj, wup, wdown), [s.reshape(shape) for s in sends],
        gpool_t, gwga, gwgb, saved, letters,
    )
    shapes = [
        s.shape if s.ndim == 2 else (1, s.shape[0])
        for s in (
            char_qkv, char_proj.T, char_up, char_down.T, char_gain_a, char_gain_b,
            pool_proj, word_qkv.T, word_proj.T, word_up, word_down.T, word_gain_a, word_gain_b,
        )
    ]
    (
        cqkv, cproj_t, cup, cdown_t, cgain_a, cgain_b, pool, gqkv_t, gproj_t, gup, gdown_t, wgain_a, wgain_b, char_grad
    ) = finish(first, second, words, char_grad, shapes)
    return (
        word_out[None], char_grad.reshape(characters.shape), cqkv, cproj_t.T, cup, cdown_t.T, cgain_a[0], cgain_b[0],
        pool, gqkv_t.T, gproj_t.T, gup, gdown_t.T, wgain_a[0], wgain_b[0],
    )


def shards(*arrays):
    char_qkv, char_proj, word_qkv, word_proj = arrays[4], arrays[5], arrays[11], arrays[12]
    tiles = (char_qkv.shape[1] + char_proj.shape[1]) // LANES, (word_qkv.shape[1] + word_proj.shape[1]) // LANES
    return (shards_packed if tiles == (1, 2) else shards_plain)(*arrays)


def solution(mesh):
    rows = ("dp", "fsdp")
    matrix, vector = P("fsdp", "dp"), P("dp")
    data = (P(rows, None, None, None), P(rows, None), P(rows, None), P(rows, None, None))
    block = (matrix,) * 4 + (vector,) * 2
    word = (matrix,) * 5 + (vector,) * 2
    return jax.shard_map(
        shards,
        mesh=mesh,
        in_specs=data + block + word,
        out_specs=(data[3], data[0]) + block + word,
        check_vma=False,
    )
```

```python
import functools
import math

import jax
import jax.numpy as jnp
from jax import lax
from jax.experimental import pallas as pl
from jax.experimental.pallas import tpu as pltpu
from jax.sharding import PartitionSpec as P

CHAR_HEADS = 4
WORD_HEADS = 8
EPS = 1e-05
NEGATIVE = -1e30
LANES = 128
SPAN = 256
STEP = 512
BATCH = 1024
VMEM_BYTES = 60 * 2**20
GELU_A = 0.7978845608028654
GELU_B = 0.044715

bf16 = jnp.bfloat16
f32 = jnp.float32


def dot(a, b):
    return jnp.dot(a, b, preferred_element_type=f32)


def dot_nt(a, b):
    return lax.dot_general(a, b, (((1,), (1,)), ((), ())), preferred_element_type=f32)


def normed(v):
    c = v - jnp.mean(v, 0, keepdims=True)
    rs = lax.rsqrt(jnp.mean(c * c, 0, keepdims=True) + EPS)
    return c * rs, rs


def wide(g, n):
    return g if n == g.shape[1] else jnp.concatenate([g] * (n // g.shape[1]), 1)


def gelu_both(u):
    s = u * u
    t = jnp.tanh(u * (GELU_A + (GELU_A * GELU_B) * s))
    h = 0.5 * u
    r = 0.5 + 0.5 * t
    slope = r + h * (1.0 - t * t) * (GELU_A + (3.0 * GELU_A * GELU_B) * s)
    return u * r, slope


def lane_word(letters):
    return lax.broadcasted_iota(jnp.int32, (letters, LANES), 1) // letters


def pick_own(full, owner, letters):
    words = LANES // letters
    out = full[:letters]
    for w in range(1, words):
        out = jnp.where(owner == w, full[w * letters : (w + 1) * letters], out)
    return out


def own_blocks(letters):
    a = lax.broadcasted_iota(jnp.int32, (LANES, LANES), 0) // letters
    b = lax.broadcasted_iota(jnp.int32, (LANES, LANES), 1) // letters
    return jnp.where(a == b, 1.0, 0.0).astype(bf16)


def spread_own(compact, blocks, letters):
    return jnp.concatenate([compact] * (LANES // letters), 0) * blocks


def char_forward_kernel(
    letters, x_ref, tok_ref, cnt_ref, ga_ref, gb_ref, wqkv_ref, wproj_ref, wup_ref, wdown_ref,
    t_ref, o_ref, p_ref, z1_ref, rs1_ref, z2_ref, rs2_ref, m_ref, gp_ref, pool_ref,
):
    step = pl.program_id(0)
    width = x_ref.shape[1]
    head = width // CHAR_HEADS
    scale = head ** (-0.5)
    steps_per_block = LANES * letters // STEP
    owner = lane_word(letters)
    blocks = own_blocks(letters)
    key_slot = lax.broadcasted_iota(jnp.int32, (letters, LANES), 0)

    @pl.when(step % steps_per_block == 0)
    def _():
        pool_ref[...] = jnp.zeros_like(pool_ref)

    for part in range(STEP // SPAN):
        at = pl.ds(part * SPAN, SPAN)
        x = x_ref[at, :].astype(f32).T
        z1, rs1 = normed(x)
        z1_ref[0, :, at] = z1.astype(bf16)
        rs1_ref[0, :, at] = rs1
        a1 = (z1 * wide(ga_ref[...], SPAN)).astype(bf16)
        for n in range(3):
            rows = pl.ds(n * width, width)
            t_ref[0, rows, at] = dot(wqkv_ref[rows, :], a1).astype(bf16)
        for g in range(SPAN // LANES):
            lanes = pl.ds(part * SPAN + g * LANES, LANES)
            allowed = key_slot < tok_ref[0, :, lanes]
            for h in range(CHAR_HEADS):
                q = t_ref[0, pl.ds(h * head, head), lanes]
                k = t_ref[0, pl.ds(width + h * head, head), lanes]
                v = t_ref[0, pl.ds(2 * width + h * head, head), lanes]
                full = dot(k.T, q)
                s = jnp.where(allowed, pick_own(full, owner, letters) * scale, NEGATIVE)
                e = jnp.exp(s - jnp.max(s, 0, keepdims=True))
                p = e / jnp.sum(e, 0, keepdims=True)
                p_ref[0, pl.ds(h * letters, letters), lanes] = p
                o = dot(v, spread_own(p.astype(bf16), blocks, letters))
                o_ref[0, pl.ds(h * head, head), lanes] = o.astype(bf16)
        h1 = x + dot(wproj_ref[...], o_ref[0, :, at])
        z2, rs2 = normed(h1)
        z2_ref[0, :, at] = z2.astype(bf16)
        rs2_ref[0, :, at] = rs2
        a2 = (z2 * wide(gb_ref[...], SPAN)).astype(bf16)
        for n in range(wup_ref.shape[0] // 256):
            rows = pl.ds(n * 256, 256)
            m, gp = gelu_both(dot(wup_ref[rows, :], a2))
            m_ref[0, rows, at] = m.astype(bf16)
            gp_ref[0, rows, at] = gp.astype(bf16)
        h2 = h1 + dot(wdown_ref[...], m_ref[0, :, at])
        high = h2.astype(bf16)
        low = (h2 - high.astype(f32)).astype(bf16)
        row = lax.broadcasted_iota(jnp.int32, (SPAN, LANES), 0)
        word = lax.broadcasted_iota(jnp.int32, (SPAN, LANES), 1)
        first = (step % steps_per_block) * (STEP // letters) + part * (SPAN // letters)
        mine = (row // letters + first == word) & (row % letters < cnt_ref[...])
        gather = jnp.where(mine, 1.0, 0.0).astype(bf16)
        pool_ref[...] += dot(high, gather) + dot(low, gather)


def full_spec(a):
    nd = len(a.shape)
    return pl.BlockSpec(a.shape, lambda i: (0,) * nd)


def char_forward(x, tok, cnt, ga, gb, wqkv_t, wproj_t, wup_t, wdown_t, letters):
    tokens, width = x.shape
    steps = tokens // STEP
    hidden = wup_t.shape[0]
    per = LANES * letters // STEP

    def strip(rows, dtype=bf16):
        return (
            jax.ShapeDtypeStruct((steps, rows, STEP), dtype),
            pl.BlockSpec((1, rows, STEP), lambda i: (i, 0, 0)),
        )

    outs = [
        strip(3 * width), strip(width), strip(CHAR_HEADS * letters, f32), strip(width), strip(1, f32),
        strip(width), strip(1, f32), strip(hidden), strip(hidden),
        (jax.ShapeDtypeStruct((width, tokens // letters), f32), pl.BlockSpec((width, LANES), lambda i: (0, i // per))),
    ]
    return pl.pallas_call(
        functools.partial(char_forward_kernel, letters),
        grid=(steps,),
        in_specs=[
            pl.BlockSpec((STEP, width), lambda i: (i, 0)),
            pl.BlockSpec((1, 1, STEP), lambda i: (i, 0, 0)),
            pl.BlockSpec((1, LANES), lambda i: (0, i // per)),
        ] + [full_spec(a) for a in (ga, gb, wqkv_t, wproj_t, wup_t, wdown_t)],
        out_specs=[o[1] for o in outs],
        out_shape=[o[0] for o in outs],
        compiler_params=pltpu.CompilerParams(
            dimension_semantics=("arbitrary",), vmem_limit_bytes=56 * 2**20
        ),
        name="char_forward",
    )(x, tok, cnt, ga, gb, wqkv_t, wproj_t, wup_t, wdown_t)


def norm_back(dy, z, rs, gain):
    dz = dy * gain
    a = jnp.mean(dz, 0, keepdims=True)
    b = jnp.mean(dz * z, 0, keepdims=True)
    return rs * (dz - a - z * b)


def fold_lanes(v):
    out = v[:, :LANES]
    for n in range(1, v.shape[1] // LANES):
        out = out + v[:, n * LANES : (n + 1) * LANES]
    return out


def char_backward_kernel(
    letters, dp_ref, tok_ref, ga_ref, gb_ref, wqkv_ref, wproj_ref, wup_ref, wdown_ref,
    t_ref, o_ref, p_ref, z1_ref, rs1_ref, z2_ref, rs2_ref, m_ref, gp_ref,
    cg_ref, gqkv_ref, gproj_ref, gup_ref, gdown_ref, gga_ref, ggb_ref,
    dh2_ref, du_ref, dh1b_ref, do_ref, dt_ref,
):
    step = pl.program_id(0)
    width = cg_ref.shape[1]
    head = width // CHAR_HEADS
    scale = head ** (-0.5)
    steps_per_block = LANES * letters // STEP
    owner = lane_word(letters)
    blocks = own_blocks(letters)

    @pl.when(step == 0)
    def _():
        for ref in (gqkv_ref, gproj_ref, gup_ref, gdown_ref, gga_ref, ggb_ref):
            ref[...] = jnp.zeros_like(ref)

    for part in range(STEP // SPAN):
        at = pl.ds(part * SPAN, SPAN)
        word = lax.broadcasted_iota(jnp.int32, (LANES, SPAN), 0)
        col = lax.broadcasted_iota(jnp.int32, (LANES, SPAN), 1)
        first = (step % steps_per_block) * (STEP // letters) + part * (SPAN // letters)
        mine = (col // letters + first == word) & (col % letters < tok_ref[0, :, at])
        scatter = jnp.where(mine, 1.0, 0.0).astype(bf16)
        dh2 = dot(dp_ref[...], scatter)
        dh2b = dh2.astype(bf16)
        dh2_ref[:, at] = dh2b
        for n in range(wdown_ref.shape[0] // 256):
            rows = pl.ds(n * 256, 256)
            du_ref[rows, at] = (dot(wdown_ref[rows, :], dh2b) * gp_ref[0, rows, at].astype(f32)).astype(bf16)
        dy = dot(wup_ref[...], du_ref[:, at])
        z = z2_ref[0, :, at].astype(f32)
        ggb_ref[...] += fold_lanes(dy * z)
        dh1 = dh2 + norm_back(dy, z, rs2_ref[0, :, at], wide(gb_ref[...], SPAN))
        dh1b = dh1.astype(bf16)
        dh1b_ref[:, at] = dh1b
        do_ref[:, at] = dot(wproj_ref[...], dh1b).astype(bf16)
        for g in range(SPAN // LANES):
            lanes = pl.ds(part * SPAN + g * LANES, LANES)
            for h in range(CHAR_HEADS):
                q_rows = pl.ds(h * head, head)
                k_rows = pl.ds(width + h * head, head)
                v_rows = pl.ds(2 * width + h * head, head)
                q = t_ref[0, q_rows, lanes]
                k = t_ref[0, k_rows, lanes]
                v = t_ref[0, v_rows, lanes]
                do = do_ref[pl.ds(h * head, head), lanes]
                p = p_ref[0, pl.ds(h * letters, letters), lanes]
                dp = pick_own(dot(v.T, do), owner, letters)
                ds = p * (dp - jnp.sum(p * dp, 0, keepdims=True))
                pb = spread_own(p.astype(bf16), blocks, letters)
                dsb = spread_own(ds.astype(bf16), blocks, letters)
                dt_ref[q_rows, lanes] = (dot(k, dsb) * scale).astype(bf16)
                dt_ref[k_rows, lanes] = (dot_nt(q, dsb) * scale).astype(bf16)
                dt_ref[v_rows, lanes] = dot_nt(do, pb).astype(bf16)
        dy = dot(wqkv_ref[...], dt_ref[:, at])
        z = z1_ref[0, :, at].astype(f32)
        gga_ref[...] += fold_lanes(dy * z)
        dx = dh1 + norm_back(dy, z, rs1_ref[0, :, at], wide(ga_ref[...], SPAN))
        cg_ref[at, :] = dx.T.astype(bf16)
    gdown_ref[...] += dot_nt(dh2_ref[...], m_ref[0])
    gup_ref[...] += dot_nt(z2_ref[0], du_ref[...])
    gproj_ref[...] += dot_nt(dh1b_ref[...], o_ref[0])
    gqkv_ref[...] += dot_nt(dt_ref[...], z1_ref[0])

    @pl.when(step == pl.num_programs(0) - 1)
    def _():
        gup_ref[...] = gup_ref[...] * wide(gb_ref[...], gup_ref.shape[1])
        gqkv_ref[...] = gqkv_ref[...] * ga_ref[...].T[:1]


def char_backward(dp, tok, ga, gb, wqkv, wproj, wup, wdown, saved, letters):
    t, o, p, z1, rs1, z2, rs2, m, gp = saved
    steps = t.shape[0]
    width = wqkv.shape[0]
    hidden = wup.shape[1]
    per = LANES * letters // STEP

    def whole(shape):
        return (jax.ShapeDtypeStruct(shape, f32), pl.BlockSpec(shape, lambda i: (0, 0)))

    outs = [
        (jax.ShapeDtypeStruct((steps * STEP, width), bf16), pl.BlockSpec((STEP, width), lambda i: (i, 0))),
        whole((3 * width, width)), whole((width, width)), whole((width, hidden)), whole((width, hidden)),
        whole((width, LANES)), whole((width, LANES)),
    ]
    return pl.pallas_call(
        functools.partial(char_backward_kernel, letters),
        grid=(steps,),
        in_specs=[
            pl.BlockSpec((width, LANES), lambda i: (0, i // per)),
            pl.BlockSpec((1, 1, STEP), lambda i: (i, 0, 0)),
        ] + [full_spec(a) for a in (ga, gb, wqkv, wproj, wup, wdown)]
        + [pl.BlockSpec((1,) + s.shape[1:], lambda i: (i, 0, 0)) for s in saved],
        out_specs=[o[1] for o in outs],
        out_shape=[o[0] for o in outs],
        scratch_shapes=[
            pltpu.VMEM((width, STEP), bf16),
            pltpu.VMEM((hidden, STEP), bf16),
            pltpu.VMEM((width, STEP), bf16),
            pltpu.VMEM((width, STEP), bf16),
            pltpu.VMEM((3 * width, STEP), bf16),
        ],
        compiler_params=pltpu.CompilerParams(
            dimension_semantics=("arbitrary",), vmem_limit_bytes=56 * 2**20
        ),
        name="char_backward",
    )(dp, tok, ga, gb, wqkv, wproj, wup, wdown, *saved)


def word_kernel(
    pool_sum_ref, cnt_ref, sep_ref, cot_ref, ga_ref, gb_ref, wpool_ref, wqkv_ref, wproj_ref, wup_ref, wdown_ref,
    out_ref, dpool_ref, gpool_ref, gqkv_ref, gproj_ref, gup_ref, gdown_ref, gga_ref, ggb_ref,
    pooled, x, z3, rs3, a3, t, p, o, h3, z4, rs4, a4, m, gp, bias, cot, du, dh3, dh3b, do, dt, dtk,
):
    width, length = x.shape
    head = width // WORD_HEADS
    scale = head ** (-0.5)
    halves = [pl.ds(n * SPAN, SPAN) for n in range(length // SPAN)]
    pooled[...] = (pool_sum_ref[...] / cnt_ref[...]).astype(bf16)
    row = lax.broadcasted_iota(jnp.int32, (length, length), 0)
    col = lax.broadcasted_iota(jnp.int32, (length, length), 1)
    tri = jnp.where(row <= col, 1.0, 0.0).astype(bf16)
    sep = jnp.broadcast_to(sep_ref[...].astype(f32).astype(bf16), (16, length))
    doc_q = dot(sep, tri)[:1]
    doc_k = lax.dot_general(tri, sep, (((0,), (1,)), ((), ())), preferred_element_type=f32)[:, :1]
    bias[...] = jnp.where((row <= col) & (doc_k == doc_q), 0.0, NEGATIVE)
    cot[...] = cot_ref[...].astype(f32).T.astype(bf16)
    for at in halves:
        x[:, at] = lax.dot_general(
            wpool_ref[...], pooled[:, at], (((0,), (0,)), ((), ())), preferred_element_type=f32
        )
        z, rs = normed(x[:, at])
        z3[:, at] = z.astype(bf16)
        rs3[:, at] = rs
        a3[:, at] = (z * wide(ga_ref[...], SPAN)).astype(bf16)
        for n in range(3):
            rows = pl.ds(n * width, width)
            t[rows, at] = lax.dot_general(
                wqkv_ref[:, rows], a3[:, at], (((0,), (0,)), ((), ())), preferred_element_type=f32
            ).astype(bf16)
    for h in range(WORD_HEADS):
        k = t[pl.ds(width + h * head, head), :].T
        for n, at in enumerate(halves):
            seen = (n + 1) * SPAN
            keys = pl.ds(0, seen)
            q = t[pl.ds(h * head, head), at]
            s = dot(k[:seen], q) * scale + bias[keys, at]
            e = jnp.exp(s - jnp.max(s, 0, keepdims=True))
            w = e / jnp.sum(e, 0, keepdims=True)
            p[h, keys, at] = w
            o[pl.ds(h * head, head), at] = dot(t[pl.ds(2 * width + h * head, head), keys], w.astype(bf16)).astype(bf16)
    for at in halves:
        h3[:, at] = x[:, at] + lax.dot_general(
            wproj_ref[...], o[:, at], (((0,), (0,)), ((), ())), preferred_element_type=f32
        )
        z, rs = normed(h3[:, at])
        z4[:, at] = z.astype(bf16)
        rs4[:, at] = rs
        a4[:, at] = (z * wide(gb_ref[...], SPAN)).astype(bf16)
        for n in range(wup_ref.shape[1] // 256):
            rows = pl.ds(n * 256, 256)
            mm, gg = gelu_both(
                lax.dot_general(wup_ref[:, rows], a4[:, at], (((0,), (0,)), ((), ())), preferred_element_type=f32)
            )
            m[rows, at] = mm.astype(bf16)
            gp[rows, at] = gg.astype(bf16)
        out = h3[:, at] + lax.dot_general(
            wdown_ref[...], m[:, at], (((0,), (0,)), ((), ())), preferred_element_type=f32
        )
        out_ref[at, :] = out.T.astype(bf16)
        for n in range(wdown_ref.shape[0] // 256):
            rows = pl.ds(n * 256, 256)
            du[rows, at] = (dot(wdown_ref[rows, :], cot[:, at]) * gp[rows, at].astype(f32)).astype(bf16)
        dy = dot(wup_ref[...], du[:, at])
        z = z4[:, at].astype(f32)
        part = fold_lanes(dy * z)
        ggb_ref[...] = part if at is halves[0] else ggb_ref[...] + part
        dh3[:, at] = cot[:, at].astype(f32) + norm_back(dy, z, rs4[:, at], wide(gb_ref[...], SPAN))
        dh3b[:, at] = dh3[:, at].astype(bf16)
        do[:, at] = dot(wproj_ref[...], dh3b[:, at]).astype(bf16)
    gdown_ref[...] = dot_nt(m[...], cot[...]).astype(gdown_ref.dtype)
    gup_ref[...] = dot_nt(a4[...], du[...]).astype(gup_ref.dtype)
    gproj_ref[...] = dot_nt(o[...], dh3b[...]).astype(gproj_ref.dtype)
    for h in range(WORD_HEADS):
        q_rows = pl.ds(h * head, head)
        k_rows = pl.ds(width + h * head, head)
        v_rows = pl.ds(2 * width + h * head, head)
        v = t[v_rows, :].T
        for n in reversed(range(len(halves))):
            at = halves[n]
            seen = (n + 1) * SPAN
            keys = pl.ds(0, seen)
            w = p[h, keys, at]
            g = do[q_rows, at]
            dp = dot(v[:seen], g)
            ds = (w * (dp - jnp.sum(w * dp, 0, keepdims=True))).astype(bf16)
            dt[q_rows, at] = (dot(t[k_rows, keys], ds) * scale).astype(bf16)
            dk = dot_nt(t[q_rows, at], ds) * scale
            dv = dot_nt(g, w.astype(bf16))
            if n == len(halves) - 1:
                dtk[0] = dk
                dtk[1] = dv
            else:
                dtk[0, :, keys] += dk
                dtk[1, :, keys] += dv
        dt[k_rows, :] = dtk[0].astype(bf16)
        dt[v_rows, :] = dtk[1].astype(bf16)
    gqkv_ref[...] = dot_nt(a3[...], dt[...]).astype(gqkv_ref.dtype)
    for at in halves:
        dy = dot(wqkv_ref[...], dt[:, at])
        z = z3[:, at].astype(f32)
        part = fold_lanes(dy * z)
        gga_ref[...] = part if at is halves[0] else gga_ref[...] + part
        dx = dh3[:, at] + norm_back(dy, z, rs3[:, at], wide(ga_ref[...], SPAN))
        dh3b[:, at] = dx.astype(bf16)
        dpool_ref[:, at] = (dot(wpool_ref[...], dh3b[:, at]) / cnt_ref[:, at]).astype(bf16)
    gpool_ref[...] = dot_nt(pooled[...], dh3b[...]).astype(gpool_ref.dtype)


def word_layer(pool_sum, cnt, sep, cot, ga, gb, wpool, wqkv, wproj, wup, wdown, grad_type=f32):
    length, width = cot.shape
    inner = pool_sum.shape[0]
    hidden = wup.shape[1]
    vm = pltpu.VMEM
    return pl.pallas_call(
        word_kernel,
        out_shape=[
            jax.ShapeDtypeStruct((length, width), bf16),
            jax.ShapeDtypeStruct((inner, length), bf16),
            jax.ShapeDtypeStruct(wpool.shape, grad_type),
            jax.ShapeDtypeStruct(wqkv.shape, grad_type),
            jax.ShapeDtypeStruct(wproj.shape, grad_type),
            jax.ShapeDtypeStruct(wup.shape, grad_type),
            jax.ShapeDtypeStruct(wdown.shape, grad_type),
            jax.ShapeDtypeStruct((width, LANES), f32),
            jax.ShapeDtypeStruct((width, LANES), f32),
        ],
        scratch_shapes=[
            vm((inner, length), bf16), vm((width, length), f32), vm((width, length), bf16), vm((1, length), f32),
            vm((width, length), bf16), vm((3 * width, length), bf16), vm((WORD_HEADS, length, length), f32),
            vm((width, length), bf16), vm((width, length), f32), vm((width, length), bf16), vm((1, length), f32),
            vm((width, length), bf16), vm((hidden, length), bf16), vm((hidden, length), bf16),
            vm((length, length), f32), vm((width, length), bf16), vm((hidden, length), bf16),
            vm((width, length), f32), vm((width, length), bf16), vm((width, length), bf16),
            vm((3 * width, length), bf16), vm((2, width // WORD_HEADS, length), f32),
        ],
        compiler_params=pltpu.CompilerParams(vmem_limit_bytes=58 * 2**20),
        name="word_layer",
    )(pool_sum, cnt, sep, cot, ga, gb, wpool, wqkv, wproj, wup, wdown)


MESH = pl.DeviceIdType.MESH


def sides():
    chips = lax.axis_size("dp") // 2
    nx = math.isqrt(chips)
    return chips // nx, nx, lax.axis_size("fsdp")


def place():
    ny, nx, nz = sides()
    me = lax.axis_index("dp")
    return me // (2 * nx), (me // 2) % nx, me % 2, lax.axis_index("fsdp")


def device(y, x, c, z):
    return {"dp": (y * sides()[1] + x) * 2 + c, "fsdp": z}


def others():
    ny, nx, nz = sides()
    y, x, c, z = place()
    return [((y + j) % ny, (x + i) % nx) for j in range(ny) for i in range(nx) if j + i > 0]


def partners():
    ny, nx, nz = sides()
    y, x, c, z = place()
    found = [device(y, x, 1 - c, z)]
    found += [device(y, x, c, (z + k) % nz) for k in range(1, nz)]
    return found + [device(j, i, c, z) for j, i in others()]


def greet():
    barrier = pltpu.get_barrier_semaphore()
    for other in partners():
        pl.semaphore_signal(barrier, inc=1, device_id=other, device_id_type=MESH)


def greeted():
    pl.semaphore_wait(pltpu.get_barrier_semaphore(), len(partners()))


def remote(src, dst, sems, n, other):
    return pltpu.make_async_remote_copy(
        src_ref=src, dst_ref=dst, send_sem=sems.at[0, n], recv_sem=sems.at[1, n],
        device_id=other, device_id_type=MESH,
    )


def gather_copies():
    ny, nx, nz = sides()
    return nz - 1 + 1 + 4 * (nx - 1) + 4 * (ny - 1)


def gather_stages(ref, sems, wanted=(0, 1, 2, 3)):
    ny, nx, nz = sides()
    y, x, c, z = place()
    every = slice(None)
    half = ref.shape[4] // 2
    low, high = pl.ds(0, half), pl.ds(half, half)
    twin = device(y, x, 1 - c, z)
    plan = [[], [], [], []]
    plan[0] += [((y, x, c, z), device(y, x, c, (z + k) % nz)) for k in range(1, nz)]
    plan[1] += [((y, x, c, every, low), device(y, (x + k) % nx, c, z)) for k in range(1, nx)]
    plan[1] += [((y, x, c, every, high), device((y + k) % ny, x, c, z)) for k in range(1, ny)]
    plan[1] += [((y, x, c), twin)]
    plan[2] += [((y, every, c, every, low), device((y + k) % ny, x, c, z)) for k in range(1, ny)]
    plan[2] += [((every, x, c, every, high), device(y, (x + k) % nx, c, z)) for k in range(1, nx)]
    plan[2] += [((y, (x + k) % nx, c, every, low), twin) for k in range(1, nx)]
    plan[2] += [(((y + k) % ny, x, c, every, high), twin) for k in range(1, ny)]
    plan[3] += [(((y + k) % ny, every, c, every, low), twin) for k in range(1, ny)]
    plan[3] += [((every, (x + k) % nx, c, every, high), twin) for k in range(1, nx)]
    count = 0
    stages = []
    for n, part in enumerate(plan):
        copies = []
        for where, other in part:
            if n in wanted:
                copies.append(remote(ref.at[where], ref.at[where], sems, count, other))
            count += 1
        stages.append(copies)
    return stages


def gather_direct(ref, sems, wanted=(0, 1, 2)):
    ny, nx, nz = sides()
    y, x, c, z = place()
    twin = device(y, x, 1 - c, z)
    plan = [[((y, x, c, z), device(y, x, c, (z + k) % nz)) for k in range(1, nz)]]
    plan += [[((y, x, c), device(j, i, c, z)) for j, i in others()] + [((y, x, c), twin)]]
    plan += [[((j, i, c), twin) for j, i in others()]]
    count, stages = 0, []
    for n, part in enumerate(plan):
        copies = []
        for where, other in part:
            if n in wanted:
                copies.append(remote(ref.at[where], ref.at[where], sems, count, other))
            count += 1
        stages.append(copies)
    return stages


def start_all(copies):
    for copy in copies:
        copy.start()


def arrive_all(copies):
    for copy in copies:
        copy.wait_recv()


def sent_all(stages):
    for copies in stages:
        for copy in copies:
            copy.wait_send()


def lanes_to(v, n):
    return v if v.shape[1] == n else jnp.concatenate([v, jnp.zeros((v.shape[0], n - v.shape[1]), v.dtype)], 1)


def turned(v):
    return v.astype(f32).T.astype(bf16)


def scatter_copies():
    ny, nx, nz = sides()
    return 1 + 2 * (nx - 1) + 2 * (ny - 1) + nz - 1


def scatter_scratch(rows, lanes):
    ny, nx, nz = sides()
    half = rows // 2
    shapes = (
        (ny, nx, nz, rows, lanes), (ny, nx, nz, rows, lanes), (nx - 1, ny, nz, half, lanes),
        (ny - 1, nx, nz, half, lanes), (ny - 1, nz, half, lanes), (nx - 1, nz, half, lanes), (nz - 1, rows, lanes),
    )
    return [pltpu.VMEM(shape, bf16) for shape in shapes] + [pltpu.SemaphoreType.DMA((2, scatter_copies()))]


def scatter_stage(n, send, work):
    acc, twin_in, one_low, one_high, two_low, two_high, last_in, sems = work
    ny, nx, nz = sides()
    y, x, c, z = place()
    half = acc.shape[3] // 2
    low, high, every = pl.ds(0, half), pl.ds(half, half), slice(None)
    plan = [[], [], [], []]
    plan[0] += [(send, (every, every, 1 - c), twin_in, device(y, x, 1 - c, z))]
    plan[1] += [
        (acc, (every, (x + k) % nx, every, low), one_low.at[k - 1], device(y, (x + k) % nx, c, z)) for k in range(1, nx)
    ]
    plan[1] += [
        (acc, ((y + k) % ny, every, every, high), one_high.at[k - 1], device((y + k) % ny, x, c, z)) for k in range(1, ny)
    ]
    plan[2] += [
        (acc, ((y + k) % ny, x, every, low), two_low.at[k - 1], device((y + k) % ny, x, c, z)) for k in range(1, ny)
    ]
    plan[2] += [
        (acc, (y, (x + k) % nx, every, high), two_high.at[k - 1], device(y, (x + k) % nx, c, z)) for k in range(1, nx)
    ]
    plan[3] += [(acc, (y, x, (z + k) % nz), last_in.at[k - 1], device(y, x, c, (z + k) % nz)) for k in range(1, nz)]
    first = sum(len(p) for p in plan[:n])
    return [remote(src.at[at], dst, sems, first + i, other) for i, (src, at, dst, other) in enumerate(plan[n])]


def direct_scratch(rows, lanes):
    ny, nx, nz = sides()
    shapes = (
        (ny, nx, nz, rows, lanes), (ny, nx, nz, rows, lanes), (ny * nx - 1, nz, rows, lanes), (nz - 1, rows, lanes)
    )
    count = 1 + ny * nx - 1 + nz - 1
    return [pltpu.VMEM(shape, bf16) for shape in shapes] + [pltpu.SemaphoreType.DMA((2, count))]


def direct_stage(n, send, work):
    acc, twin_in, near_in, last_in, sems = work
    ny, nx, nz = sides()
    y, x, c, z = place()
    if n == 0:
        return [remote(send.at[:, :, 1 - c], twin_in, sems, 0, device(y, x, 1 - c, z))]
    if n == 1:
        return [
            remote(acc.at[j, i], near_in.at[k], sems, 1 + k, device(j, i, c, z)) for k, (j, i) in enumerate(others())
        ]
    return [
        remote(acc.at[y, x, (z + k) % nz], last_in.at[k - 1], sems, ny * nx + k - 1, device(y, x, c, (z + k) % nz))
        for k in range(1, nz)
    ]


def direct_sum(n, own, work, out):
    acc, twin_in, near_in, last_in, sems = work
    ny, nx, nz = sides()
    y, x, c, z = place()
    if n == 0:
        for b in range(ny):
            for a in range(nx):
                for k in range(nz):
                    acc[b, a, k] = own(b, a, k) + twin_in[b, a, k]
    elif n == 1:
        for k in range(nz):
            total = acc[y, x, k].astype(f32) + sum(near_in[i, k].astype(f32) for i in range(ny * nx - 1))
            acc[y, x, k] = total.astype(bf16)
    else:
        out[...] = acc[y, x, z].astype(f32) + sum(last_in[i].astype(f32) for i in range(nz - 1))


def scatter_sum(n, own, work, out):
    acc, twin_in, one_low, one_high, two_low, two_high, last_in, sems = work
    ny, nx, nz = sides()
    y, x, c, z = place()
    half = acc.shape[3] // 2
    low, high = pl.ds(0, half), pl.ds(half, half)
    if n == 0:
        for b in range(ny):
            for a in range(nx):
                for k in range(nz):
                    acc[b, a, k] = own(b, a, k) + twin_in[b, a, k]
    elif n == 1:
        for k in range(nz):
            for b in range(ny):
                acc[b, x, k, low] += sum(one_low[i, b, k] for i in range(nx - 1))
            for a in range(nx):
                acc[y, a, k, high] += sum(one_high[i, a, k] for i in range(ny - 1))
    elif n == 2:
        for k in range(nz):
            acc[y, x, k, low] += sum(two_low[i, k] for i in range(ny - 1))
            acc[y, x, k, high] += sum(two_high[i, k] for i in range(nx - 1))
    else:
        out[...] = acc[y, x, z].astype(f32) + sum(last_in[i].astype(f32) for i in range(nz - 1))


def gelu_twice(u):
    s = u * u
    t = jnp.tanh(u * (GELU_A + (GELU_A * GELU_B) * s))
    a = 1.0 + t
    m = u * a
    return m, a + m * ((1.0 - t) * (GELU_A + (3.0 * GELU_A * GELU_B) * s))


def shift_of(letters):
    return letters.bit_length() - 1


def twin_owner(letters):
    lane = lax.broadcasted_iota(jnp.int32, (letters, 2 * LANES), 1)
    return lax.shift_right_logical(lane & (LANES - 1), shift_of(letters))


def twin_mask(letters):
    bits = shift_of(letters)
    a = lax.shift_right_logical(lax.broadcasted_iota(jnp.int32, (LANES, 2 * LANES), 0), bits)
    b = lax.shift_right_logical(lax.broadcasted_iota(jnp.int32, (LANES, 2 * LANES), 1) & (LANES - 1), bits)
    return jnp.where(a == b, 1.0, 0.0).astype(bf16)


def twin_blocks(v):
    half = v.shape[0] // 2
    none = jnp.zeros((half, v.shape[1]), v.dtype)
    return jnp.concatenate([jnp.concatenate([v[:half], none], 1), jnp.concatenate([none, v[half:]], 1)], 0)


def stacked(v):
    return jnp.concatenate([v[:, :LANES], v[:, LANES:]], 0)


def char_units():
    for g in range(BATCH // LANES):
        for h in range(CHAR_HEADS // 2):
            yield h, pl.ds(g * LANES, LANES), pl.ds(2 * g * LANES, 2 * LANES)


def patterns(near, far, letters):
    words, tokens = near.shape
    bits = shift_of(letters)
    word = lax.broadcasted_iota(jnp.int32, (words, tokens), 0)
    token = lax.shift_right_logical(lax.broadcasted_iota(jnp.int32, (words, tokens), 1), bits)
    near[...] = jnp.where(word == token, 1.0, 0.0).astype(bf16)
    if far is not None:
        token = lax.shift_right_logical(lax.broadcasted_iota(jnp.int32, far.shape, 0), bits)
        word = lax.broadcasted_iota(jnp.int32, far.shape, 1)
        far[...] = jnp.where(word == token, 1.0, 0.0).astype(bf16)


def own_words(s, per, v):
    words = LANES // per
    out = v[:, :words]
    for i in range(1, per):
        out = jnp.where(s % per == i, v[:, i * words : (i + 1) * words], out)
    return out


def valid_tokens(letters, counts):
    slot = lax.broadcasted_iota(jnp.int32, counts.shape, 1) & (letters - 1)
    return jnp.where(slot < counts, 1.0, 0.0)


def forward_first(s, per, x_ref, cnt_ref, tok_ref, rs1_ref, x_all, z1_all, near):
    counts = jnp.broadcast_to(own_words(s, per, cnt_ref[...].astype(f32)), (16, near.shape[0])).astype(bf16)
    tok_ref[s] = dot(counts, near[...])[:1].astype(jnp.int32)
    x = x_ref[...].astype(f32).T
    x_all[s] = x.astype(bf16)
    z1, rs1 = normed(x)
    z1_all[s] = z1.astype(bf16)
    rs1_ref[s] = rs1


def forward_attention(s, letters, tok_ref, ga_ref, wqkv_t, wproj_t, t_ref, o_ref, p_ref, z1_ref, x_all, z1_all, h1_all, j):
    width = o_ref.shape[1]
    pair = 2 * (width // CHAR_HEADS)
    scale = (width // CHAR_HEADS) ** (-0.5)
    owner, blocks = twin_owner(letters), twin_mask(letters)
    key_slot = lax.broadcasted_iota(jnp.int32, (letters, 2 * LANES), 0)
    z1 = z1_all[s]
    z1_ref[j] = z1
    a1 = (z1.astype(f32) * wide(ga_ref[...], BATCH)).astype(bf16)
    t_ref[j] = dot(wqkv_t[...], a1).astype(bf16)
    units = list(char_units())
    scores = []
    for h, lanes, lanes2 in units:
        q = twin_blocks(t_ref[j, pl.ds(h * pair, pair), lanes])
        k = t_ref[j, pl.ds(width + h * pair, pair), lanes].T
        scores.append(pick_own(dot(k, q), owner, letters))
    probs = []
    for (h, lanes, lanes2), score in zip(units, scores):
        counts = tok_ref[s, :, lanes]
        allowed = key_slot < jnp.concatenate([counts, counts], 1)
        score = jnp.where(allowed, score * scale, NEGATIVE)
        e = jnp.exp(score - jnp.max(score, 0, keepdims=True))
        p = e / jnp.sum(e, 0, keepdims=True)
        p_ref[j, pl.ds(h * letters, letters), lanes2] = p
        probs.append(p)
    for (h, lanes, lanes2), p in zip(units, probs):
        v = twin_blocks(t_ref[j, pl.ds(2 * width + h * pair, pair), lanes])
        o = dot(v, stacked(spread_own(p.astype(bf16), blocks, letters)))
        o_ref[j, pl.ds(h * pair, pair), lanes] = o.astype(bf16)
    h1_all[s] = x_all[s].astype(f32) + dot(wproj_t[...], o_ref[j])


def forward_feed(
    s, letters, per, tok_ref, gb_ref, wup_t, wdown_t, z2_ref, rs2_ref, m_ref, slope_ref, pool_ref, h1_all, far, a2_ref
):
    z2, rs2 = normed(h1_all[s])
    z2_ref[0] = z2.astype(bf16)
    rs2_ref[0] = rs2
    a2_ref[...] = (z2 * wide(gb_ref[...], BATCH)).astype(bf16)
    valid = valid_tokens(letters, tok_ref[s])
    strips = [
        (pl.ds(at, SPAN), pl.ds(n * 256, 256)) for at in range(0, BATCH, SPAN) for n in range(wup_t.shape[0] // 256)
    ]

    def close(cols):
        h2 = h1_all[s, :, cols] + dot(wdown_t[...], m_ref[0, :, cols])
        kept = (h2 * valid[:, cols.start : cols.start + cols.size]).astype(bf16)
        return dot(kept, far[cols, :])

    part = 0.0
    ahead = dot(wup_t[strips[0][1], :], a2_ref[:, strips[0][0]])
    for i, (cols, rows) in enumerate(strips):
        u = ahead
        if i + 1 < len(strips):
            ahead = dot(wup_t[strips[i + 1][1], :], a2_ref[:, strips[i + 1][0]])
        if rows.start == 0 and cols.start > 0:
            part += close(pl.ds(cols.start - SPAN, SPAN))
        m, slope = gelu_twice(u)
        m_ref[0, rows, cols] = m.astype(bf16)
        slope_ref[0, rows, cols] = slope.astype(bf16)
    part += close(pl.ds(BATCH - SPAN, SPAN))
    words = LANES // per
    for i in range(per):
        moved = part if i == 0 else pltpu.roll(part, i * words, 1)

        @pl.when(s % per == i)
        def _():
            pool_ref[...] = moved if i == 0 else pool_ref[...] + moved


def backward_feed(
    s, letters, per, dp_ref, tok_ref, gb_ref, wup, wdown, z2_ref, rs2_ref, m_ref, slope_ref, gup, gdown_t, dh1_all, spare
):
    deep = spare.shape[1]

    @pl.when(s == 0)
    def _():
        gdown_t[...] = jnp.zeros_like(gdown_t)
        gup[...] = jnp.zeros_like(gup)

    word = lax.broadcasted_iota(jnp.int32, (LANES, BATCH), 0) - (s % per) * (BATCH // letters)
    token = lax.broadcasted_iota(jnp.int32, (LANES, BATCH), 1)
    mine = lax.shift_right_logical(token, shift_of(letters)) == word
    scatter = jnp.where(mine & ((token & (letters - 1)) < tok_ref[0]), 1.0, 0.0).astype(bf16)
    dh2 = dot(dp_ref[...], scatter)
    dh2b = dh2.astype(bf16)
    for n in range(wdown.shape[0] // 256):
        rows = pl.ds(n * 256, 256)
        du = (dot(wdown[rows, :], dh2b) * slope_ref[0, rows, :].astype(f32)).astype(bf16)
        spare[n * 256 // deep, pl.ds(n * 256 % deep, 256), :] = du
    pieces = []
    for n in range(0, wdown.shape[0], deep):
        size = min(deep, wdown.shape[0] - n)
        pieces.append((pl.ds(n, size), (n // deep, pl.ds(0, size))))
    dy = sum(dot(wup[:, cols], spare[at]) for cols, at in pieces)
    gdown_t[...] += dot_nt(dh2b, m_ref[0])
    for cols, at in pieces:
        gup[:, cols] += dot_nt(z2_ref[0], spare[at])
    z = z2_ref[0].astype(f32)
    dh1 = dh2 + norm_back(dy, z, rs2_ref[0], wide(gb_ref[...], BATCH))
    dh1_all[s] = dh1.astype(bf16)


def backward_attention(s, letters, wproj, t_ref, o_ref, p_ref, z1_ref, gqkv_t, gproj_t, dh1_all, dt_all, do_ref, j):
    width = wproj.shape[0]
    pair = 2 * (width // CHAR_HEADS)
    scale = (width // CHAR_HEADS) ** (-0.5)
    owner, blocks = twin_owner(letters), twin_mask(letters)

    @pl.when(s == 0)
    def _():
        gproj_t[...] = jnp.zeros_like(gproj_t)
        gqkv_t[...] = jnp.zeros_like(gqkv_t)

    dh1b = dh1_all[s]
    do_ref[...] = dot(wproj[...], dh1b).astype(bf16)
    gproj_t[...] += dot_nt(dh1b, o_ref[j])
    units = list(char_units())
    grads = []
    for h, lanes, lanes2 in units:
        v = t_ref[j, pl.ds(2 * width + h * pair, pair), lanes].T
        grads.append(pick_own(dot(v, twin_blocks(do_ref[pl.ds(h * pair, pair), lanes])), owner, letters))
    spread = []
    for (h, lanes, lanes2), dp in zip(units, grads):
        p = p_ref[j, pl.ds(h * letters, letters), lanes2]
        ds = p * (dp - jnp.sum(p * dp, 0, keepdims=True))
        spread.append((spread_own(p.astype(bf16), blocks, letters), spread_own(ds.astype(bf16), blocks, letters)))
    for (h, lanes, lanes2), (pb, dsb) in zip(units, spread):
        q_rows = pl.ds(h * pair, pair)
        k_rows = pl.ds(width + h * pair, pair)
        v_rows = pl.ds(2 * width + h * pair, pair)
        q = twin_blocks(t_ref[j, q_rows, lanes])
        k = twin_blocks(t_ref[j, k_rows, lanes])
        do = twin_blocks(do_ref[q_rows, lanes])
        dt_all[s, q_rows, lanes] = (dot(k, stacked(dsb)) * scale).astype(bf16)
        dt_all[s, k_rows, lanes] = (dot_nt(q, dsb) * scale).astype(bf16)
        dt_all[s, v_rows, lanes] = dot_nt(do, pb).astype(bf16)
    gqkv_t[...] += dot_nt(dt_all[s], z1_ref[j])


def backward_last(s, ga_ref, wqkv, z1_ref, rs1_ref, cg_ref, dh1_all, dt_all, j):
    dy = dot(wqkv[...], dt_all[s])
    z = z1_ref[j].astype(f32)
    dx = dh1_all[s].astype(f32) + norm_back(dy, z, rs1_ref[j], wide(ga_ref[...], BATCH))
    cg_ref[pl.ds(j * BATCH, BATCH), :] = dx.T.astype(bf16)


def pack_first(slot, qkv, proj_t, gains):
    r = qkv.shape[0]
    slot[pl.ds(0, r), :] = jnp.concatenate([qkv[...], turned(lanes_to(proj_t[...], LANES))[:r]], 1)
    none = jnp.zeros((slot.shape[0] - r - gains.shape[0], LANES), f32)
    slot[pl.ds(r, slot.shape[0] - r), :] = jnp.concatenate([gains[...], none], 0).astype(bf16)


def pack_second(slot, up, down_t, pool):
    r, n = up.shape[0], down_t.shape[0]
    slot[pl.ds(0, r), :] = up[...]
    for i in range(down_t.shape[1] // LANES):
        slot[pl.ds(r + i * n, n), :] = down_t[:, pl.ds(i * LANES, LANES)]
    slot[pl.ds(2 * r, r), :] = lanes_to(pool[...], LANES)


def pack_words(slots, qkv_t, proj_t, up, down_t):
    slots[0] = turned(jnp.concatenate([qkv_t[...], proj_t[...]], 0))
    slots[1] = up[...]
    n, lanes = down_t.shape[0], up.shape[1]
    for i in range(down_t.shape[1] // lanes):
        slots[2, pl.ds(i * n, n), :] = down_t[:, pl.ds(i * lanes, lanes)]


def seats():
    ny, nx, nz = sides()
    for d in range(2 * ny * nx):
        yield d, (d // (2 * nx), (d // 2) % nx, d % 2)


def unpack_first(ref, wqkv_t, wproj_t, wqkv, wproj, cga, cgb, wga, wgb):
    ny, nx, nz = sides()
    nd = 2 * ny * nx
    r = wqkv.shape[0] // nz
    a, b, gc, gw = wqkv_t.shape[0] // nd, wproj_t.shape[0] // nd, cga.shape[0] // nd, wga.shape[0] // nd
    for d, at in seats():
        t = turned(ref[at + (slice(None), pl.ds(0, r))].reshape(nz * r, LANES))
        wqkv_t[pl.ds(d * a, a), :] = t[:a]
        wproj_t[pl.ds(d * b, b), :] = t[a:]
        g = ref[at + (0, pl.ds(r, 16))].astype(f32).T
        one, two = (jnp.broadcast_to(g[:, i : i + 1], (LANES, LANES)) for i in range(2))
        cga[pl.ds(d * gc, gc), :] = one[:gc]
        cgb[pl.ds(d * gc, gc), :] = one[gc : 2 * gc]
        wga[pl.ds(d * gw, gw), :] = one[2 * gc : 2 * gc + gw]
        wgb[pl.ds(d * gw, gw), :] = two[:gw]
    wqkv[...] = turned(wqkv_t[...])
    wproj[...] = turned(wproj_t[...])


def unpack_second(ref, wup_t, wdown_t, wup, wdown, pool_t):
    ny, nx, nz = sides()
    nd = 2 * ny * nx
    r, n, p = wup.shape[0] // nz, wdown_t.shape[0] // nd, pool_t.shape[0] // nd
    deep = wdown_t.shape[1] // nz
    for d, at in seats():
        up = ref[at + (slice(None), pl.ds(0, r))].reshape(nz * r, LANES)
        wup[:, pl.ds(d * LANES, LANES)] = up
        wup_t[pl.ds(d * LANES, LANES), :] = turned(up)
        for z in range(nz):
            for i in range(deep // LANES):
                wdown_t[pl.ds(d * n, n), pl.ds(z * deep + i * LANES, LANES)] = ref[at + (z, pl.ds(r + i * n, n))] * 0.5
        t = turned(ref[at + (slice(None), pl.ds(2 * r, r))].reshape(nz * r, LANES))
        pool_t[pl.ds(d * p, p), :] = t[:p]
    wdown[...] = turned(wdown_t[...])


def pack_first_grads(slots, gqkv_t, gproj_t, ga, wqkv_t, gup, wup, gwga, gwgb):
    ny, nx, nz = sides()
    nd = 2 * ny * nx
    width = gqkv_t.shape[1]
    r = width // nz
    tail = slots.shape[4] - r
    a, b, gc, gw = gqkv_t.shape[0] // nd, gproj_t.shape[0] // nd, width // nd, gwga.shape[1] // nd
    char_a = jnp.sum(gqkv_t[...] * wqkv_t[...].astype(f32), 0, keepdims=True)
    char_a = jnp.broadcast_to(char_a, (8, width)).T[:, :1]
    char_b = jnp.sum(gup[...] * wup[...].astype(f32), 1, keepdims=True)
    word_a, word_b = (g[...].T[:, :1] for g in (gwga, gwgb))
    gain = ga[...].T[:1]
    spot = lax.broadcasted_iota(jnp.int32, (LANES, nz * tail), 1) % tail
    none = jnp.zeros((LANES - gw, 1), f32)
    for d, at in seats():
        t = jnp.concatenate([gqkv_t[pl.ds(d * a, a), :] * gain, gproj_t[pl.ds(d * b, b), :]], 0)
        slots[at + (slice(None), pl.ds(0, r))] = t.T.astype(bf16).reshape(nz, r, LANES)
        char, word = slice(d * gc, (d + 1) * gc), slice(d * gw, (d + 1) * gw)
        one = jnp.concatenate([char_a[char], char_b[char], word_a[word]], 0)
        two = jnp.concatenate([word_b[word], none], 0)
        side = jnp.where(spot == 0, one, jnp.where(spot == 1, two, 0.0))
        slots[at + (slice(None), pl.ds(r, tail))] = side.T.astype(bf16).reshape(nz, tail, LANES)


def pack_second_grads(slots, gup, gdown_t, gb, gpool_t):
    ny, nx, nz = sides()
    nd = 2 * ny * nx
    width = gup.shape[0]
    r, n, p = width // nz, gdown_t.shape[0] // nd, gpool_t.shape[0] // nd
    deep = gdown_t.shape[1] // nz
    none = jnp.zeros((LANES - p, width), f32)
    for d, at in seats():
        up = gup[:, pl.ds(d * LANES, LANES)] * gb[...]
        slots[at + (slice(None), pl.ds(0, r))] = up.astype(bf16).reshape(nz, r, LANES)
        for z in range(nz):
            for i in range(deep // LANES):
                down = gdown_t[pl.ds(d * n, n), pl.ds(z * deep + i * LANES, LANES)] * 0.5
                slots[at + (z, pl.ds(r + i * n, n))] = down.astype(bf16)
        t = jnp.concatenate([gpool_t[pl.ds(d * p, p), :].astype(f32), none], 0)
        slots[at + (slice(None), pl.ds(2 * r, r))] = t.T.astype(bf16).reshape(nz, r, LANES)


def unpack_mixed(ref, qkv_t, proj_t):
    nd, nz, r, lanes = ref.shape
    a, b = qkv_t.shape[0] // nd, proj_t.shape[0] // nd
    for d in range(nd):
        t = turned(ref[d].reshape(nz * r, lanes))
        qkv_t[pl.ds(d * a, a), :] = t[:a]
        proj_t[pl.ds(d * b, b), :] = t[a:]


def unpack_up(ref, up_t, up):
    nd, nz, r, lanes = ref.shape
    for d in range(nd):
        piece = ref[d].reshape(nz * r, lanes)
        up[:, pl.ds(d * lanes, lanes)] = piece
        up_t[pl.ds(d * lanes, lanes), :] = turned(piece)


def unpack_down(ref, down_t):
    nd, nz, r, lanes = ref.shape
    n, deep = down_t.shape[0] // nd, down_t.shape[1] // nz
    for d in range(nd):
        for z in range(nz):
            for i in range(deep // lanes):
                down_t[pl.ds(d * n, n), pl.ds(z * deep + i * lanes, lanes)] = ref[d, z, pl.ds(i * n, n), :] * 0.5


def word_gathered_kernel(
    pool_sum_ref, cnt_ref, sep_ref, cot_ref, ga_ref, gb_ref, wpool_t, far0, far1, far2,
    out_ref, dpool_ref, gpool_ref, gone0, gone1, gone2, gga_ref, ggb_ref,
    pooled, x, z3, rs3, a3, t, p, o, h3, z4, rs4, a4, m, slope, bias, cot, du, dh3, dh3b, do, dt, dtk,
    wqkv_t, wproj_t, wup_t, wdown_t, wqkv, wproj, wup, wdown, wpool, gqkv_t, gproj_t,
    all0, all1, all2, send0, send1, send2, in_sems, out_sems,
):
    width, length = x.shape
    head = width // WORD_HEADS
    scale = head ** (-0.5)
    nd, nz, r, lanes = send0.shape
    halves = [pl.ds(n * SPAN, SPAN) for n in range(length // SPAN)]
    fetch = [pltpu.make_async_copy(a, b, in_sems.at[n]) for n, (a, b) in enumerate(((far0, all0), (far1, all1), (far2, all2)))]
    leave = [pltpu.make_async_copy(a, b, out_sems.at[n]) for n, (a, b) in enumerate(((send0, gone0), (send1, gone1), (send2, gone2)))]
    start_all(fetch)
    counts = cnt_ref[...].astype(f32)
    pooled[...] = (pool_sum_ref[...] / counts).astype(bf16)
    row = lax.broadcasted_iota(jnp.int32, (length, length), 0)
    col = lax.broadcasted_iota(jnp.int32, (length, length), 1)
    tri = jnp.where(row <= col, 1.0, 0.0).astype(bf16)
    sep = jnp.broadcast_to(sep_ref[...].astype(f32).astype(bf16), (16, length))
    doc_q = dot(sep, tri)[:1]
    doc_k = jnp.broadcast_to(doc_q, (8, length)).T[:, :1]
    bias[...] = jnp.where((row <= col) & (doc_k == doc_q), 0.0, NEGATIVE)
    cot[...] = turned(cot_ref[...])
    x[...] = dot(wpool_t[...], pooled[...])
    z, rs = normed(x[...])
    z3[...] = z.astype(bf16)
    rs3[...] = rs
    a3[...] = (z * wide(ga_ref[...], length)).astype(bf16)
    fetch[0].wait()
    unpack_mixed(all0, wqkv_t, wproj_t)
    t[...] = dot(wqkv_t[...], a3[...]).astype(bf16)
    units = [(h, n) for h in range(WORD_HEADS) for n in range(len(halves))]

    def score(h, n):
        k = t[pl.ds(width + h * head, head), pl.ds(0, (n + 1) * SPAN)].T
        return dot(k, t[pl.ds(h * head, head), halves[n]])

    def mix(h, n, w):
        keys = pl.ds(0, (n + 1) * SPAN)
        o[pl.ds(h * head, head), halves[n]] = dot(t[pl.ds(2 * width + h * head, head), keys], w).astype(bf16)

    ahead, behind = score(*units[0]), None
    for i, (h, n) in enumerate(units):
        s = ahead
        if i + 1 < len(units):
            ahead = score(*units[i + 1])
        keys = pl.ds(0, (n + 1) * SPAN)
        s = s * scale + bias[keys, halves[n]]
        e = jnp.exp(s - jnp.max(s, 0, keepdims=True))
        w = e * (1.0 / jnp.sum(e, 0, keepdims=True))
        p[h, keys, halves[n]] = w
        if behind is not None:
            mix(*behind)
        behind = (h, n, w.astype(bf16))
    mix(*behind)
    fetch[1].wait()
    unpack_up(all1, wup_t, wup)
    h3[...] = x[...] + dot(wproj_t[...], o[...])
    z, rs = normed(h3[...])
    z4[...] = z.astype(bf16)
    rs4[...] = rs
    a4[...] = (z * wide(gb_ref[...], length)).astype(bf16)
    for n in range(wup_t.shape[0] // 256):
        rows = pl.ds(n * 256, 256)
        mm, gg = gelu_twice(dot(wup_t[rows, :], a4[...]))
        m[rows, :] = mm.astype(bf16)
        slope[rows, :] = gg.astype(bf16)
    fetch[2].wait()
    unpack_down(all2, wdown_t)
    wdown[...] = turned(wdown_t[...])
    for n in range(wdown.shape[0] // 256):
        rows = pl.ds(n * 256, 256)
        du[rows, :] = (dot(wdown[rows, :], cot[...]) * slope[rows, :].astype(f32)).astype(bf16)
    out = h3[...] + dot(wdown_t[...], m[...])
    out_ref[...] = out.T.astype(bf16)
    dy = dot(wup[...], du[...])
    z = z4[...].astype(f32)
    ggb_ref[...] = jnp.broadcast_to(jnp.sum(fold_lanes(dy * z).T, 0, keepdims=True), ggb_ref.shape)
    dh3[...] = cot[...].astype(f32) + norm_back(dy, z, rs4[...], wide(gb_ref[...], length))
    dh3b[...] = dh3[...].astype(bf16)
    wproj[...] = turned(wproj_t[...])
    do[...] = dot(wproj[...], dh3b[...]).astype(bf16)
    n = width // nd
    deep = m.shape[0] // nz
    for z in range(nz):
        for i in range(deep // lanes):
            g = (dot_nt(cot[...], m[pl.ds(z * deep + i * lanes, lanes), :]) * 0.5).astype(bf16)
            for d in range(nd):
                send2[d, z, pl.ds(i * n, n), :] = g[d * n : (d + 1) * n]
    leave[2].start()
    for d in range(nd):
        g = dot_nt(a4[...], du[pl.ds(d * lanes, lanes), :]).astype(bf16)
        send1[d] = g.reshape(nz, r, lanes)
    leave[1].start()
    gproj_t[...] = dot_nt(dh3b[...], o[...]).astype(bf16)
    last = len(halves) - 1
    units = [(h, n) for h in range(WORD_HEADS) for n in reversed(range(len(halves)))]

    def rows_of(kind, h):
        return pl.ds(kind * width + h * head, head)

    def upstream(h, n):
        return dot(t[rows_of(2, h), pl.ds(0, (n + 1) * SPAN)].T, do[rows_of(0, h), halves[n]])

    def spread(h, n, ds, w):
        keys, at = pl.ds(0, (n + 1) * SPAN), halves[n]
        dt[rows_of(0, h), at] = (dot(t[rows_of(1, h), keys], ds) * scale).astype(bf16)
        dk = dot_nt(t[rows_of(0, h), at], ds) * scale
        dv = dot_nt(do[rows_of(0, h), at], w)
        if n == last:
            dtk[0] = dk
            dtk[1] = dv
        else:
            dtk[0, :, keys] += dk
            dtk[1, :, keys] += dv
        if n == 0:
            dt[rows_of(1, h), :] = dtk[0].astype(bf16)
            dt[rows_of(2, h), :] = dtk[1].astype(bf16)

    ahead, behind = upstream(*units[0]), None
    for i, (h, n) in enumerate(units):
        dp = ahead
        if i + 1 < len(units):
            ahead = upstream(*units[i + 1])
        w = p[h, pl.ds(0, (n + 1) * SPAN), halves[n]]
        ds = (w * (dp - jnp.sum(w * dp, 0, keepdims=True))).astype(bf16)
        if behind is not None:
            spread(*behind)
        behind = (h, n, ds, w.astype(bf16))
    spread(*behind)
    for n in range(3):
        part = pl.ds(n * width, width)
        gqkv_t[part, :] = dot_nt(dt[part, :], a3[...]).astype(bf16)
    a, b = gqkv_t.shape[0] // nd, gproj_t.shape[0] // nd
    for d in range(nd):
        g = turned(jnp.concatenate([gqkv_t[pl.ds(d * a, a), :], gproj_t[pl.ds(d * b, b), :]], 0))
        send0[d] = g.reshape(nz, r, lanes)
    leave[0].start()
    wqkv[...] = turned(wqkv_t[...])
    dy = dot(wqkv[...], dt[...])
    z = z3[...].astype(f32)
    gga_ref[...] = jnp.broadcast_to(jnp.sum(fold_lanes(dy * z).T, 0, keepdims=True), gga_ref.shape)
    dx = dh3[...] + norm_back(dy, z, rs3[...], wide(ga_ref[...], length))
    dh3b[...] = dx.astype(bf16)
    wpool[...] = turned(wpool_t[...])
    dpool_ref[...] = (dot(wpool[...], dh3b[...]) / counts).astype(bf16)
    gpool_ref[...] = dot_nt(dh3b[...], pooled[...]).astype(bf16)
    for copy in leave:
        copy.wait()


def word_gathered(pool_sum, cnt, sep, cot, ga, gb, pool_t, *gathered):
    length, width = cot.shape
    inner = pool_sum.shape[0]
    nd, nz, r, lanes = gathered[0].shape
    hidden = nd * lanes
    vm = pltpu.VMEM
    near, far = pl.BlockSpec(memory_space=pltpu.VMEM), pl.BlockSpec(memory_space=pl.ANY)
    return pl.pallas_call(
        word_gathered_kernel,
        in_specs=[near] * 7 + [far] * 3,
        out_specs=[near] * 3 + [far] * 3 + [near] * 2,
        out_shape=[
            jax.ShapeDtypeStruct((length, width), bf16),
            jax.ShapeDtypeStruct((inner, length), bf16),
            jax.ShapeDtypeStruct((width, inner), bf16),
            *(jax.ShapeDtypeStruct(g.shape, bf16) for g in gathered),
            jax.ShapeDtypeStruct((8, width), f32),
            jax.ShapeDtypeStruct((8, width), f32),
        ],
        scratch_shapes=[
            vm((inner, length), bf16), vm((width, length), f32), vm((width, length), bf16), vm((1, length), f32),
            vm((width, length), bf16), vm((3 * width, length), bf16), vm((WORD_HEADS, length, length), f32),
            vm((width, length), bf16), vm((width, length), f32), vm((width, length), bf16), vm((1, length), f32),
            vm((width, length), bf16), vm((hidden, length), bf16), vm((hidden, length), bf16),
            vm((length, length), f32), vm((width, length), bf16), vm((hidden, length), bf16),
            vm((width, length), f32), vm((width, length), bf16), vm((width, length), bf16),
            vm((3 * width, length), bf16), vm((2, width // WORD_HEADS, length), f32),
            vm((3 * width, width), bf16), vm((width, width), bf16), vm((hidden, width), bf16), vm((width, hidden), bf16),
            vm((width, 3 * width), bf16), vm((width, width), bf16), vm((width, hidden), bf16), vm((hidden, width), bf16),
            vm((inner, width), bf16), vm((3 * width, width), bf16), vm((width, width), bf16),
        ] + [vm(g.shape, bf16) for g in gathered] * 2 + [pltpu.SemaphoreType.DMA((3,)), pltpu.SemaphoreType.DMA((3,))],
        compiler_params=pltpu.CompilerParams(vmem_limit_bytes=VMEM_BYTES),
        name="word_gathered",
    )(pool_sum, cnt, sep, cot, ga, gb, pool_t, *gathered)


GATHER_PLAN = {
    "first": (1, 3, 6, 8),
    "second": (3, 6, 9, 13, 15),
    0: (6, 11, 14, 17, 19),
    1: (9, 14, 17, 20, 22),
    2: (11, 17, 20, 22, 24),
}
SCATTER_PLAN = {
    0: (1, 2, 4, 6, 8),
    1: (2, 5, 7, 9, 11),
    2: (3, 8, 10, 12, 15),
    "second": (8, 11, 13, 15, 18),
    "first": (16, 18, 22, 24),
}
FORWARD_HALVES = (1, 2, 1)
BACKWARD_HALVES = (1, 1, 1)


def planned(plan, event, steps):
    return [(at // 8) * steps + (at % 8) * steps // 8 for at in plan[event]]


def starts(halves, steps):
    ends = [0]
    for h in halves:
        ends.append(ends[-1] + steps // h)
    return ends


def step_of(tick, halves, steps):
    phase = min(tick // steps, 2)
    inside = tick - phase * steps
    return starts(halves, steps)[phase] + inside // halves[phase], inside % halves[phase]


def forward_gather_kernel(
    letters, steps, x_ref, cnt_ref, s_qkv, s_proj, s_gains, s_up, s_down, s_pool, w_qkv, w_proj, w_up, w_down,
    tok_ref, t_ref, o_ref, p_ref, z1_ref, rs1_ref, z2_ref, rs2_ref, m_ref, slope_ref, pool_ref, word0, word1, word2,
    wqkv_t, wqkv, wproj, wup, wdown, pool_t, cga, cgb, wga, wgb,
    first_all, second_all, word_own, wproj_t, wup_t, wdown_t, x_all, z1_all, h1_all, near, far, a2_ref,
    first_sems, second_sems, word_sems0, word_sems1, word_sems2, own_sems,
):
    step = pl.program_id(0)
    here = place()
    words = (word0, word1, word2)
    per = LANES * letters // BATCH
    streams = {
        "first": (first_all, first_sems), "second": (second_all, second_sems),
        0: (word0, word_sems0), 1: (word1, word_sems1), 2: (word2, word_sems2),
    }
    own = [pltpu.make_async_copy(word_own.at[n], words[n].at[here], own_sems.at[n]) for n in range(3)]

    def stages_of(name, wanted):
        return (gather_direct if name == "first" else gather_stages)(*streams[name], wanted)

    @pl.when(step == 0)
    def _():
        greet()
        patterns(near, far, letters)
        pack_first(first_all.at[here], s_qkv, s_proj, s_gains)

    @pl.when(step == 1)
    def _():
        greeted()

    def advance(half):
        for name in streams:
            events = planned(GATHER_PLAN, name, steps)
            for n, when in enumerate(events):
                if when == 3 * steps or step_of(when, FORWARD_HALVES, steps)[1] != half:
                    continue

                @pl.when(step == step_of(when, FORWARD_HALVES, steps)[0])
                def _():
                    if n > 0:
                        arrive_all(stages_of(name, (n - 1,))[n - 1])
                    elif name in (0, 1, 2):
                        own[name].wait()
                    if n < len(events) - 1:
                        start_all(stages_of(name, (n,))[n])
                        if name == "first" and n == 0:
                            pack_second(second_all.at[here], s_up, s_down, s_pool)
                            pack_words(word_own, w_qkv, w_proj, w_up, w_down)
                            start_all(own)
                    elif name == "first":
                        unpack_first(first_all, wqkv_t, wproj_t, wqkv, wproj, cga, cgb, wga, wgb)
                    elif name == "second":
                        unpack_second(second_all, wup_t, wdown_t, wup, wdown, pool_t)

    advance(0)
    _, one, two, end = starts(FORWARD_HALVES, steps)

    @pl.when(step < steps)
    def _():
        forward_first(step, per, x_ref, cnt_ref, tok_ref, rs1_ref, x_all, z1_all, near)

    @pl.when((step >= one) & (step < two))
    def _():
        for j in range(FORWARD_HALVES[1]):
            if j > 0:
                advance(j)
            forward_attention(
                (step - one) * FORWARD_HALVES[1] + j, letters, tok_ref, cga, wqkv_t, wproj_t, t_ref, o_ref, p_ref, z1_ref,
                x_all, z1_all, h1_all, j,
            )

    @pl.when(step >= two)
    def _():
        forward_feed(
            step - two, letters, per, tok_ref, cgb, wup_t, wdown_t, z2_ref, rs2_ref, m_ref, slope_ref, pool_ref,
            h1_all, far, a2_ref,
        )

    @pl.when(step == end - 1)
    def _():
        for name in streams:
            if planned(GATHER_PLAN, name, steps)[-1] == 3 * steps:
                arrive_all(stages_of(name, (3,))[3])
            sent_all(stages_of(name, (0, 1, 2, 3)))


def phase_map(phase, halves, steps, per=1):
    first = starts(halves, steps)[phase]
    return lambda i: jnp.clip(i - first, 0, steps // halves[phase] - 1) // per


def forward_gather(x, cnt, first_shards, second_shards, word_shards, letters):
    tokens, width = x.shape
    steps = tokens // BATCH
    ny, nx, nz = sides()
    nd = 2 * ny * nx
    hidden, outer = second_shards[0].shape[1] * nd, second_shards[2].shape[1] * nd
    r = width // nz
    per = LANES * letters // BATCH
    word_rows, word_lanes = word_shards[2].shape

    def strip(phase, rows, lanes=BATCH, dtype=bf16):
        where, many = phase_map(phase, FORWARD_HALVES, steps), FORWARD_HALVES[phase]
        return (
            jax.ShapeDtypeStruct((steps, rows, lanes), dtype),
            pl.BlockSpec((many, rows, lanes), lambda i: (where(i), 0, 0)),
        )

    def whole(shape, dtype=bf16):
        return (jax.ShapeDtypeStruct(shape, dtype), pl.BlockSpec(shape, lambda i: (0,) * len(shape)))

    pooled = phase_map(2, FORWARD_HALVES, steps, per)
    gathered = (
        jax.ShapeDtypeStruct((ny, nx, 2, nz, word_rows, word_lanes), bf16), pl.BlockSpec(memory_space=pl.ANY)
    )
    outs = [
        whole((steps, 1, BATCH), jnp.int32), strip(1, 3 * width), strip(1, width), strip(1, CHAR_HEADS // 2 * letters, 2 * BATCH, f32), strip(1, width),
        whole((steps, 1, BATCH), f32), strip(2, width), strip(2, 1, BATCH, f32), strip(2, hidden), strip(2, hidden),
        (
            jax.ShapeDtypeStruct((width, tokens // letters), f32),
            pl.BlockSpec((width, LANES), lambda i: (0, pooled(i))),
        ),
        gathered, gathered, gathered,
        whole((3 * width, width)), whole((width, 3 * width)), whole((width, width)), whole((width, hidden)),
        whole((hidden, width)), whole((outer, width)), whole((width, LANES), f32), whole((width, LANES), f32),
        whole((outer, LANES), f32), whole((outer, LANES), f32),
    ]
    shards = (*first_shards, *second_shards, *word_shards)
    at0 = phase_map(0, FORWARD_HALVES, steps)
    sems = pltpu.SemaphoreType.DMA((2, gather_copies()))
    return pl.pallas_call(
        functools.partial(forward_gather_kernel, letters, steps),
        grid=(starts(FORWARD_HALVES, steps)[3],),
        in_specs=[
            pl.BlockSpec((BATCH, width), lambda i: (at0(i), 0)),
            pl.BlockSpec((1, LANES), lambda i: (0, at0(i) // per)),
        ] + [full_spec(a) for a in shards],
        out_specs=[o[1] for o in outs],
        out_shape=[o[0] for o in outs],
        scratch_shapes=[
            pltpu.VMEM((ny, nx, 2, nz, r + 16, LANES), bf16),
            pltpu.VMEM((ny, nx, 2, nz, 3 * r, LANES), bf16),
            pltpu.VMEM((3, word_rows, word_lanes), bf16),
            pltpu.VMEM((width, width), bf16),
            pltpu.VMEM((hidden, width), bf16),
            pltpu.VMEM((width, hidden), bf16),
            pltpu.VMEM((steps, width, BATCH), bf16),
            pltpu.VMEM((steps, width, BATCH), bf16),
            pltpu.VMEM((steps, width, BATCH), f32),
            pltpu.VMEM((BATCH // letters, BATCH), bf16),
            pltpu.VMEM((BATCH, LANES), bf16),
            pltpu.VMEM((width, BATCH), bf16),
            pltpu.SemaphoreType.DMA((2, nz - 1 + 2 * ny * nx - 1)), sems, sems, sems, sems,
            pltpu.SemaphoreType.DMA((3,)),
        ],
        compiler_params=pltpu.CompilerParams(
            dimension_semantics=("arbitrary",), vmem_limit_bytes=VMEM_BYTES, collective_id=0, has_side_effects=True
        ),
        name="forward_gather",
    )(x, cnt, *shards)


def backward_scatter_kernel(
    letters, steps, dp_ref, tok_ref, ga_ref, gb_ref, wqkv_t, wqkv, wproj, wup, wdown, send0, send1, send2,
    gpool_t, gwga, gwgb, t_ref, o_ref, p_ref, z1_ref, rs1_ref, z2_ref, rs2_ref, m_ref, slope_ref,
    cg_ref, first_sum, second_sum, word_sum,
    gqkv_t, gproj_t, gup, gdown_t, dh1_all, dt_all, do_ref, first_send, second_send, own_sems, *work,
):
    step = pl.program_id(0)
    y, x, c, z = place()
    per = LANES * letters // BATCH
    size = (len(work) - 5) // 4
    work = [work[n * size : (n + 1) * size] for n in range(5)]
    sends = (send0, send1, send2)
    streams = {n: (sends[n], work[n], word_sum.at[n]) for n in range(3)}
    streams["second"] = (second_send, work[3], second_sum)
    streams["first"] = (first_send, work[4], first_sum)
    own = [pltpu.make_async_copy(sends[n].at[:, :, c], work[n][0], own_sems.at[n]) for n in range(3)]

    @pl.when(step == 0)
    def _():
        greet()
        start_all(own)

    @pl.when(step == 1)
    def _():
        greeted()

    def advance(half):
        for name, (send, scratch, total) in streams.items():
            acc = scratch[0]
            stage, add = (direct_stage, direct_sum) if name == "first" else (scatter_stage, scatter_sum)
            events = planned(SCATTER_PLAN, name, steps)
            for n, when in enumerate(events):
                if when == 3 * steps or step_of(when, BACKWARD_HALVES, steps)[1] != half:
                    continue

                @pl.when(step == step_of(when, BACKWARD_HALVES, steps)[0])
                def _():
                    if n == 0:
                        if name == "second":
                            pack_second_grads(second_send, gup, gdown_t, gb_ref, gpool_t)
                        elif name == "first":
                            pack_first_grads(first_send, gqkv_t, gproj_t, ga_ref, wqkv_t, gup, wup, gwga, gwgb)
                    else:
                        arrive_all(stage(n - 1, send, scratch))
                        if n == 1 and name in (0, 1, 2):
                            own[name].wait()
                            mine = lambda b, a, k: acc[b, a, k]
                        else:
                            mine = lambda b, a, k: send[b, a, c, k]
                        add(n - 1, mine, scratch, total)
                    if n < len(events) - 1:
                        start_all(stage(n, send, scratch))

    advance(0)
    _, one, two, end = starts(BACKWARD_HALVES, steps)

    @pl.when(step < steps)
    def _():
        backward_feed(
            step, letters, per, dp_ref, tok_ref, gb_ref, wup, wdown, z2_ref, rs2_ref, m_ref, slope_ref,
            gup, gdown_t, dh1_all, dt_all,
        )

    @pl.when((step >= one) & (step < two))
    def _():
        for j in range(BACKWARD_HALVES[1]):
            if j > 0:
                advance(j)
            backward_attention(
                (step - one) * BACKWARD_HALVES[1] + j, letters, wproj, t_ref, o_ref, p_ref, z1_ref, gqkv_t, gproj_t,
                dh1_all, dt_all, do_ref, j,
            )

    @pl.when(step >= two)
    def _():
        for j in range(BACKWARD_HALVES[2]):
            if j > 0:
                advance(j)
            backward_last((step - two) * BACKWARD_HALVES[2] + j, ga_ref, wqkv, z1_ref, rs1_ref, cg_ref, dh1_all, dt_all, j)

    @pl.when(step == end - 1)
    def _():
        for name, (send, scratch, total) in streams.items():
            if name == "first":
                arrive_all(direct_stage(2, send, scratch))
                direct_sum(2, None, scratch, total)
                sent_all([direct_stage(n, send, scratch) for n in range(3)])
            else:
                sent_all([scatter_stage(n, send, scratch) for n in range(4)])


def backward_scatter(dp, tok, ga, gb, weights, sends, gpool_t, gwga, gwgb, saved, letters):
    wqkv_t, wqkv, wproj, wup, wdown = weights
    t, o, p, z1, rs1, z2, rs2, m, slope = saved
    steps = t.shape[0]
    width, hidden = wup.shape
    per = LANES * letters // BATCH
    ny, nx, nz = sides()
    r = width // nz
    word_rows, word_lanes = sends[0].shape[4:]
    at = [phase_map(n, BACKWARD_HALVES, steps) for n in range(3)]
    words = phase_map(0, BACKWARD_HALVES, steps, per)

    def strip(a, where, many):
        return pl.BlockSpec((many,) + a.shape[1:], lambda i: (where(i), 0, 0))

    def whole(shape):
        return (jax.ShapeDtypeStruct(shape, f32), pl.BlockSpec(shape, lambda i: (0,) * len(shape)))

    def once(a):
        return pl.BlockSpec(a.shape, lambda i: (0,) * a.ndim, pipeline_mode=pl.Buffered(1))

    outs = [
        (jax.ShapeDtypeStruct((steps * BATCH, width), bf16), pl.BlockSpec((BACKWARD_HALVES[2] * BATCH, width), lambda i: (at[2](i), 0))),
        whole((r + 16, LANES)), whole((3 * r, LANES)), whole((3, word_rows, word_lanes)),
    ]
    _, one, two, end = starts(BACKWARD_HALVES, steps)
    either = lambda i: jnp.where(i < two, at[1](i), at[2](i))
    lots = BACKWARD_HALVES[1]
    saved_specs = [
        strip(t, at[1], lots), strip(o, at[1], lots), strip(p, at[1], lots), strip(z1, either, lots),
        strip(rs1, at[2], lots), strip(z2, at[0], 1), strip(rs2, at[0], 1), strip(m, at[0], 1), strip(slope, at[0], 1),
    ]
    return pl.pallas_call(
        functools.partial(backward_scatter_kernel, letters, steps),
        grid=(end,),
        in_specs=[
            pl.BlockSpec((width, LANES), lambda i: (0, words(i))),
            pl.BlockSpec((1, 1, BATCH), lambda i: (at[0](i), 0, 0)),
        ] + [once(a) for a in (ga, gb, *weights)] + [pl.BlockSpec(memory_space=pl.ANY)] * 3
        + [once(a) for a in (gpool_t, gwga, gwgb)] + saved_specs,
        out_specs=[o[1] for o in outs],
        out_shape=[o[0] for o in outs],
        scratch_shapes=[
            pltpu.VMEM((3 * width, width), f32),
            pltpu.VMEM((width, width), f32),
            pltpu.VMEM((width, hidden), f32),
            pltpu.VMEM((width, hidden), f32),
            pltpu.VMEM((steps, width, BATCH), bf16),
            pltpu.VMEM((steps, 3 * width, BATCH), bf16),
            pltpu.VMEM((width, BATCH), bf16),
            pltpu.VMEM((ny, nx, 2, nz, r + 16, LANES), bf16),
            pltpu.VMEM((ny, nx, 2, nz, 3 * r, LANES), bf16),
            pltpu.SemaphoreType.DMA((3,)),
        ] + 3 * scatter_scratch(word_rows, word_lanes) + scatter_scratch(3 * r, LANES) + direct_scratch(r + 16, LANES),
        compiler_params=pltpu.CompilerParams(
            dimension_semantics=("arbitrary",), vmem_limit_bytes=VMEM_BYTES, collective_id=1, has_side_effects=True
        ),
        name="backward_scatter",
    )(dp, tok, ga, gb, *weights, *sends, gpool_t, gwga, gwgb, *saved)


def finish_kernel(
    first, second, words, grad_in, cqkv, cproj_t, cup, cdown_t, cga, cgb, pool, wqkv_t, wproj_t, wup, wdown_t, wga, wgb,
    grad_out,
):
    grad_out[...] = grad_in[...]

    @pl.when(pl.program_id(0) == 0)
    def _():
        r, n, gc, gw = cup.shape[0], cqkv.shape[1], cga.shape[1], wga.shape[1]
        cqkv[...] = first[pl.ds(0, r), :n]
        cproj_t[...] = first[pl.ds(0, r), :].T[n:]
        side = first[pl.ds(r, 8), :]
        cga[...] = side[0:1, :gc]
        cgb[...] = side[0:1, gc : 2 * gc]
        wga[...] = side[0:1, 2 * gc : 2 * gc + gw]
        wgb[...] = side[1:2, :gw]
        cup[...] = second[pl.ds(0, r), :]
        n = cdown_t.shape[0]
        for i in range(cdown_t.shape[1] // LANES):
            cdown_t[:, pl.ds(i * LANES, LANES)] = second[pl.ds(r + i * n, n), :]
        pool[...] = second[pl.ds(2 * r, r), : pool.shape[1]]
        t = words[0].T
        n = wqkv_t.shape[0]
        wqkv_t[...] = t[:n]
        wproj_t[...] = t[n:]
        wup[...] = words[1]
        n, lanes = wdown_t.shape[0], wup.shape[1]
        for i in range(wdown_t.shape[1] // lanes):
            wdown_t[:, pl.ds(i * lanes, lanes)] = words[2, pl.ds(i * n, n), :]


def finish(first, second, words, grad, shapes):
    steps = 4
    moved = pl.BlockSpec((grad.shape[0] // steps, grad.shape[1]), lambda i: (i, 0))
    shapes = [jax.ShapeDtypeStruct(s, f32) for s in shapes]
    return pl.pallas_call(
        finish_kernel,
        grid=(steps,),
        in_specs=[full_spec(a) for a in (first, second, words)] + [moved],
        out_specs=[full_spec(a) for a in shapes] + [moved],
        out_shape=shapes + [jax.ShapeDtypeStruct(grad.shape, grad.dtype)],
        name="finish",
    )(first, second, words, grad)


def gather_all(shards, counts):
    flat = jnp.concatenate([s.reshape(-1) for s in shards])
    packed = lax.all_gather(lax.all_gather(flat, "fsdp", axis=0), "dp", axis=0)
    wide_count, deep_count = packed.shape[:2]
    out, start = [], 0
    for s in shards:
        piece = packed[:, :, start : start + s.size]
        start += s.size
        if s.ndim == 1:
            out.append(piece[:, 0].reshape(-1))
        else:
            r, c = s.shape
            piece = piece.reshape(wide_count, deep_count, r, c).transpose(1, 2, 0, 3)
            out.append(piece.reshape(deep_count * r, wide_count * c))
    return out


def scatter_all(grads, shards):
    wide_count, deep_count = lax.axis_size("dp"), lax.axis_size("fsdp")
    pieces = []
    for g, s in zip(grads, shards):
        g = g.astype(bf16)
        if s.ndim == 1:
            g = jnp.broadcast_to(g.reshape(wide_count, 1, s.size), (wide_count, deep_count, s.size))
        else:
            r, c = s.shape
            g = g.reshape(deep_count, r, wide_count, c).transpose(2, 0, 1, 3)
        pieces.append(g.reshape(wide_count, deep_count, s.size))
    packed = jnp.concatenate(pieces, 2)
    packed = lax.psum_scatter(packed, "dp", scatter_dimension=0, tiled=True)
    packed = lax.psum_scatter(packed, "fsdp", scatter_dimension=1, tiled=True).reshape(-1)
    out, start = [], 0
    for s in shards:
        out.append(packed[start : start + s.size].reshape(s.shape).astype(f32))
        start += s.size
    return out


def shards_plain(
    characters, counts, separators, cotangent, char_qkv, char_proj, char_up, char_down, char_gain_a, char_gain_b,
    pool_proj, word_qkv, word_proj, word_up, word_down, word_gain_a, word_gain_b,
):
    rows, length, letters, width = characters.shape
    char_shards = (char_qkv, char_proj, char_up, char_down, char_gain_a, char_gain_b)
    word_shards = (pool_proj, word_qkv, word_proj, word_up, word_down, word_gain_a, word_gain_b)
    cqkv, cproj, cup, cdown, cga, cgb = gather_all(char_shards, counts)
    wpool, wqkv, wproj, wup, wdown, wga, wgb = gather_all(word_shards, counts)
    x = characters.reshape(length * letters, width)
    tok = jnp.repeat(counts, letters, axis=1).reshape(length * letters // STEP, 1, STEP)
    cga, cgb, wga, wgb = (
        jnp.broadcast_to(g.astype(f32)[:, None], (g.shape[0], LANES)) for g in (cga, cgb, wga, wgb)
    )
    *saved, pool_sum = char_forward(x, tok, counts, cga, cgb, cqkv.T, cproj.T, cup.T, cdown.T, letters)
    word_out, dpool, gpool, gwqkv, gwproj, gwup, gwdown, gwga, gwgb = word_layer(
        pool_sum, counts.astype(f32), separators, cotangent.reshape(length, -1), wga, wgb, wpool, wqkv, wproj, wup, wdown
    )
    word_grads = scatter_all(
        (gpool, gwqkv, gwproj, gwup, gwdown, jnp.sum(gwga, 1), jnp.sum(gwgb, 1)), word_shards
    )
    char_grad, gcqkv, gcproj, gcup, gcdown, gcga, gcgb = char_backward(
        dpool, tok, cga, cgb, cqkv, cproj, cup, cdown, saved, letters
    )
    char_grads = scatter_all(
        (gcqkv, gcproj, gcup, gcdown, jnp.sum(gcga, 1), jnp.sum(gcgb, 1)), char_shards
    )
    return (word_out[None], char_grad.reshape(characters.shape), *char_grads, *word_grads)


def shards_packed(
    characters, counts, separators, cotangent, char_qkv, char_proj, char_up, char_down, char_gain_a, char_gain_b,
    pool_proj, word_qkv, word_proj, word_up, word_down, word_gain_a, word_gain_b,
):
    rows, length, letters, width = characters.shape
    x = characters.reshape(length * letters, width)
    gains = jnp.concatenate([char_gain_a, char_gain_b, word_gain_a, word_gain_b]).astype(f32)
    gains = jnp.pad(gains, (0, 2 * LANES - gains.shape[0])).reshape(2, LANES)
    (
        tok, *saved, pool_sum, word0, word1, word2, wqkv_t, wqkv, wproj, wup, wdown, pool_t, cga, cgb, wga, wgb
    ) = forward_gather(
        x, counts, (char_qkv, char_proj.T, gains), (char_up, char_down.T, pool_proj),
        (word_qkv.T, word_proj.T, word_up, word_down.T), letters,
    )
    shape = word0.shape
    flat = (-1,) + shape[3:]
    word_out, dpool, gpool_t, *sends, gwga, gwgb = word_gathered(
        pool_sum, counts, separators, cotangent.reshape(length, -1), wga, wgb, pool_t,
        *(w.reshape(flat) for w in (word0, word1, word2)),
    )
    char_grad, first, second, words = backward_scatter(
        dpool, tok, cga, cgb, (wqkv_t, wqkv, wproj, wup, wdown), [s.reshape(shape) for s in sends],
        gpool_t, gwga, gwgb, saved, letters,
    )
    shapes = [
        s.shape if s.ndim == 2 else (1, s.shape[0])
        for s in (
            char_qkv, char_proj.T, char_up, char_down.T, char_gain_a, char_gain_b,
            pool_proj, word_qkv.T, word_proj.T, word_up, word_down.T, word_gain_a, word_gain_b,
        )
    ]
    (
        cqkv, cproj_t, cup, cdown_t, cgain_a, cgain_b, pool, gqkv_t, gproj_t, gup, gdown_t, wgain_a, wgain_b, char_grad
    ) = finish(first, second, words, char_grad, shapes)
    return (
        word_out[None], char_grad.reshape(characters.shape), cqkv, cproj_t.T, cup, cdown_t.T, cgain_a[0], cgain_b[0],
        pool, gqkv_t.T, gproj_t.T, gup, gdown_t.T, wgain_a[0], wgain_b[0],
    )


def shards(*arrays):
    char_qkv, char_proj, word_qkv, word_proj = arrays[4], arrays[5], arrays[11], arrays[12]
    tiles = (char_qkv.shape[1] + char_proj.shape[1]) // LANES, (word_qkv.shape[1] + word_proj.shape[1]) // LANES
    return (shards_packed if tiles == (1, 2) else shards_plain)(*arrays)


def solution(mesh):
    rows = ("dp", "fsdp")
    matrix, vector = P("fsdp", "dp"), P("dp")
    data = (P(rows, None, None, None), P(rows, None), P(rows, None), P(rows, None, None))
    block = (matrix,) * 4 + (vector,) * 2
    word = (matrix,) * 5 + (vector,) * 2
    return jax.shard_map(
        shards,
        mesh=mesh,
        in_specs=data + block + word,
        out_specs=(data[3], data[0]) + block + word,
        check_vma=False,
    )
```

```python
import functools
import math

import jax
import jax.numpy as jnp
from jax import lax
from jax.experimental import pallas as pl
from jax.experimental.pallas import tpu as pltpu
from jax.sharding import PartitionSpec as P

CHAR_HEADS = 4
WORD_HEADS = 8
EPS = 1e-05
NEGATIVE = -1e30
LANES = 128
SPAN = 256
STEP = 512
BATCH = 1024
VMEM_BYTES = 60 * 2**20
GELU_A = 0.7978845608028654
GELU_B = 0.044715

bf16 = jnp.bfloat16
f32 = jnp.float32


def dot(a, b):
    return jnp.dot(a, b, preferred_element_type=f32)


def dot_nt(a, b):
    return lax.dot_general(a, b, (((1,), (1,)), ((), ())), preferred_element_type=f32)


def normed(v):
    c = v - jnp.mean(v, 0, keepdims=True)
    rs = lax.rsqrt(jnp.mean(c * c, 0, keepdims=True) + EPS)
    return c * rs, rs


def wide(g, n):
    return g if n == g.shape[1] else jnp.concatenate([g] * (n // g.shape[1]), 1)


def gelu_both(u):
    s = u * u
    t = jnp.tanh(u * (GELU_A + (GELU_A * GELU_B) * s))
    h = 0.5 * u
    r = 0.5 + 0.5 * t
    slope = r + h * (1.0 - t * t) * (GELU_A + (3.0 * GELU_A * GELU_B) * s)
    return u * r, slope


def lane_word(letters):
    return lax.broadcasted_iota(jnp.int32, (letters, LANES), 1) // letters


def pick_own(full, owner, letters):
    words = LANES // letters
    out = full[:letters]
    for w in range(1, words):
        out = jnp.where(owner == w, full[w * letters : (w + 1) * letters], out)
    return out


def own_blocks(letters):
    a = lax.broadcasted_iota(jnp.int32, (LANES, LANES), 0) // letters
    b = lax.broadcasted_iota(jnp.int32, (LANES, LANES), 1) // letters
    return jnp.where(a == b, 1.0, 0.0).astype(bf16)


def spread_own(compact, blocks, letters):
    return jnp.concatenate([compact] * (LANES // letters), 0) * blocks


def char_forward_kernel(
    letters, x_ref, tok_ref, cnt_ref, ga_ref, gb_ref, wqkv_ref, wproj_ref, wup_ref, wdown_ref,
    t_ref, o_ref, p_ref, z1_ref, rs1_ref, z2_ref, rs2_ref, m_ref, gp_ref, pool_ref,
):
    step = pl.program_id(0)
    width = x_ref.shape[1]
    head = width // CHAR_HEADS
    scale = head ** (-0.5)
    steps_per_block = LANES * letters // STEP
    owner = lane_word(letters)
    blocks = own_blocks(letters)
    key_slot = lax.broadcasted_iota(jnp.int32, (letters, LANES), 0)

    @pl.when(step % steps_per_block == 0)
    def _():
        pool_ref[...] = jnp.zeros_like(pool_ref)

    for part in range(STEP // SPAN):
        at = pl.ds(part * SPAN, SPAN)
        x = x_ref[at, :].astype(f32).T
        z1, rs1 = normed(x)
        z1_ref[0, :, at] = z1.astype(bf16)
        rs1_ref[0, :, at] = rs1
        a1 = (z1 * wide(ga_ref[...], SPAN)).astype(bf16)
        for n in range(3):
            rows = pl.ds(n * width, width)
            t_ref[0, rows, at] = dot(wqkv_ref[rows, :], a1).astype(bf16)
        for g in range(SPAN // LANES):
            lanes = pl.ds(part * SPAN + g * LANES, LANES)
            allowed = key_slot < tok_ref[0, :, lanes]
            for h in range(CHAR_HEADS):
                q = t_ref[0, pl.ds(h * head, head), lanes]
                k = t_ref[0, pl.ds(width + h * head, head), lanes]
                v = t_ref[0, pl.ds(2 * width + h * head, head), lanes]
                full = dot(k.T, q)
                s = jnp.where(allowed, pick_own(full, owner, letters) * scale, NEGATIVE)
                e = jnp.exp(s - jnp.max(s, 0, keepdims=True))
                p = e / jnp.sum(e, 0, keepdims=True)
                p_ref[0, pl.ds(h * letters, letters), lanes] = p
                o = dot(v, spread_own(p.astype(bf16), blocks, letters))
                o_ref[0, pl.ds(h * head, head), lanes] = o.astype(bf16)
        h1 = x + dot(wproj_ref[...], o_ref[0, :, at])
        z2, rs2 = normed(h1)
        z2_ref[0, :, at] = z2.astype(bf16)
        rs2_ref[0, :, at] = rs2
        a2 = (z2 * wide(gb_ref[...], SPAN)).astype(bf16)
        for n in range(wup_ref.shape[0] // 256):
            rows = pl.ds(n * 256, 256)
            m, gp = gelu_both(dot(wup_ref[rows, :], a2))
            m_ref[0, rows, at] = m.astype(bf16)
            gp_ref[0, rows, at] = gp.astype(bf16)
        h2 = h1 + dot(wdown_ref[...], m_ref[0, :, at])
        high = h2.astype(bf16)
        low = (h2 - high.astype(f32)).astype(bf16)
        row = lax.broadcasted_iota(jnp.int32, (SPAN, LANES), 0)
        word = lax.broadcasted_iota(jnp.int32, (SPAN, LANES), 1)
        first = (step % steps_per_block) * (STEP // letters) + part * (SPAN // letters)
        mine = (row // letters + first == word) & (row % letters < cnt_ref[...])
        gather = jnp.where(mine, 1.0, 0.0).astype(bf16)
        pool_ref[...] += dot(high, gather) + dot(low, gather)


def full_spec(a):
    nd = len(a.shape)
    return pl.BlockSpec(a.shape, lambda i: (0,) * nd)


def char_forward(x, tok, cnt, ga, gb, wqkv_t, wproj_t, wup_t, wdown_t, letters):
    tokens, width = x.shape
    steps = tokens // STEP
    hidden = wup_t.shape[0]
    per = LANES * letters // STEP

    def strip(rows, dtype=bf16):
        return (
            jax.ShapeDtypeStruct((steps, rows, STEP), dtype),
            pl.BlockSpec((1, rows, STEP), lambda i: (i, 0, 0)),
        )

    outs = [
        strip(3 * width), strip(width), strip(CHAR_HEADS * letters, f32), strip(width), strip(1, f32),
        strip(width), strip(1, f32), strip(hidden), strip(hidden),
        (jax.ShapeDtypeStruct((width, tokens // letters), f32), pl.BlockSpec((width, LANES), lambda i: (0, i // per))),
    ]
    return pl.pallas_call(
        functools.partial(char_forward_kernel, letters),
        grid=(steps,),
        in_specs=[
            pl.BlockSpec((STEP, width), lambda i: (i, 0)),
            pl.BlockSpec((1, 1, STEP), lambda i: (i, 0, 0)),
            pl.BlockSpec((1, LANES), lambda i: (0, i // per)),
        ] + [full_spec(a) for a in (ga, gb, wqkv_t, wproj_t, wup_t, wdown_t)],
        out_specs=[o[1] for o in outs],
        out_shape=[o[0] for o in outs],
        compiler_params=pltpu.CompilerParams(
            dimension_semantics=("arbitrary",), vmem_limit_bytes=56 * 2**20
        ),
        name="char_forward",
    )(x, tok, cnt, ga, gb, wqkv_t, wproj_t, wup_t, wdown_t)


def norm_back(dy, z, rs, gain):
    dz = dy * gain
    a = jnp.mean(dz, 0, keepdims=True)
    b = jnp.mean(dz * z, 0, keepdims=True)
    return rs * (dz - a - z * b)


def fold_lanes(v):
    out = v[:, :LANES]
    for n in range(1, v.shape[1] // LANES):
        out = out + v[:, n * LANES : (n + 1) * LANES]
    return out


def char_backward_kernel(
    letters, dp_ref, tok_ref, ga_ref, gb_ref, wqkv_ref, wproj_ref, wup_ref, wdown_ref,
    t_ref, o_ref, p_ref, z1_ref, rs1_ref, z2_ref, rs2_ref, m_ref, gp_ref,
    cg_ref, gqkv_ref, gproj_ref, gup_ref, gdown_ref, gga_ref, ggb_ref,
    dh2_ref, du_ref, dh1b_ref, do_ref, dt_ref,
):
    step = pl.program_id(0)
    width = cg_ref.shape[1]
    head = width // CHAR_HEADS
    scale = head ** (-0.5)
    steps_per_block = LANES * letters // STEP
    owner = lane_word(letters)
    blocks = own_blocks(letters)

    @pl.when(step == 0)
    def _():
        for ref in (gqkv_ref, gproj_ref, gup_ref, gdown_ref, gga_ref, ggb_ref):
            ref[...] = jnp.zeros_like(ref)

    for part in range(STEP // SPAN):
        at = pl.ds(part * SPAN, SPAN)
        word = lax.broadcasted_iota(jnp.int32, (LANES, SPAN), 0)
        col = lax.broadcasted_iota(jnp.int32, (LANES, SPAN), 1)
        first = (step % steps_per_block) * (STEP // letters) + part * (SPAN // letters)
        mine = (col // letters + first == word) & (col % letters < tok_ref[0, :, at])
        scatter = jnp.where(mine, 1.0, 0.0).astype(bf16)
        dh2 = dot(dp_ref[...], scatter)
        dh2b = dh2.astype(bf16)
        dh2_ref[:, at] = dh2b
        for n in range(wdown_ref.shape[0] // 256):
            rows = pl.ds(n * 256, 256)
            du_ref[rows, at] = (dot(wdown_ref[rows, :], dh2b) * gp_ref[0, rows, at].astype(f32)).astype(bf16)
        dy = dot(wup_ref[...], du_ref[:, at])
        z = z2_ref[0, :, at].astype(f32)
        ggb_ref[...] += fold_lanes(dy * z)
        dh1 = dh2 + norm_back(dy, z, rs2_ref[0, :, at], wide(gb_ref[...], SPAN))
        dh1b = dh1.astype(bf16)
        dh1b_ref[:, at] = dh1b
        do_ref[:, at] = dot(wproj_ref[...], dh1b).astype(bf16)
        for g in range(SPAN // LANES):
            lanes = pl.ds(part * SPAN + g * LANES, LANES)
            for h in range(CHAR_HEADS):
                q_rows = pl.ds(h * head, head)
                k_rows = pl.ds(width + h * head, head)
                v_rows = pl.ds(2 * width + h * head, head)
                q = t_ref[0, q_rows, lanes]
                k = t_ref[0, k_rows, lanes]
                v = t_ref[0, v_rows, lanes]
                do = do_ref[pl.ds(h * head, head), lanes]
                p = p_ref[0, pl.ds(h * letters, letters), lanes]
                dp = pick_own(dot(v.T, do), owner, letters)
                ds = p * (dp - jnp.sum(p * dp, 0, keepdims=True))
                pb = spread_own(p.astype(bf16), blocks, letters)
                dsb = spread_own(ds.astype(bf16), blocks, letters)
                dt_ref[q_rows, lanes] = (dot(k, dsb) * scale).astype(bf16)
                dt_ref[k_rows, lanes] = (dot_nt(q, dsb) * scale).astype(bf16)
                dt_ref[v_rows, lanes] = dot_nt(do, pb).astype(bf16)
        dy = dot(wqkv_ref[...], dt_ref[:, at])
        z = z1_ref[0, :, at].astype(f32)
        gga_ref[...] += fold_lanes(dy * z)
        dx = dh1 + norm_back(dy, z, rs1_ref[0, :, at], wide(ga_ref[...], SPAN))
        cg_ref[at, :] = dx.T.astype(bf16)
    gdown_ref[...] += dot_nt(dh2_ref[...], m_ref[0])
    gup_ref[...] += dot_nt(z2_ref[0], du_ref[...])
    gproj_ref[...] += dot_nt(dh1b_ref[...], o_ref[0])
    gqkv_ref[...] += dot_nt(dt_ref[...], z1_ref[0])

    @pl.when(step == pl.num_programs(0) - 1)
    def _():
        gup_ref[...] = gup_ref[...] * wide(gb_ref[...], gup_ref.shape[1])
        gqkv_ref[...] = gqkv_ref[...] * ga_ref[...].T[:1]


def char_backward(dp, tok, ga, gb, wqkv, wproj, wup, wdown, saved, letters):
    t, o, p, z1, rs1, z2, rs2, m, gp = saved
    steps = t.shape[0]
    width = wqkv.shape[0]
    hidden = wup.shape[1]
    per = LANES * letters // STEP

    def whole(shape):
        return (jax.ShapeDtypeStruct(shape, f32), pl.BlockSpec(shape, lambda i: (0, 0)))

    outs = [
        (jax.ShapeDtypeStruct((steps * STEP, width), bf16), pl.BlockSpec((STEP, width), lambda i: (i, 0))),
        whole((3 * width, width)), whole((width, width)), whole((width, hidden)), whole((width, hidden)),
        whole((width, LANES)), whole((width, LANES)),
    ]
    return pl.pallas_call(
        functools.partial(char_backward_kernel, letters),
        grid=(steps,),
        in_specs=[
            pl.BlockSpec((width, LANES), lambda i: (0, i // per)),
            pl.BlockSpec((1, 1, STEP), lambda i: (i, 0, 0)),
        ] + [full_spec(a) for a in (ga, gb, wqkv, wproj, wup, wdown)]
        + [pl.BlockSpec((1,) + s.shape[1:], lambda i: (i, 0, 0)) for s in saved],
        out_specs=[o[1] for o in outs],
        out_shape=[o[0] for o in outs],
        scratch_shapes=[
            pltpu.VMEM((width, STEP), bf16),
            pltpu.VMEM((hidden, STEP), bf16),
            pltpu.VMEM((width, STEP), bf16),
            pltpu.VMEM((width, STEP), bf16),
            pltpu.VMEM((3 * width, STEP), bf16),
        ],
        compiler_params=pltpu.CompilerParams(
            dimension_semantics=("arbitrary",), vmem_limit_bytes=56 * 2**20
        ),
        name="char_backward",
    )(dp, tok, ga, gb, wqkv, wproj, wup, wdown, *saved)


def word_kernel(
    pool_sum_ref, cnt_ref, sep_ref, cot_ref, ga_ref, gb_ref, wpool_ref, wqkv_ref, wproj_ref, wup_ref, wdown_ref,
    out_ref, dpool_ref, gpool_ref, gqkv_ref, gproj_ref, gup_ref, gdown_ref, gga_ref, ggb_ref,
    pooled, x, z3, rs3, a3, t, p, o, h3, z4, rs4, a4, m, gp, bias, cot, du, dh3, dh3b, do, dt, dtk,
):
    width, length = x.shape
    head = width // WORD_HEADS
    scale = head ** (-0.5)
    halves = [pl.ds(n * SPAN, SPAN) for n in range(length // SPAN)]
    pooled[...] = (pool_sum_ref[...] / cnt_ref[...]).astype(bf16)
    row = lax.broadcasted_iota(jnp.int32, (length, length), 0)
    col = lax.broadcasted_iota(jnp.int32, (length, length), 1)
    tri = jnp.where(row <= col, 1.0, 0.0).astype(bf16)
    sep = jnp.broadcast_to(sep_ref[...].astype(f32).astype(bf16), (16, length))
    doc_q = dot(sep, tri)[:1]
    doc_k = lax.dot_general(tri, sep, (((0,), (1,)), ((), ())), preferred_element_type=f32)[:, :1]
    bias[...] = jnp.where((row <= col) & (doc_k == doc_q), 0.0, NEGATIVE)
    cot[...] = cot_ref[...].astype(f32).T.astype(bf16)
    for at in halves:
        x[:, at] = lax.dot_general(
            wpool_ref[...], pooled[:, at], (((0,), (0,)), ((), ())), preferred_element_type=f32
        )
        z, rs = normed(x[:, at])
        z3[:, at] = z.astype(bf16)
        rs3[:, at] = rs
        a3[:, at] = (z * wide(ga_ref[...], SPAN)).astype(bf16)
        for n in range(3):
            rows = pl.ds(n * width, width)
            t[rows, at] = lax.dot_general(
                wqkv_ref[:, rows], a3[:, at], (((0,), (0,)), ((), ())), preferred_element_type=f32
            ).astype(bf16)
    for h in range(WORD_HEADS):
        k = t[pl.ds(width + h * head, head), :].T
        for n, at in enumerate(halves):
            seen = (n + 1) * SPAN
            keys = pl.ds(0, seen)
            q = t[pl.ds(h * head, head), at]
            s = dot(k[:seen], q) * scale + bias[keys, at]
            e = jnp.exp(s - jnp.max(s, 0, keepdims=True))
            w = e / jnp.sum(e, 0, keepdims=True)
            p[h, keys, at] = w
            o[pl.ds(h * head, head), at] = dot(t[pl.ds(2 * width + h * head, head), keys], w.astype(bf16)).astype(bf16)
    for at in halves:
        h3[:, at] = x[:, at] + lax.dot_general(
            wproj_ref[...], o[:, at], (((0,), (0,)), ((), ())), preferred_element_type=f32
        )
        z, rs = normed(h3[:, at])
        z4[:, at] = z.astype(bf16)
        rs4[:, at] = rs
        a4[:, at] = (z * wide(gb_ref[...], SPAN)).astype(bf16)
        for n in range(wup_ref.shape[1] // 256):
            rows = pl.ds(n * 256, 256)
            mm, gg = gelu_both(
                lax.dot_general(wup_ref[:, rows], a4[:, at], (((0,), (0,)), ((), ())), preferred_element_type=f32)
            )
            m[rows, at] = mm.astype(bf16)
            gp[rows, at] = gg.astype(bf16)
        out = h3[:, at] + lax.dot_general(
            wdown_ref[...], m[:, at], (((0,), (0,)), ((), ())), preferred_element_type=f32
        )
        out_ref[at, :] = out.T.astype(bf16)
        for n in range(wdown_ref.shape[0] // 256):
            rows = pl.ds(n * 256, 256)
            du[rows, at] = (dot(wdown_ref[rows, :], cot[:, at]) * gp[rows, at].astype(f32)).astype(bf16)
        dy = dot(wup_ref[...], du[:, at])
        z = z4[:, at].astype(f32)
        part = fold_lanes(dy * z)
        ggb_ref[...] = part if at is halves[0] else ggb_ref[...] + part
        dh3[:, at] = cot[:, at].astype(f32) + norm_back(dy, z, rs4[:, at], wide(gb_ref[...], SPAN))
        dh3b[:, at] = dh3[:, at].astype(bf16)
        do[:, at] = dot(wproj_ref[...], dh3b[:, at]).astype(bf16)
    gdown_ref[...] = dot_nt(m[...], cot[...]).astype(gdown_ref.dtype)
    gup_ref[...] = dot_nt(a4[...], du[...]).astype(gup_ref.dtype)
    gproj_ref[...] = dot_nt(o[...], dh3b[...]).astype(gproj_ref.dtype)
    for h in range(WORD_HEADS):
        q_rows = pl.ds(h * head, head)
        k_rows = pl.ds(width + h * head, head)
        v_rows = pl.ds(2 * width + h * head, head)
        v = t[v_rows, :].T
        for n in reversed(range(len(halves))):
            at = halves[n]
            seen = (n + 1) * SPAN
            keys = pl.ds(0, seen)
            w = p[h, keys, at]
            g = do[q_rows, at]
            dp = dot(v[:seen], g)
            ds = (w * (dp - jnp.sum(w * dp, 0, keepdims=True))).astype(bf16)
            dt[q_rows, at] = (dot(t[k_rows, keys], ds) * scale).astype(bf16)
            dk = dot_nt(t[q_rows, at], ds) * scale
            dv = dot_nt(g, w.astype(bf16))
            if n == len(halves) - 1:
                dtk[0] = dk
                dtk[1] = dv
            else:
                dtk[0, :, keys] += dk
                dtk[1, :, keys] += dv
        dt[k_rows, :] = dtk[0].astype(bf16)
        dt[v_rows, :] = dtk[1].astype(bf16)
    gqkv_ref[...] = dot_nt(a3[...], dt[...]).astype(gqkv_ref.dtype)
    for at in halves:
        dy = dot(wqkv_ref[...], dt[:, at])
        z = z3[:, at].astype(f32)
        part = fold_lanes(dy * z)
        gga_ref[...] = part if at is halves[0] else gga_ref[...] + part
        dx = dh3[:, at] + norm_back(dy, z, rs3[:, at], wide(ga_ref[...], SPAN))
        dh3b[:, at] = dx.astype(bf16)
        dpool_ref[:, at] = (dot(wpool_ref[...], dh3b[:, at]) / cnt_ref[:, at]).astype(bf16)
    gpool_ref[...] = dot_nt(pooled[...], dh3b[...]).astype(gpool_ref.dtype)


def word_layer(pool_sum, cnt, sep, cot, ga, gb, wpool, wqkv, wproj, wup, wdown, grad_type=f32):
    length, width = cot.shape
    inner = pool_sum.shape[0]
    hidden = wup.shape[1]
    vm = pltpu.VMEM
    return pl.pallas_call(
        word_kernel,
        out_shape=[
            jax.ShapeDtypeStruct((length, width), bf16),
            jax.ShapeDtypeStruct((inner, length), bf16),
            jax.ShapeDtypeStruct(wpool.shape, grad_type),
            jax.ShapeDtypeStruct(wqkv.shape, grad_type),
            jax.ShapeDtypeStruct(wproj.shape, grad_type),
            jax.ShapeDtypeStruct(wup.shape, grad_type),
            jax.ShapeDtypeStruct(wdown.shape, grad_type),
            jax.ShapeDtypeStruct((width, LANES), f32),
            jax.ShapeDtypeStruct((width, LANES), f32),
        ],
        scratch_shapes=[
            vm((inner, length), bf16), vm((width, length), f32), vm((width, length), bf16), vm((1, length), f32),
            vm((width, length), bf16), vm((3 * width, length), bf16), vm((WORD_HEADS, length, length), f32),
            vm((width, length), bf16), vm((width, length), f32), vm((width, length), bf16), vm((1, length), f32),
            vm((width, length), bf16), vm((hidden, length), bf16), vm((hidden, length), bf16),
            vm((length, length), f32), vm((width, length), bf16), vm((hidden, length), bf16),
            vm((width, length), f32), vm((width, length), bf16), vm((width, length), bf16),
            vm((3 * width, length), bf16), vm((2, width // WORD_HEADS, length), f32),
        ],
        compiler_params=pltpu.CompilerParams(vmem_limit_bytes=58 * 2**20),
        name="word_layer",
    )(pool_sum, cnt, sep, cot, ga, gb, wpool, wqkv, wproj, wup, wdown)


MESH = pl.DeviceIdType.MESH


def sides():
    chips = lax.axis_size("dp") // 2
    nx = math.isqrt(chips)
    return chips // nx, nx, lax.axis_size("fsdp")


def place():
    ny, nx, nz = sides()
    me = lax.axis_index("dp")
    return me // (2 * nx), (me // 2) % nx, me % 2, lax.axis_index("fsdp")


def device(y, x, c, z):
    return {"dp": (y * sides()[1] + x) * 2 + c, "fsdp": z}


def others():
    ny, nx, nz = sides()
    y, x, c, z = place()
    return [((y + j) % ny, (x + i) % nx) for j in range(ny) for i in range(nx) if j + i > 0]


def partners():
    ny, nx, nz = sides()
    y, x, c, z = place()
    found = [device(y, x, 1 - c, z)]
    found += [device(y, x, c, (z + k) % nz) for k in range(1, nz)]
    return found + [device(j, i, c, z) for j, i in others()]


def greet():
    barrier = pltpu.get_barrier_semaphore()
    for other in partners():
        pl.semaphore_signal(barrier, inc=1, device_id=other, device_id_type=MESH)


def greeted():
    pl.semaphore_wait(pltpu.get_barrier_semaphore(), len(partners()))


def remote(src, dst, sems, n, other):
    return pltpu.make_async_remote_copy(
        src_ref=src, dst_ref=dst, send_sem=sems.at[0, n], recv_sem=sems.at[1, n],
        device_id=other, device_id_type=MESH,
    )


def gather_copies():
    ny, nx, nz = sides()
    return nz - 1 + 1 + 4 * (nx - 1) + 4 * (ny - 1)


def gather_stages(ref, sems, wanted=(0, 1, 2, 3)):
    ny, nx, nz = sides()
    y, x, c, z = place()
    every = slice(None)
    half = ref.shape[4] // 2
    low, high = pl.ds(0, half), pl.ds(half, half)
    twin = device(y, x, 1 - c, z)
    plan = [[], [], [], []]
    plan[0] += [((y, x, c, z), device(y, x, c, (z + k) % nz)) for k in range(1, nz)]
    plan[1] += [((y, x, c, every, low), device(y, (x + k) % nx, c, z)) for k in range(1, nx)]
    plan[1] += [((y, x, c, every, high), device((y + k) % ny, x, c, z)) for k in range(1, ny)]
    plan[1] += [((y, x, c), twin)]
    plan[2] += [((y, every, c, every, low), device((y + k) % ny, x, c, z)) for k in range(1, ny)]
    plan[2] += [((every, x, c, every, high), device(y, (x + k) % nx, c, z)) for k in range(1, nx)]
    plan[2] += [((y, (x + k) % nx, c, every, low), twin) for k in range(1, nx)]
    plan[2] += [(((y + k) % ny, x, c, every, high), twin) for k in range(1, ny)]
    plan[3] += [(((y + k) % ny, every, c, every, low), twin) for k in range(1, ny)]
    plan[3] += [((every, (x + k) % nx, c, every, high), twin) for k in range(1, nx)]
    count = 0
    stages = []
    for n, part in enumerate(plan):
        copies = []
        for where, other in part:
            if n in wanted:
                copies.append(remote(ref.at[where], ref.at[where], sems, count, other))
            count += 1
        stages.append(copies)
    return stages


def gather_direct(ref, sems, wanted=(0, 1, 2)):
    ny, nx, nz = sides()
    y, x, c, z = place()
    twin = device(y, x, 1 - c, z)
    plan = [[((y, x, c, z), device(y, x, c, (z + k) % nz)) for k in range(1, nz)]]
    plan += [[((y, x, c), device(j, i, c, z)) for j, i in others()] + [((y, x, c), twin)]]
    plan += [[((j, i, c), twin) for j, i in others()]]
    count, stages = 0, []
    for n, part in enumerate(plan):
        copies = []
        for where, other in part:
            if n in wanted:
                copies.append(remote(ref.at[where], ref.at[where], sems, count, other))
            count += 1
        stages.append(copies)
    return stages


def start_all(copies):
    for copy in copies:
        copy.start()


def arrive_all(copies):
    for copy in copies:
        copy.wait_recv()


def sent_all(stages):
    for copies in stages:
        for copy in copies:
            copy.wait_send()


def lanes_to(v, n):
    return v if v.shape[1] == n else jnp.concatenate([v, jnp.zeros((v.shape[0], n - v.shape[1]), v.dtype)], 1)


def turned(v):
    return v.astype(f32).T.astype(bf16)


def scatter_copies():
    ny, nx, nz = sides()
    return 1 + 2 * (nx - 1) + 2 * (ny - 1) + nz - 1


def scatter_scratch(rows, lanes):
    ny, nx, nz = sides()
    half = rows // 2
    shapes = (
        (ny, nx, nz, rows, lanes), (ny, nx, nz, rows, lanes), (nx - 1, ny, nz, half, lanes),
        (ny - 1, nx, nz, half, lanes), (ny - 1, nz, half, lanes), (nx - 1, nz, half, lanes), (nz - 1, rows, lanes),
    )
    return [pltpu.VMEM(shape, bf16) for shape in shapes] + [pltpu.SemaphoreType.DMA((2, scatter_copies()))]


def scatter_stage(n, send, work):
    acc, twin_in, one_low, one_high, two_low, two_high, last_in, sems = work
    ny, nx, nz = sides()
    y, x, c, z = place()
    half = acc.shape[3] // 2
    low, high, every = pl.ds(0, half), pl.ds(half, half), slice(None)
    plan = [[], [], [], []]
    plan[0] += [(send, (every, every, 1 - c), twin_in, device(y, x, 1 - c, z))]
    plan[1] += [
        (acc, (every, (x + k) % nx, every, low), one_low.at[k - 1], device(y, (x + k) % nx, c, z)) for k in range(1, nx)
    ]
    plan[1] += [
        (acc, ((y + k) % ny, every, every, high), one_high.at[k - 1], device((y + k) % ny, x, c, z)) for k in range(1, ny)
    ]
    plan[2] += [
        (acc, ((y + k) % ny, x, every, low), two_low.at[k - 1], device((y + k) % ny, x, c, z)) for k in range(1, ny)
    ]
    plan[2] += [
        (acc, (y, (x + k) % nx, every, high), two_high.at[k - 1], device(y, (x + k) % nx, c, z)) for k in range(1, nx)
    ]
    plan[3] += [(acc, (y, x, (z + k) % nz), last_in.at[k - 1], device(y, x, c, (z + k) % nz)) for k in range(1, nz)]
    first = sum(len(p) for p in plan[:n])
    return [remote(src.at[at], dst, sems, first + i, other) for i, (src, at, dst, other) in enumerate(plan[n])]


def direct_scratch(rows, lanes):
    ny, nx, nz = sides()
    shapes = (
        (ny, nx, nz, rows, lanes), (ny, nx, nz, rows, lanes), (ny * nx - 1, nz, rows, lanes), (nz - 1, rows, lanes)
    )
    count = 1 + ny * nx - 1 + nz - 1
    return [pltpu.VMEM(shape, bf16) for shape in shapes] + [pltpu.SemaphoreType.DMA((2, count))]


def direct_stage(n, send, work):
    acc, twin_in, near_in, last_in, sems = work
    ny, nx, nz = sides()
    y, x, c, z = place()
    if n == 0:
        return [remote(send.at[:, :, 1 - c], twin_in, sems, 0, device(y, x, 1 - c, z))]
    if n == 1:
        return [
            remote(acc.at[j, i], near_in.at[k], sems, 1 + k, device(j, i, c, z)) for k, (j, i) in enumerate(others())
        ]
    return [
        remote(acc.at[y, x, (z + k) % nz], last_in.at[k - 1], sems, ny * nx + k - 1, device(y, x, c, (z + k) % nz))
        for k in range(1, nz)
    ]


def direct_sum(n, own, work, out):
    acc, twin_in, near_in, last_in, sems = work
    ny, nx, nz = sides()
    y, x, c, z = place()
    if n == 0:
        for b in range(ny):
            for a in range(nx):
                for k in range(nz):
                    acc[b, a, k] = own(b, a, k) + twin_in[b, a, k]
    elif n == 1:
        for k in range(nz):
            total = acc[y, x, k].astype(f32) + sum(near_in[i, k].astype(f32) for i in range(ny * nx - 1))
            acc[y, x, k] = total.astype(bf16)
    else:
        out[...] = acc[y, x, z].astype(f32) + sum(last_in[i].astype(f32) for i in range(nz - 1))


def scatter_sum(n, own, work, out):
    acc, twin_in, one_low, one_high, two_low, two_high, last_in, sems = work
    ny, nx, nz = sides()
    y, x, c, z = place()
    half = acc.shape[3] // 2
    low, high = pl.ds(0, half), pl.ds(half, half)
    if n == 0:
        for b in range(ny):
            for a in range(nx):
                for k in range(nz):
                    acc[b, a, k] = own(b, a, k) + twin_in[b, a, k]
    elif n == 1:
        for k in range(nz):
            for b in range(ny):
                acc[b, x, k, low] += sum(one_low[i, b, k] for i in range(nx - 1))
            for a in range(nx):
                acc[y, a, k, high] += sum(one_high[i, a, k] for i in range(ny - 1))
    elif n == 2:
        for k in range(nz):
            acc[y, x, k, low] += sum(two_low[i, k] for i in range(ny - 1))
            acc[y, x, k, high] += sum(two_high[i, k] for i in range(nx - 1))
    else:
        out[...] = acc[y, x, z].astype(f32) + sum(last_in[i].astype(f32) for i in range(nz - 1))


def gelu_twice(u):
    s = u * u
    t = jnp.tanh(u * (GELU_A + (GELU_A * GELU_B) * s))
    a = 1.0 + t
    m = u * a
    return m, a + m * ((1.0 - t) * (GELU_A + (3.0 * GELU_A * GELU_B) * s))


def shift_of(letters):
    return letters.bit_length() - 1


def twin_owner(letters):
    lane = lax.broadcasted_iota(jnp.int32, (letters, 2 * LANES), 1)
    return lax.shift_right_logical(lane & (LANES - 1), shift_of(letters))


def twin_mask(letters):
    bits = shift_of(letters)
    a = lax.shift_right_logical(lax.broadcasted_iota(jnp.int32, (LANES, 2 * LANES), 0), bits)
    b = lax.shift_right_logical(lax.broadcasted_iota(jnp.int32, (LANES, 2 * LANES), 1) & (LANES - 1), bits)
    return jnp.where(a == b, 1.0, 0.0).astype(bf16)


def twin_blocks(v):
    half = v.shape[0] // 2
    none = jnp.zeros((half, v.shape[1]), v.dtype)
    return jnp.concatenate([jnp.concatenate([v[:half], none], 1), jnp.concatenate([none, v[half:]], 1)], 0)


def stacked(v):
    return jnp.concatenate([v[:, :LANES], v[:, LANES:]], 0)


def char_units():
    for g in range(BATCH // LANES):
        for h in range(CHAR_HEADS // 2):
            yield h, pl.ds(g * LANES, LANES), pl.ds(2 * g * LANES, 2 * LANES)


def patterns(near, far, letters):
    words, tokens = near.shape
    bits = shift_of(letters)
    word = lax.broadcasted_iota(jnp.int32, (words, tokens), 0)
    token = lax.shift_right_logical(lax.broadcasted_iota(jnp.int32, (words, tokens), 1), bits)
    near[...] = jnp.where(word == token, 1.0, 0.0).astype(bf16)
    if far is not None:
        token = lax.shift_right_logical(lax.broadcasted_iota(jnp.int32, far.shape, 0), bits)
        word = lax.broadcasted_iota(jnp.int32, far.shape, 1)
        far[...] = jnp.where(word == token, 1.0, 0.0).astype(bf16)


def own_words(s, per, v):
    words = LANES // per
    out = v[:, :words]
    for i in range(1, per):
        out = jnp.where(s % per == i, v[:, i * words : (i + 1) * words], out)
    return out


def valid_tokens(letters, counts):
    slot = lax.broadcasted_iota(jnp.int32, counts.shape, 1) & (letters - 1)
    return jnp.where(slot < counts, 1.0, 0.0)


def forward_first(s, per, x_ref, cnt_ref, tok_ref, rs1_ref, x_all, z1_all, near):
    counts = jnp.broadcast_to(own_words(s, per, cnt_ref[...].astype(f32)), (16, near.shape[0])).astype(bf16)
    tok_ref[s] = dot(counts, near[...])[:1].astype(jnp.int32)
    x = x_ref[...].astype(f32).T
    x_all[s] = x.astype(bf16)
    z1, rs1 = normed(x)
    z1_all[s] = z1.astype(bf16)
    rs1_ref[s] = rs1


def forward_attention(s, letters, tok_ref, ga_ref, wqkv_t, wproj_t, t_ref, o_ref, p_ref, z1_ref, x_all, z1_all, h1_all, j):
    width = o_ref.shape[1]
    pair = 2 * (width // CHAR_HEADS)
    scale = (width // CHAR_HEADS) ** (-0.5)
    owner, blocks = twin_owner(letters), twin_mask(letters)
    key_slot = lax.broadcasted_iota(jnp.int32, (letters, 2 * LANES), 0)
    z1 = z1_all[s]
    z1_ref[j] = z1
    a1 = (z1.astype(f32) * wide(ga_ref[...], BATCH)).astype(bf16)
    t_ref[j] = dot(wqkv_t[...], a1).astype(bf16)
    units = list(char_units())
    scores = []
    for h, lanes, lanes2 in units:
        q = twin_blocks(t_ref[j, pl.ds(h * pair, pair), lanes])
        k = t_ref[j, pl.ds(width + h * pair, pair), lanes].T
        scores.append(pick_own(dot(k, q), owner, letters))
    probs = []
    for (h, lanes, lanes2), score in zip(units, scores):
        counts = tok_ref[s, :, lanes]
        allowed = key_slot < jnp.concatenate([counts, counts], 1)
        score = jnp.where(allowed, score * scale, NEGATIVE)
        e = jnp.exp(score - jnp.max(score, 0, keepdims=True))
        p = e / jnp.sum(e, 0, keepdims=True)
        p_ref[j, pl.ds(h * letters, letters), lanes2] = p
        probs.append(p)
    for (h, lanes, lanes2), p in zip(units, probs):
        v = twin_blocks(t_ref[j, pl.ds(2 * width + h * pair, pair), lanes])
        o = dot(v, stacked(spread_own(p.astype(bf16), blocks, letters)))
        o_ref[j, pl.ds(h * pair, pair), lanes] = o.astype(bf16)
    h1_all[s] = x_all[s].astype(f32) + dot(wproj_t[...], o_ref[j])


def forward_feed(
    s, letters, per, tok_ref, gb_ref, wup_t, wdown_t, z2_ref, rs2_ref, m_ref, slope_ref, pool_ref, h1_all, far, a2_ref
):
    z2, rs2 = normed(h1_all[s])
    z2_ref[0] = z2.astype(bf16)
    rs2_ref[0] = rs2
    a2_ref[...] = (z2 * wide(gb_ref[...], BATCH)).astype(bf16)
    valid = valid_tokens(letters, tok_ref[s])
    strips = [
        (pl.ds(at, SPAN), pl.ds(n * 256, 256)) for at in range(0, BATCH, SPAN) for n in range(wup_t.shape[0] // 256)
    ]

    def close(cols):
        h2 = h1_all[s, :, cols] + dot(wdown_t[...], m_ref[0, :, cols])
        kept = (h2 * valid[:, cols.start : cols.start + cols.size]).astype(bf16)
        return dot(kept, far[cols, :])

    part = 0.0
    ahead = dot(wup_t[strips[0][1], :], a2_ref[:, strips[0][0]])
    for i, (cols, rows) in enumerate(strips):
        u = ahead
        if i + 1 < len(strips):
            ahead = dot(wup_t[strips[i + 1][1], :], a2_ref[:, strips[i + 1][0]])
        if rows.start == 0 and cols.start > 0:
            part += close(pl.ds(cols.start - SPAN, SPAN))
        m, slope = gelu_twice(u)
        m_ref[0, rows, cols] = m.astype(bf16)
        slope_ref[0, rows, cols] = slope.astype(bf16)
    part += close(pl.ds(BATCH - SPAN, SPAN))
    words = LANES // per
    for i in range(per):
        moved = part if i == 0 else pltpu.roll(part, i * words, 1)

        @pl.when(s % per == i)
        def _():
            pool_ref[...] = moved if i == 0 else pool_ref[...] + moved


def backward_feed(
    s, letters, per, dp_ref, tok_ref, gb_ref, wup, wdown, z2_ref, rs2_ref, m_ref, slope_ref, gup, gdown_t, dh1_all, spare
):
    deep = spare.shape[1]

    @pl.when(s == 0)
    def _():
        gdown_t[...] = jnp.zeros_like(gdown_t)
        gup[...] = jnp.zeros_like(gup)

    word = lax.broadcasted_iota(jnp.int32, (LANES, BATCH), 0) - (s % per) * (BATCH // letters)
    token = lax.broadcasted_iota(jnp.int32, (LANES, BATCH), 1)
    mine = lax.shift_right_logical(token, shift_of(letters)) == word
    scatter = jnp.where(mine & ((token & (letters - 1)) < tok_ref[0]), 1.0, 0.0).astype(bf16)
    dh2 = dot(dp_ref[...], scatter)
    dh2b = dh2.astype(bf16)
    for n in range(wdown.shape[0] // 256):
        rows = pl.ds(n * 256, 256)
        du = (dot(wdown[rows, :], dh2b) * slope_ref[0, rows, :].astype(f32)).astype(bf16)
        spare[n * 256 // deep, pl.ds(n * 256 % deep, 256), :] = du
    pieces = []
    for n in range(0, wdown.shape[0], deep):
        size = min(deep, wdown.shape[0] - n)
        pieces.append((pl.ds(n, size), (n // deep, pl.ds(0, size))))
    dy = sum(dot(wup[:, cols], spare[at]) for cols, at in pieces)
    gdown_t[...] += dot_nt(dh2b, m_ref[0])
    for cols, at in pieces:
        gup[:, cols] += dot_nt(z2_ref[0], spare[at])
    z = z2_ref[0].astype(f32)
    dh1 = dh2 + norm_back(dy, z, rs2_ref[0], wide(gb_ref[...], BATCH))
    dh1_all[s] = dh1.astype(bf16)


def backward_attention(s, letters, wproj, t_ref, o_ref, p_ref, z1_ref, gqkv_t, gproj_t, dh1_all, dt_all, do_ref, j):
    width = wproj.shape[0]
    pair = 2 * (width // CHAR_HEADS)
    scale = (width // CHAR_HEADS) ** (-0.5)
    owner, blocks = twin_owner(letters), twin_mask(letters)

    @pl.when(s == 0)
    def _():
        gproj_t[...] = jnp.zeros_like(gproj_t)
        gqkv_t[...] = jnp.zeros_like(gqkv_t)

    dh1b = dh1_all[s]
    do_ref[...] = dot(wproj[...], dh1b).astype(bf16)
    gproj_t[...] += dot_nt(dh1b, o_ref[j])
    units = list(char_units())
    grads = []
    for h, lanes, lanes2 in units:
        v = t_ref[j, pl.ds(2 * width + h * pair, pair), lanes].T
        grads.append(pick_own(dot(v, twin_blocks(do_ref[pl.ds(h * pair, pair), lanes])), owner, letters))
    spread = []
    for (h, lanes, lanes2), dp in zip(units, grads):
        p = p_ref[j, pl.ds(h * letters, letters), lanes2]
        ds = p * (dp - jnp.sum(p * dp, 0, keepdims=True))
        spread.append((spread_own(p.astype(bf16), blocks, letters), spread_own(ds.astype(bf16), blocks, letters)))
    for (h, lanes, lanes2), (pb, dsb) in zip(units, spread):
        q_rows = pl.ds(h * pair, pair)
        k_rows = pl.ds(width + h * pair, pair)
        v_rows = pl.ds(2 * width + h * pair, pair)
        q = twin_blocks(t_ref[j, q_rows, lanes])
        k = twin_blocks(t_ref[j, k_rows, lanes])
        do = twin_blocks(do_ref[q_rows, lanes])
        dt_all[s, q_rows, lanes] = (dot(k, stacked(dsb)) * scale).astype(bf16)
        dt_all[s, k_rows, lanes] = (dot_nt(q, dsb) * scale).astype(bf16)
        dt_all[s, v_rows, lanes] = dot_nt(do, pb).astype(bf16)
    gqkv_t[...] += dot_nt(dt_all[s], z1_ref[j])


def backward_last(s, ga_ref, wqkv, z1_ref, rs1_ref, cg_ref, dh1_all, dt_all, j):
    dy = dot(wqkv[...], dt_all[s])
    z = z1_ref[j].astype(f32)
    dx = dh1_all[s].astype(f32) + norm_back(dy, z, rs1_ref[j], wide(ga_ref[...], BATCH))
    cg_ref[pl.ds(j * BATCH, BATCH), :] = dx.T.astype(bf16)


def pack_first(slot, qkv, proj_t, gains):
    r = qkv.shape[0]
    slot[pl.ds(0, r), :] = jnp.concatenate([qkv[...], turned(lanes_to(proj_t[...], LANES))[:r]], 1)
    a, b, c, d = (g[...].astype(f32).reshape(1, g.shape[0]) for g in gains)
    one = jnp.concatenate([a, b, c], 1)
    two = lanes_to(d, LANES)
    none = jnp.zeros((slot.shape[0] - r - 2, LANES), f32)
    slot[pl.ds(r, slot.shape[0] - r), :] = jnp.concatenate([one, two, none], 0).astype(bf16)


def pack_second(slot, up, down_t, pool):
    r, n = up.shape[0], down_t.shape[0]
    slot[pl.ds(0, r), :] = up[...]
    for i in range(down_t.shape[1] // LANES):
        slot[pl.ds(r + i * n, n), :] = down_t[:, pl.ds(i * LANES, LANES)]
    slot[pl.ds(2 * r, r), :] = lanes_to(pool[...], LANES)


def pack_words(slots, qkv_t, proj_t, up, down_t):
    slots[0] = turned(jnp.concatenate([qkv_t[...], proj_t[...]], 0))
    slots[1] = up[...]
    n, lanes = down_t.shape[0], up.shape[1]
    for i in range(down_t.shape[1] // lanes):
        slots[2, pl.ds(i * n, n), :] = down_t[:, pl.ds(i * lanes, lanes)]


def seats():
    ny, nx, nz = sides()
    for d in range(2 * ny * nx):
        yield d, (d // (2 * nx), (d // 2) % nx, d % 2)


def unpack_first(ref, wqkv_t, wproj_t, wqkv, wproj, cga, cgb, wga, wgb):
    ny, nx, nz = sides()
    nd = 2 * ny * nx
    r = wqkv.shape[0] // nz
    a, b, gc, gw = wqkv_t.shape[0] // nd, wproj_t.shape[0] // nd, cga.shape[0] // nd, wga.shape[0] // nd
    for d, at in seats():
        t = turned(ref[at + (slice(None), pl.ds(0, r))].reshape(nz * r, LANES))
        wqkv_t[pl.ds(d * a, a), :] = t[:a]
        wproj_t[pl.ds(d * b, b), :] = t[a:]
        g = ref[at + (0, pl.ds(r, 16))].astype(f32).T
        one, two = (jnp.broadcast_to(g[:, i : i + 1], (LANES, LANES)) for i in range(2))
        cga[pl.ds(d * gc, gc), :] = one[:gc]
        cgb[pl.ds(d * gc, gc), :] = one[gc : 2 * gc]
        wga[pl.ds(d * gw, gw), :] = one[2 * gc : 2 * gc + gw]
        wgb[pl.ds(d * gw, gw), :] = two[:gw]
    wqkv[...] = turned(wqkv_t[...])
    wproj[...] = turned(wproj_t[...])


def unpack_second(ref, wup_t, wdown_t, wup, wdown, pool_t):
    ny, nx, nz = sides()
    nd = 2 * ny * nx
    r, n, p = wup.shape[0] // nz, wdown_t.shape[0] // nd, pool_t.shape[0] // nd
    deep = wdown_t.shape[1] // nz
    for d, at in seats():
        up = ref[at + (slice(None), pl.ds(0, r))].reshape(nz * r, LANES)
        wup[:, pl.ds(d * LANES, LANES)] = up
        wup_t[pl.ds(d * LANES, LANES), :] = turned(up)
        for z in range(nz):
            for i in range(deep // LANES):
                wdown_t[pl.ds(d * n, n), pl.ds(z * deep + i * LANES, LANES)] = ref[at + (z, pl.ds(r + i * n, n))] * 0.5
        t = turned(ref[at + (slice(None), pl.ds(2 * r, r))].reshape(nz * r, LANES))
        pool_t[pl.ds(d * p, p), :] = t[:p]
    wdown[...] = turned(wdown_t[...])


def pack_first_grads(slots, gqkv_t, gproj_t, ga, wqkv_t, gup, wup, gwga, gwgb):
    ny, nx, nz = sides()
    nd = 2 * ny * nx
    width = gqkv_t.shape[1]
    r = width // nz
    tail = slots.shape[4] - r
    a, b, gc, gw = gqkv_t.shape[0] // nd, gproj_t.shape[0] // nd, width // nd, gwga.shape[1] // nd
    char_a = jnp.sum(gqkv_t[...] * wqkv_t[...].astype(f32), 0, keepdims=True)
    char_a = jnp.broadcast_to(char_a, (8, width)).T[:, :1]
    char_b = jnp.sum(gup[...] * wup[...].astype(f32), 1, keepdims=True)
    word_a, word_b = (g[...].T[:, :1] for g in (gwga, gwgb))
    gain = ga[...].T[:1]
    spot = lax.broadcasted_iota(jnp.int32, (LANES, nz * tail), 1) % tail
    none = jnp.zeros((LANES - gw, 1), f32)
    for d, at in seats():
        t = jnp.concatenate([gqkv_t[pl.ds(d * a, a), :] * gain, gproj_t[pl.ds(d * b, b), :]], 0)
        slots[at + (slice(None), pl.ds(0, r))] = t.T.astype(bf16).reshape(nz, r, LANES)
        char, word = slice(d * gc, (d + 1) * gc), slice(d * gw, (d + 1) * gw)
        one = jnp.concatenate([char_a[char], char_b[char], word_a[word]], 0)
        two = jnp.concatenate([word_b[word], none], 0)
        side = jnp.where(spot == 0, one, jnp.where(spot == 1, two, 0.0))
        slots[at + (slice(None), pl.ds(r, tail))] = side.T.astype(bf16).reshape(nz, tail, LANES)


def pack_second_grads(slots, gup, gdown_t, gb, gpool_t):
    ny, nx, nz = sides()
    nd = 2 * ny * nx
    width = gup.shape[0]
    r, n, p = width // nz, gdown_t.shape[0] // nd, gpool_t.shape[0] // nd
    deep = gdown_t.shape[1] // nz
    none = jnp.zeros((LANES - p, width), f32)
    for d, at in seats():
        up = gup[:, pl.ds(d * LANES, LANES)] * gb[...]
        slots[at + (slice(None), pl.ds(0, r))] = up.astype(bf16).reshape(nz, r, LANES)
        for z in range(nz):
            for i in range(deep // LANES):
                down = gdown_t[pl.ds(d * n, n), pl.ds(z * deep + i * LANES, LANES)] * 0.5
                slots[at + (z, pl.ds(r + i * n, n))] = down.astype(bf16)
        t = jnp.concatenate([gpool_t[pl.ds(d * p, p), :].astype(f32), none], 0)
        slots[at + (slice(None), pl.ds(2 * r, r))] = t.T.astype(bf16).reshape(nz, r, LANES)


def unpack_mixed(ref, qkv_t, proj_t):
    nd, nz, r, lanes = ref.shape
    a, b = qkv_t.shape[0] // nd, proj_t.shape[0] // nd
    for d in range(nd):
        t = turned(ref[d].reshape(nz * r, lanes))
        qkv_t[pl.ds(d * a, a), :] = t[:a]
        proj_t[pl.ds(d * b, b), :] = t[a:]


def unpack_up(ref, up_t, up):
    nd, nz, r, lanes = ref.shape
    for d in range(nd):
        piece = ref[d].reshape(nz * r, lanes)
        up[:, pl.ds(d * lanes, lanes)] = piece
        up_t[pl.ds(d * lanes, lanes), :] = turned(piece)


def unpack_down(ref, down_t):
    nd, nz, r, lanes = ref.shape
    n, deep = down_t.shape[0] // nd, down_t.shape[1] // nz
    for d in range(nd):
        for z in range(nz):
            for i in range(deep // lanes):
                down_t[pl.ds(d * n, n), pl.ds(z * deep + i * lanes, lanes)] = ref[d, z, pl.ds(i * n, n), :] * 0.5


def word_gathered_kernel(
    pool_sum_ref, cnt_ref, sep_ref, cot_ref, ga_ref, gb_ref, wpool_t, far0, far1, far2,
    out_ref, dpool_ref, gpool_ref, gone0, gone1, gone2, gga_ref, ggb_ref,
    pooled, x, z3, rs3, a3, t, p, o, h3, z4, rs4, a4, m, slope, bias, cot, du, dh3, dh3b, do, dt, dtk,
    wqkv_t, wproj_t, wup_t, wdown_t, wqkv, wproj, wup, wdown, wpool, gqkv_t, gproj_t,
    all0, all1, all2, send0, send1, send2, in_sems, out_sems,
):
    width, length = x.shape
    head = width // WORD_HEADS
    scale = head ** (-0.5)
    nd, nz, r, lanes = send0.shape
    halves = [pl.ds(n * SPAN, SPAN) for n in range(length // SPAN)]
    fetch = [pltpu.make_async_copy(a, b, in_sems.at[n]) for n, (a, b) in enumerate(((far0, all0), (far1, all1), (far2, all2)))]
    leave = [pltpu.make_async_copy(a, b, out_sems.at[n]) for n, (a, b) in enumerate(((send0, gone0), (send1, gone1), (send2, gone2)))]
    start_all(fetch)
    counts = cnt_ref[...].astype(f32)
    pooled[...] = (pool_sum_ref[...] / counts).astype(bf16)
    row = lax.broadcasted_iota(jnp.int32, (length, length), 0)
    col = lax.broadcasted_iota(jnp.int32, (length, length), 1)
    tri = jnp.where(row <= col, 1.0, 0.0).astype(bf16)
    sep = jnp.broadcast_to(sep_ref[...].astype(f32).astype(bf16), (16, length))
    doc_q = dot(sep, tri)[:1]
    doc_k = jnp.broadcast_to(doc_q, (8, length)).T[:, :1]
    bias[...] = jnp.where((row <= col) & (doc_k == doc_q), 0.0, NEGATIVE)
    cot[...] = turned(cot_ref[...])
    x[...] = dot(wpool_t[...], pooled[...])
    z, rs = normed(x[...])
    z3[...] = z.astype(bf16)
    rs3[...] = rs
    a3[...] = (z * wide(ga_ref[...], length)).astype(bf16)
    fetch[0].wait()
    unpack_mixed(all0, wqkv_t, wproj_t)
    t[...] = dot(wqkv_t[...], a3[...]).astype(bf16)
    units = [(h, n) for h in range(WORD_HEADS) for n in range(len(halves))]

    def score(h, n):
        k = t[pl.ds(width + h * head, head), pl.ds(0, (n + 1) * SPAN)].T
        return dot(k, t[pl.ds(h * head, head), halves[n]])

    def mix(h, n, w):
        keys = pl.ds(0, (n + 1) * SPAN)
        o[pl.ds(h * head, head), halves[n]] = dot(t[pl.ds(2 * width + h * head, head), keys], w).astype(bf16)

    ahead, behind = score(*units[0]), None
    for i, (h, n) in enumerate(units):
        s = ahead
        if i + 1 < len(units):
            ahead = score(*units[i + 1])
        keys = pl.ds(0, (n + 1) * SPAN)
        s = s * scale + bias[keys, halves[n]]
        e = jnp.exp(s - jnp.max(s, 0, keepdims=True))
        w = e * (1.0 / jnp.sum(e, 0, keepdims=True))
        p[h, keys, halves[n]] = w
        if behind is not None:
            mix(*behind)
        behind = (h, n, w.astype(bf16))
    mix(*behind)
    fetch[1].wait()
    unpack_up(all1, wup_t, wup)
    h3[...] = x[...] + dot(wproj_t[...], o[...])
    z, rs = normed(h3[...])
    z4[...] = z.astype(bf16)
    rs4[...] = rs
    a4[...] = (z * wide(gb_ref[...], length)).astype(bf16)
    for n in range(wup_t.shape[0] // 256):
        rows = pl.ds(n * 256, 256)
        mm, gg = gelu_twice(dot(wup_t[rows, :], a4[...]))
        m[rows, :] = mm.astype(bf16)
        slope[rows, :] = gg.astype(bf16)
    fetch[2].wait()
    unpack_down(all2, wdown_t)
    wdown[...] = turned(wdown_t[...])
    for n in range(wdown.shape[0] // 256):
        rows = pl.ds(n * 256, 256)
        du[rows, :] = (dot(wdown[rows, :], cot[...]) * slope[rows, :].astype(f32)).astype(bf16)
    out = h3[...] + dot(wdown_t[...], m[...])
    out_ref[...] = out.T.astype(bf16)
    dy = dot(wup[...], du[...])
    z = z4[...].astype(f32)
    ggb_ref[...] = jnp.broadcast_to(jnp.sum(fold_lanes(dy * z).T, 0, keepdims=True), ggb_ref.shape)
    dh3[...] = cot[...].astype(f32) + norm_back(dy, z, rs4[...], wide(gb_ref[...], length))
    dh3b[...] = dh3[...].astype(bf16)
    wproj[...] = turned(wproj_t[...])
    do[...] = dot(wproj[...], dh3b[...]).astype(bf16)
    n = width // nd
    deep = m.shape[0] // nz
    for z in range(nz):
        for i in range(deep // lanes):
            g = (dot_nt(cot[...], m[pl.ds(z * deep + i * lanes, lanes), :]) * 0.5).astype(bf16)
            for d in range(nd):
                send2[d, z, pl.ds(i * n, n), :] = g[d * n : (d + 1) * n]
    leave[2].start()
    for d in range(nd):
        g = dot_nt(a4[...], du[pl.ds(d * lanes, lanes), :]).astype(bf16)
        send1[d] = g.reshape(nz, r, lanes)
    leave[1].start()
    gproj_t[...] = dot_nt(dh3b[...], o[...]).astype(bf16)
    last = len(halves) - 1
    units = [(h, n) for h in range(WORD_HEADS) for n in reversed(range(len(halves)))]

    def rows_of(kind, h):
        return pl.ds(kind * width + h * head, head)

    def upstream(h, n):
        return dot(t[rows_of(2, h), pl.ds(0, (n + 1) * SPAN)].T, do[rows_of(0, h), halves[n]])

    def spread(h, n, ds, w):
        keys, at = pl.ds(0, (n + 1) * SPAN), halves[n]
        dt[rows_of(0, h), at] = (dot(t[rows_of(1, h), keys], ds) * scale).astype(bf16)
        dk = dot_nt(t[rows_of(0, h), at], ds) * scale
        dv = dot_nt(do[rows_of(0, h), at], w)
        if n == last:
            dtk[0] = dk
            dtk[1] = dv
        else:
            dtk[0, :, keys] += dk
            dtk[1, :, keys] += dv
        if n == 0:
            dt[rows_of(1, h), :] = dtk[0].astype(bf16)
            dt[rows_of(2, h), :] = dtk[1].astype(bf16)

    ahead, behind = upstream(*units[0]), None
    for i, (h, n) in enumerate(units):
        dp = ahead
        if i + 1 < len(units):
            ahead = upstream(*units[i + 1])
        w = p[h, pl.ds(0, (n + 1) * SPAN), halves[n]]
        ds = (w * (dp - jnp.sum(w * dp, 0, keepdims=True))).astype(bf16)
        if behind is not None:
            spread(*behind)
        behind = (h, n, ds, w.astype(bf16))
    spread(*behind)
    for n in range(3):
        part = pl.ds(n * width, width)
        gqkv_t[part, :] = dot_nt(dt[part, :], a3[...]).astype(bf16)
    a, b = gqkv_t.shape[0] // nd, gproj_t.shape[0] // nd
    for d in range(nd):
        g = turned(jnp.concatenate([gqkv_t[pl.ds(d * a, a), :], gproj_t[pl.ds(d * b, b), :]], 0))
        send0[d] = g.reshape(nz, r, lanes)
    leave[0].start()
    wqkv[...] = turned(wqkv_t[...])
    dy = dot(wqkv[...], dt[...])
    z = z3[...].astype(f32)
    gga_ref[...] = jnp.broadcast_to(jnp.sum(fold_lanes(dy * z).T, 0, keepdims=True), gga_ref.shape)
    dx = dh3[...] + norm_back(dy, z, rs3[...], wide(ga_ref[...], length))
    dh3b[...] = dx.astype(bf16)
    wpool[...] = turned(wpool_t[...])
    dpool_ref[...] = (dot(wpool[...], dh3b[...]) / counts).astype(bf16)
    gpool_ref[...] = dot_nt(dh3b[...], pooled[...]).astype(bf16)
    for copy in leave:
        copy.wait()


def word_gathered(pool_sum, cnt, sep, cot, ga, gb, pool_t, *gathered):
    length, width = cot.shape
    inner = pool_sum.shape[0]
    nd, nz, r, lanes = gathered[0].shape
    hidden = nd * lanes
    vm = pltpu.VMEM
    near, far = pl.BlockSpec(memory_space=pltpu.VMEM), pl.BlockSpec(memory_space=pl.ANY)
    return pl.pallas_call(
        word_gathered_kernel,
        in_specs=[near] * 7 + [far] * 3,
        out_specs=[near] * 3 + [far] * 3 + [near] * 2,
        out_shape=[
            jax.ShapeDtypeStruct((length, width), bf16),
            jax.ShapeDtypeStruct((inner, length), bf16),
            jax.ShapeDtypeStruct((width, inner), bf16),
            *(jax.ShapeDtypeStruct(g.shape, bf16) for g in gathered),
            jax.ShapeDtypeStruct((8, width), f32),
            jax.ShapeDtypeStruct((8, width), f32),
        ],
        scratch_shapes=[
            vm((inner, length), bf16), vm((width, length), f32), vm((width, length), bf16), vm((1, length), f32),
            vm((width, length), bf16), vm((3 * width, length), bf16), vm((WORD_HEADS, length, length), f32),
            vm((width, length), bf16), vm((width, length), f32), vm((width, length), bf16), vm((1, length), f32),
            vm((width, length), bf16), vm((hidden, length), bf16), vm((hidden, length), bf16),
            vm((length, length), f32), vm((width, length), bf16), vm((hidden, length), bf16),
            vm((width, length), f32), vm((width, length), bf16), vm((width, length), bf16),
            vm((3 * width, length), bf16), vm((2, width // WORD_HEADS, length), f32),
            vm((3 * width, width), bf16), vm((width, width), bf16), vm((hidden, width), bf16), vm((width, hidden), bf16),
            vm((width, 3 * width), bf16), vm((width, width), bf16), vm((width, hidden), bf16), vm((hidden, width), bf16),
            vm((inner, width), bf16), vm((3 * width, width), bf16), vm((width, width), bf16),
        ] + [vm(g.shape, bf16) for g in gathered] * 2 + [pltpu.SemaphoreType.DMA((3,)), pltpu.SemaphoreType.DMA((3,))],
        compiler_params=pltpu.CompilerParams(vmem_limit_bytes=VMEM_BYTES),
        name="word_gathered",
    )(pool_sum, cnt, sep, cot, ga, gb, pool_t, *gathered)


GATHER_PLAN = {
    "first": (1, 3, 6, 8),
    "second": (3, 6, 9, 13, 15),
    0: (6, 11, 14, 17, 19),
    1: (9, 14, 17, 20, 22),
    2: (11, 17, 20, 22, 24),
}
SCATTER_PLAN = {
    0: (1, 2, 4, 6, 8),
    1: (2, 5, 7, 9, 11),
    2: (3, 8, 10, 12, 15),
    "second": (8, 11, 13, 15, 18),
    "first": (16, 18, 22, 24),
}
FORWARD_HALVES = (1, 2, 1)
BACKWARD_HALVES = (1, 1, 1)


def planned(plan, event, steps):
    return [(at // 8) * steps + (at % 8) * steps // 8 for at in plan[event]]


def starts(halves, steps):
    ends = [0]
    for h in halves:
        ends.append(ends[-1] + steps // h)
    return ends


def step_of(tick, halves, steps):
    phase = min(tick // steps, 2)
    inside = tick - phase * steps
    return starts(halves, steps)[phase] + inside // halves[phase], inside % halves[phase]


def forward_gather_kernel(
    letters, steps, x_ref, cnt_ref, s_qkv, s_proj, s_gain0, s_gain1, s_gain2, s_gain3, s_up, s_down, s_pool, w_qkv, w_proj, w_up, w_down,
    tok_ref, t_ref, o_ref, p_ref, z1_ref, rs1_ref, z2_ref, rs2_ref, m_ref, slope_ref, pool_ref, word0, word1, word2,
    wqkv_t, wqkv, wproj, wup, wdown, pool_t, cga, cgb, wga, wgb,
    first_all, second_all, word_own, wproj_t, wup_t, wdown_t, x_all, z1_all, h1_all, near, far, a2_ref,
    first_sems, second_sems, word_sems0, word_sems1, word_sems2, own_sems,
):
    step = pl.program_id(0)
    here = place()
    words = (word0, word1, word2)
    per = LANES * letters // BATCH
    streams = {
        "first": (first_all, first_sems), "second": (second_all, second_sems),
        0: (word0, word_sems0), 1: (word1, word_sems1), 2: (word2, word_sems2),
    }
    own = [pltpu.make_async_copy(word_own.at[n], words[n].at[here], own_sems.at[n]) for n in range(3)]

    def stages_of(name, wanted):
        return (gather_direct if name == "first" else gather_stages)(*streams[name], wanted)

    @pl.when(step == 0)
    def _():
        greet()
        patterns(near, far, letters)
        pack_first(first_all.at[here], s_qkv, s_proj, (s_gain0, s_gain1, s_gain2, s_gain3))

    @pl.when(step == 1)
    def _():
        greeted()

    def advance(half):
        for name in streams:
            events = planned(GATHER_PLAN, name, steps)
            for n, when in enumerate(events):
                if when == 3 * steps or step_of(when, FORWARD_HALVES, steps)[1] != half:
                    continue

                @pl.when(step == step_of(when, FORWARD_HALVES, steps)[0])
                def _():
                    if n > 0:
                        arrive_all(stages_of(name, (n - 1,))[n - 1])
                    elif name in (0, 1, 2):
                        own[name].wait()
                    if n < len(events) - 1:
                        start_all(stages_of(name, (n,))[n])
                        if name == "first" and n == 0:
                            pack_second(second_all.at[here], s_up, s_down, s_pool)
                            pack_words(word_own, w_qkv, w_proj, w_up, w_down)
                            start_all(own)
                    elif name == "first":
                        unpack_first(first_all, wqkv_t, wproj_t, wqkv, wproj, cga, cgb, wga, wgb)
                    elif name == "second":
                        unpack_second(second_all, wup_t, wdown_t, wup, wdown, pool_t)

    advance(0)
    _, one, two, end = starts(FORWARD_HALVES, steps)

    @pl.when(step < steps)
    def _():
        forward_first(step, per, x_ref, cnt_ref, tok_ref, rs1_ref, x_all, z1_all, near)

    @pl.when((step >= one) & (step < two))
    def _():
        for j in range(FORWARD_HALVES[1]):
            if j > 0:
                advance(j)
            forward_attention(
                (step - one) * FORWARD_HALVES[1] + j, letters, tok_ref, cga, wqkv_t, wproj_t, t_ref, o_ref, p_ref, z1_ref,
                x_all, z1_all, h1_all, j,
            )

    @pl.when(step >= two)
    def _():
        forward_feed(
            step - two, letters, per, tok_ref, cgb, wup_t, wdown_t, z2_ref, rs2_ref, m_ref, slope_ref, pool_ref,
            h1_all, far, a2_ref,
        )

    @pl.when(step == end - 1)
    def _():
        for name in streams:
            if planned(GATHER_PLAN, name, steps)[-1] == 3 * steps:
                arrive_all(stages_of(name, (3,))[3])
            sent_all(stages_of(name, (0, 1, 2, 3)))


def phase_map(phase, halves, steps, per=1):
    first = starts(halves, steps)[phase]
    return lambda i: jnp.clip(i - first, 0, steps // halves[phase] - 1) // per


def forward_gather(x, cnt, first_shards, second_shards, word_shards, letters):
    tokens, width = x.shape
    steps = tokens // BATCH
    ny, nx, nz = sides()
    nd = 2 * ny * nx
    hidden, outer = second_shards[0].shape[1] * nd, second_shards[2].shape[1] * nd
    r = width // nz
    per = LANES * letters // BATCH
    word_rows, word_lanes = word_shards[2].shape

    def strip(phase, rows, lanes=BATCH, dtype=bf16):
        where, many = phase_map(phase, FORWARD_HALVES, steps), FORWARD_HALVES[phase]
        return (
            jax.ShapeDtypeStruct((steps, rows, lanes), dtype),
            pl.BlockSpec((many, rows, lanes), lambda i: (where(i), 0, 0)),
        )

    def whole(shape, dtype=bf16):
        return (jax.ShapeDtypeStruct(shape, dtype), pl.BlockSpec(shape, lambda i: (0,) * len(shape)))

    pooled = phase_map(2, FORWARD_HALVES, steps, per)
    gathered = (
        jax.ShapeDtypeStruct((ny, nx, 2, nz, word_rows, word_lanes), bf16), pl.BlockSpec(memory_space=pl.ANY)
    )
    outs = [
        whole((steps, 1, BATCH), jnp.int32), strip(1, 3 * width), strip(1, width), strip(1, CHAR_HEADS // 2 * letters, 2 * BATCH, f32), strip(1, width),
        whole((steps, 1, BATCH), f32), strip(2, width), strip(2, 1, BATCH, f32), strip(2, hidden), strip(2, hidden),
        (
            jax.ShapeDtypeStruct((width, tokens // letters), f32),
            pl.BlockSpec((width, LANES), lambda i: (0, pooled(i))),
        ),
        gathered, gathered, gathered,
        whole((3 * width, width)), whole((width, 3 * width)), whole((width, width)), whole((width, hidden)),
        whole((hidden, width)), whole((outer, width)), whole((width, LANES), f32), whole((width, LANES), f32),
        whole((outer, LANES), f32), whole((outer, LANES), f32),
    ]
    shards = (*first_shards, *second_shards, *word_shards)
    at0 = phase_map(0, FORWARD_HALVES, steps)
    sems = pltpu.SemaphoreType.DMA((2, gather_copies()))
    return pl.pallas_call(
        functools.partial(forward_gather_kernel, letters, steps),
        grid=(starts(FORWARD_HALVES, steps)[3],),
        in_specs=[
            pl.BlockSpec((BATCH, width), lambda i: (at0(i), 0)),
            pl.BlockSpec((1, LANES), lambda i: (0, at0(i) // per)),
        ] + [full_spec(a) for a in shards],
        out_specs=[o[1] for o in outs],
        out_shape=[o[0] for o in outs],
        scratch_shapes=[
            pltpu.VMEM((ny, nx, 2, nz, r + 16, LANES), bf16),
            pltpu.VMEM((ny, nx, 2, nz, 3 * r, LANES), bf16),
            pltpu.VMEM((3, word_rows, word_lanes), bf16),
            pltpu.VMEM((width, width), bf16),
            pltpu.VMEM((hidden, width), bf16),
            pltpu.VMEM((width, hidden), bf16),
            pltpu.VMEM((steps, width, BATCH), bf16),
            pltpu.VMEM((steps, width, BATCH), bf16),
            pltpu.VMEM((steps, width, BATCH), f32),
            pltpu.VMEM((BATCH // letters, BATCH), bf16),
            pltpu.VMEM((BATCH, LANES), bf16),
            pltpu.VMEM((width, BATCH), bf16),
            pltpu.SemaphoreType.DMA((2, nz - 1 + 2 * ny * nx - 1)), sems, sems, sems, sems,
            pltpu.SemaphoreType.DMA((3,)),
        ],
        compiler_params=pltpu.CompilerParams(
            dimension_semantics=("arbitrary",), vmem_limit_bytes=VMEM_BYTES, collective_id=0, has_side_effects=True
        ),
        name="forward_gather",
    )(x, cnt, *shards)


def backward_scatter_kernel(
    letters, steps, dp_ref, tok_ref, ga_ref, gb_ref, wqkv_t, wqkv, wproj, wup, wdown, send0, send1, send2,
    gpool_t, gwga, gwgb, t_ref, o_ref, p_ref, z1_ref, rs1_ref, z2_ref, rs2_ref, m_ref, slope_ref,
    cg_ref, first_sum, second_sum, word_sum,
    gqkv_t, gproj_t, gup, gdown_t, dh1_all, dt_all, do_ref, first_send, second_send, own_sems, *work,
):
    step = pl.program_id(0)
    y, x, c, z = place()
    per = LANES * letters // BATCH
    size = (len(work) - 5) // 4
    work = [work[n * size : (n + 1) * size] for n in range(5)]
    sends = (send0, send1, send2)
    streams = {n: (sends[n], work[n], word_sum.at[n]) for n in range(3)}
    streams["second"] = (second_send, work[3], second_sum)
    streams["first"] = (first_send, work[4], first_sum)
    own = [pltpu.make_async_copy(sends[n].at[:, :, c], work[n][0], own_sems.at[n]) for n in range(3)]

    @pl.when(step == 0)
    def _():
        greet()
        start_all(own)

    @pl.when(step == 1)
    def _():
        greeted()

    def advance(half):
        for name, (send, scratch, total) in streams.items():
            acc = scratch[0]
            stage, add = (direct_stage, direct_sum) if name == "first" else (scatter_stage, scatter_sum)
            events = planned(SCATTER_PLAN, name, steps)
            for n, when in enumerate(events):
                if when == 3 * steps or step_of(when, BACKWARD_HALVES, steps)[1] != half:
                    continue

                @pl.when(step == step_of(when, BACKWARD_HALVES, steps)[0])
                def _():
                    if n == 0:
                        if name == "second":
                            pack_second_grads(second_send, gup, gdown_t, gb_ref, gpool_t)
                        elif name == "first":
                            pack_first_grads(first_send, gqkv_t, gproj_t, ga_ref, wqkv_t, gup, wup, gwga, gwgb)
                    else:
                        arrive_all(stage(n - 1, send, scratch))
                        if n == 1 and name in (0, 1, 2):
                            own[name].wait()
                            mine = lambda b, a, k: acc[b, a, k]
                        else:
                            mine = lambda b, a, k: send[b, a, c, k]
                        add(n - 1, mine, scratch, total)
                    if n < len(events) - 1:
                        start_all(stage(n, send, scratch))

    advance(0)
    _, one, two, end = starts(BACKWARD_HALVES, steps)

    @pl.when(step < steps)
    def _():
        backward_feed(
            step, letters, per, dp_ref, tok_ref, gb_ref, wup, wdown, z2_ref, rs2_ref, m_ref, slope_ref,
            gup, gdown_t, dh1_all, dt_all,
        )

    @pl.when((step >= one) & (step < two))
    def _():
        for j in range(BACKWARD_HALVES[1]):
            if j > 0:
                advance(j)
            backward_attention(
                (step - one) * BACKWARD_HALVES[1] + j, letters, wproj, t_ref, o_ref, p_ref, z1_ref, gqkv_t, gproj_t,
                dh1_all, dt_all, do_ref, j,
            )

    @pl.when(step >= two)
    def _():
        for j in range(BACKWARD_HALVES[2]):
            if j > 0:
                advance(j)
            backward_last((step - two) * BACKWARD_HALVES[2] + j, ga_ref, wqkv, z1_ref, rs1_ref, cg_ref, dh1_all, dt_all, j)

    @pl.when(step == end - 1)
    def _():
        for name, (send, scratch, total) in streams.items():
            if name == "first":
                arrive_all(direct_stage(2, send, scratch))
                direct_sum(2, None, scratch, total)
                sent_all([direct_stage(n, send, scratch) for n in range(3)])
            else:
                sent_all([scatter_stage(n, send, scratch) for n in range(4)])


def backward_scatter(dp, tok, ga, gb, weights, sends, gpool_t, gwga, gwgb, saved, letters):
    wqkv_t, wqkv, wproj, wup, wdown = weights
    t, o, p, z1, rs1, z2, rs2, m, slope = saved
    steps = t.shape[0]
    width, hidden = wup.shape
    per = LANES * letters // BATCH
    ny, nx, nz = sides()
    r = width // nz
    word_rows, word_lanes = sends[0].shape[4:]
    at = [phase_map(n, BACKWARD_HALVES, steps) for n in range(3)]
    words = phase_map(0, BACKWARD_HALVES, steps, per)

    def strip(a, where, many):
        return pl.BlockSpec((many,) + a.shape[1:], lambda i: (where(i), 0, 0))

    def whole(shape):
        return (jax.ShapeDtypeStruct(shape, f32), pl.BlockSpec(shape, lambda i: (0,) * len(shape)))

    def once(a):
        return pl.BlockSpec(a.shape, lambda i: (0,) * a.ndim, pipeline_mode=pl.Buffered(1))

    outs = [
        (jax.ShapeDtypeStruct((steps * BATCH, width), bf16), pl.BlockSpec((BACKWARD_HALVES[2] * BATCH, width), lambda i: (at[2](i), 0))),
        whole((r + 16, LANES)), whole((3 * r, LANES)), whole((3, word_rows, word_lanes)),
    ]
    _, one, two, end = starts(BACKWARD_HALVES, steps)
    either = lambda i: jnp.where(i < two, at[1](i), at[2](i))
    lots = BACKWARD_HALVES[1]
    saved_specs = [
        strip(t, at[1], lots), strip(o, at[1], lots), strip(p, at[1], lots), strip(z1, either, lots),
        strip(rs1, at[2], lots), strip(z2, at[0], 1), strip(rs2, at[0], 1), strip(m, at[0], 1), strip(slope, at[0], 1),
    ]
    return pl.pallas_call(
        functools.partial(backward_scatter_kernel, letters, steps),
        grid=(end,),
        in_specs=[
            pl.BlockSpec((width, LANES), lambda i: (0, words(i))),
            pl.BlockSpec((1, 1, BATCH), lambda i: (at[0](i), 0, 0)),
        ] + [once(a) for a in (ga, gb, *weights)] + [pl.BlockSpec(memory_space=pl.ANY)] * 3
        + [once(a) for a in (gpool_t, gwga, gwgb)] + saved_specs,
        out_specs=[o[1] for o in outs],
        out_shape=[o[0] for o in outs],
        scratch_shapes=[
            pltpu.VMEM((3 * width, width), f32),
            pltpu.VMEM((width, width), f32),
            pltpu.VMEM((width, hidden), f32),
            pltpu.VMEM((width, hidden), f32),
            pltpu.VMEM((steps, width, BATCH), bf16),
            pltpu.VMEM((steps, 3 * width, BATCH), bf16),
            pltpu.VMEM((width, BATCH), bf16),
            pltpu.VMEM((ny, nx, 2, nz, r + 16, LANES), bf16),
            pltpu.VMEM((ny, nx, 2, nz, 3 * r, LANES), bf16),
            pltpu.SemaphoreType.DMA((3,)),
        ] + 3 * scatter_scratch(word_rows, word_lanes) + scatter_scratch(3 * r, LANES) + direct_scratch(r + 16, LANES),
        compiler_params=pltpu.CompilerParams(
            dimension_semantics=("arbitrary",), vmem_limit_bytes=VMEM_BYTES, collective_id=1, has_side_effects=True
        ),
        name="backward_scatter",
    )(dp, tok, ga, gb, *weights, *sends, gpool_t, gwga, gwgb, *saved)


def finish_kernel(
    first, second, words, grad_in, cqkv, cproj_t, cup, cdown_t, cga, cgb, pool, wqkv_t, wproj_t, wup, wdown_t, wga, wgb,
    grad_out,
):
    grad_out[...] = grad_in[...]

    @pl.when(pl.program_id(0) == 0)
    def _():
        r, n, gc, gw = cup.shape[0], cqkv.shape[1], cga.shape[1], wga.shape[1]
        cqkv[...] = first[pl.ds(0, r), :n]
        cproj_t[...] = first[pl.ds(0, r), :].T[n:]
        side = first[pl.ds(r, 8), :]
        cga[...] = side[0:1, :gc]
        cgb[...] = side[0:1, gc : 2 * gc]
        wga[...] = side[0:1, 2 * gc : 2 * gc + gw]
        wgb[...] = side[1:2, :gw]
        cup[...] = second[pl.ds(0, r), :]
        n = cdown_t.shape[0]
        for i in range(cdown_t.shape[1] // LANES):
            cdown_t[:, pl.ds(i * LANES, LANES)] = second[pl.ds(r + i * n, n), :]
        pool[...] = second[pl.ds(2 * r, r), : pool.shape[1]]
        t = words[0].T
        n = wqkv_t.shape[0]
        wqkv_t[...] = t[:n]
        wproj_t[...] = t[n:]
        wup[...] = words[1]
        n, lanes = wdown_t.shape[0], wup.shape[1]
        for i in range(wdown_t.shape[1] // lanes):
            wdown_t[:, pl.ds(i * lanes, lanes)] = words[2, pl.ds(i * n, n), :]


def finish(first, second, words, grad, shapes):
    steps = 2
    moved = pl.BlockSpec((grad.shape[0] // steps, grad.shape[1]), lambda i: (i, 0))
    shapes = [jax.ShapeDtypeStruct(s, f32) for s in shapes]
    return pl.pallas_call(
        finish_kernel,
        grid=(steps,),
        in_specs=[full_spec(a) for a in (first, second, words)] + [moved],
        out_specs=[full_spec(a) for a in shapes] + [moved],
        out_shape=shapes + [jax.ShapeDtypeStruct(grad.shape, grad.dtype)],
        compiler_params=pltpu.CompilerParams(vmem_limit_bytes=32 * 2**20),
        name="finish",
    )(first, second, words, grad)


def gather_all(shards, counts):
    flat = jnp.concatenate([s.reshape(-1) for s in shards])
    packed = lax.all_gather(lax.all_gather(flat, "fsdp", axis=0), "dp", axis=0)
    wide_count, deep_count = packed.shape[:2]
    out, start = [], 0
    for s in shards:
        piece = packed[:, :, start : start + s.size]
        start += s.size
        if s.ndim == 1:
            out.append(piece[:, 0].reshape(-1))
        else:
            r, c = s.shape
            piece = piece.reshape(wide_count, deep_count, r, c).transpose(1, 2, 0, 3)
            out.append(piece.reshape(deep_count * r, wide_count * c))
    return out


def scatter_all(grads, shards):
    wide_count, deep_count = lax.axis_size("dp"), lax.axis_size("fsdp")
    pieces = []
    for g, s in zip(grads, shards):
        g = g.astype(bf16)
        if s.ndim == 1:
            g = jnp.broadcast_to(g.reshape(wide_count, 1, s.size), (wide_count, deep_count, s.size))
        else:
            r, c = s.shape
            g = g.reshape(deep_count, r, wide_count, c).transpose(2, 0, 1, 3)
        pieces.append(g.reshape(wide_count, deep_count, s.size))
    packed = jnp.concatenate(pieces, 2)
    packed = lax.psum_scatter(packed, "dp", scatter_dimension=0, tiled=True)
    packed = lax.psum_scatter(packed, "fsdp", scatter_dimension=1, tiled=True).reshape(-1)
    out, start = [], 0
    for s in shards:
        out.append(packed[start : start + s.size].reshape(s.shape).astype(f32))
        start += s.size
    return out


def shards_plain(
    characters, counts, separators, cotangent, char_qkv, char_proj, char_up, char_down, char_gain_a, char_gain_b,
    pool_proj, word_qkv, word_proj, word_up, word_down, word_gain_a, word_gain_b,
):
    rows, length, letters, width = characters.shape
    char_shards = (char_qkv, char_proj, char_up, char_down, char_gain_a, char_gain_b)
    word_shards = (pool_proj, word_qkv, word_proj, word_up, word_down, word_gain_a, word_gain_b)
    cqkv, cproj, cup, cdown, cga, cgb = gather_all(char_shards, counts)
    wpool, wqkv, wproj, wup, wdown, wga, wgb = gather_all(word_shards, counts)
    x = characters.reshape(length * letters, width)
    tok = jnp.repeat(counts, letters, axis=1).reshape(length * letters // STEP, 1, STEP)
    cga, cgb, wga, wgb = (
        jnp.broadcast_to(g.astype(f32)[:, None], (g.shape[0], LANES)) for g in (cga, cgb, wga, wgb)
    )
    *saved, pool_sum = char_forward(x, tok, counts, cga, cgb, cqkv.T, cproj.T, cup.T, cdown.T, letters)
    word_out, dpool, gpool, gwqkv, gwproj, gwup, gwdown, gwga, gwgb = word_layer(
        pool_sum, counts.astype(f32), separators, cotangent.reshape(length, -1), wga, wgb, wpool, wqkv, wproj, wup, wdown
    )
    word_grads = scatter_all(
        (gpool, gwqkv, gwproj, gwup, gwdown, jnp.sum(gwga, 1), jnp.sum(gwgb, 1)), word_shards
    )
    char_grad, gcqkv, gcproj, gcup, gcdown, gcga, gcgb = char_backward(
        dpool, tok, cga, cgb, cqkv, cproj, cup, cdown, saved, letters
    )
    char_grads = scatter_all(
        (gcqkv, gcproj, gcup, gcdown, jnp.sum(gcga, 1), jnp.sum(gcgb, 1)), char_shards
    )
    return (word_out[None], char_grad.reshape(characters.shape), *char_grads, *word_grads)


def shards_packed(
    characters, counts, separators, cotangent, char_qkv, char_proj, char_up, char_down, char_gain_a, char_gain_b,
    pool_proj, word_qkv, word_proj, word_up, word_down, word_gain_a, word_gain_b,
):
    rows, length, letters, width = characters.shape
    x = characters.reshape(length * letters, width)
    (
        tok, *saved, pool_sum, word0, word1, word2, wqkv_t, wqkv, wproj, wup, wdown, pool_t, cga, cgb, wga, wgb
    ) = forward_gather(
        x, counts, (char_qkv, char_proj.T, char_gain_a, char_gain_b, word_gain_a, word_gain_b), (char_up, char_down.T, pool_proj),
        (word_qkv.T, word_proj.T, word_up, word_down.T), letters,
    )
    shape = word0.shape
    flat = (-1,) + shape[3:]
    word_out, dpool, gpool_t, *sends, gwga, gwgb = word_gathered(
        pool_sum, counts, separators, cotangent.reshape(length, -1), wga, wgb, pool_t,
        *(w.reshape(flat) for w in (word0, word1, word2)),
    )
    char_grad, first, second, words = backward_scatter(
        dpool, tok, cga, cgb, (wqkv_t, wqkv, wproj, wup, wdown), [s.reshape(shape) for s in sends],
        gpool_t, gwga, gwgb, saved, letters,
    )
    shapes = [
        s.shape if s.ndim == 2 else (1, s.shape[0])
        for s in (
            char_qkv, char_proj.T, char_up, char_down.T, char_gain_a, char_gain_b,
            pool_proj, word_qkv.T, word_proj.T, word_up, word_down.T, word_gain_a, word_gain_b,
        )
    ]
    (
        cqkv, cproj_t, cup, cdown_t, cgain_a, cgain_b, pool, gqkv_t, gproj_t, gup, gdown_t, wgain_a, wgain_b, char_grad
    ) = finish(first, second, words, char_grad, shapes)
    return (
        word_out[None], char_grad.reshape(characters.shape), cqkv, cproj_t.T, cup, cdown_t.T, cgain_a[0], cgain_b[0],
        pool, gqkv_t.T, gproj_t.T, gup, gdown_t.T, wgain_a[0], wgain_b[0],
    )


def shards(*arrays):
    char_qkv, char_proj, word_qkv, word_proj = arrays[4], arrays[5], arrays[11], arrays[12]
    tiles = (char_qkv.shape[1] + char_proj.shape[1]) // LANES, (word_qkv.shape[1] + word_proj.shape[1]) // LANES
    return (shards_packed if tiles == (1, 2) else shards_plain)(*arrays)


def solution(mesh):
    rows = ("dp", "fsdp")
    matrix, vector = P("fsdp", "dp"), P("dp")
    data = (P(rows, None, None, None), P(rows, None), P(rows, None), P(rows, None, None))
    block = (matrix,) * 4 + (vector,) * 2
    word = (matrix,) * 5 + (vector,) * 2
    return jax.shard_map(
        shards,
        mesh=mesh,
        in_specs=data + block + word,
        out_specs=(data[3], data[0]) + block + word,
        check_vma=False,
    )
```
